128 devices in a mesh: fsdp: 32 (over y, z, core), ctx: 2 (over x_lo), tp: 2 (over x_hi).
Axes of the slice: x: 4 (x_hi: 2, x_lo: 2; x = x_hi * 2 + x_lo), y: 4, z: 4, core: 2. Of those that a mesh axis runs over, the one named last changes fastest.
Arguments:
- tokens: bfloat16 [32, 1024, 1024], P('fsdp', 'ctx'), may hold values from -6 to 6
- segments: int32 [32, 1024], P('fsdp'), may hold values from 0 to 3, as said below
- cotangent: bfloat16 [32, 1024, 1024], P('fsdp', 'ctx'), may hold values from -6 to 6
- gain_mixer: bfloat16 [1024], P('fsdp'), may hold values from 0.5 to 1.5
- gain_ffn: bfloat16 [1024], P('fsdp'), may hold values from 0.5 to 1.5
- query_proj: bfloat16 [1024, 512], P('fsdp', 'tp'), may hold values from -0.1875 to 0.1875
- key_value_weight: bfloat16 [1024, 2, 128], P('fsdp', None, 'tp'), may hold values from -0.1875 to 0.1875
- attn_out: bfloat16 [512, 1024], P('tp', 'fsdp'), may hold values from -2 to 2
- inner_proj: bfloat16 [1024, 2, 1536], P('fsdp', None, 'tp'), may hold values from -0.1875 to 0.1875
- state_proj: bfloat16 [1024, 256], P('fsdp'), may hold values from -0.1875 to 0.1875
- step_proj: bfloat16 [1024, 24], P('fsdp', 'tp'), may hold values from -0.09375 to 0.09375
- conv_inner: bfloat16 [4, 1536], P(None, 'tp'), may hold values from -3 to 3
- conv_state: bfloat16 [4, 256], replicated, may hold values from -3 to 3
- decay_log: float32 [24], P('tp'), may hold values from 0 to 2.77
- step_bias: float32 [24], P('tp'), may hold values from -6.9 to -2.3
- skip_gain: float32 [24], P('tp'), may hold values from 0.5 to 2
- inner_out: bfloat16 [1536, 1024], P('tp', 'fsdp'), may hold values from -0.15625 to 0.15625
- gate_up: bfloat16 [1024, 2, 2048], P('fsdp', None, 'tp'), may hold values from -0.1875 to 0.1875
- down_proj: bfloat16 [2048, 1024], P('tp', 'fsdp'), may hold values from -0.125 to 0.125
Outputs:
- block_out: bfloat16 [32, 1024, 1024], P('fsdp', 'ctx')
- tokens_grad: float32 [32, 1024, 1024], P('fsdp', 'ctx')
- gain_mixer_grad: float32 [1024], P('fsdp')
- gain_ffn_grad: float32 [1024], P('fsdp')
- query_proj_grad: float32 [1024, 512], P('fsdp', 'tp')
- keyval_proj_grad: float32 [1024, 2, 128], P('fsdp', None, 'tp')
- attn_out_grad: float32 [512, 1024], P('tp', 'fsdp')
- inner_proj_grad: float32 [1024, 2, 1536], P('fsdp', None, 'tp')
- state_proj_grad: float32 [1024, 256], P('fsdp')
- step_proj_grad: float32 [1024, 24], P('fsdp', 'tp')
- conv_inner_grad: float32 [4, 1536], P(None, 'tp')
- conv_state_grad: float32 [4, 256], replicated
- decay_log_grad: float32 [24], P('tp')
- step_bias_grad: float32 [24], P('tp')
- skip_gain_grad: float32 [24], P('tp')
- inner_out_grad: float32 [1536, 1024], P('tp', 'fsdp')
- gate_up_grad: float32 [1024, 2, 2048], P('fsdp', None, 'tp')
- down_proj_grad: float32 [2048, 1024], P('tp', 'fsdp')
The draws below stay inside these ranges and needn't reach their ends.
Inputs may be any that keep to these rules, and one draw needn't show every extreme that they name: `segments`: segment numbers of a sequence start at 0, never fall and rise by at most one from a token to the next; every sequence holds four documents, and each document has at least 60 tokens.
All inputs are finite; a program needn't handle non-finite values.
Results may differ from the reference program's by a relative error of at most 0.029.
Values may be sent and summed in bfloat16 or wider, within the bound.
A program may use at most 192 MiB of HBM per device.

```python
import math
import jax
import jax.numpy as jnp
from jax import lax

MODEL_WIDTH = 1024
QUERY_HEADS = 8
KEY_VALUE_HEADS = 2
HEAD_WIDTH = 64
HM = 24
P_SIZE = 64
N = 128
KC = 4
FF = 2048
LEN = 1024
SEQS = 32


def draw_segments(key, part):
    key = jax.random.fold_in(key, 11)
    subkeys = jax.random.split(key, 3)
    shortest = max(LEN * 60 // 1024, 1)
    margin = LEN // 16
    longest = LEN * 800 // 1024
    middle = LEN // 2
    first_cut = jax.random.randint(subkeys[0], (SEQS,), shortest, middle - margin + 1)
    second_cut = jax.random.randint(subkeys[1], (SEQS,), middle + margin, jnp.minimum(first_cut + longest, LEN - 2 * shortest) + 1)
    third_cut = jax.random.randint(subkeys[2], (SEQS,), second_cut + shortest, LEN - shortest + 1)
    position = jnp.arange(LEN)[None, :]
    return (position >= first_cut[:, None]).astype(jnp.int32) + (position >= second_cut[:, None]).astype(jnp.int32) + (position >= third_cut[:, None]).astype(jnp.int32)


def levels(key, dims, shards, smallest, largest):
    def one(dim, shards_of):
        steps = jax.random.uniform(jax.random.fold_in(jax.random.fold_in(key, 6), dim), (shards_of,), jnp.float32, smallest / len(shards), largest / len(shards))
        return jnp.repeat(jnp.exp(steps), dims[dim] // shards_of).reshape((-1,) + (1,) * (len(dims) - dim - 1))

    level = one(*shards[0])
    for cut in shards[1:]:
        level = level * one(*cut)
    return level


def bell_draw(key, extent, deviation, reach, cuts=(), dtype=jnp.bfloat16):
    entries = deviation * jax.random.normal(key, extent, jnp.float32)
    if cuts:
        entries = entries * levels(key, extent, cuts, -0.22, 0.18)
    return jnp.clip(entries, -reach, reach).astype(dtype)


def setup_inputs(seed: int = 0) -> dict:
    seeds = jax.random.split(jax.random.key(seed), 20)
    return {
        "tokens": bell_draw(seeds[0], (SEQS, LEN, MODEL_WIDTH), 1.0, 6.0, ((0, 32), (1, 2))),
        "segments": draw_segments(jax.random.fold_in(seeds[19], 71), 0),
        "cotangent": bell_draw(seeds[2], (SEQS, LEN, MODEL_WIDTH), 1.0, 6.0, ((0, 32), (1, 2))),
        "gain_mixer": jnp.clip(1.0 + 0.1 * jax.random.normal(seeds[3], (MODEL_WIDTH,), jnp.float32), 0.5, 1.5).astype(jnp.bfloat16),
        "gain_ffn": jnp.clip(1.0 + 0.1 * jax.random.normal(seeds[4], (MODEL_WIDTH,), jnp.float32), 0.5, 1.5).astype(jnp.bfloat16),
        "query_proj": bell_draw(seeds[5], (MODEL_WIDTH, QUERY_HEADS * HEAD_WIDTH), MODEL_WIDTH ** -0.5, 0.1875, ((0, 32), (1, 2))),
        "key_value_weight": bell_draw(seeds[6], (MODEL_WIDTH, 2, KEY_VALUE_HEADS * HEAD_WIDTH), MODEL_WIDTH ** -0.5, 0.1875, ((0, 32), (2, 2))),
        "attn_out": bell_draw(seeds[7], (QUERY_HEADS * HEAD_WIDTH, MODEL_WIDTH), (QUERY_HEADS * HEAD_WIDTH // 64) ** -0.5, 2.0, ((0, 2), (1, 32))),
        "inner_proj": bell_draw(seeds[8], (MODEL_WIDTH, 2, HM * P_SIZE), MODEL_WIDTH ** -0.5, 0.1875, ((0, 32), (2, 2))),
        "state_proj": bell_draw(seeds[9], (MODEL_WIDTH, 2 * N), MODEL_WIDTH ** -0.5, 0.1875, ((0, 32),)),
        "step_proj": bell_draw(seeds[10], (MODEL_WIDTH, HM), (4 * MODEL_WIDTH) ** -0.5, 0.09375, ((0, 32), (1, 2))),
        "conv_inner": bell_draw(seeds[11], (KC, HM * P_SIZE), KC ** -0.5, 3.0, ((1, 2),)),
        "conv_state": bell_draw(seeds[12], (KC, 2 * N), KC ** -0.5, 3.0),
        "decay_log": jnp.clip(2.77 * jax.random.uniform(seeds[13], (HM,), jnp.float32) ** levels(seeds[13], (HM,), ((0, 2),), -0.2, 0.2), 0.0, 2.77),
        "step_bias": jnp.clip(-6.9 + 4.6000001430511475 * jax.random.uniform(seeds[14], (HM,), jnp.float32) ** levels(seeds[14], (HM,), ((0, 2),), -0.2, 0.2), -6.9, -2.3),
        "skip_gain": jnp.clip(0.5 + 1.5 * jax.random.uniform(seeds[15], (HM,), jnp.float32) ** levels(seeds[15], (HM,), ((0, 2),), -0.2, 0.2), 0.5, 2.0),
        "inner_out": bell_draw(seeds[16], (HM * P_SIZE, MODEL_WIDTH), (HM * P_SIZE) ** -0.5, 0.15625, ((0, 2), (1, 32))),
        "gate_up": bell_draw(seeds[17], (MODEL_WIDTH, 2, FF), MODEL_WIDTH ** -0.5, 0.1875, ((0, 32), (2, 2))),
        "down_proj": bell_draw(seeds[18], (FF, MODEL_WIDTH), FF ** -0.5, 0.125, ((0, 2), (1, 32))),
    }


eps_norm = 1e-05
neg_large = -1e+30
rope_base = 100000000000.0
highest = lax.Precision.HIGHEST

@jax.custom_vjp
def reduced_precision(v):
    return lax.optimization_barrier(v.astype(jnp.bfloat16)).astype(jnp.float32)

@jax.custom_vjp
def reduced_backward(v):
    return v

def low_keep(v):
    return (reduced_precision(v), None)

def low_pass(kept, grad):
    return (grad,)

def back_keep(v):
    return (v, None)

def back_low(kept, grad):
    return (reduced_precision(grad),)
reduced_precision.defvjp(low_keep, low_pass)
reduced_backward.defvjp(back_keep, back_low)

def matrix_product(left, right):
    return jnp.dot(left, right, precision=highest, preferred_element_type=jnp.float32)

def rms_norm(values, gain_vec):
    return values * lax.rsqrt(lax.optimization_barrier(jnp.mean(values * values, axis=-1, keepdims=True)) + eps_norm) * gain_vec

def rope_tables(positions, rot_width):
    indices = jnp.arange(rot_width // 2).astype(jnp.float32)
    frequency = jnp.exp(indices * (-2.0 * math.log(rope_base) / rot_width))
    angles = positions[:, None] * frequency[None, :]
    return (jnp.cos(angles), jnp.sin(angles))

def rotary_rotate(vectors, cosine_table, sine_table):
    halfway = vectors.shape[-1] // 2
    front_half = vectors[..., :halfway]
    back_part = vectors[..., halfway:]
    cos_b = cosine_table[:, None, :]
    sin_b = sine_table[:, None, :]
    return jnp.concatenate([front_half * cos_b - back_part * sin_b, back_part * cos_b + front_half * sin_b], axis=-1)

def conv_silu(current, rim_rows, weight, seg_now, seg_rim):
    conv_taps = weight.shape[0]
    span_rows = current.shape[0]
    extended = jnp.concatenate([rim_rows, current], axis=0)
    seg_ext = jnp.concatenate([seg_rim, seg_now], axis=0)
    running = jnp.zeros_like(current)
    for offset in range(conv_taps):
        window = lax.slice_in_dim(extended, offset, offset + span_rows, axis=0)
        same_doc = (lax.slice_in_dim(seg_ext, offset, offset + span_rows, axis=0) == seg_now).astype(jnp.float32)
        running = running + window * weight[offset][None, :] * same_doc[:, None]
    return jax.nn.silu(running)

def span_step(carry, pieces):
    state_now, seg_last = carry
    x_scaled, b_mat, c_mat, log_decay, seg_now = pieces
    span_rows = seg_now.shape[0]
    lower_tri = jnp.arange(span_rows)[:, None] >= jnp.arange(span_rows)[None, :]
    cumulative = jnp.cumsum(log_decay, axis=0)
    same_doc = lower_tri & (seg_now[:, None] == seg_now[None, :])
    decays = jnp.exp(jnp.where(same_doc[:, :, None], cumulative[:, None, :] - cumulative[None, :, :], neg_large))
    intersection = jnp.dot(c_mat, b_mat.T, precision=highest, preferred_element_type=jnp.float32)
    intra_out = jnp.einsum('tsh,shp->thp', decays * intersection[:, :, None], x_scaled, precision=highest)
    carry_on = (seg_now == seg_last).astype(jnp.float32)
    entering = jnp.exp(cumulative) * carry_on[:, None]
    from_state = jnp.einsum('tn,hpn->thp', c_mat, state_now, precision=highest) * entering[:, :, None]
    last_seg = seg_now[span_rows - 1]
    tail_decay = jnp.exp(jnp.where((seg_now == last_seg)[:, None], cumulative[span_rows - 1][None, :] - cumulative, neg_large))
    new_state = state_now * entering[span_rows - 1][:, None, None] + jnp.einsum('shp,sn->hpn', x_scaled * tail_decay[:, :, None], b_mat, precision=highest)
    return ((new_state, last_seg), intra_out + from_state)

def ssd_scan(x_scaled, b_mat, c_mat, log_decay, seg_now, seg_before, state_start):
    total_rows = seg_now.shape[0]
    span_len = math.gcd(128, total_rows)
    pieces = tuple((array.reshape((total_rows // span_len, span_len) + array.shape[1:]) for array in (x_scaled, b_mat, c_mat, log_decay, seg_now)))
    (final_state, last_seg), span_outs = lax.scan(jax.checkpoint(span_step), (state_start, seg_before), pieces)
    return (span_outs.reshape(x_scaled.shape), final_state)

def attend(query_vectors, every_key, every_value, seg_row):
    sequence_length = query_vectors.shape[0]
    block_row_count = min(512, sequence_length)
    query_group_width = QUERY_HEADS // KEY_VALUE_HEADS
    score_scale = HEAD_WIDTH ** (-0.5)
    key_pos = jnp.arange(sequence_length)
    grouped_heads = query_vectors.reshape(sequence_length // block_row_count, block_row_count, KEY_VALUE_HEADS, query_group_width, HEAD_WIDTH)

    def one_block(items):
        query_blk, query_pos, query_seg = items
        scores = jnp.einsum('qkgd,tkd->kgqt', query_blk, every_key, precision=highest) * score_scale
        scores = reduced_backward(scores)
        key_mask = (key_pos[None, :] <= query_pos[:, None]) & (seg_row[None, :] == query_seg[:, None])
        scores = jnp.where(key_mask[None, None], scores, neg_large)
        weights = reduced_precision(jax.nn.softmax(scores, axis=-1))
        mixed = jnp.einsum('kgqt,tkd->qkgd', weights, every_value, precision=highest)
        return mixed.reshape(block_row_count, QUERY_HEADS * HEAD_WIDTH)
    blocks = lax.map(jax.checkpoint(one_block), (grouped_heads, key_pos.reshape(-1, block_row_count), seg_row.reshape(-1, block_row_count)))
    return reduced_precision(reduced_backward(blocks.reshape(sequence_length, QUERY_HEADS * HEAD_WIDTH)))

def layer(residual, seg_row, gain_mixer, gain_ffn, query_proj, key_value_weight, attn_out, inner_proj, state_proj, step_proj, conv_inner, conv_state, decay_log, step_bias, skip_gain, inner_out, gate_up, down_proj):
    sequence_length = residual.shape[0]
    normalized_input = reduced_precision(rms_norm(residual, gain_mixer))
    positions = jnp.arange(sequence_length).astype(jnp.float32)
    cosine_table, sine_table = rope_tables(positions, HEAD_WIDTH)
    query_lin = reduced_backward(matrix_product(normalized_input, query_proj)).reshape(sequence_length, QUERY_HEADS, HEAD_WIDTH)
    key_value_linear = reduced_backward(matrix_product(normalized_input, key_value_weight.reshape(MODEL_WIDTH, 2 * KEY_VALUE_HEADS * HEAD_WIDTH)))
    query_vectors = reduced_precision(rotary_rotate(query_lin, cosine_table, sine_table))
    every_key = reduced_precision(rotary_rotate(key_value_linear[:, :KEY_VALUE_HEADS * HEAD_WIDTH].reshape(sequence_length, KEY_VALUE_HEADS, HEAD_WIDTH), cosine_table, sine_table))
    every_value = reduced_precision(key_value_linear[:, KEY_VALUE_HEADS * HEAD_WIDTH:].reshape(sequence_length, KEY_VALUE_HEADS, HEAD_WIDTH))
    attended = attend(query_vectors, every_key, every_value, seg_row)
    inner_lin = reduced_backward(matrix_product(normalized_input, inner_proj.reshape(MODEL_WIDTH, 2 * HM * P_SIZE)))
    state_lin = reduced_backward(matrix_product(normalized_input, state_proj))
    step_lin = reduced_backward(matrix_product(normalized_input, step_proj))
    conv_in = jnp.concatenate([inner_lin[:, HM * P_SIZE:], state_lin], axis=1)
    rim_rows = jnp.zeros((KC - 1, conv_in.shape[1]), jnp.float32)
    seg_rim = jnp.full((KC - 1,), -1, jnp.int32)
    conv_out = conv_silu(conv_in, rim_rows, jnp.concatenate([conv_inner, conv_state], axis=1), seg_row, seg_rim)
    x_heads = conv_out[:, :HM * P_SIZE].reshape(sequence_length, HM, P_SIZE)
    b_mat = conv_out[:, HM * P_SIZE:HM * P_SIZE + N]
    c_mat = conv_out[:, HM * P_SIZE + N:]
    step_size = jax.nn.softplus(step_lin + step_bias)
    log_decay = step_size * -jnp.exp(decay_log)
    initial = jnp.zeros((HM, P_SIZE, N), jnp.float32)
    ssd_out, final_state = ssd_scan(x_heads * step_size[:, :, None], b_mat, c_mat, log_decay, seg_row, jnp.array(-1, jnp.int32), initial)
    y_flat = (ssd_out + x_heads * skip_gain[None, :, None]).reshape(sequence_length, HM * P_SIZE)
    gated = reduced_precision(y_flat * jax.nn.silu(inner_lin[:, :HM * P_SIZE]))
    mixer_sum = reduced_backward(matrix_product(attended, attn_out) + matrix_product(gated, inner_out))
    mid_stream = residual + mixer_sum
    normed_ffn = reduced_precision(rms_norm(mid_stream, gain_ffn))
    gate_lin = reduced_backward(matrix_product(normed_ffn, gate_up.reshape(MODEL_WIDTH, 2 * FF)))
    hidden_act = reduced_precision(jax.nn.silu(gate_lin[:, :FF]) * gate_lin[:, FF:])
    return mid_stream + matrix_product(hidden_act, down_proj)

def reference(tokens, segments, cotangent, gain_mixer, gain_ffn, query_proj, key_value_weight, attn_out, inner_proj, state_proj, step_proj, conv_inner, conv_state, decay_log, step_bias, skip_gain, inner_out, gate_up, down_proj):
    weights = tuple((weight.astype(jnp.float32) for weight in (gain_mixer, gain_ffn, query_proj, key_value_weight, attn_out, inner_proj, state_proj, step_proj, conv_inner, conv_state, decay_log, step_bias, skip_gain, inner_out, gate_up, down_proj)))

    def one_seq(grad_sums, items):
        tok_row, seg_row, cot_row = items

        def forward(residual, *params):
            return layer(residual, seg_row, *params)
        out_row, pullback = jax.vjp(forward, tok_row.astype(jnp.float32), *weights)
        grad_all = pullback(cot_row.astype(jnp.float32))
        updated = tuple((running + fresh for running, fresh in zip(grad_sums, grad_all[1:])))
        return (updated, (out_row.astype(jnp.bfloat16), grad_all[0]))
    zero_sums = tuple((jnp.zeros_like(weight) for weight in weights))
    grad_sums, (outputs, token_grads) = lax.scan(one_seq, zero_sums, (tokens, segments, cotangent))
    return (outputs, token_grads) + tuple(grad_sums)
```

```python
import functools
import math

import jax
import jax.numpy as jnp
from jax import lax
from jax.experimental import pallas as pl
from jax.experimental.pallas import tpu as pltpu
from jax.sharding import Mesh
from jax.sharding import PartitionSpec as P

f32 = jnp.float32
bf16 = jnp.bfloat16
EPS = 1e-05
NEG = -1e30
ROPE_BASE = 100000000000.0
HEAD_WIDTH = 64
HIGH = lax.Precision.HIGHEST

TOK = 512
WID = 1024
SPAN = 128
SPANS = TOK // SPAN
QW = 256
HEADS = 12
INNER = 768
STATE = 128
CONV = INNER + 2 * STATE
HALO = 16
W1C = 2304
W2C = 1024
W3C = 3072
FFH = 1024
C_Q, C_KV, C_DT, C_Z, C_U = 0, 256, 384, 512, 1280


def vmem(n):
    return [pl.BlockSpec(memory_space=pltpu.VMEM)] * n


def kernel_call(body, outs, scratch=(), mem=56, cost=None):
    def call(*args):
        return pl.pallas_call(
            body,
            out_shape=[jax.ShapeDtypeStruct(s, d) for s, d in outs],
            in_specs=vmem(len(args)),
            out_specs=vmem(len(outs)),
            scratch_shapes=list(scratch),
            compiler_params=pltpu.CompilerParams(vmem_limit_bytes=mem * 1024 * 1024),
            cost_estimate=cost,
        )(*args)

    return call


def nt(a, b):
    return lax.dot_general(a, b, (((1,), (1,)), ((), ())), preferred_element_type=f32)


def tn(a, b):
    return lax.dot_general(a, b, (((0,), (0,)), ((), ())), preferred_element_type=f32)


def nn(a, b):
    return jnp.dot(a, b, preferred_element_type=f32)


def split_halves(v):
    hi = v.astype(bf16)
    return hi, (v - hi.astype(f32)).astype(bf16)


def head_matrix(rows, columns):
    row = lax.broadcasted_iota(jnp.int32, (rows, columns), 0)
    col = lax.broadcasted_iota(jnp.int32, (rows, columns), 1)
    return row, col


def spread(v):
    row, col = head_matrix(128, INNER)
    e = jnp.where(row == col // 64, 1.0, 0.0).astype(bf16)
    hi, lo = split_halves(v)
    return nn(hi, e) + nn(lo, e)


def gathered_heads(v):
    row, col = head_matrix(INNER, 128)
    e = jnp.where(row // 64 == col, 1.0, 0.0).astype(bf16)
    hi, lo = split_halves(v)
    return nn(hi, e) + nn(lo, e)


def low_half(shape):
    return lax.broadcasted_iota(jnp.int32, shape, len(shape) - 1) % 128 < 64


def sigmoid(v):
    return 1.0 / (1.0 + jnp.exp(-v))


def turned(v, cos, sin):
    lane = lax.broadcasted_iota(jnp.int32, v.shape, 1) % 64
    w = v.shape[1]
    swapped = jnp.where(lane < 32, pltpu.roll(v, w - 32, 1), pltpu.roll(v, 32, 1))
    return v * cos + jnp.where(lane < 32, -swapped, swapped) * sin


def unit_rows(v):
    r = lax.rsqrt(jnp.mean(v * v, axis=1, keepdims=True) + EPS)
    return v * r, r


def project_body(
    tok, prior, w1, gain, cos, sin, cosp, sinp, normed, q, k2, v2, k2p, v2p, z, cin, step, norm_p
):
    g = gain[...]
    normed[...] = (unit_rows(tok[...].astype(f32))[0] * g).astype(bf16)
    norm_p[...] = (unit_rows(prior[...].astype(f32))[0] * g).astype(bf16)
    lin = nn(normed[...], w1[:, 0:256])
    c, s = cos[...], sin[...]
    for i in range(2):
        cols = slice(128 * i, 128 * i + 128)
        q[:, cols] = turned(lin[:, cols], c, s).astype(bf16)
    low = low_half((TOK, 128))

    def pair(block, cc, ss, kk, vv):
        rot = turned(block, cc, ss)
        shifted = pltpu.roll(rot, 64, 1)
        kk[...] = jnp.where(low, rot, shifted).astype(bf16)
        flat = pltpu.roll(block, 64, 1)
        vv[...] = jnp.where(low, flat, block).astype(bf16)

    lin = nn(normed[...], w1[:, 256:512])
    pair(lin[:, 0:128], c, s, k2, v2)
    step[...] = lin[:, 128:256]
    pair(nn(norm_p[...], w1[:, 256:384]), cosp[...], sinp[...], k2p, v2p)

    @pl.loop(0, 3)
    def _(j):
        at = pl.ds(pl.multiple_of(C_Z + j * 256, 256), 256)
        to = pl.ds(pl.multiple_of(j * 256, 256), 256)
        z[:, to] = nn(normed[...], w1[:, at])

    @pl.loop(0, 4)
    def _(j):
        at = pl.ds(pl.multiple_of(C_U + j * 256, 256), 256)
        to = pl.ds(pl.multiple_of(j * 256, 256), 256)
        cin[0:HALO, to] = nn(norm_p[TOK - HALO : TOK, :], w1[:, at])
        cin[HALO : HALO + TOK, to] = nn(normed[...], w1[:, at])


project = kernel_call(
    project_body,
    [
        ((TOK, WID), bf16),
        ((TOK, QW), bf16),
        ((TOK, 128), bf16),
        ((TOK, 128), bf16),
        ((TOK, 128), bf16),
        ((TOK, 128), bf16),
        ((TOK, INNER), f32),
        ((HALO + TOK, CONV), f32),
        ((TOK, 128), f32),
    ],
    [pltpu.VMEM((TOK, WID), bf16)],
)


def own_bias(rows, start, seg_col, seg_row):
    end = start + rows
    query = lax.broadcasted_iota(jnp.int32, (rows, end), 0) + start
    key = lax.broadcasted_iota(jnp.int32, (rows, end), 1)
    keep = (key <= query) & (seg_col[start:end, 0:1] == seg_row[0:1, TOK : TOK + end])
    return keep


QB = 256


def attend_body(q, k2, v2, k2p, v2p, seg_col, seg_row, out, lse):
    low = low_half((QB, 128))
    for b in range(TOK // QB):
        start, end = b * QB, (b + 1) * QB
        keep = own_bias(QB, start, seg_col, seg_row)
        keep_p = seg_col[start:end, 0:1] == seg_row[0:1, 0:TOK]
        logs = []
        for pair in range(2):
            cols = slice(128 * pair, 128 * pair + 128)
            qp = q[start:end, cols]
            halves = []
            for side in range(2):
                mine = low if side == 0 else ~low
                qh = jnp.where(mine, qp.astype(f32) * 0.125, 0.0).astype(bf16)
                s1 = jnp.where(keep, nt(qh, k2[0:end, :]), NEG)
                s0 = jnp.where(keep_p, nt(qh, k2p[...]), NEG)
                m = jnp.maximum(
                    jnp.max(s1, axis=1, keepdims=True), jnp.max(s0, axis=1, keepdims=True)
                )
                p1, p0 = jnp.exp(s1 - m), jnp.exp(s0 - m)
                total = jnp.sum(p1, axis=1, keepdims=True) + jnp.sum(p0, axis=1, keepdims=True)
                o = nn(p1.astype(bf16), v2[0:end, :]) + nn(p0.astype(bf16), v2p[...])
                halves.append(o / total)
                logs.append(m + jnp.log(total))
            out[start:end, cols] = jnp.where(low, halves[0], halves[1]).astype(bf16)
        lane = lax.broadcasted_iota(jnp.int32, (QB, 128), 1)
        kept = jnp.zeros((QB, 128), f32)
        for h in range(4):
            kept = jnp.where(lane == h, logs[h], kept)
        lse[start:end, :] = kept


attend = kernel_call(attend_body, [((TOK, QW), bf16), ((TOK, 128), f32)])


def attend_back_body(
    q, k2, v2, k2p, v2p, seg_col, seg_row, lse, dout, cos, sin, dq, dkv, dkv_p, dk_s, dv_s, dkp_s, dvp_s
):
    low = low_half((QB, 128))
    for ref in (dk_s, dv_s, dkp_s, dvp_s):
        ref[...] = jnp.zeros_like(ref)
    for b in range(TOK // QB):
        start, end = b * QB, (b + 1) * QB
        keep = own_bias(QB, start, seg_col, seg_row)
        keep_p = seg_col[start:end, 0:1] == seg_row[0:1, 0:TOK]
        for pair in range(2):
            cols = slice(128 * pair, 128 * pair + 128)
            qp = q[start:end, cols]
            dop = dout[start:end, cols]
            halves = []
            for side in range(2):
                mine = low if side == 0 else ~low
                qh = jnp.where(mine, qp.astype(f32) * 0.125, 0.0).astype(bf16)
                doh = jnp.where(mine, dop.astype(f32), 0.0).astype(bf16)
                h = 2 * pair + side
                log_total = lse[start:end, h : h + 1]
                p1 = jnp.exp(jnp.where(keep, nt(qh, k2[0:end, :]), NEG) - log_total)
                p0 = jnp.exp(jnp.where(keep_p, nt(qh, k2p[...]), NEG) - log_total)
                dp1 = nt(doh, v2[0:end, :])
                dp0 = nt(doh, v2p[...])
                delta = jnp.sum(p1 * dp1, axis=1, keepdims=True) + jnp.sum(
                    p0 * dp0, axis=1, keepdims=True
                )
                ds1 = (p1 * (dp1 - delta)).astype(bf16)
                ds0 = (p0 * (dp0 - delta)).astype(bf16)
                dv_s[0:end, :] += tn(p1.astype(bf16), doh)
                dvp_s[...] += tn(p0.astype(bf16), doh)
                dk_s[0:end, :] += tn(ds1, qh)
                dkp_s[...] += tn(ds0, qh)
                halves.append(nn(ds1, k2[0:end, :]) + nn(ds0, k2p[...]))
            dqp = jnp.where(low, halves[0], halves[1]) * 0.125
            dq[start:end, cols] = turned(dqp, cos[start:end, :], -sin[start:end, :]).astype(bf16)
    low = low_half((TOK, 128))

    def joined(dk, dv):
        dk, dv = dk[...], dv[...]
        return jnp.where(low, dk + pltpu.roll(dk, 64, 1), dv + pltpu.roll(dv, 64, 1))

    dkv[...] = joined(dk_s, dv_s)
    dkv_p[...] = joined(dkp_s, dvp_s).astype(bf16)


attend_back = kernel_call(
    attend_back_body,
    [((TOK, QW), bf16), ((TOK, 128), f32), ((TOK, 128), bf16)],
    [pltpu.VMEM((TOK, 128), f32)] * 4,
)


def tap_mask(seg_ext, k):
    now = seg_ext[HALO : HALO + TOK, 0:1]
    at = HALO - 3 + k
    return jnp.where(seg_ext[at : at + TOK, 0:1] == now, 1.0, 0.0)


def lower_ones():
    row, col = head_matrix(SPAN, SPAN)
    return jnp.where(row >= col, 1.0, 0.0)


def rows_of(c):
    return slice(c * SPAN, (c + 1) * SPAN)


def mixer_in_body(cin, taps, step, bias, rate, seg_ext, pre, dt, cum, last):
    run = jnp.zeros((TOK, CONV), f32)
    for k in range(4):
        at = HALO - 3 + k
        run = run + cin[at : at + TOK, :] * taps[k : k + 1, :] * tap_mask(seg_ext, k)
    pre[...] = run
    lane = lax.broadcasted_iota(jnp.int32, (TOK, 128), 1)
    steps = step[...] + bias[...]
    soft = jnp.maximum(steps, 0.0) + jnp.log(1.0 + jnp.exp(-jnp.abs(steps)))
    dt[...] = jnp.where(lane < HEADS, soft, 0.0)
    tri = lower_ones()
    state = jnp.zeros((STATE, INNER), f32)
    for c in range(SPANS):
        rows = rows_of(c)
        own_dt = dt[rows, :]
        total = jnp.dot(tri, own_dt * rate[...], precision=HIGH, preferred_element_type=f32)
        cum[rows, :] = total
        out = pre[rows, 0 : INNER + STATE]
        out = out * sigmoid(out)
        seg = seg_ext[HALO + c * SPAN : HALO + (c + 1) * SPAN, 0:1]
        seg_last = seg[SPAN - 1 : SPAN, :]
        end = total[SPAN - 1 : SPAN, :]
        tail = jnp.where(seg == seg_last, jnp.exp(jnp.minimum(end - total, 0.0)), 0.0) * own_dt
        fresh = tn(out[:, INNER:].astype(bf16), (out[:, 0:INNER] * spread(tail)).astype(bf16))
        if c == 0:
            state = fresh
        else:
            seg_prev = seg_ext[HALO + c * SPAN - 1 : HALO + c * SPAN, 0:1]
            keep = jnp.where(seg_last == seg_prev, jnp.exp(end), 0.0)
            state = state * spread(jnp.broadcast_to(keep, (8, 128)))[0:1, :] + fresh
    last[...] = state.astype(bf16)


mixer_in = kernel_call(
    mixer_in_body,
    [
        ((TOK, CONV), f32),
        ((TOK, 128), f32),
        ((TOK, 128), f32),
        ((STATE, INNER), bf16),
    ],
)


def span_parts(c, cum, seg_ext):
    total = cum[rows_of(c), :]
    seg = seg_ext[HALO + c * SPAN : HALO + (c + 1) * SPAN, 0:1]
    seg_last = seg[SPAN - 1 : SPAN, :]
    seg_prev = seg_ext[HALO + c * SPAN - 1 : HALO + c * SPAN, 0:1]
    end = total[SPAN - 1 : SPAN, :]
    entering = jnp.where(seg == seg_prev, jnp.exp(total), 0.0)
    tail = jnp.where(seg == seg_last, jnp.exp(jnp.minimum(end - total, 0.0)), 0.0)
    return total, entering, tail


def span_bias(c, seg_ext, seg_row):
    row, col = head_matrix(SPAN, SPAN)
    seg = seg_ext[HALO + c * SPAN : HALO + (c + 1) * SPAN, 0:1]
    other = seg_row[0:1, TOK + c * SPAN : TOK + (c + 1) * SPAN]
    return jnp.where((row >= col) & (seg == other), 0.0, NEG)


def mixer_out_body(
    pre, dt, cum, seg_ext, seg_row, first, z, skip, y, gated, states, sc_state
):
    sc_state[...] = first[...].astype(f32)
    low2 = low_half((SPAN, 128))
    for c in range(SPANS):
        rows = rows_of(c)
        total, entering, tail = span_parts(c, cum, seg_ext)
        out = pre[rows, :]
        out = out * sigmoid(out)
        x = out[:, 0:INNER]
        b = out[:, INNER : INNER + STATE].astype(bf16)
        cm = out[:, INNER + STATE :].astype(bf16)
        own_dt = dt[rows, :]
        xs = x * spread(own_dt)
        state = sc_state[...]
        state_b = state.astype(bf16)
        states[c] = state_b
        wide_in = spread(entering)
        run = nn(cm, state_b) * wide_in + x * skip[...]
        inter = nt(cm, b)
        bias = span_bias(c, seg_ext, seg_row)
        total_t = total.T
        gate = z[rows, :]
        gate = gate * sigmoid(gate)
        for pair in range(HEADS // 2):
            cols = slice(128 * pair, 128 * pair + 128)
            parts = []
            for side in range(2):
                h = 2 * pair + side
                decay = jnp.exp(total[:, h : h + 1] - total_t[h : h + 1, :] + bias)
                parts.append((decay * inter).astype(bf16))
            xp = xs[:, cols]
            stack = jnp.concatenate(
                [jnp.where(low2, xp, 0.0).astype(bf16), jnp.where(low2, 0.0, xp).astype(bf16)], axis=0
            )
            yp = run[:, cols] + nn(jnp.concatenate(parts, axis=1), stack)
            y[rows, cols] = yp
            gated[rows, cols] = (yp * gate[:, cols]).astype(bf16)
        if c < SPANS - 1:
            sc_state[...] = state * wide_in[SPAN - 1 : SPAN, :] + tn(
                b, (xs * spread(tail)).astype(bf16)
            )


mixer_out = kernel_call(
    mixer_out_body,
    [((TOK, INNER), f32), ((TOK, INNER), bf16), ((SPANS, STATE, INNER), bf16)],
    [pltpu.VMEM((STATE, INNER), f32)],
)


def mixer_back_in_body(dgated, z, y, pre, cum, seg_ext, dy, dz, first):
    state = jnp.zeros((STATE, INNER), f32)
    for c in reversed(range(SPANS)):
        rows = rows_of(c)
        total, entering, tail = span_parts(c, cum, seg_ext)
        gate = z[rows, :]
        sig = sigmoid(gate)
        grad = dgated[rows, :]
        own = grad * (gate * sig)
        dy[rows, :] = own
        dz[rows, :] = (grad * y[rows, :] * (sig * (1.0 + gate * (1.0 - sig)))).astype(bf16)
        cm = pre[rows, INNER + STATE :]
        cm = (cm * sigmoid(cm)).astype(bf16)
        wide_in = spread(entering)
        fresh = tn(cm, (own * wide_in).astype(bf16))
        state = fresh if c == SPANS - 1 else state * wide_in[SPAN - 1 : SPAN, :] + fresh
    first[...] = state.astype(bf16)


mixer_back_in = kernel_call(
    mixer_back_in_body,
    [((TOK, INNER), f32), ((TOK, INNER), bf16), ((STATE, INNER), bf16)],
)


def mixer_back_body(
    dy, pre, dt, cum, seg_ext, seg_row, states, last, skip, rate, step, bias,
    dpre, dstep, heads, sc_state,
):
    sc_state[...] = last[...].astype(f32)
    low2 = low_half((SPAN, 128))
    lane = lax.broadcasted_iota(jnp.int32, (SPAN, 128), 1)
    tri = lower_ones()
    sum_decay = jnp.zeros((1, 128), f32)
    sum_bias = jnp.zeros((1, 128), f32)
    sum_skip = jnp.zeros((1, 128), f32)
    for c in reversed(range(SPANS)):
        rows = rows_of(c)
        total, entering, tail = span_parts(c, cum, seg_ext)
        lin = pre[rows, :]
        sig = sigmoid(lin)
        out = lin * sig
        slope = sig * (1.0 + lin * (1.0 - sig))
        x = out[:, 0:INNER]
        b = out[:, INNER : INNER + STATE].astype(bf16)
        cm = out[:, INNER + STATE :].astype(bf16)
        own_dt = dt[rows, :]
        wide_dt = spread(own_dt)
        xs = x * wide_dt
        grad = dy[rows, :]
        wide_in = spread(entering)
        wide_tail = spread(tail)
        dstate = sc_state[...]
        dstate_b = dstate.astype(bf16)
        state_b = states[c]
        gin = grad * wide_in
        gin_b = gin.astype(bf16)
        y_state = nn(cm, state_b)
        xt = xs * wide_tail
        xt_b = xt.astype(bf16)
        from_state = nn(b, dstate_b)
        dcm = nt(gin_b, state_b)
        db = nt(xt_b, dstate_b)
        dcum = gathered_heads(gin * y_state)
        moved = gathered_heads(xt * from_state)
        kept = jnp.sum(dstate * state_b.astype(f32), axis=0, keepdims=True)
        kept = kept * wide_in[SPAN - 1 : SPAN, :]
        kept = gathered_heads(jnp.broadcast_to(kept, (8, INNER)))[0:1, :]
        at_end = jnp.sum(moved, axis=0, keepdims=True) + kept
        sub = lax.broadcasted_iota(jnp.int32, (SPAN, 128), 0)
        dcum = dcum - moved + jnp.where(sub == SPAN - 1, at_end, 0.0)
        sc_state[...] = dstate * wide_in[SPAN - 1 : SPAN, :] + tn(cm, gin_b)
        inter = nt(cm, b)
        bias_m = span_bias(c, seg_ext, seg_row)
        total_t = total.T
        dinter = jnp.zeros((SPAN, SPAN), f32)
        col_sums = jnp.zeros((128, SPAN), f32)
        sub_t = lax.broadcasted_iota(jnp.int32, (128, SPAN), 0)
        ddt = jnp.zeros((SPAN, 128), f32)
        dskip = jnp.zeros((SPAN, 128), f32)
        for pair in range(HEADS // 2):
            cols = slice(128 * pair, 128 * pair + 128)
            gp, xp = grad[:, cols], xs[:, cols]
            gp_b, xp_b = gp.astype(bf16), xp.astype(bf16)
            stack = jnp.concatenate(
                [jnp.where(low2, gp, 0.0).astype(bf16), jnp.where(low2, 0.0, gp).astype(bf16)], axis=0
            )
            dm = nt(stack, xp_b)
            parts = []
            for side in range(2):
                h = 2 * pair + side
                decay = jnp.exp(total[:, h : h + 1] - total_t[h : h + 1, :] + bias_m)
                dmh = dm[side * SPAN : (side + 1) * SPAN, :] * decay
                dinter = dinter + dmh
                weight = decay * inter
                parts.append(weight.astype(bf16))
                q = dmh * inter
                dcum = dcum + jnp.where(lane == h, jnp.sum(q, axis=1, keepdims=True), 0.0)
                col_sums = col_sums + jnp.where(sub_t == h, jnp.sum(q, axis=0, keepdims=True), 0.0)
            both = tn(jnp.concatenate(parts, axis=1), gp_b)
            dxs = jnp.where(low2, both[0:SPAN, :], both[SPAN:, :]) + from_state[:, cols] * wide_tail[:, cols]
            xo = x[:, cols]
            dx = dxs * wide_dt[:, cols] + gp * skip[:, cols]
            dpre[rows, cols] = dx * slope[:, cols]
            pick_row, pick_col = head_matrix(128, 128)
            pick = jnp.where(pick_col == 2 * pair + pick_row // 64, 1.0, 0.0).astype(bf16)
            hi, lo = split_halves(dxs * xo)
            ddt = ddt + nn(hi, pick) + nn(lo, pick)
            hi, lo = split_halves(gp * xo)
            dskip = dskip + nn(hi, pick) + nn(lo, pick)
        dinter_b = dinter.astype(bf16)
        dcm = dcm + nn(dinter_b, b)
        db = db + tn(dinter_b, cm)
        dpre[rows, INNER : INNER + STATE] = db * slope[:, INNER : INNER + STATE]
        dpre[rows, INNER + STATE :] = dcm * slope[:, INNER + STATE :]
        dcum = dcum - col_sums.T
        dlog = lax.dot_general(
            tri, dcum, (((0,), (0,)), ((), ())), precision=HIGH, preferred_element_type=f32
        )
        ddt = ddt + dlog * rate[...]
        dsp = jnp.where(lane < HEADS, ddt * sigmoid(step[rows, :] + bias[...]), 0.0)
        dstep[rows, :] = dsp.astype(bf16)
        sum_decay = sum_decay + jnp.sum(dlog * own_dt, axis=0, keepdims=True)
        sum_bias = sum_bias + jnp.sum(dsp, axis=0, keepdims=True)
        sum_skip = sum_skip + jnp.sum(dskip, axis=0, keepdims=True)
    sub8 = lax.broadcasted_iota(jnp.int32, (8, 128), 0)
    heads[...] = jnp.where(
        sub8 == 0,
        sum_decay * rate[...],
        jnp.where(sub8 == 1, sum_bias, jnp.where(sub8 == 2, sum_skip, 0.0)),
    )


mixer_back = kernel_call(
    mixer_back_body,
    [((TOK, CONV), f32), ((TOK, 128), bf16), ((8, 128), f32)],
    [pltpu.VMEM((STATE, INNER), f32)],
)


def inputs_back_body(
    dpre, dpre_next, cin, taps, seg_ext, seg_next, dkv, dkv_back, cos, sin, dq, dstep, dz,
    grads, dtaps, ext,
):
    ext[0:TOK, :] = dpre[...]
    ext[TOK : TOK + 8, :] = dpre_next[...]
    run = jnp.zeros((TOK, CONV), f32)
    now = seg_next[0:TOK, 0:1]
    sub = lax.broadcasted_iota(jnp.int32, (8, CONV), 0)
    taken = jnp.zeros((8, CONV), f32)
    for k in range(4):
        ahead = 3 - k
        same = jnp.where(seg_next[ahead : ahead + TOK, 0:1] == now, 1.0, 0.0)
        run = run + ext[ahead : ahead + TOK, :] * taps[k : k + 1, :] * same
        at = HALO - 3 + k
        part = dpre[...] * cin[at : at + TOK, :] * tap_mask(seg_ext, k)
        taken = taken + jnp.where(sub == k, jnp.sum(part, axis=0, keepdims=True), 0.0)
    dtaps[...] = taken
    grads[:, C_U:] = run.astype(bf16)
    grads[:, C_Q : C_Q + QW] = dq[...]
    both = dkv[...] + dkv_back[...].astype(f32)
    low = low_half((TOK, 128))
    grads[:, C_KV : C_KV + 128] = jnp.where(low, turned(both, cos[...], -sin[...]), both).astype(bf16)
    grads[:, C_DT : C_DT + 128] = dstep[...]
    grads[:, C_Z : C_Z + INNER] = dz[...]


inputs_back = kernel_call(
    inputs_back_body,
    [((TOK, W1C), bf16), ((8, CONV), f32)],
    [pltpu.VMEM((TOK + 8, CONV), f32)],
)


def swapped(block, axis):
    return lax.ppermute(block, axis, [(0, 1), (1, 0)])


def pair_sum(block, axis):
    return block.astype(f32) + swapped(block, axis).astype(f32)


def rope_tables(positions):
    indices = jnp.arange(HEAD_WIDTH // 2).astype(f32)
    frequency = jnp.exp(indices * (-2.0 * math.log(ROPE_BASE) / HEAD_WIDTH))
    angles = positions[:, None] * frequency[None, :]
    return (jnp.tile(jnp.cos(angles), (1, 4)), jnp.tile(jnp.sin(angles), (1, 4)))


def norm_back(v, gain_row, dh):
    r = lax.rsqrt(jnp.mean(v * v, axis=1, keepdims=True) + EPS)
    scaled = dh * gain_row
    dv = r * scaled - v * (r * r * r) * jnp.mean(v * scaled, axis=1, keepdims=True)
    return dv, jnp.sum(dh * v * r, axis=0)


def lanes(vector):
    return jnp.pad(vector, (0, 128 - vector.shape[0]))[None, :]


def shards(
    tokens, segments, cotangent, gain_mixer, gain_ffn, query_proj, key_value_weight, attn_out,
    inner_proj, state_proj, step_proj, conv_inner, conv_state, decay_log, step_bias, skip_gain,
    inner_out, gate_up, down_proj,
):
    rows = query_proj.shape[0]
    ctx = lax.axis_index("ctx")
    tok = tokens.reshape(TOK, WID)
    prior = lax.ppermute(tok, "ctx", [(0, 1)])
    blocks = (
        jnp.concatenate(
            [
                query_proj,
                key_value_weight.reshape(rows, 128),
                step_proj,
                gain_mixer[:, None],
                gain_ffn[:, None],
                jnp.zeros((rows, 114), bf16),
                inner_proj.reshape(rows, 2 * INNER),
                state_proj,
            ],
            axis=1,
        ),
        jnp.concatenate([attn_out.T, inner_out.T], axis=1),
        jnp.concatenate([gate_up.reshape(rows, 2 * FFH), down_proj.T], axis=1),
    )
    w1, w2, w3 = (lax.all_gather(b, "fsdp", axis=0, tiled=True) for b in blocks)
    gains = w1[:, C_DT + HEADS : C_DT + HEADS + 2].astype(f32).T
    gain1, gain2 = gains[0:1], gains[1:2]

    start = ctx * TOK
    cos, sin = rope_tables((start + jnp.arange(TOK)).astype(f32))
    cosp, sinp = rope_tables((start - TOK + jnp.arange(TOK)).astype(f32))
    seg = segments.reshape(-1)
    late = ctx > 0
    seg_now = lax.dynamic_slice_in_dim(seg, start, TOK)
    seg_prior = jnp.where(late, seg[0:TOK], -1)
    seg_after = jnp.where(late, -2, seg[TOK : TOK + 8])
    seg_row = jnp.concatenate([seg_prior, seg_now])[None, :]
    seg_ext = jnp.concatenate([seg_prior[TOK - HALO :], seg_now])[:, None]
    seg_next = jnp.concatenate([seg_now, seg_after])[:, None]
    seg_col = seg_now[:, None]
    taps = jnp.concatenate([conv_inner, conv_state], axis=1).astype(f32)
    bias = lanes(step_bias)
    rate = lanes(-jnp.exp(decay_log))
    skip = jnp.repeat(skip_gain, 64)[None, :]

    normed, q, k2, v2, k2p, v2p, z, cin, step = project(tok, prior, w1, gain1, cos, sin, cosp, sinp)
    pre, dt, cum, last = mixer_in(cin, taps, step, bias, rate, seg_ext)
    first = lax.ppermute(last, "ctx", [(0, 1)])
    attended, lse = attend(q, k2, v2, k2p, v2p, seg_col, seg_row)
    y, gated, states = mixer_out(pre, dt, cum, seg_ext, seg_row, first, z, skip)

    mixed = jnp.concatenate([attended, gated], axis=1)
    branch = pair_sum(nt(mixed, w2).astype(bf16), "tp")
    mid = tok.astype(f32) + branch

    normed2 = (unit_rows(mid)[0] * gain2).astype(bf16)
    wgu, wdown = w3[:, 0 : 2 * FFH], w3[:, 2 * FFH :]
    gu = nn(normed2, wgu)
    gate, up = gu[:, :FFH], gu[:, FFH:]
    sig = sigmoid(gate)
    silu = gate * sig
    act = (silu * up).astype(bf16)
    cot = cotangent.reshape(TOK, WID)
    dact = nn(cot, wdown)
    dgate = dact * up * sig * (1.0 + gate * (1.0 - sig))
    dgu = jnp.concatenate([dgate, dact * silu], axis=1).astype(bf16)
    dnormed2 = pair_sum(nt(dgu, wgu).astype(bf16), "tp")
    block_out = (mid + pair_sum(nt(act, wdown).astype(bf16), "tp")).astype(bf16)
    dmid, dgain2 = norm_back(mid, gain2, dnormed2)
    grad_mid = cot.astype(f32) + dmid
    dmix = grad_mid.astype(bf16)

    w3_grad = jnp.concatenate([tn(normed2, dgu), tn(cot, act)], axis=1).astype(bf16)
    w3_part = lax.psum_scatter(w3_grad, "fsdp", scatter_dimension=0, tiled=True)

    dmixed = nn(dmix, w2)
    dattended, dgated = dmixed[:, :QW].astype(bf16), dmixed[:, QW:]
    dy, dz, dfirst = mixer_back_in(dgated, z, y, pre, cum, seg_ext)
    dlast = lax.ppermute(dfirst, "ctx", [(1, 0)])
    dq, dkv, dkv_p = attend_back(
        q, k2, v2, k2p, v2p, seg_col, seg_row, lse, dattended, cos, sin
    )
    dkv_back = lax.ppermute(dkv_p, "ctx", [(1, 0)])
    dpre, dstep, heads = mixer_back(
        dy, pre, dt, cum, seg_ext, seg_row, states, dlast, skip, rate, step, bias
    )
    dpre_next = lax.ppermute(dpre[0:8], "ctx", [(1, 0)])
    grads, dtaps = inputs_back(
        dpre, dpre_next, cin, taps, seg_ext, seg_next, dkv, dkv_back, cos, sin, dq, dstep, dz
    )
    dnormed = pair_sum(nt(grads, w1).astype(bf16), "tp")
    dtok, dgain1 = norm_back(tok.astype(f32), gain1, dnormed)
    tokens_grad = grad_mid + dtok

    w1_grad = tn(normed, grads).astype(bf16)
    w2_grad = tn(dmix, mixed).astype(bf16)
    w12_part = lax.psum_scatter(
        jnp.concatenate([w1_grad, w2_grad], axis=1), "fsdp", scatter_dimension=0, tiled=True
    )
    parts = pair_sum(jnp.concatenate([w12_part, w3_part], axis=1), "ctx")
    bc = pair_sum(parts[:, C_U + INNER : W1C].astype(bf16), "tp")

    small = jnp.concatenate([dtaps[0:4].reshape(-1), heads[0:3].reshape(-1), dgain1, dgain2])
    small = lax.psum(small, ("fsdp", "ctx"))
    taps_sum = small[0 : 4 * CONV].reshape(4, CONV)
    heads_sum = small[4 * CONV : 4 * CONV + 384].reshape(3, 128)
    gains_sum = small[4 * CONV + 384 :].reshape(2, -1, rows)
    mine = lax.dynamic_index_in_dim(gains_sum, lax.axis_index("fsdp"), 1, keepdims=False)
    state_taps = pair_sum(taps_sum[:, INNER:], "tp")

    at2, at3 = W1C, W1C + W2C
    return (
        block_out[None],
        tokens_grad[None],
        mine[0],
        mine[1],
        parts[:, 0:QW],
        parts[:, C_KV : C_KV + 128].reshape(rows, 2, 64),
        parts[:, at2 : at2 + QW].T,
        parts[:, C_Z : C_Z + 2 * INNER].reshape(rows, 2, INNER),
        bc,
        parts[:, C_DT : C_DT + HEADS],
        taps_sum[:, :INNER],
        state_taps,
        heads_sum[0, :HEADS],
        heads_sum[1, :HEADS],
        heads_sum[2, :HEADS],
        parts[:, at2 + QW : at3].T,
        parts[:, at3 : at3 + 2 * FFH].reshape(rows, 2, FFH),
        parts[:, at3 + 2 * FFH :].T,
    )


def solution(mesh):
    return jax.shard_map(
        shards,
        mesh=mesh,
        in_specs=(
            P("fsdp", "ctx", None), P("fsdp", None), P("fsdp", "ctx", None), P("fsdp"), P("fsdp"),
            P("fsdp", "tp"), P("fsdp", None, "tp"), P("tp", "fsdp"), P("fsdp", None, "tp"),
            P("fsdp", None), P("fsdp", "tp"), P(None, "tp"), P(), P("tp"), P("tp"), P("tp"),
            P("tp", "fsdp"), P("fsdp", None, "tp"), P("tp", "fsdp"),
        ),
        out_specs=(
            P("fsdp", "ctx", None), P("fsdp", "ctx", None), P("fsdp"), P("fsdp"), P("fsdp", "tp"),
            P("fsdp", None, "tp"), P("tp", "fsdp"), P("fsdp", None, "tp"), P("fsdp", None),
            P("fsdp", "tp"), P(None, "tp"), P(), P("tp"), P("tp"), P("tp"), P("tp", "fsdp"),
            P("fsdp", None, "tp"), P("tp", "fsdp"),
        ),
        check_vma=False,
    )
```

```python
import functools
import math

import jax
import jax.numpy as jnp
from jax import lax
from jax.experimental import pallas as pl
from jax.experimental.pallas import tpu as pltpu
from jax.sharding import Mesh
from jax.sharding import PartitionSpec as P

f32 = jnp.float32
bf16 = jnp.bfloat16
EPS = 1e-05
NEG = -1e30
ROPE_BASE = 100000000000.0
HEAD_WIDTH = 64
HIGH = lax.Precision.HIGHEST

TOK = 512
WID = 1024
SPAN = 128
SPANS = TOK // SPAN
QW = 256
HEADS = 12
INNER = 768
STATE = 128
CONV = INNER + 2 * STATE
HALO = 16
W1C = 2304
W2C = 1024
W3C = 3072
FFH = 1024
C_Q, C_KV, C_DT, C_Z, C_U = 0, 256, 384, 512, 1280


def vmem(n):
    return [pl.BlockSpec(memory_space=pltpu.VMEM)] * n


def kernel_call(body, outs, scratch=(), mem=56, cost=None):
    def call(*args):
        return pl.pallas_call(
            body,
            out_shape=[jax.ShapeDtypeStruct(s, d) for s, d in outs],
            in_specs=vmem(len(args)),
            out_specs=vmem(len(outs)),
            scratch_shapes=list(scratch),
            compiler_params=pltpu.CompilerParams(vmem_limit_bytes=mem * 1024 * 1024),
            cost_estimate=cost,
        )(*args)

    return call


def nt(a, b):
    return lax.dot_general(a, b, (((1,), (1,)), ((), ())), preferred_element_type=f32)


def tn(a, b):
    return lax.dot_general(a, b, (((0,), (0,)), ((), ())), preferred_element_type=f32)


def nn(a, b):
    return jnp.dot(a, b, preferred_element_type=f32)


def split_halves(v):
    hi = v.astype(bf16)
    return hi, (v - hi.astype(f32)).astype(bf16)


def head_matrix(rows, columns):
    row = lax.broadcasted_iota(jnp.int32, (rows, columns), 0)
    col = lax.broadcasted_iota(jnp.int32, (rows, columns), 1)
    return row, col


def spread(v):
    row, col = head_matrix(128, INNER)
    e = jnp.where(row == col // 64, 1.0, 0.0).astype(bf16)
    hi, lo = split_halves(v)
    return nn(hi, e) + nn(lo, e)


def gathered_heads(v):
    row, col = head_matrix(INNER, 128)
    e = jnp.where(row // 64 == col, 1.0, 0.0).astype(bf16)
    hi, lo = split_halves(v)
    return nn(hi, e) + nn(lo, e)


def low_half(shape):
    return lax.broadcasted_iota(jnp.int32, shape, len(shape) - 1) % 128 < 64


def sigmoid(v):
    return 1.0 / (1.0 + jnp.exp(-v))


def turned(v, cos, sin):
    lane = lax.broadcasted_iota(jnp.int32, v.shape, 1) % 64
    w = v.shape[1]
    swapped = jnp.where(lane < 32, pltpu.roll(v, w - 32, 1), pltpu.roll(v, 32, 1))
    return v * cos + jnp.where(lane < 32, -swapped, swapped) * sin


def unit_rows(v):
    r = lax.rsqrt(jnp.mean(v * v, axis=1, keepdims=True) + EPS)
    return v * r, r


def project_body(
    tok, prior, w1, gain, cos, sin, cosp, sinp, normed, q, k2, v2, k2p, v2p, z, cin, step, norm_p
):
    g = gain[...]
    normed[...] = (unit_rows(tok[...].astype(f32))[0] * g).astype(bf16)
    norm_p[...] = (unit_rows(prior[...].astype(f32))[0] * g).astype(bf16)
    lin = nn(normed[...], w1[:, 0:256])
    c, s = cos[...], sin[...]
    for i in range(2):
        cols = slice(128 * i, 128 * i + 128)
        q[:, cols] = turned(lin[:, cols], c, s).astype(bf16)
    low = low_half((TOK, 128))

    def pair(block, cc, ss, kk, vv):
        rot = turned(block, cc, ss)
        shifted = pltpu.roll(rot, 64, 1)
        kk[...] = jnp.where(low, rot, shifted).astype(bf16)
        flat = pltpu.roll(block, 64, 1)
        vv[...] = jnp.where(low, flat, block).astype(bf16)

    lin = nn(normed[...], w1[:, 256:512])
    pair(lin[:, 0:128], c, s, k2, v2)
    step[...] = lin[:, 128:256]
    pair(nn(norm_p[...], w1[:, 256:384]), cosp[...], sinp[...], k2p, v2p)

    @pl.loop(0, 3)
    def _(j):
        at = pl.ds(pl.multiple_of(C_Z + j * 256, 256), 256)
        to = pl.ds(pl.multiple_of(j * 256, 256), 256)
        z[:, to] = nn(normed[...], w1[:, at])

    @pl.loop(0, 4)
    def _(j):
        at = pl.ds(pl.multiple_of(C_U + j * 256, 256), 256)
        to = pl.ds(pl.multiple_of(j * 256, 256), 256)
        cin[0:HALO, to] = nn(norm_p[TOK - HALO : TOK, :], w1[:, at])
        cin[HALO : HALO + TOK, to] = nn(normed[...], w1[:, at])


project = kernel_call(
    project_body,
    [
        ((TOK, WID), bf16),
        ((TOK, QW), bf16),
        ((TOK, 128), bf16),
        ((TOK, 128), bf16),
        ((TOK, 128), bf16),
        ((TOK, 128), bf16),
        ((TOK, INNER), f32),
        ((HALO + TOK, CONV), f32),
        ((TOK, 128), f32),
    ],
    [pltpu.VMEM((TOK, WID), bf16)],
)


def own_bias(rows, start, seg_col, seg_row):
    end = start + rows
    query = lax.broadcasted_iota(jnp.int32, (rows, end), 0) + start
    key = lax.broadcasted_iota(jnp.int32, (rows, end), 1)
    keep = (key <= query) & (seg_col[start:end, 0:1] == seg_row[0:1, TOK : TOK + end])
    return keep


QB = 256


def attend_body(q, k2, v2, k2p, v2p, seg_col, seg_row, out, lse):
    low = low_half((QB, 128))
    for b in range(TOK // QB):
        start, end = b * QB, (b + 1) * QB
        keep = own_bias(QB, start, seg_col, seg_row)
        keep_p = seg_col[start:end, 0:1] == seg_row[0:1, 0:TOK]
        logs = []
        for pair in range(2):
            cols = slice(128 * pair, 128 * pair + 128)
            qp = q[start:end, cols]
            halves = []
            for side in range(2):
                mine = low if side == 0 else ~low
                qh = jnp.where(mine, qp.astype(f32) * 0.125, 0.0).astype(bf16)
                s1 = jnp.where(keep, nt(qh, k2[0:end, :]), NEG)
                s0 = jnp.where(keep_p, nt(qh, k2p[...]), NEG)
                m = jnp.maximum(
                    jnp.max(s1, axis=1, keepdims=True), jnp.max(s0, axis=1, keepdims=True)
                )
                p1, p0 = jnp.exp(s1 - m), jnp.exp(s0 - m)
                total = jnp.sum(p1, axis=1, keepdims=True) + jnp.sum(p0, axis=1, keepdims=True)
                o = nn(p1.astype(bf16), v2[0:end, :]) + nn(p0.astype(bf16), v2p[...])
                halves.append(o / total)
                logs.append(m + jnp.log(total))
            out[start:end, cols] = jnp.where(low, halves[0], halves[1]).astype(bf16)
        lane = lax.broadcasted_iota(jnp.int32, (QB, 128), 1)
        kept = jnp.zeros((QB, 128), f32)
        for h in range(4):
            kept = jnp.where(lane == h, logs[h], kept)
        lse[start:end, :] = kept


attend = kernel_call(attend_body, [((TOK, QW), bf16), ((TOK, 128), f32)])


def attend_back_body(
    q, k2, v2, k2p, v2p, seg_col, seg_row, lse, dout, cos, sin, dq, dkv, dkv_p, dk_s, dv_s, dkp_s, dvp_s
):
    low = low_half((QB, 128))
    for ref in (dk_s, dv_s, dkp_s, dvp_s):
        ref[...] = jnp.zeros_like(ref)
    for b in range(TOK // QB):
        start, end = b * QB, (b + 1) * QB
        keep = own_bias(QB, start, seg_col, seg_row)
        keep_p = seg_col[start:end, 0:1] == seg_row[0:1, 0:TOK]
        for pair in range(2):
            cols = slice(128 * pair, 128 * pair + 128)
            qp = q[start:end, cols]
            dop = dout[start:end, cols]
            halves = []
            for side in range(2):
                mine = low if side == 0 else ~low
                qh = jnp.where(mine, qp.astype(f32) * 0.125, 0.0).astype(bf16)
                doh = jnp.where(mine, dop.astype(f32), 0.0).astype(bf16)
                h = 2 * pair + side
                log_total = lse[start:end, h : h + 1]
                p1 = jnp.exp(jnp.where(keep, nt(qh, k2[0:end, :]), NEG) - log_total)
                p0 = jnp.exp(jnp.where(keep_p, nt(qh, k2p[...]), NEG) - log_total)
                dp1 = nt(doh, v2[0:end, :])
                dp0 = nt(doh, v2p[...])
                delta = jnp.sum(p1 * dp1, axis=1, keepdims=True) + jnp.sum(
                    p0 * dp0, axis=1, keepdims=True
                )
                ds1 = (p1 * (dp1 - delta)).astype(bf16)
                ds0 = (p0 * (dp0 - delta)).astype(bf16)
                dv_s[0:end, :] += tn(p1.astype(bf16), doh)
                dvp_s[...] += tn(p0.astype(bf16), doh)
                dk_s[0:end, :] += tn(ds1, qh)
                dkp_s[...] += tn(ds0, qh)
                halves.append(nn(ds1, k2[0:end, :]) + nn(ds0, k2p[...]))
            dqp = jnp.where(low, halves[0], halves[1]) * 0.125
            dq[start:end, cols] = turned(dqp, cos[start:end, :], -sin[start:end, :]).astype(bf16)
    low = low_half((TOK, 128))

    def joined(dk, dv):
        dk, dv = dk[...], dv[...]
        return jnp.where(low, dk + pltpu.roll(dk, 64, 1), dv + pltpu.roll(dv, 64, 1))

    dkv[...] = joined(dk_s, dv_s)
    dkv_p[...] = joined(dkp_s, dvp_s).astype(bf16)


attend_back = kernel_call(
    attend_back_body,
    [((TOK, QW), bf16), ((TOK, 128), f32), ((TOK, 128), bf16)],
    [pltpu.VMEM((TOK, 128), f32)] * 4,
)


def tap_mask(seg_ext, k):
    now = seg_ext[HALO : HALO + TOK, 0:1]
    at = HALO - 3 + k
    return jnp.where(seg_ext[at : at + TOK, 0:1] == now, 1.0, 0.0)


def lower_ones():
    row, col = head_matrix(SPAN, SPAN)
    return jnp.where(row >= col, 1.0, 0.0)


def rows_of(c):
    return slice(c * SPAN, (c + 1) * SPAN)


def mixer_in_body(cin, taps, step, bias, rate, seg_ext, pre, dt, cum, last):
    run = jnp.zeros((TOK, CONV), f32)
    for k in range(4):
        at = HALO - 3 + k
        run = run + cin[at : at + TOK, :] * taps[k : k + 1, :] * tap_mask(seg_ext, k)
    pre[...] = run
    lane = lax.broadcasted_iota(jnp.int32, (TOK, 128), 1)
    steps = step[...] + bias[...]
    soft = jnp.maximum(steps, 0.0) + jnp.log(1.0 + jnp.exp(-jnp.abs(steps)))
    dt[...] = jnp.where(lane < HEADS, soft, 0.0)
    tri = lower_ones()
    state = jnp.zeros((STATE, INNER), f32)
    for c in range(SPANS):
        rows = rows_of(c)
        own_dt = dt[rows, :]
        total = jnp.dot(tri, own_dt * rate[...], precision=HIGH, preferred_element_type=f32)
        cum[rows, :] = total
        out = pre[rows, 0 : INNER + STATE]
        out = out * sigmoid(out)
        seg = seg_ext[HALO + c * SPAN : HALO + (c + 1) * SPAN, 0:1]
        seg_last = seg[SPAN - 1 : SPAN, :]
        end = total[SPAN - 1 : SPAN, :]
        tail = jnp.where(seg == seg_last, jnp.exp(jnp.minimum(end - total, 0.0)), 0.0) * own_dt
        fresh = tn(out[:, INNER:].astype(bf16), (out[:, 0:INNER] * spread(tail)).astype(bf16))
        if c == 0:
            state = fresh
        else:
            seg_prev = seg_ext[HALO + c * SPAN - 1 : HALO + c * SPAN, 0:1]
            keep = jnp.where(seg_last == seg_prev, jnp.exp(end), 0.0)
            state = state * spread(jnp.broadcast_to(keep, (8, 128)))[0:1, :] + fresh
    last[...] = state.astype(bf16)


mixer_in = kernel_call(
    mixer_in_body,
    [
        ((TOK, CONV), f32),
        ((TOK, 128), f32),
        ((TOK, 128), f32),
        ((STATE, INNER), bf16),
    ],
)


def span_parts(c, cum, seg_ext):
    total = cum[rows_of(c), :]
    seg = seg_ext[HALO + c * SPAN : HALO + (c + 1) * SPAN, 0:1]
    seg_last = seg[SPAN - 1 : SPAN, :]
    seg_prev = seg_ext[HALO + c * SPAN - 1 : HALO + c * SPAN, 0:1]
    end = total[SPAN - 1 : SPAN, :]
    entering = jnp.where(seg == seg_prev, jnp.exp(total), 0.0)
    tail = jnp.where(seg == seg_last, jnp.exp(jnp.minimum(end - total, 0.0)), 0.0)
    return total, entering, tail


def span_bias(c, seg_ext, seg_row):
    row, col = head_matrix(SPAN, SPAN)
    seg = seg_ext[HALO + c * SPAN : HALO + (c + 1) * SPAN, 0:1]
    other = seg_row[0:1, TOK + c * SPAN : TOK + (c + 1) * SPAN]
    return jnp.where((row >= col) & (seg == other), 0.0, NEG)


def mixer_out_body(
    pre, dt, cum, seg_ext, seg_row, first, z, skip, y, gated, states, sc_state
):
    sc_state[...] = first[...].astype(f32)
    low2 = low_half((SPAN, 128))
    for c in range(SPANS):
        rows = rows_of(c)
        total, entering, tail = span_parts(c, cum, seg_ext)
        out = pre[rows, :]
        out = out * sigmoid(out)
        x = out[:, 0:INNER]
        b = out[:, INNER : INNER + STATE].astype(bf16)
        cm = out[:, INNER + STATE :].astype(bf16)
        own_dt = dt[rows, :]
        xs = x * spread(own_dt)
        state = sc_state[...]
        state_b = state.astype(bf16)
        states[c] = state_b
        wide_in = spread(entering)
        run = nn(cm, state_b) * wide_in + x * skip[...]
        inter = nt(cm, b)
        bias = span_bias(c, seg_ext, seg_row)
        total_t = total.T
        gate = z[rows, :]
        gate = gate * sigmoid(gate)
        for pair in range(HEADS // 2):
            cols = slice(128 * pair, 128 * pair + 128)
            parts = []
            for side in range(2):
                h = 2 * pair + side
                decay = jnp.exp(total[:, h : h + 1] - total_t[h : h + 1, :] + bias)
                parts.append((decay * inter).astype(bf16))
            xp = xs[:, cols]
            stack = jnp.concatenate(
                [jnp.where(low2, xp, 0.0).astype(bf16), jnp.where(low2, 0.0, xp).astype(bf16)], axis=0
            )
            yp = run[:, cols] + nn(jnp.concatenate(parts, axis=1), stack)
            y[rows, cols] = yp
            gated[rows, cols] = (yp * gate[:, cols]).astype(bf16)
        if c < SPANS - 1:
            sc_state[...] = state * wide_in[SPAN - 1 : SPAN, :] + tn(
                b, (xs * spread(tail)).astype(bf16)
            )


mixer_out = kernel_call(
    mixer_out_body,
    [((TOK, INNER), f32), ((TOK, INNER), bf16), ((SPANS, STATE, INNER), bf16)],
    [pltpu.VMEM((STATE, INNER), f32)],
)


def mixer_back_in_body(dgated, z, y, pre, cum, seg_ext, dy, dz, first):
    state = jnp.zeros((STATE, INNER), f32)
    for c in reversed(range(SPANS)):
        rows = rows_of(c)
        total, entering, tail = span_parts(c, cum, seg_ext)
        gate = z[rows, :]
        sig = sigmoid(gate)
        grad = dgated[rows, :]
        own = grad * (gate * sig)
        dy[rows, :] = own
        dz[rows, :] = (grad * y[rows, :] * (sig * (1.0 + gate * (1.0 - sig)))).astype(bf16)
        cm = pre[rows, INNER + STATE :]
        cm = (cm * sigmoid(cm)).astype(bf16)
        wide_in = spread(entering)
        fresh = tn(cm, (own * wide_in).astype(bf16))
        state = fresh if c == SPANS - 1 else state * wide_in[SPAN - 1 : SPAN, :] + fresh
    first[...] = state.astype(bf16)


mixer_back_in = kernel_call(
    mixer_back_in_body,
    [((TOK, INNER), f32), ((TOK, INNER), bf16), ((STATE, INNER), bf16)],
)


def mixer_back_body(
    dy, pre, dt, cum, seg_ext, seg_row, states, last, skip, rate, step, bias,
    dpre, dstep, heads, sc_state,
):
    sc_state[...] = last[...].astype(f32)
    low2 = low_half((SPAN, 128))
    lane = lax.broadcasted_iota(jnp.int32, (SPAN, 128), 1)
    tri = lower_ones()
    sum_decay = jnp.zeros((1, 128), f32)
    sum_bias = jnp.zeros((1, 128), f32)
    sum_skip = jnp.zeros((1, 128), f32)
    for c in reversed(range(SPANS)):
        rows = rows_of(c)
        total, entering, tail = span_parts(c, cum, seg_ext)
        lin = pre[rows, :]
        sig = sigmoid(lin)
        out = lin * sig
        slope = sig * (1.0 + lin * (1.0 - sig))
        x = out[:, 0:INNER]
        b = out[:, INNER : INNER + STATE].astype(bf16)
        cm = out[:, INNER + STATE :].astype(bf16)
        own_dt = dt[rows, :]
        wide_dt = spread(own_dt)
        xs = x * wide_dt
        grad = dy[rows, :]
        wide_in = spread(entering)
        wide_tail = spread(tail)
        dstate = sc_state[...]
        dstate_b = dstate.astype(bf16)
        state_b = states[c]
        gin = grad * wide_in
        gin_b = gin.astype(bf16)
        y_state = nn(cm, state_b)
        xt = xs * wide_tail
        xt_b = xt.astype(bf16)
        from_state = nn(b, dstate_b)
        dcm = nt(gin_b, state_b)
        db = nt(xt_b, dstate_b)
        dcum = gathered_heads(gin * y_state)
        moved = gathered_heads(xt * from_state)
        kept = jnp.sum(dstate * state_b.astype(f32), axis=0, keepdims=True)
        kept = kept * wide_in[SPAN - 1 : SPAN, :]
        kept = gathered_heads(jnp.broadcast_to(kept, (8, INNER)))[0:1, :]
        at_end = jnp.sum(moved, axis=0, keepdims=True) + kept
        sub = lax.broadcasted_iota(jnp.int32, (SPAN, 128), 0)
        dcum = dcum - moved + jnp.where(sub == SPAN - 1, at_end, 0.0)
        sc_state[...] = dstate * wide_in[SPAN - 1 : SPAN, :] + tn(cm, gin_b)
        inter = nt(cm, b)
        bias_m = span_bias(c, seg_ext, seg_row)
        total_t = total.T
        dinter = jnp.zeros((SPAN, SPAN), f32)
        col_sums = jnp.zeros((128, SPAN), f32)
        sub_t = lax.broadcasted_iota(jnp.int32, (128, SPAN), 0)
        ddt = jnp.zeros((SPAN, 128), f32)
        dskip = jnp.zeros((SPAN, 128), f32)
        for pair in range(HEADS // 2):
            cols = slice(128 * pair, 128 * pair + 128)
            gp, xp = grad[:, cols], xs[:, cols]
            gp_b, xp_b = gp.astype(bf16), xp.astype(bf16)
            stack = jnp.concatenate(
                [jnp.where(low2, gp, 0.0).astype(bf16), jnp.where(low2, 0.0, gp).astype(bf16)], axis=0
            )
            dm = nt(stack, xp_b)
            parts = []
            for side in range(2):
                h = 2 * pair + side
                decay = jnp.exp(total[:, h : h + 1] - total_t[h : h + 1, :] + bias_m)
                dmh = dm[side * SPAN : (side + 1) * SPAN, :] * decay
                dinter = dinter + dmh
                weight = decay * inter
                parts.append(weight.astype(bf16))
                q = dmh * inter
                dcum = dcum + jnp.where(lane == h, jnp.sum(q, axis=1, keepdims=True), 0.0)
                col_sums = col_sums + jnp.where(sub_t == h, jnp.sum(q, axis=0, keepdims=True), 0.0)
            both = tn(jnp.concatenate(parts, axis=1), gp_b)
            dxs = jnp.where(low2, both[0:SPAN, :], both[SPAN:, :]) + from_state[:, cols] * wide_tail[:, cols]
            xo = x[:, cols]
            dx = dxs * wide_dt[:, cols] + gp * skip[:, cols]
            dpre[rows, cols] = dx * slope[:, cols]
            pick_row, pick_col = head_matrix(128, 128)
            pick = jnp.where(pick_col == 2 * pair + pick_row // 64, 1.0, 0.0).astype(bf16)
            hi, lo = split_halves(dxs * xo)
            ddt = ddt + nn(hi, pick) + nn(lo, pick)
            hi, lo = split_halves(gp * xo)
            dskip = dskip + nn(hi, pick) + nn(lo, pick)
        dinter_b = dinter.astype(bf16)
        dcm = dcm + nn(dinter_b, b)
        db = db + tn(dinter_b, cm)
        dpre[rows, INNER : INNER + STATE] = db * slope[:, INNER : INNER + STATE]
        dpre[rows, INNER + STATE :] = dcm * slope[:, INNER + STATE :]
        dcum = dcum - col_sums.T
        dlog = lax.dot_general(
            tri, dcum, (((0,), (0,)), ((), ())), precision=HIGH, preferred_element_type=f32
        )
        ddt = ddt + dlog * rate[...]
        dsp = jnp.where(lane < HEADS, ddt * sigmoid(step[rows, :] + bias[...]), 0.0)
        dstep[rows, :] = dsp.astype(bf16)
        sum_decay = sum_decay + jnp.sum(dlog * own_dt, axis=0, keepdims=True)
        sum_bias = sum_bias + jnp.sum(dsp, axis=0, keepdims=True)
        sum_skip = sum_skip + jnp.sum(dskip, axis=0, keepdims=True)
    sub8 = lax.broadcasted_iota(jnp.int32, (8, 128), 0)
    heads[...] = jnp.where(
        sub8 == 0,
        sum_decay * rate[...],
        jnp.where(sub8 == 1, sum_bias, jnp.where(sub8 == 2, sum_skip, 0.0)),
    )


mixer_back = kernel_call(
    mixer_back_body,
    [((TOK, CONV), f32), ((TOK, 128), bf16), ((8, 128), f32)],
    [pltpu.VMEM((STATE, INNER), f32)],
)


def inputs_back_body(
    dpre, dpre_next, cin, taps, seg_ext, seg_next, dkv, dkv_back, cos, sin, dq, dstep, dz,
    grads, dtaps, ext,
):
    ext[0:TOK, :] = dpre[...]
    ext[TOK : TOK + 8, :] = dpre_next[...]
    run = jnp.zeros((TOK, CONV), f32)
    now = seg_next[0:TOK, 0:1]
    sub = lax.broadcasted_iota(jnp.int32, (8, CONV), 0)
    taken = jnp.zeros((8, CONV), f32)
    for k in range(4):
        ahead = 3 - k
        same = jnp.where(seg_next[ahead : ahead + TOK, 0:1] == now, 1.0, 0.0)
        run = run + ext[ahead : ahead + TOK, :] * taps[k : k + 1, :] * same
        at = HALO - 3 + k
        part = dpre[...] * cin[at : at + TOK, :] * tap_mask(seg_ext, k)
        taken = taken + jnp.where(sub == k, jnp.sum(part, axis=0, keepdims=True), 0.0)
    dtaps[...] = taken
    grads[:, C_U:] = run.astype(bf16)
    grads[:, C_Q : C_Q + QW] = dq[...]
    both = dkv[...] + dkv_back[...].astype(f32)
    low = low_half((TOK, 128))
    grads[:, C_KV : C_KV + 128] = jnp.where(low, turned(both, cos[...], -sin[...]), both).astype(bf16)
    grads[:, C_DT : C_DT + 128] = dstep[...]
    grads[:, C_Z : C_Z + INNER] = dz[...]


inputs_back = kernel_call(
    inputs_back_body,
    [((TOK, W1C), bf16), ((8, CONV), f32)],
    [pltpu.VMEM((TOK + 8, CONV), f32)],
)


MESH = pl.DeviceIdType.MESH
GC = W1C + W2C
PIECE = 256
PIECES = GC // PIECE
A_PIECES = 7
COLS = (slice(0, A_PIECES * PIECE), slice(A_PIECES * PIECE, GC))
BC0 = C_U + INNER
SHARE = 384
SMALL = CONV + 128


def place():
    f = lax.axis_index("fsdp")
    core = lax.rem(f, 2)
    chip = lax.div(f, 2)
    return lax.div(chip, 4), lax.rem(chip, 4), core


def at_yz(y, z, core):
    return {"fsdp": (lax.rem(y, 4) * 4 + lax.rem(z, 4)) * 2 + core}


def greet(peers):
    barrier = pltpu.get_barrier_semaphore()
    for peer in peers:
        pl.semaphore_signal(barrier, inc=1, device_id=peer, device_id_type=MESH)
    pl.semaphore_wait(barrier, len(peers))


def send(src, dst, sems, k, peer):
    copy = pltpu.make_async_remote_copy(
        src_ref=src,
        dst_ref=dst,
        send_sem=sems.at[0, k],
        recv_sem=sems.at[1, k],
        device_id=peer,
        device_id_type=MESH,
    )
    copy.start()
    return copy


class RingSum:
    def __init__(self, chunk, me, right, left, sems, far, near, joined):
        self.chunk, self.me, self.sems = chunk, me, sems
        self.right, self.left = right, left
        self.far, self.near, self.joined = far, near, joined
        self.sent = []

    def ahead(self, n):
        return lax.rem(self.me + n, 4)

    def start(self):
        c, s = self.chunk, self.sems
        self.far_copies = (
            send(c(self.ahead(2), 0), self.far.at[0], s, 0, self.right),
            send(c(self.ahead(2), 1), self.far.at[1], s, 1, self.left),
        )
        self.direct = (
            send(c(self.ahead(1), 1), self.near.at[0, 1], s, 2, self.right),
            send(c(self.ahead(3), 0), self.near.at[1, 0], s, 3, self.left),
        )

    def forward(self):
        c, s = self.chunk, self.sems
        passed = []
        for side, (peer, n) in enumerate(((self.right, 1), (self.left, 3))):
            self.far_copies[side].wait_recv()
            own = c(self.ahead(n), side)[...]
            self.joined[side] = (own.astype(f32) + self.far[side].astype(f32)).astype(bf16)
            passed.append(send(self.joined.at[side], self.near.at[side, side], s, 4 + side, peer))
        self.passed = tuple(passed)

    def finish(self):
        for copy in self.direct + self.passed:
            copy.wait_recv()

    def total(self, half):
        own = self.chunk(self.me, half)[...].astype(f32)
        return own + self.near[0, half].astype(f32) + self.near[1, half].astype(f32)

    def close(self):
        for copy in self.far_copies + self.direct + self.passed:
            copy.wait_send()


def tail_body(
    normed, grads, dmix, mixed, w1, tok, gain, gmid, dgain2, small,
    parts, tok_grad, small_out,
    dn, dn_back, gbuf, crecv, acc, far_a, near_a, join_a, far_b, near_b, join_b, one_a, one_b,
    far_a2, near_a2, join_a2, far_b2, near_b2, join_b2, fin, fin_back, share, share_back,
    sm_core, sm_z, sm_y, sm_ctx, sm_tp,
    tp_sems, core_sems, a_sems, b_sems, a2_sems, b2_sems, ctx_sems, small_sems,
):
    y, z, core = place()
    ctx, tp = lax.axis_index("ctx"), lax.axis_index("tp")
    sibling = at_yz(y, z, 1 - core)
    z_peers = [at_yz(y, z + n, core) for n in (1, 2, 3)]
    y_peers = [at_yz(y + n, z, core) for n in (1, 2, 3)]
    ctx_peer, tp_peer = {"ctx": 1 - ctx}, {"tp": 1 - tp}
    greet([sibling, ctx_peer, tp_peer] + z_peers + y_peers)

    sm_core[core] = small[...]
    small_copies = [send(sm_core.at[core], sm_core.at[core], small_sems, 0, sibling)]

    @pl.loop(0, WID // 256)
    def _(j):
        to = pl.ds(pl.multiple_of(j * 256, 256), 256)
        dn[:, to] = nt(grads[...], w1[to, :]).astype(bf16)

    dn_copy = send(dn, dn_back, tp_sems, 0, tp_peer)
    v = tok[...].astype(f32)
    dgain1 = jnp.sum(dn[...].astype(f32) * unit_rows(v)[0], axis=0, keepdims=True)
    sub = lax.broadcasted_iota(jnp.int32, (128, WID), 0)
    gain_rows = jnp.where(sub == HEADS, dgain1, jnp.where(sub == HEADS + 1, dgain2[...] * 0.5, 0.0))

    core_copies = []

    def piece(j):
        cols = slice(j * PIECE, (j + 1) * PIECE)
        if j < W1C // PIECE:
            block = tn(normed[...], grads[:, cols])
        else:
            at = slice(j * PIECE - W1C, (j + 1) * PIECE - W1C)
            block = tn(dmix[...], mixed[:, at])
        if j == C_DT // PIECE:
            block = jnp.concatenate([block[:, 0:128], block[:, 128:256] + gain_rows.T], axis=1)
        gbuf[:, :, :, :, cols] = block.astype(bf16).reshape(4, 4, 2, 32, PIECE)
        core_copies.append(
            send(
                gbuf.at[:, :, 1 - core, :, cols], crecv.at[:, :, :, cols], core_sems, j, sibling
            )
        )

    def add_piece(j):
        cols = slice(j * PIECE, (j + 1) * PIECE)
        core_copies[j].wait_recv()
        own = gbuf[:, :, core, :, cols]
        acc[:, :, :, cols] = (own.astype(f32) + crecv[:, :, :, cols].astype(f32)).astype(bf16)

    ca, cb = COLS
    ring_a = RingSum(
        lambda d, h: acc.at[2 * h : 2 * h + 2, d, :, ca], z, z_peers[0], z_peers[2], a_sems,
        far_a, near_a, join_a,
    )
    ring_b = RingSum(
        lambda d, h: acc.at[d, 2 * h : 2 * h + 2, :, cb], y, y_peers[0], y_peers[2], b_sems,
        far_b, near_b, join_b,
    )
    ring_a2 = RingSum(
        lambda d, h: one_a.at[d, 16 * h : 16 * h + 16, :], y, y_peers[0], y_peers[2], a2_sems,
        far_a2, near_a2, join_a2,
    )
    ring_b2 = RingSum(
        lambda d, h: one_b.at[d, 16 * h : 16 * h + 16, :], z, z_peers[0], z_peers[2], b2_sems,
        far_b2, near_b2, join_b2,
    )

    for j in range(PIECES + 1):
        if j < PIECES:
            piece(j)
        if j > 0:
            add_piece(j - 1)
        if j == A_PIECES:
            ring_a.start()
            small_copies[0].wait_recv()
            sm_z[z] = sm_core[0] + sm_core[1]
            z_copies = [
                send(sm_z.at[z], sm_z.at[z], small_sems, 1 + n, peer)
                for n, peer in enumerate(z_peers)
            ]
            small_copies += z_copies
    ring_b.start()
    ring_a.forward()
    ring_b.forward()
    ring_a.finish()
    for h in range(2):
        one_a[2 * h : 2 * h + 2] = ring_a.total(h).astype(bf16)
    ring_a2.start()
    for copy in z_copies:
        copy.wait_recv()
    sm_y[y] = (sm_z[0] + sm_z[1]) + (sm_z[2] + sm_z[3])
    y_copies = [
        send(sm_y.at[y], sm_y.at[y], small_sems, 4 + n, peer) for n, peer in enumerate(y_peers)
    ]
    small_copies += y_copies
    ring_b.finish()
    for h in range(2):
        one_b[2 * h : 2 * h + 2] = ring_b.total(h).astype(bf16)
    ring_b2.start()
    ring_a2.forward()
    ring_b2.forward()
    ring_a2.finish()
    for h in range(2):
        fin[16 * h : 16 * h + 16, ca] = ring_a2.total(h).astype(bf16)
    ring_b2.finish()
    for h in range(2):
        fin[16 * h : 16 * h + 16, cb] = ring_b2.total(h).astype(bf16)
    fin_copy = send(fin, fin_back, ctx_sems, 0, ctx_peer)
    for copy in y_copies:
        copy.wait_recv()
    sm_ctx[ctx] = (sm_y[0] + sm_y[1]) + (sm_y[2] + sm_y[3])
    ctx_copy = send(sm_ctx.at[ctx], sm_ctx.at[ctx], small_sems, 7, ctx_peer)

    dn_copy.wait_recv()
    dh = (dn[...].astype(f32) + dn_back[...].astype(f32)) * gain[...]
    r = lax.rsqrt(jnp.mean(v * v, axis=1, keepdims=True) + EPS)
    inner = jnp.mean(v * dh, axis=1, keepdims=True)
    tok_grad[...] = gmid[...] + r * dh - v * (r * r * r * inner)

    fin_copy.wait_recv()
    total = fin[...].astype(f32) + fin_back[...].astype(f32)
    parts[...] = total
    share[:, 0:128] = total[:, C_DT : C_DT + 128].astype(bf16)
    share[:, 128:384] = total[:, BC0 : BC0 + 256].astype(bf16)
    share_copy = send(share, share_back, ctx_sems, 1, tp_peer)
    ctx_copy.wait_recv()
    sums = sm_ctx[0] + sm_ctx[1]
    small_out[...] = sums
    sm_tp[tp] = sums[0:4, INNER:CONV]
    last_copy = send(sm_tp.at[tp], sm_tp.at[tp], small_sems, 8, tp_peer)
    share_copy.wait_recv()
    both = share[...].astype(f32) + share_back[...].astype(f32)
    lane = lax.broadcasted_iota(jnp.int32, (32, 128), 1)
    parts[:, C_DT : C_DT + 128] = jnp.where(lane < HEADS, total[:, C_DT : C_DT + 128], both[:, 0:128])
    parts[:, BC0 : BC0 + 256] = both[:, 128:384]
    last_copy.wait_recv()
    small_out[0:4, INNER:CONV] = sm_tp[0] + sm_tp[1]

    for ring in (ring_a, ring_b, ring_a2, ring_b2):
        ring.close()
    for copy in core_copies + small_copies + [dn_copy, fin_copy, ctx_copy, share_copy, last_copy]:
        copy.wait_send()


def tail(*args):
    wide_a, wide_b = A_PIECES * PIECE, GC - A_PIECES * PIECE

    def ring_space(lead, wide):
        return [
            pltpu.VMEM((2,) + lead + (wide,), bf16),
            pltpu.VMEM((2, 2) + lead + (wide,), bf16),
            pltpu.VMEM((2,) + lead + (wide,), bf16),
        ]

    def sems(n):
        return pltpu.SemaphoreType.DMA((2, n))

    return pl.pallas_call(
        tail_body,
        out_shape=[
            jax.ShapeDtypeStruct((32, GC), f32),
            jax.ShapeDtypeStruct((TOK, WID), f32),
            jax.ShapeDtypeStruct((8, SMALL), f32),
        ],
        in_specs=vmem(len(args)),
        out_specs=vmem(3),
        scratch_shapes=[
            pltpu.VMEM((TOK, WID), bf16),
            pltpu.VMEM((TOK, WID), bf16),
            pltpu.VMEM((4, 4, 2, 32, GC), bf16),
            pltpu.VMEM((4, 4, 32, GC), bf16),
            pltpu.VMEM((4, 4, 32, GC), bf16),
            *ring_space((2, 32), wide_a),
            *ring_space((2, 32), wide_b),
            pltpu.VMEM((4, 32, wide_a), bf16),
            pltpu.VMEM((4, 32, wide_b), bf16),
            *ring_space((16,), wide_a),
            *ring_space((16,), wide_b),
            pltpu.VMEM((32, GC), bf16),
            pltpu.VMEM((32, GC), bf16),
            pltpu.VMEM((32, SHARE), bf16),
            pltpu.VMEM((32, SHARE), bf16),
            pltpu.VMEM((2, 8, SMALL), f32),
            pltpu.VMEM((4, 8, SMALL), f32),
            pltpu.VMEM((4, 8, SMALL), f32),
            pltpu.VMEM((2, 8, SMALL), f32),
            pltpu.VMEM((2, 4, CONV - INNER), f32),
            sems(1),
            sems(PIECES),
            sems(6),
            sems(6),
            sems(6),
            sems(6),
            sems(2),
            sems(9),
        ],
        compiler_params=pltpu.CompilerParams(
            vmem_limit_bytes=60 * 1024 * 1024, collective_id=0, has_side_effects=True
        ),
    )(*args)


def swapped(block, axis):
    return lax.ppermute(block, axis, [(0, 1), (1, 0)])


def pair_sum(block, axis):
    return block.astype(f32) + swapped(block, axis).astype(f32)


def rope_tables(positions):
    indices = jnp.arange(HEAD_WIDTH // 2).astype(f32)
    frequency = jnp.exp(indices * (-2.0 * math.log(ROPE_BASE) / HEAD_WIDTH))
    angles = positions[:, None] * frequency[None, :]
    return (jnp.tile(jnp.cos(angles), (1, 4)), jnp.tile(jnp.sin(angles), (1, 4)))


def norm_back(v, gain_row, dh):
    r = lax.rsqrt(jnp.mean(v * v, axis=1, keepdims=True) + EPS)
    scaled = dh * gain_row
    dv = r * scaled - v * (r * r * r) * jnp.mean(v * scaled, axis=1, keepdims=True)
    return dv, jnp.sum(dh * v * r, axis=0)


def lanes(vector):
    return jnp.pad(vector, (0, 128 - vector.shape[0]))[None, :]


def shards(
    tokens, segments, cotangent, gain_mixer, gain_ffn, query_proj, key_value_weight, attn_out,
    inner_proj, state_proj, step_proj, conv_inner, conv_state, decay_log, step_bias, skip_gain,
    inner_out, gate_up, down_proj,
):
    rows = query_proj.shape[0]
    ctx = lax.axis_index("ctx")
    tok = tokens.reshape(TOK, WID)
    prior = lax.ppermute(tok, "ctx", [(0, 1)])
    blocks = (
        jnp.concatenate(
            [
                query_proj,
                key_value_weight.reshape(rows, 128),
                step_proj,
                gain_mixer[:, None],
                gain_ffn[:, None],
                jnp.zeros((rows, 114), bf16),
                inner_proj.reshape(rows, 2 * INNER),
                state_proj,
            ],
            axis=1,
        ),
        jnp.concatenate([attn_out.T, inner_out.T], axis=1),
        jnp.concatenate([gate_up.reshape(rows, 2 * FFH), down_proj.T], axis=1),
    )
    w1, w2, w3 = (lax.all_gather(b, "fsdp", axis=0, tiled=True) for b in blocks)
    gains = w1[:, C_DT + HEADS : C_DT + HEADS + 2].astype(f32).T
    gain1, gain2 = gains[0:1], gains[1:2]

    start = ctx * TOK
    cos, sin = rope_tables((start + jnp.arange(TOK)).astype(f32))
    cosp, sinp = rope_tables((start - TOK + jnp.arange(TOK)).astype(f32))
    seg = segments.reshape(-1)
    late = ctx > 0
    seg_now = lax.dynamic_slice_in_dim(seg, start, TOK)
    seg_prior = jnp.where(late, seg[0:TOK], -1)
    seg_after = jnp.where(late, -2, seg[TOK : TOK + 8])
    seg_row = jnp.concatenate([seg_prior, seg_now])[None, :]
    seg_ext = jnp.concatenate([seg_prior[TOK - HALO :], seg_now])[:, None]
    seg_next = jnp.concatenate([seg_now, seg_after])[:, None]
    seg_col = seg_now[:, None]
    taps = jnp.concatenate([conv_inner, conv_state], axis=1).astype(f32)
    bias = lanes(step_bias)
    rate = lanes(-jnp.exp(decay_log))
    skip = jnp.repeat(skip_gain, 64)[None, :]

    normed, q, k2, v2, k2p, v2p, z, cin, step = project(tok, prior, w1, gain1, cos, sin, cosp, sinp)
    pre, dt, cum, last = mixer_in(cin, taps, step, bias, rate, seg_ext)
    first = lax.ppermute(last, "ctx", [(0, 1)])
    attended, lse = attend(q, k2, v2, k2p, v2p, seg_col, seg_row)
    y, gated, states = mixer_out(pre, dt, cum, seg_ext, seg_row, first, z, skip)

    mixed = jnp.concatenate([attended, gated], axis=1)
    branch = pair_sum(nt(mixed, w2).astype(bf16), "tp")
    mid = tok.astype(f32) + branch

    normed2 = (unit_rows(mid)[0] * gain2).astype(bf16)
    wgu, wdown = w3[:, 0 : 2 * FFH], w3[:, 2 * FFH :]
    gu = nn(normed2, wgu)
    gate, up = gu[:, :FFH], gu[:, FFH:]
    sig = sigmoid(gate)
    silu = gate * sig
    act = (silu * up).astype(bf16)
    cot = cotangent.reshape(TOK, WID)
    dact = nn(cot, wdown)
    dgate = dact * up * sig * (1.0 + gate * (1.0 - sig))
    dgu = jnp.concatenate([dgate, dact * silu], axis=1).astype(bf16)
    dnormed2 = pair_sum(nt(dgu, wgu).astype(bf16), "tp")
    down, dnormed2 = lax.optimization_barrier((nt(act, wdown).astype(bf16), dnormed2))
    block_out = (mid + pair_sum(down, "tp")).astype(bf16)
    dmid, dgain2 = norm_back(mid, gain2, dnormed2)
    grad_mid = cot.astype(f32) + dmid
    dmix = grad_mid.astype(bf16)

    w3_grad = jnp.concatenate([tn(normed2, dgu), tn(cot, act)], axis=1).astype(bf16)
    w3_part = lax.psum_scatter(w3_grad, "fsdp", scatter_dimension=0, tiled=True)

    dmixed = nn(dmix, w2)
    dattended, dgated = dmixed[:, :QW].astype(bf16), dmixed[:, QW:]
    dy, dz, dfirst = mixer_back_in(dgated, z, y, pre, cum, seg_ext)
    dlast = lax.ppermute(dfirst, "ctx", [(1, 0)])
    dq, dkv, dkv_p = attend_back(
        q, k2, v2, k2p, v2p, seg_col, seg_row, lse, dattended, cos, sin
    )
    dkv_back = lax.ppermute(dkv_p, "ctx", [(1, 0)])
    dpre, dstep, heads = mixer_back(
        dy, pre, dt, cum, seg_ext, seg_row, states, dlast, skip, rate, step, bias
    )
    dpre_next = lax.ppermute(dpre[0:8], "ctx", [(1, 0)])
    grads, dtaps = inputs_back(
        dpre, dpre_next, cin, taps, seg_ext, seg_next, dkv, dkv_back, cos, sin, dq, dstep, dz
    )
    small = jnp.concatenate([dtaps, heads], axis=1)
    parts, tokens_grad, sums = tail(
        normed, grads, dmix, mixed, w1, tok, gain1, grad_mid, dgain2[None, :], small
    )
    parts3 = pair_sum(w3_part, "ctx")
    mine = parts[:, C_DT + HEADS : C_DT + HEADS + 2]

    at2 = W1C
    return (
        block_out[None],
        tokens_grad[None],
        mine[:, 0],
        mine[:, 1],
        parts[:, 0:QW],
        parts[:, C_KV : C_KV + 128].reshape(rows, 2, 64),
        parts[:, at2 : at2 + QW].T,
        parts[:, C_Z : C_Z + 2 * INNER].reshape(rows, 2, INNER),
        parts[:, BC0 : BC0 + 256],
        parts[:, C_DT : C_DT + HEADS],
        sums[0:4, :INNER],
        sums[0:4, INNER:CONV],
        sums[0, CONV : CONV + HEADS],
        sums[1, CONV : CONV + HEADS],
        sums[2, CONV : CONV + HEADS],
        parts[:, at2 + QW :].T,
        parts3[:, : 2 * FFH].reshape(rows, 2, FFH),
        parts3[:, 2 * FFH :].T,
    )


def solution(mesh):
    return jax.shard_map(
        shards,
        mesh=mesh,
        in_specs=(
            P("fsdp", "ctx", None), P("fsdp", None), P("fsdp", "ctx", None), P("fsdp"), P("fsdp"),
            P("fsdp", "tp"), P("fsdp", None, "tp"), P("tp", "fsdp"), P("fsdp", None, "tp"),
            P("fsdp", None), P("fsdp", "tp"), P(None, "tp"), P(), P("tp"), P("tp"), P("tp"),
            P("tp", "fsdp"), P("fsdp", None, "tp"), P("tp", "fsdp"),
        ),
        out_specs=(
            P("fsdp", "ctx", None), P("fsdp", "ctx", None), P("fsdp"), P("fsdp"), P("fsdp", "tp"),
            P("fsdp", None, "tp"), P("tp", "fsdp"), P("fsdp", None, "tp"), P("fsdp", None),
            P("fsdp", "tp"), P(None, "tp"), P(), P("tp"), P("tp"), P("tp"), P("tp", "fsdp"),
            P("fsdp", None, "tp"), P("tp", "fsdp"),
        ),
        check_vma=False,
    )
```

```python
import functools
import math

import jax
import jax.numpy as jnp
from jax import lax
from jax.experimental import pallas as pl
from jax.experimental.pallas import tpu as pltpu
from jax.sharding import Mesh
from jax.sharding import PartitionSpec as P

f32 = jnp.float32
bf16 = jnp.bfloat16
EPS = 1e-05
NEG = -1e30
ROPE_BASE = 100000000000.0
HEAD_WIDTH = 64
HIGH = lax.Precision.HIGHEST

TOK = 512
WID = 1024
SPAN = 128
SPANS = TOK // SPAN
QW = 256
HEADS = 12
INNER = 768
STATE = 128
CONV = INNER + 2 * STATE
HALO = 16
W1C = 2304
W2C = 1024
W3C = 3072
FFH = 1024
C_Q, C_KV, C_DT, C_Z, C_U = 0, 256, 384, 512, 1280


def vmem(n):
    return [pl.BlockSpec(memory_space=pltpu.VMEM)] * n


def kernel_call(body, outs, scratch=(), mem=24, cost=None):
    def call(*args):
        return pl.pallas_call(
            body,
            out_shape=[jax.ShapeDtypeStruct(s, d) for s, d in outs],
            in_specs=vmem(len(args)),
            out_specs=vmem(len(outs)),
            scratch_shapes=list(scratch),
            compiler_params=pltpu.CompilerParams(vmem_limit_bytes=mem * 1024 * 1024),
            cost_estimate=cost,
        )(*args)

    return call


def nt(a, b):
    return lax.dot_general(a, b, (((1,), (1,)), ((), ())), preferred_element_type=f32)


def tn(a, b):
    return lax.dot_general(a, b, (((0,), (0,)), ((), ())), preferred_element_type=f32)


def nn(a, b):
    return jnp.dot(a, b, preferred_element_type=f32)


def split_halves(v):
    hi = v.astype(bf16)
    return hi, (v - hi.astype(f32)).astype(bf16)


def head_matrix(rows, columns):
    row = lax.broadcasted_iota(jnp.int32, (rows, columns), 0)
    col = lax.broadcasted_iota(jnp.int32, (rows, columns), 1)
    return row, col


def spread(v):
    row, col = head_matrix(128, INNER)
    e = jnp.where(row == col // 64, 1.0, 0.0).astype(bf16)
    hi, lo = split_halves(v)
    return nn(hi, e) + nn(lo, e)


def gathered_heads(v):
    row, col = head_matrix(INNER, 128)
    e = jnp.where(row // 64 == col, 1.0, 0.0).astype(bf16)
    hi, lo = split_halves(v)
    return nn(hi, e) + nn(lo, e)


def low_half(shape):
    return lax.broadcasted_iota(jnp.int32, shape, len(shape) - 1) % 128 < 64


def sigmoid(v):
    return 1.0 / (1.0 + jnp.exp(-v))


def turned(v, cos, sin):
    lane = lax.broadcasted_iota(jnp.int32, v.shape, 1) % 64
    w = v.shape[1]
    swapped = jnp.where(lane < 32, pltpu.roll(v, w - 32, 1), pltpu.roll(v, 32, 1))
    return v * cos + jnp.where(lane < 32, -swapped, swapped) * sin


def unit_rows(v):
    r = lax.rsqrt(jnp.mean(v * v, axis=1, keepdims=True) + EPS)
    return v * r, r


def project_body(
    tok, prior, w1, cos, sin, cosp, sinp, normed, q, k2, v2, k2p, v2p, z, cin, step, gains, norm_p
):
    flipped = w1[:, C_DT : C_DT + 128].astype(f32).T
    gains[...] = flipped[8:16, :]
    g = flipped[HEADS : HEADS + 1, :]
    normed[...] = (unit_rows(tok[...].astype(f32))[0] * g).astype(bf16)
    norm_p[...] = (unit_rows(prior[...].astype(f32))[0] * g).astype(bf16)
    lin = nn(normed[...], w1[:, 0:256])
    c, s = cos[...], sin[...]
    for i in range(2):
        cols = slice(128 * i, 128 * i + 128)
        q[:, cols] = turned(lin[:, cols], c, s).astype(bf16)
    low = low_half((TOK, 128))

    def pair(block, cc, ss, kk, vv):
        rot = turned(block, cc, ss)
        shifted = pltpu.roll(rot, 64, 1)
        kk[...] = jnp.where(low, rot, shifted).astype(bf16)
        flat = pltpu.roll(block, 64, 1)
        vv[...] = jnp.where(low, flat, block).astype(bf16)

    lin = nn(normed[...], w1[:, 256:512])
    pair(lin[:, 0:128], c, s, k2, v2)
    step[...] = lin[:, 128:256]
    pair(nn(norm_p[...], w1[:, 256:384]), cosp[...], sinp[...], k2p, v2p)

    @pl.loop(0, 3)
    def _(j):
        at = pl.ds(pl.multiple_of(C_Z + j * 256, 256), 256)
        to = pl.ds(pl.multiple_of(j * 256, 256), 256)
        z[:, to] = nn(normed[...], w1[:, at])

    @pl.loop(0, 4)
    def _(j):
        at = pl.ds(pl.multiple_of(C_U + j * 256, 256), 256)
        to = pl.ds(pl.multiple_of(j * 256, 256), 256)
        cin[0:HALO, to] = nn(norm_p[TOK - HALO : TOK, :], w1[:, at])
        cin[HALO : HALO + TOK, to] = nn(normed[...], w1[:, at])


project = kernel_call(
    project_body,
    [
        ((TOK, WID), bf16),
        ((TOK, QW), bf16),
        ((TOK, 128), bf16),
        ((TOK, 128), bf16),
        ((TOK, 128), bf16),
        ((TOK, 128), bf16),
        ((TOK, INNER), f32),
        ((HALO + TOK, CONV), f32),
        ((TOK, 128), f32),
        ((8, WID), f32),
    ],
    [pltpu.VMEM((TOK, WID), bf16)],
)


def own_bias(rows, start, seg_col, seg_row):
    end = start + rows
    query = lax.broadcasted_iota(jnp.int32, (rows, end), 0) + start
    key = lax.broadcasted_iota(jnp.int32, (rows, end), 1)
    keep = (key <= query) & (seg_col[start:end, 0:1] == seg_row[0:1, TOK : TOK + end])
    return keep


QB = 256


def attend_body(q, k2, v2, k2p, v2p, seg_col, seg_row, out, lse):
    low = low_half((QB, 128))
    for b in range(TOK // QB):
        start, end = b * QB, (b + 1) * QB
        keep = own_bias(QB, start, seg_col, seg_row)
        keep_p = seg_col[start:end, 0:1] == seg_row[0:1, 0:TOK]
        logs = []
        for pair in range(2):
            cols = slice(128 * pair, 128 * pair + 128)
            qp = q[start:end, cols]
            halves = []
            for side in range(2):
                mine = low if side == 0 else ~low
                qh = jnp.where(mine, qp.astype(f32) * 0.125, 0.0).astype(bf16)
                s1 = jnp.where(keep, nt(qh, k2[0:end, :]), NEG)
                s0 = jnp.where(keep_p, nt(qh, k2p[...]), NEG)
                m = jnp.maximum(
                    jnp.max(s1, axis=1, keepdims=True), jnp.max(s0, axis=1, keepdims=True)
                )
                p1, p0 = jnp.exp(s1 - m), jnp.exp(s0 - m)
                total = jnp.sum(p1, axis=1, keepdims=True) + jnp.sum(p0, axis=1, keepdims=True)
                o = nn(p1.astype(bf16), v2[0:end, :]) + nn(p0.astype(bf16), v2p[...])
                halves.append(o / total)
                logs.append(m + jnp.log(total))
            out[start:end, cols] = jnp.where(low, halves[0], halves[1]).astype(bf16)
        lane = lax.broadcasted_iota(jnp.int32, (QB, 128), 1)
        kept = jnp.zeros((QB, 128), f32)
        for h in range(4):
            kept = jnp.where(lane == h, logs[h], kept)
        lse[start:end, :] = kept


attend = kernel_call(attend_body, [((TOK, QW), bf16), ((TOK, 128), f32)])


def attend_back_body(
    q, k2, v2, k2p, v2p, seg_col, seg_row, lse, dout, cos, sin, dq, dkv, dkv_p, dk_s, dv_s, dkp_s, dvp_s
):
    low = low_half((QB, 128))
    for ref in (dk_s, dv_s, dkp_s, dvp_s):
        ref[...] = jnp.zeros_like(ref)
    for b in range(TOK // QB):
        start, end = b * QB, (b + 1) * QB
        keep = own_bias(QB, start, seg_col, seg_row)
        keep_p = seg_col[start:end, 0:1] == seg_row[0:1, 0:TOK]
        for pair in range(2):
            cols = slice(128 * pair, 128 * pair + 128)
            qp = q[start:end, cols]
            dop = dout[start:end, cols]
            halves = []
            for side in range(2):
                mine = low if side == 0 else ~low
                qh = jnp.where(mine, qp.astype(f32) * 0.125, 0.0).astype(bf16)
                doh = jnp.where(mine, dop.astype(f32), 0.0).astype(bf16)
                h = 2 * pair + side
                log_total = lse[start:end, h : h + 1]
                p1 = jnp.exp(jnp.where(keep, nt(qh, k2[0:end, :]), NEG) - log_total)
                p0 = jnp.exp(jnp.where(keep_p, nt(qh, k2p[...]), NEG) - log_total)
                dp1 = nt(doh, v2[0:end, :])
                dp0 = nt(doh, v2p[...])
                delta = jnp.sum(p1 * dp1, axis=1, keepdims=True) + jnp.sum(
                    p0 * dp0, axis=1, keepdims=True
                )
                ds1 = (p1 * (dp1 - delta)).astype(bf16)
                ds0 = (p0 * (dp0 - delta)).astype(bf16)
                dv_s[0:end, :] += tn(p1.astype(bf16), doh)
                dvp_s[...] += tn(p0.astype(bf16), doh)
                dk_s[0:end, :] += tn(ds1, qh)
                dkp_s[...] += tn(ds0, qh)
                halves.append(nn(ds1, k2[0:end, :]) + nn(ds0, k2p[...]))
            dqp = jnp.where(low, halves[0], halves[1]) * 0.125
            dq[start:end, cols] = turned(dqp, cos[start:end, :], -sin[start:end, :]).astype(bf16)
    low = low_half((TOK, 128))

    def joined(dk, dv):
        dk, dv = dk[...], dv[...]
        return jnp.where(low, dk + pltpu.roll(dk, 64, 1), dv + pltpu.roll(dv, 64, 1))

    dkv[...] = joined(dk_s, dv_s)
    dkv_p[...] = joined(dkp_s, dvp_s).astype(bf16)


attend_back = kernel_call(
    attend_back_body,
    [((TOK, QW), bf16), ((TOK, 128), f32), ((TOK, 128), bf16)],
    [pltpu.VMEM((TOK, 128), f32)] * 4,
)


def tap_mask(seg_ext, k):
    now = seg_ext[HALO : HALO + TOK, 0:1]
    at = HALO - 3 + k
    return jnp.where(seg_ext[at : at + TOK, 0:1] == now, 1.0, 0.0)


def lower_ones():
    row, col = head_matrix(SPAN, SPAN)
    return jnp.where(row >= col, 1.0, 0.0)


def rows_of(c):
    return slice(c * SPAN, (c + 1) * SPAN)


def mixer_in_body(cin, taps, step, bias, rate, seg_ext, pre, dt, cum, last):
    run = jnp.zeros((TOK, CONV), f32)
    for k in range(4):
        at = HALO - 3 + k
        run = run + cin[at : at + TOK, :] * taps[k : k + 1, :] * tap_mask(seg_ext, k)
    pre[...] = run
    lane = lax.broadcasted_iota(jnp.int32, (TOK, 128), 1)
    steps = step[...] + bias[...]
    soft = jnp.maximum(steps, 0.0) + jnp.log(1.0 + jnp.exp(-jnp.abs(steps)))
    dt[...] = jnp.where(lane < HEADS, soft, 0.0)
    tri = lower_ones()
    state = jnp.zeros((STATE, INNER), f32)
    for c in range(SPANS):
        rows = rows_of(c)
        own_dt = dt[rows, :]
        total = jnp.dot(tri, own_dt * rate[...], precision=HIGH, preferred_element_type=f32)
        cum[rows, :] = total
        out = pre[rows, 0 : INNER + STATE]
        out = out * sigmoid(out)
        seg = seg_ext[HALO + c * SPAN : HALO + (c + 1) * SPAN, 0:1]
        seg_last = seg[SPAN - 1 : SPAN, :]
        end = total[SPAN - 1 : SPAN, :]
        tail = jnp.where(seg == seg_last, jnp.exp(jnp.minimum(end - total, 0.0)), 0.0) * own_dt
        fresh = tn(out[:, INNER:].astype(bf16), (out[:, 0:INNER] * spread(tail)).astype(bf16))
        if c == 0:
            state = fresh
        else:
            seg_prev = seg_ext[HALO + c * SPAN - 1 : HALO + c * SPAN, 0:1]
            keep = jnp.where(seg_last == seg_prev, jnp.exp(end), 0.0)
            state = state * spread(jnp.broadcast_to(keep, (8, 128)))[0:1, :] + fresh
    last[...] = state.astype(bf16)


mixer_in = kernel_call(
    mixer_in_body,
    [
        ((TOK, CONV), f32),
        ((TOK, 128), f32),
        ((TOK, 128), f32),
        ((STATE, INNER), bf16),
    ],
)


def span_parts(c, cum, seg_ext):
    total = cum[rows_of(c), :]
    seg = seg_ext[HALO + c * SPAN : HALO + (c + 1) * SPAN, 0:1]
    seg_last = seg[SPAN - 1 : SPAN, :]
    seg_prev = seg_ext[HALO + c * SPAN - 1 : HALO + c * SPAN, 0:1]
    end = total[SPAN - 1 : SPAN, :]
    entering = jnp.where(seg == seg_prev, jnp.exp(total), 0.0)
    tail = jnp.where(seg == seg_last, jnp.exp(jnp.minimum(end - total, 0.0)), 0.0)
    return total, entering, tail


def span_bias(c, seg_ext, seg_row):
    row, col = head_matrix(SPAN, SPAN)
    seg = seg_ext[HALO + c * SPAN : HALO + (c + 1) * SPAN, 0:1]
    other = seg_row[0:1, TOK + c * SPAN : TOK + (c + 1) * SPAN]
    return jnp.where((row >= col) & (seg == other), 0.0, NEG)


def mixer_out_body(
    pre, dt, cum, seg_ext, seg_row, first, z, skip, y, gated, states, sc_state
):
    sc_state[...] = first[...].astype(f32)
    low2 = low_half((SPAN, 128))
    for c in range(SPANS):
        rows = rows_of(c)
        total, entering, tail = span_parts(c, cum, seg_ext)
        out = pre[rows, :]
        out = out * sigmoid(out)
        x = out[:, 0:INNER]
        b = out[:, INNER : INNER + STATE].astype(bf16)
        cm = out[:, INNER + STATE :].astype(bf16)
        own_dt = dt[rows, :]
        xs = x * spread(own_dt)
        state = sc_state[...]
        state_b = state.astype(bf16)
        states[c] = state_b
        wide_in = spread(entering)
        run = nn(cm, state_b) * wide_in + x * skip[...]
        inter = nt(cm, b)
        bias = span_bias(c, seg_ext, seg_row)
        total_t = total.T
        gate = z[rows, :]
        gate = gate * sigmoid(gate)
        for pair in range(HEADS // 2):
            cols = slice(128 * pair, 128 * pair + 128)
            parts = []
            for side in range(2):
                h = 2 * pair + side
                decay = jnp.exp(total[:, h : h + 1] - total_t[h : h + 1, :] + bias)
                parts.append((decay * inter).astype(bf16))
            xp = xs[:, cols]
            stack = jnp.concatenate(
                [jnp.where(low2, xp, 0.0).astype(bf16), jnp.where(low2, 0.0, xp).astype(bf16)], axis=0
            )
            yp = run[:, cols] + nn(jnp.concatenate(parts, axis=1), stack)
            y[rows, cols] = yp
            gated[rows, cols] = (yp * gate[:, cols]).astype(bf16)
        if c < SPANS - 1:
            sc_state[...] = state * wide_in[SPAN - 1 : SPAN, :] + tn(
                b, (xs * spread(tail)).astype(bf16)
            )


mixer_out = kernel_call(
    mixer_out_body,
    [((TOK, INNER), f32), ((TOK, INNER), bf16), ((SPANS, STATE, INNER), bf16)],
    [pltpu.VMEM((STATE, INNER), f32)],
)


def mixer_back_in_body(dgated, z, y, pre, cum, seg_ext, dy, dz, first):
    state = jnp.zeros((STATE, INNER), f32)
    for c in reversed(range(SPANS)):
        rows = rows_of(c)
        total, entering, tail = span_parts(c, cum, seg_ext)
        gate = z[rows, :]
        sig = sigmoid(gate)
        grad = dgated[rows, :]
        own = grad * (gate * sig)
        dy[rows, :] = own
        dz[rows, :] = (grad * y[rows, :] * (sig * (1.0 + gate * (1.0 - sig)))).astype(bf16)
        cm = pre[rows, INNER + STATE :]
        cm = (cm * sigmoid(cm)).astype(bf16)
        wide_in = spread(entering)
        fresh = tn(cm, (own * wide_in).astype(bf16))
        state = fresh if c == SPANS - 1 else state * wide_in[SPAN - 1 : SPAN, :] + fresh
    first[...] = state.astype(bf16)


mixer_back_in = kernel_call(
    mixer_back_in_body,
    [((TOK, INNER), f32), ((TOK, INNER), bf16), ((STATE, INNER), bf16)],
)


def mixer_back_body(
    dy, pre, dt, cum, seg_ext, seg_row, states, last, skip, rate, step, bias,
    dpre, dstep, heads, sc_state,
):
    sc_state[...] = last[...].astype(f32)
    low2 = low_half((SPAN, 128))
    lane = lax.broadcasted_iota(jnp.int32, (SPAN, 128), 1)
    tri = lower_ones()
    sum_decay = jnp.zeros((1, 128), f32)
    sum_bias = jnp.zeros((1, 128), f32)
    sum_skip = jnp.zeros((1, 128), f32)
    for c in reversed(range(SPANS)):
        rows = rows_of(c)
        total, entering, tail = span_parts(c, cum, seg_ext)
        lin = pre[rows, :]
        sig = sigmoid(lin)
        out = lin * sig
        slope = sig * (1.0 + lin * (1.0 - sig))
        x = out[:, 0:INNER]
        b = out[:, INNER : INNER + STATE].astype(bf16)
        cm = out[:, INNER + STATE :].astype(bf16)
        own_dt = dt[rows, :]
        wide_dt = spread(own_dt)
        xs = x * wide_dt
        grad = dy[rows, :]
        wide_in = spread(entering)
        wide_tail = spread(tail)
        dstate = sc_state[...]
        dstate_b = dstate.astype(bf16)
        state_b = states[c]
        gin = grad * wide_in
        gin_b = gin.astype(bf16)
        y_state = nn(cm, state_b)
        xt = xs * wide_tail
        xt_b = xt.astype(bf16)
        from_state = nn(b, dstate_b)
        dcm = nt(gin_b, state_b)
        db = nt(xt_b, dstate_b)
        dcum = gathered_heads(gin * y_state)
        moved = gathered_heads(xt * from_state)
        kept = jnp.sum(dstate * state_b.astype(f32), axis=0, keepdims=True)
        kept = kept * wide_in[SPAN - 1 : SPAN, :]
        kept = gathered_heads(jnp.broadcast_to(kept, (8, INNER)))[0:1, :]
        at_end = jnp.sum(moved, axis=0, keepdims=True) + kept
        sub = lax.broadcasted_iota(jnp.int32, (SPAN, 128), 0)
        dcum = dcum - moved + jnp.where(sub == SPAN - 1, at_end, 0.0)
        sc_state[...] = dstate * wide_in[SPAN - 1 : SPAN, :] + tn(cm, gin_b)
        inter = nt(cm, b)
        bias_m = span_bias(c, seg_ext, seg_row)
        total_t = total.T
        dinter = jnp.zeros((SPAN, SPAN), f32)
        col_sums = jnp.zeros((128, SPAN), f32)
        sub_t = lax.broadcasted_iota(jnp.int32, (128, SPAN), 0)
        ddt = jnp.zeros((SPAN, 128), f32)
        dskip = jnp.zeros((SPAN, 128), f32)
        for pair in range(HEADS // 2):
            cols = slice(128 * pair, 128 * pair + 128)
            gp, xp = grad[:, cols], xs[:, cols]
            gp_b, xp_b = gp.astype(bf16), xp.astype(bf16)
            stack = jnp.concatenate(
                [jnp.where(low2, gp, 0.0).astype(bf16), jnp.where(low2, 0.0, gp).astype(bf16)], axis=0
            )
            dm = nt(stack, xp_b)
            parts = []
            for side in range(2):
                h = 2 * pair + side
                decay = jnp.exp(total[:, h : h + 1] - total_t[h : h + 1, :] + bias_m)
                dmh = dm[side * SPAN : (side + 1) * SPAN, :] * decay
                dinter = dinter + dmh
                weight = decay * inter
                parts.append(weight.astype(bf16))
                q = dmh * inter
                dcum = dcum + jnp.where(lane == h, jnp.sum(q, axis=1, keepdims=True), 0.0)
                col_sums = col_sums + jnp.where(sub_t == h, jnp.sum(q, axis=0, keepdims=True), 0.0)
            both = tn(jnp.concatenate(parts, axis=1), gp_b)
            dxs = jnp.where(low2, both[0:SPAN, :], both[SPAN:, :]) + from_state[:, cols] * wide_tail[:, cols]
            xo = x[:, cols]
            dx = dxs * wide_dt[:, cols] + gp * skip[:, cols]
            dpre[rows, cols] = dx * slope[:, cols]
            pick_row, pick_col = head_matrix(128, 128)
            pick = jnp.where(pick_col == 2 * pair + pick_row // 64, 1.0, 0.0).astype(bf16)
            hi, lo = split_halves(dxs * xo)
            ddt = ddt + nn(hi, pick) + nn(lo, pick)
            hi, lo = split_halves(gp * xo)
            dskip = dskip + nn(hi, pick) + nn(lo, pick)
        dinter_b = dinter.astype(bf16)
        dcm = dcm + nn(dinter_b, b)
        db = db + tn(dinter_b, cm)
        dpre[rows, INNER : INNER + STATE] = db * slope[:, INNER : INNER + STATE]
        dpre[rows, INNER + STATE :] = dcm * slope[:, INNER + STATE :]
        dcum = dcum - col_sums.T
        dlog = lax.dot_general(
            tri, dcum, (((0,), (0,)), ((), ())), precision=HIGH, preferred_element_type=f32
        )
        ddt = ddt + dlog * rate[...]
        dsp = jnp.where(lane < HEADS, ddt * sigmoid(step[rows, :] + bias[...]), 0.0)
        dstep[rows, :] = dsp.astype(bf16)
        sum_decay = sum_decay + jnp.sum(dlog * own_dt, axis=0, keepdims=True)
        sum_bias = sum_bias + jnp.sum(dsp, axis=0, keepdims=True)
        sum_skip = sum_skip + jnp.sum(dskip, axis=0, keepdims=True)
    sub8 = lax.broadcasted_iota(jnp.int32, (8, 128), 0)
    heads[...] = jnp.where(
        sub8 == 0,
        sum_decay * rate[...],
        jnp.where(sub8 == 1, sum_bias, jnp.where(sub8 == 2, sum_skip, 0.0)),
    )


mixer_back = kernel_call(
    mixer_back_body,
    [((TOK, CONV), f32), ((TOK, 128), bf16), ((8, 128), f32)],
    [pltpu.VMEM((STATE, INNER), f32)],
)


def inputs_back_body(
    dpre, dpre_next, cin, taps, seg_ext, seg_next, dkv, dkv_back, cos, sin, dq, dstep, dz,
    grads, dtaps, ext,
):
    ext[0:TOK, :] = dpre[...]
    ext[TOK : TOK + 8, :] = dpre_next[...]
    run = jnp.zeros((TOK, CONV), f32)
    now = seg_next[0:TOK, 0:1]
    sub = lax.broadcasted_iota(jnp.int32, (8, CONV), 0)
    taken = jnp.zeros((8, CONV), f32)
    for k in range(4):
        ahead = 3 - k
        same = jnp.where(seg_next[ahead : ahead + TOK, 0:1] == now, 1.0, 0.0)
        run = run + ext[ahead : ahead + TOK, :] * taps[k : k + 1, :] * same
        at = HALO - 3 + k
        part = dpre[...] * cin[at : at + TOK, :] * tap_mask(seg_ext, k)
        taken = taken + jnp.where(sub == k, jnp.sum(part, axis=0, keepdims=True), 0.0)
    dtaps[...] = taken
    grads[:, C_U:] = run.astype(bf16)
    grads[:, C_Q : C_Q + QW] = dq[...]
    both = dkv[...] + dkv_back[...].astype(f32)
    low = low_half((TOK, 128))
    grads[:, C_KV : C_KV + 128] = jnp.where(low, turned(both, cos[...], -sin[...]), both).astype(bf16)
    grads[:, C_DT : C_DT + 128] = dstep[...]
    grads[:, C_Z : C_Z + INNER] = dz[...]


inputs_back = kernel_call(
    inputs_back_body,
    [((TOK, W1C), bf16), ((8, CONV), f32)],
    [pltpu.VMEM((TOK + 8, CONV), f32)],
)


MESH = pl.DeviceIdType.MESH
GC = W1C + W2C
PIECE = 256
PIECES = GC // PIECE
A_PIECES = 7
COLS = (slice(0, A_PIECES * PIECE), slice(A_PIECES * PIECE, GC))
BC0 = C_U + INNER
SHARE = 384
SMALL = CONV + 128


def place():
    f = lax.axis_index("fsdp")
    core = lax.rem(f, 2)
    chip = lax.div(f, 2)
    return lax.div(chip, 4), lax.rem(chip, 4), core


def at_yz(y, z, core):
    return {"fsdp": (lax.rem(y, 4) * 4 + lax.rem(z, 4)) * 2 + core}


def greet(peers):
    barrier = pltpu.get_barrier_semaphore()
    for peer in peers:
        pl.semaphore_signal(barrier, inc=1, device_id=peer, device_id_type=MESH)
    pl.semaphore_wait(barrier, len(peers))


def send(src, dst, sems, k, peer):
    copy = pltpu.make_async_remote_copy(
        src_ref=src,
        dst_ref=dst,
        send_sem=sems.at[0, k],
        recv_sem=sems.at[1, k],
        device_id=peer,
        device_id_type=MESH,
    )
    copy.start()
    return copy


class RingSum:
    def __init__(self, chunk, me, right, left, sems, far, near, joined):
        self.chunk, self.me, self.sems = chunk, me, sems
        self.right, self.left = right, left
        self.far, self.near, self.joined = far, near, joined
        self.sent = []

    def ahead(self, n):
        return lax.rem(self.me + n, 4)

    def start(self):
        c, s = self.chunk, self.sems
        self.far_copies = (
            send(c(self.ahead(2), 0), self.far.at[0], s, 0, self.right),
            send(c(self.ahead(2), 1), self.far.at[1], s, 1, self.left),
        )
        self.direct = (
            send(c(self.ahead(1), 1), self.near.at[0, 1], s, 2, self.right),
            send(c(self.ahead(3), 0), self.near.at[1, 0], s, 3, self.left),
        )

    def forward(self):
        c, s = self.chunk, self.sems
        passed = []
        for side, (peer, n) in enumerate(((self.right, 1), (self.left, 3))):
            self.far_copies[side].wait_recv()
            own = c(self.ahead(n), side)[...]
            self.joined[side] = (own.astype(f32) + self.far[side].astype(f32)).astype(bf16)
            passed.append(send(self.joined.at[side], self.near.at[side, side], s, 4 + side, peer))
        self.passed = tuple(passed)

    def finish(self):
        for copy in self.direct + self.passed:
            copy.wait_recv()

    def total(self, half):
        own = self.chunk(self.me, half)[...].astype(f32)
        return own + self.near[0, half].astype(f32) + self.near[1, half].astype(f32)

    def close(self):
        for copy in self.far_copies + self.direct + self.passed:
            copy.wait_send()


def tail_body(
    normed, grads, dmix, mixed, w1, tok, gain, gmid, dgain2, small,
    parts, tok_grad, small_out,
    dn, dn_back, gbuf, crecv, acc, far_a, near_a, join_a, far_b, near_b, join_b, one_a, one_b,
    far_a2, near_a2, join_a2, far_b2, near_b2, join_b2, fin, fin_back, share, share_back,
    sm_core, sm_z, sm_y, sm_ctx, sm_tp,
    tp_sems, core_sems, a_sems, b_sems, a2_sems, b2_sems, ctx_sems, small_sems,
):
    y, z, core = place()
    ctx, tp = lax.axis_index("ctx"), lax.axis_index("tp")
    sibling = at_yz(y, z, 1 - core)
    z_peers = [at_yz(y, z + n, core) for n in (1, 2, 3)]
    y_peers = [at_yz(y + n, z, core) for n in (1, 2, 3)]
    ctx_peer, tp_peer = {"ctx": 1 - ctx}, {"tp": 1 - tp}
    greet([sibling, ctx_peer, tp_peer] + z_peers + y_peers)

    sm_core[core] = small[...]
    small_copies = [send(sm_core.at[core], sm_core.at[core], small_sems, 0, sibling)]

    @pl.loop(0, WID // 256)
    def _(j):
        to = pl.ds(pl.multiple_of(j * 256, 256), 256)
        dn[:, to] = nt(grads[...], w1[to, :]).astype(bf16)

    dn_copy = send(dn, dn_back, tp_sems, 0, tp_peer)
    v = tok[...].astype(f32)
    dgain1 = jnp.sum(dn[...].astype(f32) * unit_rows(v)[0], axis=0, keepdims=True)
    sub = lax.broadcasted_iota(jnp.int32, (128, WID), 0)
    gain_rows = jnp.where(sub == HEADS, dgain1, jnp.where(sub == HEADS + 1, dgain2[...] * 0.5, 0.0))

    core_copies = []

    def piece(j):
        cols = slice(j * PIECE, (j + 1) * PIECE)
        if j < W1C // PIECE:
            block = tn(normed[...], grads[:, cols])
        else:
            at = slice(j * PIECE - W1C, (j + 1) * PIECE - W1C)
            block = tn(dmix[...], mixed[:, at])
        if j == C_DT // PIECE:
            block = jnp.concatenate([block[:, 0:128], block[:, 128:256] + gain_rows.T], axis=1)
        gbuf[:, :, :, :, cols] = block.astype(bf16).reshape(4, 4, 2, 32, PIECE)
        core_copies.append(
            send(
                gbuf.at[:, :, 1 - core, :, cols], crecv.at[:, :, :, cols], core_sems, j, sibling
            )
        )

    def add_piece(j):
        cols = slice(j * PIECE, (j + 1) * PIECE)
        core_copies[j].wait_recv()
        own = gbuf[:, :, core, :, cols]
        acc[:, :, :, cols] = (own.astype(f32) + crecv[:, :, :, cols].astype(f32)).astype(bf16)

    ca, cb = COLS
    ring_a = RingSum(
        lambda d, h: acc.at[2 * h : 2 * h + 2, d, :, ca], z, z_peers[0], z_peers[2], a_sems,
        far_a, near_a, join_a,
    )
    ring_b = RingSum(
        lambda d, h: acc.at[d, 2 * h : 2 * h + 2, :, cb], y, y_peers[0], y_peers[2], b_sems,
        far_b, near_b, join_b,
    )
    ring_a2 = RingSum(
        lambda d, h: one_a.at[d, 16 * h : 16 * h + 16, :], y, y_peers[0], y_peers[2], a2_sems,
        far_a2, near_a2, join_a2,
    )
    ring_b2 = RingSum(
        lambda d, h: one_b.at[d, 16 * h : 16 * h + 16, :], z, z_peers[0], z_peers[2], b2_sems,
        far_b2, near_b2, join_b2,
    )

    for j in range(PIECES + 1):
        if j < PIECES:
            piece(j)
        if j > 0:
            add_piece(j - 1)
        if j == A_PIECES:
            ring_a.start()
            small_copies[0].wait_recv()
            sm_z[z] = sm_core[0] + sm_core[1]
            z_copies = [
                send(sm_z.at[z], sm_z.at[z], small_sems, 1 + n, peer)
                for n, peer in enumerate(z_peers)
            ]
            small_copies += z_copies
    ring_b.start()
    ring_a.forward()
    ring_b.forward()
    ring_a.finish()
    for h in range(2):
        one_a[2 * h : 2 * h + 2] = ring_a.total(h).astype(bf16)
    ring_a2.start()
    for copy in z_copies:
        copy.wait_recv()
    sm_y[y] = (sm_z[0] + sm_z[1]) + (sm_z[2] + sm_z[3])
    y_copies = [
        send(sm_y.at[y], sm_y.at[y], small_sems, 4 + n, peer) for n, peer in enumerate(y_peers)
    ]
    small_copies += y_copies
    ring_b.finish()
    for h in range(2):
        one_b[2 * h : 2 * h + 2] = ring_b.total(h).astype(bf16)
    ring_b2.start()
    ring_a2.forward()
    ring_b2.forward()
    ring_a2.finish()
    for h in range(2):
        fin[16 * h : 16 * h + 16, ca] = ring_a2.total(h).astype(bf16)
    ring_b2.finish()
    for h in range(2):
        fin[16 * h : 16 * h + 16, cb] = ring_b2.total(h).astype(bf16)
    fin_copy = send(fin, fin_back, ctx_sems, 0, ctx_peer)
    for copy in y_copies:
        copy.wait_recv()
    sm_ctx[ctx] = (sm_y[0] + sm_y[1]) + (sm_y[2] + sm_y[3])
    ctx_copy = send(sm_ctx.at[ctx], sm_ctx.at[ctx], small_sems, 7, ctx_peer)

    dn_copy.wait_recv()
    dh = (dn[...].astype(f32) + dn_back[...].astype(f32)) * gain[...]
    r = lax.rsqrt(jnp.mean(v * v, axis=1, keepdims=True) + EPS)
    inner = jnp.mean(v * dh, axis=1, keepdims=True)
    tok_grad[...] = gmid[...] + r * dh - v * (r * r * r * inner)

    fin_copy.wait_recv()
    total = fin[...].astype(f32) + fin_back[...].astype(f32)
    parts[...] = total
    share[:, 0:128] = total[:, C_DT : C_DT + 128].astype(bf16)
    share[:, 128:384] = total[:, BC0 : BC0 + 256].astype(bf16)
    share_copy = send(share, share_back, ctx_sems, 1, tp_peer)
    ctx_copy.wait_recv()
    sums = sm_ctx[0] + sm_ctx[1]
    small_out[...] = sums
    sm_tp[tp] = sums[0:4, INNER:CONV]
    last_copy = send(sm_tp.at[tp], sm_tp.at[tp], small_sems, 8, tp_peer)
    share_copy.wait_recv()
    both = share[...].astype(f32) + share_back[...].astype(f32)
    lane = lax.broadcasted_iota(jnp.int32, (32, 128), 1)
    parts[:, C_DT : C_DT + 128] = jnp.where(lane < HEADS, total[:, C_DT : C_DT + 128], both[:, 0:128])
    parts[:, BC0 : BC0 + 256] = both[:, 128:384]
    last_copy.wait_recv()
    small_out[0:4, INNER:CONV] = sm_tp[0] + sm_tp[1]

    for ring in (ring_a, ring_b, ring_a2, ring_b2):
        ring.close()
    for copy in core_copies + small_copies + [dn_copy, fin_copy, ctx_copy, share_copy, last_copy]:
        copy.wait_send()


def tail(*args):
    wide_a, wide_b = A_PIECES * PIECE, GC - A_PIECES * PIECE

    def ring_space(lead, wide):
        return [
            pltpu.VMEM((2,) + lead + (wide,), bf16),
            pltpu.VMEM((2, 2) + lead + (wide,), bf16),
            pltpu.VMEM((2,) + lead + (wide,), bf16),
        ]

    def sems(n):
        return pltpu.SemaphoreType.DMA((2, n))

    return pl.pallas_call(
        tail_body,
        out_shape=[
            jax.ShapeDtypeStruct((32, GC), f32),
            jax.ShapeDtypeStruct((TOK, WID), f32),
            jax.ShapeDtypeStruct((8, SMALL), f32),
        ],
        in_specs=vmem(len(args)),
        out_specs=vmem(3),
        scratch_shapes=[
            pltpu.VMEM((TOK, WID), bf16),
            pltpu.VMEM((TOK, WID), bf16),
            pltpu.VMEM((4, 4, 2, 32, GC), bf16),
            pltpu.VMEM((4, 4, 32, GC), bf16),
            pltpu.VMEM((4, 4, 32, GC), bf16),
            *ring_space((2, 32), wide_a),
            *ring_space((2, 32), wide_b),
            pltpu.VMEM((4, 32, wide_a), bf16),
            pltpu.VMEM((4, 32, wide_b), bf16),
            *ring_space((16,), wide_a),
            *ring_space((16,), wide_b),
            pltpu.VMEM((32, GC), bf16),
            pltpu.VMEM((32, GC), bf16),
            pltpu.VMEM((32, SHARE), bf16),
            pltpu.VMEM((32, SHARE), bf16),
            pltpu.VMEM((2, 8, SMALL), f32),
            pltpu.VMEM((4, 8, SMALL), f32),
            pltpu.VMEM((4, 8, SMALL), f32),
            pltpu.VMEM((2, 8, SMALL), f32),
            pltpu.VMEM((2, 4, CONV - INNER), f32),
            sems(1),
            sems(PIECES),
            sems(6),
            sems(6),
            sems(6),
            sems(6),
            sems(2),
            sems(9),
        ],
        compiler_params=pltpu.CompilerParams(
            vmem_limit_bytes=60 * 1024 * 1024, collective_id=0, has_side_effects=True
        ),
    )(*args)


class RingGather:
    def __init__(self, block, me, right, left, sems):
        self.block, self.me, self.sems = block, me, sems
        self.right, self.left = right, left

    def ahead(self, n):
        return lax.rem(self.me + n, 4)

    def start(self):
        own = self.block(self.me, None)
        self.near = (
            send(own, own, self.sems, 0, self.right),
            send(own, own, self.sems, 1, self.left),
        )

    def forward(self):
        self.far = []
        for side, (peer, n) in enumerate(((self.right, 3), (self.left, 1))):
            self.near[side].wait_recv()
            part = self.block(self.ahead(n), side)
            self.far.append(send(part, part, self.sems, 2 + side, peer))

    def finish(self):
        for copy in self.far:
            copy.wait_recv()

    def close(self):
        for copy in list(self.near) + self.far:
            copy.wait_send()


def fetch_body(
    mine, tok, whole, prior, a_sems, b_sems, a2_sems, b2_sems, core_sems, ctx_sems
):
    y, z, core = place()
    ctx = lax.axis_index("ctx")
    width = mine.shape[1]
    half = width // 256 * 128
    ca, cb = slice(0, half), slice(half, width)
    sibling, ctx_peer = at_yz(y, z, 1 - core), {"ctx": 1 - ctx}
    zr, zl = at_yz(y, z + 1, core), at_yz(y, z + 3, core)
    yr, yl = at_yz(y + 1, z, core), at_yz(y + 3, z, core)
    greet([sibling, ctx_peer, zr, zl, yr, yl])
    whole[y, z, core] = mine[...]
    tok_copy = send(tok, prior, ctx_sems, 0, ctx_peer)
    across = []

    def cross(view):
        across.append(send(view, view, core_sems, len(across), sibling))

    def rows16(h):
        return slice(0, 32) if h is None else slice(16 * h, 16 * h + 16)

    def two(h):
        return slice(0, 4) if h is None else slice(2 * h, 2 * h + 2)

    a1 = RingGather(lambda d, h: whole.at[y, d, core, rows16(h), ca], z, zr, zl, a_sems)
    b1 = RingGather(lambda d, h: whole.at[d, z, core, rows16(h), cb], y, yr, yl, b_sems)
    a2 = RingGather(lambda d, h: whole.at[d, two(h), core, :, ca], y, yr, yl, a2_sems)
    b2 = RingGather(lambda d, h: whole.at[two(h), d, core, :, cb], z, zr, zl, b2_sems)
    a1.start()
    b1.start()
    cross(whole.at[y, z, core])
    a1.forward()
    b1.forward()
    a1.finish()
    a2.start()
    b1.finish()
    b2.start()
    for n in (1, 2, 3):
        cross(whole.at[y, a1.ahead(n), core, :, ca])
        cross(whole.at[b1.ahead(n), z, core, :, cb])
    a2.forward()
    b2.forward()
    for n in (1, 3):
        cross(a2.block(a2.ahead(n), None))
        cross(b2.block(b2.ahead(n), None))
    a2.finish()
    cross(a2.block(a2.ahead(2), None))
    b2.finish()
    cross(b2.block(b2.ahead(2), None))
    for copy in across:
        copy.wait_recv()
    tok_copy.wait_recv()
    for ring in (a1, b1, a2, b2):
        ring.close()
    for copy in across + [tok_copy]:
        copy.wait_send()


def fetch(mine, tok):
    def sems(n):
        return pltpu.SemaphoreType.DMA((2, n))

    return pl.pallas_call(
        fetch_body,
        out_shape=[
            jax.ShapeDtypeStruct((4, 4, 2) + mine.shape, bf16),
            jax.ShapeDtypeStruct(tok.shape, bf16),
        ],
        in_specs=vmem(2),
        out_specs=vmem(2),
        scratch_shapes=[sems(4), sems(4), sems(4), sems(4), sems(13), sems(1)],
        compiler_params=pltpu.CompilerParams(
            vmem_limit_bytes=32 * 1024 * 1024, collective_id=1, has_side_effects=True
        ),
    )(mine, tok)


def outputs_body(
    parts, sums, w3, w3_back,
    gain1, gain2, query, keyval, attn, inner, state, step, conv_i, conv_s, decay, bias, skip,
    inner_o, gate_up, down,
):
    flipped = parts[:, C_DT : C_DT + 128].T
    gain1[...] = flipped[HEADS : HEADS + 1, :]
    gain2[...] = flipped[HEADS + 1 : HEADS + 2, :]
    query[...] = parts[:, 0:QW]
    for i in range(2):
        keyval[:, i, :] = parts[:, C_KV + 64 * i : C_KV + 64 * i + 64]
        inner[:, i, :] = parts[:, C_Z + INNER * i : C_Z + INNER * (i + 1)]
        at = slice(FFH * i, FFH * (i + 1))
        gate_up[:, i, :] = w3[:, at].astype(f32) + w3_back[:, at].astype(f32)
    state[...] = parts[:, BC0 : BC0 + 256]
    step[...] = parts[:, C_DT : C_DT + HEADS]
    attn[...] = parts[:, W1C : W1C + QW].T
    inner_o[...] = parts[:, W1C + QW :].T
    at = slice(2 * FFH, 3 * FFH)
    down[...] = (w3[:, at].astype(f32) + w3_back[:, at].astype(f32)).T
    conv_i[...] = sums[0:4, 0:INNER]
    conv_s[...] = sums[0:4, INNER:CONV]
    for n, ref in enumerate((decay, bias, skip)):
        ref[...] = sums[n : n + 1, CONV : CONV + HEADS]


outputs = kernel_call(
    outputs_body,
    [
        ((1, 32), f32),
        ((1, 32), f32),
        ((32, QW), f32),
        ((32, 2, 64), f32),
        ((QW, 32), f32),
        ((32, 2, INNER), f32),
        ((32, 256), f32),
        ((32, HEADS), f32),
        ((4, INNER), f32),
        ((4, CONV - INNER), f32),
        ((1, HEADS), f32),
        ((1, HEADS), f32),
        ((1, HEADS), f32),
        ((INNER, 32), f32),
        ((32, 2, FFH), f32),
        ((FFH, 32), f32),
    ],
    mem=32,
)


def swapped(block, axis):
    return lax.ppermute(block, axis, [(0, 1), (1, 0)])


def pair_sum(block, axis):
    return block.astype(f32) + swapped(block, axis).astype(f32)


def rope_tables(positions):
    indices = jnp.arange(HEAD_WIDTH // 2).astype(f32)
    frequency = jnp.exp(indices * (-2.0 * math.log(ROPE_BASE) / HEAD_WIDTH))
    angles = positions[:, None] * frequency[None, :]
    return (jnp.tile(jnp.cos(angles), (1, 4)), jnp.tile(jnp.sin(angles), (1, 4)))


def norm_back(v, gain_row, dh):
    r = lax.rsqrt(jnp.mean(v * v, axis=1, keepdims=True) + EPS)
    scaled = dh * gain_row
    dv = r * scaled - v * (r * r * r) * jnp.mean(v * scaled, axis=1, keepdims=True)
    return dv, jnp.sum(dh * v * r, axis=0)


def lanes(vector):
    return jnp.pad(vector, (0, 128 - vector.shape[0]))[None, :]


def shards(
    tokens, segments, cotangent, gain_mixer, gain_ffn, query_proj, key_value_weight, attn_out,
    inner_proj, state_proj, step_proj, conv_inner, conv_state, decay_log, step_bias, skip_gain,
    inner_out, gate_up, down_proj,
):
    rows = query_proj.shape[0]
    ctx = lax.axis_index("ctx")
    tok = tokens.reshape(TOK, WID)
    blocks = (
        jnp.concatenate(
            [
                query_proj,
                key_value_weight.reshape(rows, 128),
                step_proj,
                gain_mixer[:, None],
                gain_ffn[:, None],
                jnp.zeros((rows, 114), bf16),
                inner_proj.reshape(rows, 2 * INNER),
                state_proj,
            ],
            axis=1,
        ),
        jnp.concatenate([attn_out.T, inner_out.T], axis=1),
        jnp.concatenate([gate_up.reshape(rows, 2 * FFH), down_proj.T], axis=1),
    )
    w1, prior = fetch(blocks[0], tok)
    w1 = w1.reshape(WID, W1C)
    w2, w3 = (lax.all_gather(b, "fsdp", axis=0, tiled=True) for b in blocks[1:])

    start = ctx * TOK
    cos, sin = rope_tables((start + jnp.arange(TOK)).astype(f32))
    cosp, sinp = rope_tables((start - TOK + jnp.arange(TOK)).astype(f32))
    seg = segments.reshape(-1)
    late = ctx > 0
    seg_now = lax.dynamic_slice_in_dim(seg, start, TOK)
    seg_prior = jnp.where(late, seg[0:TOK], -1)
    seg_after = jnp.where(late, -2, seg[TOK : TOK + 8])
    seg_row = jnp.concatenate([seg_prior, seg_now])[None, :]
    seg_ext = jnp.concatenate([seg_prior[TOK - HALO :], seg_now])[:, None]
    seg_next = jnp.concatenate([seg_now, seg_after])[:, None]
    seg_col = seg_now[:, None]
    taps = jnp.concatenate([conv_inner, conv_state], axis=1).astype(f32)
    bias = lanes(step_bias)
    rate = lanes(-jnp.exp(decay_log))
    skip = jnp.repeat(skip_gain, 64)[None, :]

    normed, q, k2, v2, k2p, v2p, z, cin, step, gains = project(
        tok, prior, w1, cos, sin, cosp, sinp
    )
    gain1, gain2 = gains[HEADS - 8 : HEADS - 7], gains[HEADS - 7 : HEADS - 6]
    pre, dt, cum, last = mixer_in(cin, taps, step, bias, rate, seg_ext)
    first = lax.ppermute(last, "ctx", [(0, 1)])
    attended, lse = attend(q, k2, v2, k2p, v2p, seg_col, seg_row)
    y, gated, states = mixer_out(pre, dt, cum, seg_ext, seg_row, first, z, skip)

    mixed = jnp.concatenate([attended, gated], axis=1)
    branch = pair_sum(nt(mixed, w2).astype(bf16), "tp")
    mid = tok.astype(f32) + branch

    normed2 = (unit_rows(mid)[0] * gain2).astype(bf16)
    wgu, wdown = w3[:, 0 : 2 * FFH], w3[:, 2 * FFH :]
    gu = nn(normed2, wgu)
    gate, up = gu[:, :FFH], gu[:, FFH:]
    sig = sigmoid(gate)
    silu = gate * sig
    act = (silu * up).astype(bf16)
    cot = cotangent.reshape(TOK, WID)
    dact = nn(cot, wdown)
    dgate = dact * up * sig * (1.0 + gate * (1.0 - sig))
    dgu = jnp.concatenate([dgate, dact * silu], axis=1).astype(bf16)
    dnormed2 = pair_sum(nt(dgu, wgu).astype(bf16), "tp")
    dmid, dgain2 = norm_back(mid, gain2, dnormed2)
    grad_mid = cot.astype(f32) + dmid
    dmix = grad_mid.astype(bf16)

    w3_grad = jnp.concatenate([tn(normed2, dgu), tn(cot, act)], axis=1).astype(bf16)
    w3_part = lax.psum_scatter(w3_grad, "fsdp", scatter_dimension=0, tiled=True)

    dmixed = nn(dmix, w2)
    dattended, dgated = dmixed[:, :QW].astype(bf16), dmixed[:, QW:]
    dy, dz, dfirst = mixer_back_in(dgated, z, y, pre, cum, seg_ext)
    dlast = lax.ppermute(dfirst, "ctx", [(1, 0)])
    dq, dkv, dkv_p = attend_back(
        q, k2, v2, k2p, v2p, seg_col, seg_row, lse, dattended, cos, sin
    )
    dkv_back = lax.ppermute(dkv_p, "ctx", [(1, 0)])
    dpre, dstep, heads = mixer_back(
        dy, pre, dt, cum, seg_ext, seg_row, states, dlast, skip, rate, step, bias
    )
    down, dpre = lax.optimization_barrier((nt(act, wdown).astype(bf16), dpre))
    block_out = (mid + pair_sum(down, "tp")).astype(bf16)
    dpre_next = lax.ppermute(dpre[0:8], "ctx", [(1, 0)])
    grads, dtaps = inputs_back(
        dpre, dpre_next, cin, taps, seg_ext, seg_next, dkv, dkv_back, cos, sin, dq, dstep, dz
    )
    small = jnp.concatenate([dtaps, heads], axis=1)
    parts, tokens_grad, sums = tail(
        normed, grads, dmix, mixed, w1, tok, gain1, grad_mid, dgain2[None, :], small
    )
    out = outputs(parts, sums, w3_part, swapped(w3_part, "ctx"))
    shapes = [(rows,)] * 2 + [None] * 8 + [(HEADS,)] * 3 + [None] * 3
    out = [a if s is None else a.reshape(s) for a, s in zip(out, shapes)]
    return (block_out[None], tokens_grad[None], *out)


def solution(mesh):
    return jax.shard_map(
        shards,
        mesh=mesh,
        in_specs=(
            P("fsdp", "ctx", None), P("fsdp", None), P("fsdp", "ctx", None), P("fsdp"), P("fsdp"),
            P("fsdp", "tp"), P("fsdp", None, "tp"), P("tp", "fsdp"), P("fsdp", None, "tp"),
            P("fsdp", None), P("fsdp", "tp"), P(None, "tp"), P(), P("tp"), P("tp"), P("tp"),
            P("tp", "fsdp"), P("fsdp", None, "tp"), P("tp", "fsdp"),
        ),
        out_specs=(
            P("fsdp", "ctx", None), P("fsdp", "ctx", None), P("fsdp"), P("fsdp"), P("fsdp", "tp"),
            P("fsdp", None, "tp"), P("tp", "fsdp"), P("fsdp", None, "tp"), P("fsdp", None),
            P("fsdp", "tp"), P(None, "tp"), P(), P("tp"), P("tp"), P("tp"), P("tp", "fsdp"),
            P("fsdp", None, "tp"), P("tp", "fsdp"),
        ),
        check_vma=False,
    )
```

```python
import functools
import math

import jax
import jax.numpy as jnp
import numpy as np
from jax import lax
from jax.experimental import pallas as pl
from jax.experimental.pallas import tpu as pltpu

from jax.sharding import PartitionSpec as P

f32 = jnp.float32
bf16 = jnp.bfloat16
EPS = 1e-05
NEG = -1e30
ROPE_BASE = 100000000000.0
HEAD_WIDTH = 64
HIGH = lax.Precision.HIGHEST

TOK = 512
WID = 1024
SPAN = 128
SPANS = TOK // SPAN
QW = 256
HEADS = 12
INNER = 768
STATE = 128
CONV = INNER + 2 * STATE
HALO = 16
W1C = 2304
W2C = 1024
W3C = 3072
FFH = 1024
C_Q, C_KV, C_DT, C_Z, C_U = 0, 256, 384, 512, 1280


def vmem(n):
    return [pl.BlockSpec(memory_space=pltpu.VMEM)] * n


def kernel_call(body, outs, scratch=(), mem=24, cost=None):
    def call(*args):
        return pl.pallas_call(
            body,
            out_shape=[jax.ShapeDtypeStruct(s, d) for s, d in outs],
            in_specs=vmem(len(args)),
            out_specs=vmem(len(outs)),
            scratch_shapes=list(scratch),
            compiler_params=pltpu.CompilerParams(vmem_limit_bytes=mem * 1024 * 1024),
            cost_estimate=cost,
        )(*args)

    return call


def nt(a, b):
    return lax.dot_general(a, b, (((1,), (1,)), ((), ())), preferred_element_type=f32)


def tn(a, b):
    return lax.dot_general(a, b, (((0,), (0,)), ((), ())), preferred_element_type=f32)


def nn(a, b):
    return jnp.dot(a, b, preferred_element_type=f32)


def split_halves(v):
    hi = v.astype(bf16)
    return hi, (v - hi.astype(f32)).astype(bf16)


def head_matrix(rows, columns):
    row = lax.broadcasted_iota(jnp.int32, (rows, columns), 0)
    col = lax.broadcasted_iota(jnp.int32, (rows, columns), 1)
    return row, col


def spread(v):
    row, col = head_matrix(128, INNER)
    e = jnp.where(row == col // 64, 1.0, 0.0).astype(bf16)
    hi, lo = split_halves(v)
    return nn(hi, e) + nn(lo, e)


def gathered_heads(v):
    row, col = head_matrix(INNER, 128)
    e = jnp.where(row // 64 == col, 1.0, 0.0).astype(bf16)
    hi, lo = split_halves(v)
    return nn(hi, e) + nn(lo, e)


def low_half(shape):
    return lax.broadcasted_iota(jnp.int32, shape, len(shape) - 1) % 128 < 64


def sigmoid(v):
    return 1.0 / (1.0 + jnp.exp(-v))


def turned(v, cos, sin):
    lane = lax.broadcasted_iota(jnp.int32, v.shape, 1) % 64
    w = v.shape[1]
    swapped = jnp.where(lane < 32, pltpu.roll(v, w - 32, 1), pltpu.roll(v, 32, 1))
    return v * cos + jnp.where(lane < 32, -swapped, swapped) * sin


def unit_rows(v):
    r = lax.rsqrt(jnp.mean(v * v, axis=1, keepdims=True) + EPS)
    return v * r, r


def own_bias(rows, start, seg_col, seg_row):
    end = start + rows
    query = lax.broadcasted_iota(jnp.int32, (rows, end), 0) + start
    key = lax.broadcasted_iota(jnp.int32, (rows, end), 1)
    keep = (key <= query) & (seg_col[start:end, 0:1] == seg_row[0:1, TOK : TOK + end])
    return keep


QB = 256


def attend_body(q, k2, v2, k2p, v2p, seg_col, seg_row, out, lse):
    low = low_half((QB, 128))
    for b in range(TOK // QB):
        start, end = b * QB, (b + 1) * QB
        keep = own_bias(QB, start, seg_col, seg_row)
        keep_p = seg_col[start:end, 0:1] == seg_row[0:1, 0:TOK]
        logs = []
        for pair in range(2):
            cols = slice(128 * pair, 128 * pair + 128)
            qp = q[start:end, cols]
            halves = []
            for side in range(2):
                mine = low if side == 0 else ~low
                qh = jnp.where(mine, qp.astype(f32) * 0.125, 0.0).astype(bf16)
                s1 = jnp.where(keep, nt(qh, k2[0:end, :]), NEG)
                s0 = jnp.where(keep_p, nt(qh, k2p[...]), NEG)
                m = jnp.maximum(
                    jnp.max(s1, axis=1, keepdims=True), jnp.max(s0, axis=1, keepdims=True)
                )
                p1, p0 = jnp.exp(s1 - m), jnp.exp(s0 - m)
                total = jnp.sum(p1, axis=1, keepdims=True) + jnp.sum(p0, axis=1, keepdims=True)
                o = nn(p1.astype(bf16), v2[0:end, :]) + nn(p0.astype(bf16), v2p[...])
                halves.append(o / total)
                logs.append(m + jnp.log(total))
            out[start:end, cols] = jnp.where(low, halves[0], halves[1]).astype(bf16)
        lane = lax.broadcasted_iota(jnp.int32, (QB, 128), 1)
        kept = jnp.zeros((QB, 128), f32)
        for h in range(4):
            kept = jnp.where(lane == h, logs[h], kept)
        lse[start:end, :] = kept


def attend_back_body(
    q, k2, v2, k2p, v2p, seg_col, seg_row, lse, dout, cos, sin, dq, dkv, dkv_p, dk_s, dv_s, dkp_s, dvp_s,
    between=None,
):
    low = low_half((QB, 128))
    for ref in (dk_s, dv_s, dkp_s, dvp_s):
        ref[...] = jnp.zeros_like(ref)
    for b in range(TOK // QB):
        start, end = b * QB, (b + 1) * QB
        keep = own_bias(QB, start, seg_col, seg_row)
        keep_p = seg_col[start:end, 0:1] == seg_row[0:1, 0:TOK]
        for pair in range(2):
            cols = slice(128 * pair, 128 * pair + 128)
            qp = q[start:end, cols]
            dop = dout[start:end, cols]
            halves = []
            for side in range(2):
                mine = low if side == 0 else ~low
                qh = jnp.where(mine, qp.astype(f32) * 0.125, 0.0).astype(bf16)
                doh = jnp.where(mine, dop.astype(f32), 0.0).astype(bf16)
                h = 2 * pair + side
                log_total = lse[start:end, h : h + 1]
                p1 = jnp.exp(jnp.where(keep, nt(qh, k2[0:end, :]), NEG) - log_total)
                p0 = jnp.exp(jnp.where(keep_p, nt(qh, k2p[...]), NEG) - log_total)
                dp1 = nt(doh, v2[0:end, :])
                dp0 = nt(doh, v2p[...])
                delta = jnp.sum(p1 * dp1, axis=1, keepdims=True) + jnp.sum(
                    p0 * dp0, axis=1, keepdims=True
                )
                ds1 = (p1 * (dp1 - delta)).astype(bf16)
                ds0 = (p0 * (dp0 - delta)).astype(bf16)
                dv_s[0:end, :] += tn(p1.astype(bf16), doh)
                dvp_s[...] += tn(p0.astype(bf16), doh)
                dk_s[0:end, :] += tn(ds1, qh)
                dkp_s[...] += tn(ds0, qh)
                halves.append(nn(ds1, k2[0:end, :]) + nn(ds0, k2p[...]))
            if between is not None and pair == 0:
                between()
            dqp = jnp.where(low, halves[0], halves[1]) * 0.125
            dq[start:end, cols] = turned(dqp, cos[start:end, :], -sin[start:end, :]).astype(bf16)
    low = low_half((TOK, 128))

    def joined(dk, dv):
        dk, dv = dk[...], dv[...]
        return jnp.where(low, dk + pltpu.roll(dk, 64, 1), dv + pltpu.roll(dv, 64, 1))

    dkv[...] = joined(dk_s, dv_s)
    dkv_p[...] = joined(dkp_s, dvp_s).astype(bf16)


def tap_mask(seg_ext, k):
    now = seg_ext[HALO : HALO + TOK, 0:1]
    at = HALO - 3 + k
    return jnp.where(seg_ext[at : at + TOK, 0:1] == now, 1.0, 0.0)


def lower_ones():
    row, col = head_matrix(SPAN, SPAN)
    return jnp.where(row >= col, 1.0, 0.0)


def rows_of(c):
    return slice(c * SPAN, (c + 1) * SPAN)


def mixer_in_body(cin, taps, step, bias, rate, seg_ext, pre, dt, cum, last):
    run = jnp.zeros((TOK, CONV), f32)
    for k in range(4):
        at = HALO - 3 + k
        run = run + cin[at : at + TOK, :] * taps[k : k + 1, :] * tap_mask(seg_ext, k)
    pre[...] = run
    lane = lax.broadcasted_iota(jnp.int32, (TOK, 128), 1)
    steps = step[...] + bias[...]
    soft = jnp.maximum(steps, 0.0) + jnp.log(1.0 + jnp.exp(-jnp.abs(steps)))
    dt[...] = jnp.where(lane < HEADS, soft, 0.0)
    tri = lower_ones()
    state = jnp.zeros((STATE, INNER), f32)
    for c in range(SPANS):
        rows = rows_of(c)
        own_dt = dt[rows, :]
        total = jnp.dot(tri, own_dt * rate[...], precision=HIGH, preferred_element_type=f32)
        cum[rows, :] = total
        out = pre[rows, 0 : INNER + STATE]
        out = out * sigmoid(out)
        seg = seg_ext[HALO + c * SPAN : HALO + (c + 1) * SPAN, 0:1]
        seg_last = seg[SPAN - 1 : SPAN, :]
        end = total[SPAN - 1 : SPAN, :]
        tail = jnp.where(seg == seg_last, jnp.exp(jnp.minimum(end - total, 0.0)), 0.0) * own_dt
        fresh = tn(out[:, INNER:].astype(bf16), (out[:, 0:INNER] * spread(tail)).astype(bf16))
        if c == 0:
            state = fresh
        else:
            seg_prev = seg_ext[HALO + c * SPAN - 1 : HALO + c * SPAN, 0:1]
            keep = jnp.where(seg_last == seg_prev, jnp.exp(end), 0.0)
            state = state * spread(jnp.broadcast_to(keep, (8, 128)))[0:1, :] + fresh
    last[...] = state.astype(bf16)


def span_parts(c, cum, seg_ext):
    total = cum[rows_of(c), :]
    seg = seg_ext[HALO + c * SPAN : HALO + (c + 1) * SPAN, 0:1]
    seg_last = seg[SPAN - 1 : SPAN, :]
    seg_prev = seg_ext[HALO + c * SPAN - 1 : HALO + c * SPAN, 0:1]
    end = total[SPAN - 1 : SPAN, :]
    entering = jnp.where(seg == seg_prev, jnp.exp(total), 0.0)
    tail = jnp.where(seg == seg_last, jnp.exp(jnp.minimum(end - total, 0.0)), 0.0)
    return total, entering, tail


def span_bias(c, seg_ext, seg_row):
    row, col = head_matrix(SPAN, SPAN)
    seg = seg_ext[HALO + c * SPAN : HALO + (c + 1) * SPAN, 0:1]
    other = seg_row[0:1, TOK + c * SPAN : TOK + (c + 1) * SPAN]
    return jnp.where((row >= col) & (seg == other), 0.0, NEG)


def mixer_out_body(
    pre, dt, cum, seg_ext, seg_row, first, z, skip, y, gated, states, sc_state
):
    if first is not None:
        sc_state[...] = first[...].astype(f32)
    low2 = low_half((SPAN, 128))
    for c in range(SPANS):
        rows = rows_of(c)
        total, entering, tail = span_parts(c, cum, seg_ext)
        out = pre[rows, :]
        out = out * sigmoid(out)
        x = out[:, 0:INNER]
        b = out[:, INNER : INNER + STATE].astype(bf16)
        cm = out[:, INNER + STATE :].astype(bf16)
        own_dt = dt[rows, :]
        xs = x * spread(own_dt)
        state = sc_state[...]
        state_b = state.astype(bf16)
        states[c] = state_b
        wide_in = spread(entering)
        run = nn(cm, state_b) * wide_in + x * skip[...]
        inter = nt(cm, b)
        bias = span_bias(c, seg_ext, seg_row)
        total_t = total.T
        gate = z[rows, :]
        gate = gate * sigmoid(gate)
        for pair in range(HEADS // 2):
            cols = slice(128 * pair, 128 * pair + 128)
            parts = []
            for side in range(2):
                h = 2 * pair + side
                decay = jnp.exp(total[:, h : h + 1] - total_t[h : h + 1, :] + bias)
                parts.append((decay * inter).astype(bf16))
            xp = xs[:, cols]
            stack = jnp.concatenate(
                [jnp.where(low2, xp, 0.0).astype(bf16), jnp.where(low2, 0.0, xp).astype(bf16)], axis=0
            )
            yp = run[:, cols] + nn(jnp.concatenate(parts, axis=1), stack)
            y[rows, cols] = yp
            gated[rows, cols] = (yp * gate[:, cols]).astype(bf16)
        if c < SPANS - 1:
            sc_state[...] = state * wide_in[SPAN - 1 : SPAN, :] + tn(
                b, (xs * spread(tail)).astype(bf16)
            )


def mixer_back_in_body(dgated, z, y, pre, cum, seg_ext, dy, dz, first):
    state = jnp.zeros((STATE, INNER), f32)
    for c in reversed(range(SPANS)):
        rows = rows_of(c)
        total, entering, tail = span_parts(c, cum, seg_ext)
        gate = z[rows, :]
        sig = sigmoid(gate)
        grad = dgated[rows, :]
        own = grad * (gate * sig)
        dy[rows, :] = own
        dz[rows, :] = (grad * y[rows, :] * (sig * (1.0 + gate * (1.0 - sig)))).astype(bf16)
        cm = pre[rows, INNER + STATE :]
        cm = (cm * sigmoid(cm)).astype(bf16)
        wide_in = spread(entering)
        fresh = tn(cm, (own * wide_in).astype(bf16))
        state = fresh if c == SPANS - 1 else state * wide_in[SPAN - 1 : SPAN, :] + fresh
    first[...] = state.astype(bf16)


def mixer_back_body(
    dy, pre, dt, cum, seg_ext, seg_row, states, last, skip, rate, step, bias,
    dpre, dstep, heads, sc_state, between=None,
):
    if last is not None:
        sc_state[...] = last[...].astype(f32)
    low2 = low_half((SPAN, 128))
    lane = lax.broadcasted_iota(jnp.int32, (SPAN, 128), 1)
    tri = lower_ones()
    sum_decay = jnp.zeros((1, 128), f32)
    sum_bias = jnp.zeros((1, 128), f32)
    sum_skip = jnp.zeros((1, 128), f32)
    for c in reversed(range(SPANS)):
        if between and c in between:
            between[c]()
        rows = rows_of(c)
        total, entering, tail = span_parts(c, cum, seg_ext)
        lin = pre[rows, :]
        sig = sigmoid(lin)
        out = lin * sig
        slope = sig * (1.0 + lin * (1.0 - sig))
        x = out[:, 0:INNER]
        b = out[:, INNER : INNER + STATE].astype(bf16)
        cm = out[:, INNER + STATE :].astype(bf16)
        own_dt = dt[rows, :]
        wide_dt = spread(own_dt)
        xs = x * wide_dt
        grad = dy[rows, :]
        wide_in = spread(entering)
        wide_tail = spread(tail)
        dstate = sc_state[...]
        dstate_b = dstate.astype(bf16)
        state_b = states[c]
        gin = grad * wide_in
        gin_b = gin.astype(bf16)
        y_state = nn(cm, state_b)
        xt = xs * wide_tail
        xt_b = xt.astype(bf16)
        from_state = nn(b, dstate_b)
        dcm = nt(gin_b, state_b)
        db = nt(xt_b, dstate_b)
        dcum = gathered_heads(gin * y_state)
        moved = gathered_heads(xt * from_state)
        kept = jnp.sum(dstate * state_b.astype(f32), axis=0, keepdims=True)
        kept = kept * wide_in[SPAN - 1 : SPAN, :]
        kept = gathered_heads(jnp.broadcast_to(kept, (8, INNER)))[0:1, :]
        at_end = jnp.sum(moved, axis=0, keepdims=True) + kept
        sub = lax.broadcasted_iota(jnp.int32, (SPAN, 128), 0)
        dcum = dcum - moved + jnp.where(sub == SPAN - 1, at_end, 0.0)
        sc_state[...] = dstate * wide_in[SPAN - 1 : SPAN, :] + tn(cm, gin_b)
        inter = nt(cm, b)
        bias_m = span_bias(c, seg_ext, seg_row)
        total_t = total.T
        dinter = jnp.zeros((SPAN, SPAN), f32)
        col_sums = jnp.zeros((128, SPAN), f32)
        sub_t = lax.broadcasted_iota(jnp.int32, (128, SPAN), 0)
        ddt = jnp.zeros((SPAN, 128), f32)
        dskip = jnp.zeros((SPAN, 128), f32)
        for pair in range(HEADS // 2):
            cols = slice(128 * pair, 128 * pair + 128)
            gp, xp = grad[:, cols], xs[:, cols]
            gp_b, xp_b = gp.astype(bf16), xp.astype(bf16)
            stack = jnp.concatenate(
                [jnp.where(low2, gp, 0.0).astype(bf16), jnp.where(low2, 0.0, gp).astype(bf16)], axis=0
            )
            dm = nt(stack, xp_b)
            parts = []
            for side in range(2):
                h = 2 * pair + side
                decay = jnp.exp(total[:, h : h + 1] - total_t[h : h + 1, :] + bias_m)
                dmh = dm[side * SPAN : (side + 1) * SPAN, :] * decay
                dinter = dinter + dmh
                weight = decay * inter
                parts.append(weight.astype(bf16))
                q = dmh * inter
                dcum = dcum + jnp.where(lane == h, jnp.sum(q, axis=1, keepdims=True), 0.0)
                col_sums = col_sums + jnp.where(sub_t == h, jnp.sum(q, axis=0, keepdims=True), 0.0)
            both = tn(jnp.concatenate(parts, axis=1), gp_b)
            dxs = jnp.where(low2, both[0:SPAN, :], both[SPAN:, :]) + from_state[:, cols] * wide_tail[:, cols]
            xo = x[:, cols]
            dx = dxs * wide_dt[:, cols] + gp * skip[:, cols]
            dpre[rows, cols] = dx * slope[:, cols]
            pick_row, pick_col = head_matrix(128, 128)
            pick = jnp.where(pick_col == 2 * pair + pick_row // 64, 1.0, 0.0).astype(bf16)
            hi, lo = split_halves(dxs * xo)
            ddt = ddt + nn(hi, pick) + nn(lo, pick)
            hi, lo = split_halves(gp * xo)
            dskip = dskip + nn(hi, pick) + nn(lo, pick)
        dinter_b = dinter.astype(bf16)
        dcm = dcm + nn(dinter_b, b)
        db = db + tn(dinter_b, cm)
        dpre[rows, INNER : INNER + STATE] = db * slope[:, INNER : INNER + STATE]
        dpre[rows, INNER + STATE :] = dcm * slope[:, INNER + STATE :]
        dcum = dcum - col_sums.T
        dlog = lax.dot_general(
            tri, dcum, (((0,), (0,)), ((), ())), precision=HIGH, preferred_element_type=f32
        )
        ddt = ddt + dlog * rate[...]
        dsp = jnp.where(lane < HEADS, ddt * sigmoid(step[rows, :] + bias[...]), 0.0)
        dstep[rows, :] = dsp.astype(bf16)
        sum_decay = sum_decay + jnp.sum(dlog * own_dt, axis=0, keepdims=True)
        sum_bias = sum_bias + jnp.sum(dsp, axis=0, keepdims=True)
        sum_skip = sum_skip + jnp.sum(dskip, axis=0, keepdims=True)
    sub8 = lax.broadcasted_iota(jnp.int32, (8, 128), 0)
    sums = jnp.where(
        sub8 == 0,
        sum_decay * rate[...],
        jnp.where(sub8 == 1, sum_bias, jnp.where(sub8 == 2, sum_skip, 0.0)),
    )
    if heads is not None:
        heads[...] = sums
    return sums


MESH = pl.DeviceIdType.MESH
SMALL = CONV + 128
BC0 = C_U + INNER


def place():
    f = lax.axis_index("fsdp")
    core = lax.rem(f, 2)
    chip = lax.div(f, 2)
    return lax.div(chip, 4), lax.rem(chip, 4), core


def at_yz(y, z, core):
    return {"fsdp": (lax.rem(y, 4) * 4 + lax.rem(z, 4)) * 2 + core}


def torus_peers():
    y, z, core = place()
    return (
        [at_yz(y, z, 1 - core), {"ctx": 1 - lax.axis_index("ctx")}]
        + [at_yz(y, z + n, core) for n in (1, 2, 3)]
        + [at_yz(y + n, z, core) for n in (1, 2, 3)]
    )


def greet(peers):
    barrier = pltpu.get_barrier_semaphore()
    for peer in peers:
        pl.semaphore_signal(barrier, inc=1, device_id=peer, device_id_type=MESH)
    pl.semaphore_wait(barrier, len(peers))


def send(src, dst, sems, k, peer):
    copy = pltpu.make_async_remote_copy(
        src_ref=src,
        dst_ref=dst,
        send_sem=sems.at[0, k],
        recv_sem=sems.at[1, k],
        device_id=peer,
        device_id_type=MESH,
    )
    copy.start()
    return copy


class Refs:
    def __init__(self, names, refs):
        self.__dict__.update(zip(names, refs))
        self.pending, self.stored, self.used = {}, [], 0

    def fetch(self, *names):
        for name in names:
            self.fetch_from(name, getattr(self, "h_" + name))

    def fetch_from(self, name, src):
        copy = pltpu.make_async_copy(src, getattr(self, name), self.io_sems.at[self.used])
        self.used += 1
        copy.start()
        self.pending[name] = copy

    def need(self, *names):
        for name in names:
            if name in self.pending:
                self.pending.pop(name).wait()
        return getattr(self, names[0])

    def store(self, *names):
        for name in names:
            copy = pltpu.make_async_copy(
                getattr(self, name), getattr(self, "h_" + name), self.io_sems.at[self.used]
            )
            self.used += 1
            copy.start()
            self.stored.append(copy)

    def settle(self):
        for copy in self.stored:
            copy.wait()


def run(body, ins, outs, scratch, collective_id):
    any_spec, vmem_spec = pl.BlockSpec(memory_space=pl.ANY), pl.BlockSpec(memory_space=pltpu.VMEM)
    spaces = [(s[0], s[1] if len(s) == 2 else pltpu.VMEM(s[1], s[2])) for s in scratch]
    spaces.append(("io_sems", pltpu.SemaphoreType.DMA((len(ins) + len(outs) + 4,))))
    names = (
        [("h_" if hbm else "") + n for n, _, hbm in ins]
        + [("h_" if hbm else "") + n for n, _, _, hbm in outs]
        + [n for n, _ in spaces]
    )

    def kernel(*refs):
        body(Refs(names, refs))

    return pl.pallas_call(
        kernel,
        out_shape=[jax.ShapeDtypeStruct(s, d) for _, s, d, _ in outs],
        in_specs=[any_spec if hbm else vmem_spec for _, _, hbm in ins],
        out_specs=[any_spec if hbm else vmem_spec for _, _, _, hbm in outs],
        scratch_shapes=[s for _, s in spaces],
        compiler_params=pltpu.CompilerParams(
            vmem_limit_bytes=62 * 1024 * 1024, collective_id=collective_id, has_side_effects=True
        ),
        cost_estimate=pl.CostEstimate(flops=10**11, bytes_accessed=10**8, transcendentals=0),
    )(*[a for _, a, _ in ins])


def dma_sems(*shape):
    return pltpu.SemaphoreType.DMA(shape)


class DirectGather:
    def __init__(self, block, me, peers, sems):
        self.block, self.me, self.sems, self.peers = block, me, sems, peers

    def start(self):
        own = self.block(self.me)
        self.copies = [send(own, own, self.sems, n, p) for n, p in enumerate(self.peers)]

    def finish(self):
        for copy in self.copies:
            copy.wait_recv()

    def close(self):
        for copy in self.copies:
            copy.wait_send()


class RingGather:
    def __init__(self, block, me, peers, sems):
        self.block, self.me, self.sems = block, me, sems
        self.right, self.left = peers[0], peers[2]

    def ahead(self, n):
        return lax.rem(self.me + n, 4)

    def start(self):
        own = self.block(self.me, None)
        self.near = (
            send(own, own, self.sems, 0, self.right),
            send(own, own, self.sems, 1, self.left),
        )

    def forward(self):
        self.far = []
        for side, (peer, n) in enumerate(((self.right, 3), (self.left, 1))):
            self.near[side].wait_recv()
            part = self.block(self.ahead(n), side)
            self.far.append(send(part, part, self.sems, 2 + side, peer))

    def finish(self):
        for copy in self.far:
            copy.wait_recv()

    def close(self):
        for copy in list(self.near) + self.far:
            copy.wait_send()


class Gather:
    def __init__(self, whole, sems, cross_sems):
        y, z, core = place()
        self.whole, self.y, self.z, self.core = whole, y, z, core
        width = whole.shape[-1]
        half = width // 256 * 128
        ca, cb = slice(0, half), slice(half, width)
        self.ca, self.cb = ca, cb
        peers = torus_peers()
        self.sibling, zs, ys = peers[0], peers[2:5], peers[5:8]
        self.sems, self.across = cross_sems, []

        def two(h):
            return slice(0, 4) if h is None else slice(2 * h, 2 * h + 2)

        self.a1 = DirectGather(lambda d: whole.at[y, d, core, :, ca], z, zs, sems.at[0])
        self.b1 = DirectGather(lambda d: whole.at[d, z, core, :, cb], y, ys, sems.at[1])
        self.a2 = RingGather(lambda d, h: whole.at[d, two(h), core, :, ca], y, ys, sems.at[2])
        self.b2 = RingGather(lambda d, h: whole.at[two(h), d, core, :, cb], z, zs, sems.at[3])

    def cross(self, view):
        self.across.append(send(view, view, self.sems, len(self.across), self.sibling))

    def start(self):
        self.a1.start()
        self.b1.start()

    def turn(self):
        self.a1.finish()
        self.a2.start()
        self.b1.finish()
        self.b2.start()
        self.cross(self.whole.at[self.y, :, self.core, :, self.ca])
        self.cross(self.whole.at[:, self.z, self.core, :, self.cb])

    def forward(self):
        a2, b2 = self.a2, self.b2
        a2.forward()
        b2.forward()
        for n in (1, 3):
            self.cross(a2.block(a2.ahead(n), None))
            self.cross(b2.block(b2.ahead(n), None))

    def finish(self):
        a2, b2 = self.a2, self.b2
        a2.finish()
        self.cross(a2.block(a2.ahead(2), None))
        b2.finish()
        self.cross(b2.block(b2.ahead(2), None))

    def arrived(self):
        for copy in self.across:
            copy.wait_recv()

    def close(self):
        for ring in (self.a1, self.b1, self.a2, self.b2):
            ring.close()
        for copy in self.across:
            copy.wait_send()


class RingSum:
    def __init__(self, chunk, me, peers, sems, far, near, joined):
        self.chunk, self.me, self.sems = chunk, me, sems
        self.right, self.left = peers[0], peers[2]
        self.far, self.near, self.joined = far, near, joined

    def ahead(self, n):
        return lax.rem(self.me + n, 4)

    def start(self):
        c, s = self.chunk, self.sems
        self.far_copies = (
            send(c(self.ahead(2), 0), self.far.at[0], s, 0, self.right),
            send(c(self.ahead(2), 1), self.far.at[1], s, 1, self.left),
        )
        self.direct = (
            send(c(self.ahead(1), 1), self.near.at[0, 1], s, 2, self.right),
            send(c(self.ahead(3), 0), self.near.at[1, 0], s, 3, self.left),
        )

    def forward(self):
        c, s = self.chunk, self.sems
        passed = []
        for side, (peer, n) in enumerate(((self.right, 1), (self.left, 3))):
            self.far_copies[side].wait_recv()
            own = c(self.ahead(n), side)[...]
            self.joined[side] = (own.astype(f32) + self.far[side].astype(f32)).astype(bf16)
            passed.append(send(self.joined.at[side], self.near.at[side, side], s, 4 + side, peer))
        self.passed = tuple(passed)

    def finish(self):
        for copy in self.direct + self.passed:
            copy.wait_recv()

    def total(self, half):
        own = self.chunk(self.me, half)[...].astype(f32)
        return own + self.near[0, half].astype(f32) + self.near[1, half].astype(f32)

    def close(self):
        for copy in self.far_copies + self.direct + self.passed:
            copy.wait_send()


class DirectSum:
    def __init__(self, chunk, me, peers, sems, arrived):
        self.chunk, self.me, self.peers, self.sems, self.arrived = chunk, me, peers, sems, arrived

    def start(self):
        self.copies = [
            send(self.chunk(lax.rem(self.me + n + 1, 4)), self.arrived.at[n], self.sems, n, p)
            for n, p in enumerate(self.peers)
        ]

    def total(self):
        for copy in self.copies:
            copy.wait_recv()
        a = self.arrived
        own = self.chunk(self.me)[...].astype(f32)
        return (own + a[0].astype(f32)) + (a[1].astype(f32) + a[2].astype(f32))

    def close(self):
        for copy in self.copies:
            copy.wait_send()


class Reduce:
    def __init__(self, e, name, fin):
        y, z, core = place()
        g = lambda part: getattr(e, name + part)
        self.gbuf, crecv, self.core, self.fin = getattr(e, name + "gbuf", None), g("crecv"), core, fin
        self.crecv, self.core_sems = crecv, g("core_sems")
        peers = torus_peers()
        self.sibling, zs, ys = peers[0], peers[2:5], peers[5:8]
        width = crecv.shape[-1]
        half = width // 256 * 128
        ca, cb = self.ca, self.cb = slice(0, half), slice(half, width)
        one_a, one_b = self.one_a, self.one_b = g("one_a"), g("one_b")
        s = g("ring_sems")
        self.a = RingSum(
            lambda d, h: crecv.at[2 * h : 2 * h + 2, d, :, ca], z, zs, s.at[0],
            g("far_a"), g("near_a"), g("join_a"),
        )
        self.b = RingSum(
            lambda d, h: crecv.at[d, 2 * h : 2 * h + 2, :, cb], y, ys, s.at[1],
            g("far_b"), g("near_b"), g("join_b"),
        )
        self.a2 = DirectSum(lambda d: one_a.at[d], y, ys, s.at[2], g("late_a"))
        self.b2 = DirectSum(lambda d: one_b.at[d], z, zs, s.at[3], g("late_b"))
        self.copies = {}

    def piece(self, j, block):
        cols = slice(j * 256, (j + 1) * 256)
        self.gbuf[:, :, :, :, cols] = block.astype(bf16).reshape(4, 4, 2, 32, 256)
        self.copies[j] = send(
            self.gbuf.at[:, :, 1 - self.core, :, cols],
            self.crecv.at[:, :, :, cols],
            self.core_sems,
            j,
            self.sibling,
        )

    def add(self, j):
        cols = slice(j * 256, (j + 1) * 256)
        self.copies[j].wait_recv()
        own = self.gbuf[:, :, self.core, :, cols].astype(f32)
        self.crecv[:, :, :, cols] = (own + self.crecv[:, :, :, cols].astype(f32)).astype(bf16)

    def start(self):
        self.a.start()
        self.b.start()

    def forward(self):
        self.a.forward()
        self.b.forward()

    def turn(self):
        for ring, one, second in ((self.a, self.one_a, self.a2), (self.b, self.one_b, self.b2)):
            ring.finish()
            for h in range(2):
                one[2 * h : 2 * h + 2] = ring.total(h).astype(bf16)
            second.start()

    def finish(self):
        self.fin[:, self.ca] = self.a2.total().astype(bf16)
        self.fin[:, self.cb] = self.b2.total().astype(bf16)

    def close(self):
        for ring in (self.a, self.b, self.a2, self.b2):
            ring.close()
        for copy in self.copies.values():
            copy.wait_send()


def reduce_space(name, width, own_buffer=True):
    half = width // 256 * 128
    space = [(name + "crecv", (4, 4, 32, width), bf16)]
    if own_buffer:
        space.append((name + "gbuf", (4, 4, 2, 32, width), bf16))
    for side, wide in (("a", half), ("b", width - half)):
        space += [
            (name + "far_" + side, (2, 2, 32, wide), bf16),
            (name + "near_" + side, (2, 2, 2, 32, wide), bf16),
            (name + "join_" + side, (2, 2, 32, wide), bf16),
            (name + "one_" + side, (4, 32, wide), bf16),
            (name + "late_" + side, (3, 32, wide), bf16),
        ]
    return space + [
        (name + "core_sems", dma_sems(2, width // 256)),
        (name + "ring_sems", dma_sems(4, 2, 6)),
    ]


class SmallSum:
    def __init__(self, e):
        self.sems = e.small_sems
        self.bufs = e.sm_core, e.sm_z, e.sm_y, e.sm_ctx, e.sm_tp
        self.y, self.z, self.core = place()
        self.all = []

    def spread_to(self, buf, at, first_sem, peers):
        self.last = [
            send(buf.at[at], buf.at[at], self.sems, first_sem + n, peer)
            for n, peer in enumerate(peers)
        ]
        self.all += self.last

    def wait(self):
        for copy in self.last:
            copy.wait_recv()

    def start(self, block):
        buf = self.bufs[0]
        buf[self.core] = block
        self.spread_to(buf, self.core, 0, torus_peers()[0:1])

    def along_z(self):
        self.wait()
        buf = self.bufs[1]
        buf[self.z] = self.bufs[0][0] + self.bufs[0][1]
        self.spread_to(buf, self.z, 1, torus_peers()[2:5])

    def along_y(self):
        self.wait()
        buf, old = self.bufs[2], self.bufs[1]
        buf[self.y] = (old[0] + old[1]) + (old[2] + old[3])
        self.spread_to(buf, self.y, 4, torus_peers()[5:8])

    def along_ctx(self):
        self.wait()
        ctx = lax.axis_index("ctx")
        buf, old = self.bufs[3], self.bufs[2]
        buf[ctx] = (old[0] + old[1]) + (old[2] + old[3])
        self.spread_to(buf, ctx, 7, torus_peers()[1:2])

    def along_tp(self):
        self.wait()
        tp = lax.axis_index("tp")
        sums = self.bufs[3][0] + self.bufs[3][1]
        self.bufs[4][tp] = sums[0:4, INNER:CONV]
        self.spread_to(self.bufs[4], tp, 8, [{"tp": 1 - tp}])
        return sums

    def over_tp(self):
        self.wait()
        return self.bufs[4][0] + self.bufs[4][1]

    def close(self):
        for copy in self.all:
            copy.wait_send()


def column_of(row):
    r, c = head_matrix(32, 32)
    return jnp.sum(jnp.where(r == c, jnp.broadcast_to(row.astype(f32), (32, 32)), 0.0), axis=1, keepdims=True)


def pack_body(
    query, keyval, attn, inner, state, step, gain1, gain2, inner_o, gate_up, down, first, second
):
    first[:, C_Q : C_Q + QW] = query[...]
    lane = lax.broadcasted_iota(jnp.int32, (32, 128), 1)
    tail_cols = jnp.where(lane == HEADS, column_of(gain1[...]), 0.0)
    tail_cols = jnp.where(lane == HEADS + 1, column_of(gain2[...]), tail_cols)
    first[:, C_DT : C_DT + 128] = tail_cols.astype(bf16)
    first[:, C_DT : C_DT + HEADS] = step[...].astype(f32).T.astype(bf16)
    for i in range(2):
        first[:, C_KV + 64 * i : C_KV + 64 * i + 64] = keyval[:, i, :]
        first[:, C_Z + INNER * i : C_Z + INNER * (i + 1)] = inner[:, i, :]
        second[:, W2C + FFH * i : W2C + FFH * (i + 1)] = gate_up[:, i, :]
    first[:, BC0 : BC0 + 256] = state[...]
    second[:, 0:QW] = attn[...]
    second[:, QW:W2C] = inner_o[...]
    second[:, W2C + 2 * FFH :] = down[...]


pack = kernel_call(pack_body, [((32, W1C), bf16), ((32, W2C + W3C), bf16)], mem=61)


def place_segments(e):
    seg, seg_ext, seg_row, wide = e.seg, e.seg_ext, e.seg_row, e.wide
    late = lax.axis_index("ctx")
    row = seg[...].astype(f32)
    wide[...] = jnp.broadcast_to(row, (128, 2 * TOK)).T
    own = pl.ds(pl.multiple_of(late * TOK, TOK), TOK)
    before = pl.ds(pl.multiple_of(late * (TOK - HALO), HALO), HALO)
    after = pl.ds(pl.multiple_of((1 - late) * TOK, TOK), 8)
    seg_ext[0:HALO, :] = jnp.where(late > 0, wide[before, :], -1.0)
    seg_ext[HALO : HALO + TOK, :] = wide[own, :]
    seg_ext[HALO + TOK :, :] = jnp.where(late > 0, -2.0, wide[after, :])
    seg_row[:, 0:TOK] = jnp.broadcast_to(jnp.where(late > 0, row[:, 0:TOK], -1.0), (8, TOK))
    seg_row[:, TOK:] = jnp.broadcast_to(seg[0:1, own].astype(f32), (8, TOK))


def forward_body(e):
    py, pz, core = place()
    late = lax.axis_index("ctx")
    ctx_peer = {"ctx": 1 - late}
    e.fetch("tok", "cos", "sin")
    load1 = pltpu.make_async_copy(e.h_shard1, e.w1.at[py, pz, core], e.own_sems.at[0])
    load2 = pltpu.make_async_copy(e.h_shard2, e.w23.at[py, pz, core], e.own_sems.at[1])
    load1.start()
    load2.start()
    greet(torus_peers())
    one = Gather(e.w1, e.sems1, e.cross1)
    two = Gather(e.w23, e.sems2, e.cross2)
    load1.wait()
    one.start()
    load2.wait()
    tok = e.need("tok")
    tok_copy = send(tok, e.prior, e.ctx_sems, 0, ctx_peer)
    two.start()
    e.unit[...] = unit_rows(tok[...].astype(f32))[0]
    one.turn()
    place_segments(e)
    taps, hp, skip = e.taps, e.hp, e.skip
    taps[...] = jnp.zeros_like(taps)
    taps[0:4, 0:INNER] = e.taps_i[...].astype(f32)
    taps[0:4, INNER:] = e.taps_s[...].astype(f32)
    hp[...] = jnp.zeros_like(hp)
    hp[0:1, 0:HEADS] = e.step_bias[...]
    hp[1:2, 0:HEADS] = -jnp.exp(e.decay_log[...])
    hp[2:3, 0:HEADS] = e.skip_gain[...]
    skip[...] = spread(jnp.broadcast_to(hp[2:3, :], (8, 128)))
    e.store("seg_ext", "seg_row", "taps", "hp")
    one.forward()
    two.turn()
    tok_copy.wait_recv()
    one.finish()
    one.arrived()
    e.store("w1")
    w1, normed, norm_p = e.w1, e.normed, e.norm_p

    def columns(at, size):
        return w1[:, :, :, :, at].reshape(WID, size)

    flipped = columns(slice(C_DT, C_DT + 128), 128).astype(f32).T
    e.gains[...] = flipped[8:16, :]
    g = flipped[HEADS : HEADS + 1, :]
    normed[...] = (e.unit[...] * g).astype(bf16)
    norm_p[...] = (unit_rows(e.prior[...].astype(f32))[0] * g).astype(bf16)
    e.store("normed", "gains")
    own = pl.ds(pl.multiple_of(late * TOK, TOK), TOK)
    lin = nn(normed[...], columns(slice(0, 256), 256))
    e.need("cos", "sin")
    c, s = e.cos[own, :], e.sin[own, :]
    for i in range(2):
        cols = slice(128 * i, 128 * i + 128)
        e.q[:, cols] = turned(lin[:, cols], c, s).astype(bf16)
    low = low_half((TOK, 128))

    def pair(block, cc, ss, kk, vv):
        rot = turned(block, cc, ss)
        kk[...] = jnp.where(low, rot, pltpu.roll(rot, 64, 1)).astype(bf16)
        vv[...] = jnp.where(low, pltpu.roll(block, 64, 1), block).astype(bf16)

    lin = nn(normed[...], columns(slice(256, 512), 256))
    pair(lin[:, 0:128], c, s, e.k2, e.v2)
    e.step[...] = lin[:, 128:256]
    pair(nn(norm_p[...], columns(slice(256, 384), 128)), e.cos[0:TOK, :], e.sin[0:TOK, :], e.k2p, e.v2p)
    e.store("q", "k2", "v2", "k2p", "v2p", "step")

    @pl.loop(0, 4)
    def _(j):
        at = pl.ds(pl.multiple_of(C_U + j * 256, 256), 256)
        to = pl.ds(pl.multiple_of(j * 256, 256), 256)
        block = columns(at, 256)
        e.cin[0:HALO, to] = nn(norm_p[TOK - HALO : TOK, :], block)
        e.cin[HALO : HALO + TOK, to] = nn(normed[...], block)

    e.store("cin")
    mixer_in_body(
        e.cin, taps, e.step, hp.at[0:1], hp.at[1:2], e.seg_ext, e.pre, e.dt, e.cum, e.last
    )
    state_copy = send(e.last, e.first, e.ctx_sems, 1, ctx_peer)
    e.store("pre", "dt", "cum")

    @pl.loop(0, 3)
    def _(j):
        at = pl.ds(pl.multiple_of(C_Z + j * 256, 256), 256)
        to = pl.ds(pl.multiple_of(j * 256, 256), 256)
        e.z[:, to] = nn(normed[...], columns(at, 256))

    e.store("z")
    attend_body(
        e.q, e.k2, e.v2, e.k2p, e.v2p, e.seg_ext.at[HALO : HALO + TOK], e.seg_row,
        e.mixed.at[:, 0:QW], e.lse,
    )
    e.store("lse")
    two.forward()
    state_copy.wait_recv()
    e.sc_state[...] = jnp.where(late > 0, e.first[...].astype(f32), 0.0)
    mixer_out_body(
        e.pre, e.dt, e.cum, e.seg_ext, e.seg_row, None, e.z, skip.at[0:1], e.y,
        e.mixed.at[:, QW:], e.states, e.sc_state,
    )
    e.store("mixed", "y", "states")
    two.finish()
    two.arrived()
    e.store("w23")
    one.close()
    two.close()
    tok_copy.wait_send()
    state_copy.wait_send()
    e.settle()


FORWARD_OUTS = [
    ("w1", (4, 4, 2, 32, W1C), bf16),
    ("w23", (4, 4, 2, 32, W2C + W3C), bf16),
    ("normed", (TOK, WID), bf16),
    ("q", (TOK, QW), bf16),
    ("k2", (TOK, 128), bf16),
    ("v2", (TOK, 128), bf16),
    ("k2p", (TOK, 128), bf16),
    ("v2p", (TOK, 128), bf16),
    ("z", (TOK, INNER), f32),
    ("cin", (HALO + TOK, CONV), f32),
    ("step", (TOK, 128), f32),
    ("gains", (8, WID), f32),
    ("pre", (TOK, CONV), f32),
    ("dt", (TOK, 128), f32),
    ("cum", (TOK, 128), f32),
    ("states", (SPANS, STATE, INNER), bf16),
    ("y", (TOK, INNER), f32),
    ("mixed", (TOK, QW + INNER), bf16),
    ("lse", (TOK, 128), f32),
    ("seg_ext", (HALO + TOK + 8, 128), f32),
    ("seg_row", (8, 2 * TOK), f32),
    ("taps", (8, CONV), f32),
    ("hp", (8, 128), f32),
]


def forward(ins):
    hbm = ("shard1", "shard2", "tok", "cos", "sin")
    outs = run(
        forward_body,
        [(n, a, n in hbm) for n, a in ins.items()],
        [(n, s, d, True) for n, s, d in FORWARD_OUTS],
        FORWARD_OUTS
        + [
            ("tok", (TOK, WID), bf16),
            ("cos", (2 * TOK, 128), f32),
            ("sin", (2 * TOK, 128), f32),
            ("prior", (TOK, WID), bf16),
            ("norm_p", (TOK, WID), bf16),
            ("unit", (TOK, WID), f32),
            ("wide", (2 * TOK, 128), f32),
            ("last", (STATE, INNER), bf16),
            ("first", (STATE, INNER), bf16),
            ("skip", (8, INNER), f32),
            ("sc_state", (STATE, INNER), f32),
            ("own_sems", dma_sems(2)),
            ("sems1", dma_sems(4, 2, 4)),
            ("cross1", dma_sems(2, 8)),
            ("sems2", dma_sems(4, 2, 4)),
            ("cross2", dma_sems(2, 8)),
            ("ctx_sems", dma_sems(2, 2)),
        ],
        1,
    )
    return dict(zip([n for n, _, _ in FORWARD_OUTS], outs))


CHUNK = 128
CHUNKS = TOK // CHUNK


def middle_body(e):
    tp_peer = {"tp": 1 - lax.axis_index("tp")}
    e.fetch_from("w2", e.h_w23.at[:, :, :, :, 0:W2C])
    e.fetch("mixed", "gains", "tok", "cot")
    e.fetch_from("w3", e.h_w23.at[:, :, :, :, W2C:])
    greet([tp_peer])
    w2, w3, mixed = e.w2, e.w3, e.mixed
    part, part_back, dn, dn_back = e.part, e.part_back, e.dn, e.dn_back
    normed2, act, dgu, dact, mid = e.normed2, e.act, e.dgu, e.dact, e.mid

    def w3_cols(at, size):
        return w3[:, :, :, :, at].reshape(WID, size)

    def rows_at(c):
        return slice(c * CHUNK, (c + 1) * CHUNK)

    e.need("w2", "mixed")
    copies = []
    for c in range(CHUNKS):
        rows = rows_at(c)
        part[rows, :] = nt(mixed[rows, :], w2[...].reshape(WID, W2C)).astype(bf16)
        copies.append(send(part.at[rows], part_back.at[rows], e.sems, c, tp_peer))
    tok, cot, gains = e.need("tok"), e.need("cot"), e.need("gains")
    gain = gains[HEADS + 1 - 8 : HEADS + 2 - 8, :]
    e.need("w3")

    @pl.loop(0, FFH // 256)
    def _(j):
        at = pl.ds(pl.multiple_of(2 * FFH + j * 256, 256), 256)
        to = pl.ds(pl.multiple_of(j * 256, 256), 256)
        dact[:, to] = nn(cot[...], w3_cols(at, 256))

    backs = []
    for c in range(CHUNKS):
        rows = rows_at(c)
        copies[c].wait_recv()
        m = tok[rows, :].astype(f32) + (part[rows, :].astype(f32) + part_back[rows, :].astype(f32))
        mid[rows, :] = m
        normed2[rows, :] = (unit_rows(m)[0] * gain).astype(bf16)

        @pl.loop(0, FFH // 256)
        def _(j):
            at = pl.ds(pl.multiple_of(j * 256, 256), 256)
            at_up = pl.ds(pl.multiple_of(FFH + j * 256, 256), 256)
            gate = nn(normed2[rows, :], w3_cols(at, 256))
            up = nn(normed2[rows, :], w3_cols(at_up, 256))
            sig = sigmoid(gate)
            silu = gate * sig
            da = dact[rows, at]
            act[rows, at] = (silu * up).astype(bf16)
            dgu[rows, at] = (da * up * (sig + silu * (1.0 - sig))).astype(bf16)
            dgu[rows, at_up] = (da * silu).astype(bf16)

        @pl.loop(0, 4)
        def _(j):
            to = pl.ds(pl.multiple_of(j * 256, 256), 256)
            block = w3[j, :, :, :, 0 : 2 * FFH].reshape(256, 2 * FFH)
            dn[rows, to] = nt(dgu[rows, :], block).astype(bf16)

        backs.append(send(dn.at[rows], dn_back.at[rows], e.back_sems, c, tp_peer))

    e.store("mid")

    @pl.loop(0, FFH // 256)
    def _(j):
        at = pl.ds(pl.multiple_of(j * 256, 256), 256)
        to = pl.ds(pl.multiple_of(2 * FFH + j * 256, 256), 256)
        e.w3_grad[:, :, :, :, to] = tn(cot[...], act[:, at]).astype(bf16).reshape(4, 4, 2, 32, 256)

    @pl.loop(0, 4)
    def _(j):
        at = pl.ds(pl.multiple_of(j * 256, 256), 256)
        block = w3[j, :, :, :, 2 * FFH :].reshape(256, FFH)
        e.down[:, at] = nt(act[...], block).astype(bf16)

    e.store("down")

    @pl.loop(0, 2 * FFH // 256)
    def _(j):
        at = pl.ds(pl.multiple_of(j * 256, 256), 256)
        e.w3_grad[:, :, :, :, at] = tn(normed2[...], dgu[:, at]).astype(bf16).reshape(4, 4, 2, 32, 256)

    e.store("w3_grad")
    taken = jnp.zeros((1, WID), f32)
    for c in range(CHUNKS):
        rows = rows_at(c)
        backs[c].wait_recv()
        dh = dn[rows, :].astype(f32) + dn_back[rows, :].astype(f32)
        unit, r = unit_rows(mid[rows, :])
        taken = taken + jnp.sum(dh * unit, axis=0, keepdims=True)
        scaled = dh * gain
        g = cot[rows, :].astype(f32) + r * (
            scaled - unit * jnp.mean(unit * scaled, axis=1, keepdims=True)
        )
        e.grad_mid[rows, :] = g
        e.dmix[rows, :] = g.astype(bf16)
    e.dgain2[...] = jnp.broadcast_to(taken, (8, WID))
    e.store("dmix", "grad_mid", "dgain2")
    for copy in copies + backs:
        copy.wait_send()
    e.settle()


MIDDLE_OUTS = [
    ("mid", (TOK, WID), f32),
    ("grad_mid", (TOK, WID), f32),
    ("dmix", (TOK, WID), bf16),
    ("down", (TOK, WID), bf16),
    ("w3_grad", (4, 4, 2, 32, W3C), bf16),
    ("dgain2", (8, WID), f32),
]


def middle(ins):
    outs = run(
        middle_body,
        [(n, a, True) for n, a in ins.items()],
        [(n, s, d, True) for n, s, d in MIDDLE_OUTS],
        MIDDLE_OUTS
        + [
            ("w2", (4, 4, 2, 32, W2C), bf16),
            ("w3", (4, 4, 2, 32, W3C), bf16),
            ("mixed", (TOK, WID), bf16),
            ("gains", (8, WID), f32),
            ("tok", (TOK, WID), bf16),
            ("cot", (TOK, WID), bf16),
            ("part", (TOK, WID), bf16),
            ("part_back", (TOK, WID), bf16),
            ("dn", (TOK, WID), bf16),
            ("dn_back", (TOK, WID), bf16),
            ("normed2", (TOK, WID), bf16),
            ("act", (TOK, FFH), bf16),
            ("dgu", (TOK, 2 * FFH), bf16),
            ("dact", (TOK, FFH), f32),
            ("sems", dma_sems(2, CHUNKS)),
            ("back_sems", dma_sems(2, CHUNKS)),
        ],
        2,
    )
    return dict(zip([n for n, _, _ in MIDDLE_OUTS], outs))


EARLY = W2C + INNER + QW
LATE = CONV + 256
DOWN_PIECES = 8


def conv_back(ext, taps, seg_ext, cin, grads):
    run = jnp.zeros((TOK, CONV), f32)
    now = seg_ext[HALO : HALO + TOK, 0:1]
    sub = lax.broadcasted_iota(jnp.int32, (8, CONV), 0)
    taken = jnp.zeros((8, CONV), f32)
    for k in range(4):
        ahead = 3 - k
        same = jnp.where(seg_ext[HALO + ahead : HALO + ahead + TOK, 0:1] == now, 1.0, 0.0)
        run = run + ext[ahead : ahead + TOK, :] * taps[k : k + 1, :] * same
        at = HALO - 3 + k
        part = ext[0:TOK, :] * cin[at : at + TOK, :] * tap_mask(seg_ext, k)
        taken = taken + jnp.where(sub == k, jnp.sum(part, axis=0, keepdims=True), 0.0)
    grads[:, C_U:] = run.astype(bf16)
    return taken


def backward_body(e):
    py, pz, core = place()
    ctx, tp = lax.axis_index("ctx"), lax.axis_index("tp")
    ctx_peer, tp_peer = {"ctx": 1 - ctx}, {"tp": 1 - tp}
    own_rows = pl.ds(pl.multiple_of(ctx * TOK, TOK), TOK)
    e.fetch_from("w2", e.h_w23.at[:, :, :, :, 0:W2C])
    e.fetch("dmix", "z", "y", "pre", "cum", "seg_ext", "mixed", "down")
    half3 = W3C // 2
    e.fetch_from("own3", e.h_w3_grad.at[:, :, core, :, 0:half3])
    e.fetch("q", "k2", "v2", "k2p", "v2p", "seg_row", "lse")
    e.fetch_from("cos", e.h_cos.at[own_rows])
    e.fetch_from("sin", e.h_sin.at[own_rows])
    e.fetch("hp", "dt", "states", "step", "normed", "taps", "cin", "tok", "gains", "dgain2")
    e.fetch_from("late", e.h_mid)
    greet(torus_peers() + [tp_peer])
    sum3 = Reduce(e, "s3_", e.fin_early.at[:, 0:W3C])
    early = Reduce(e, "se_", e.fin_early.at[:, W3C:])
    tail = Reduce(e, "sl_", e.fin_late)
    small = SmallSum(e)
    core3 = send(e.h_w3_grad.at[:, :, 1 - core], sum3.crecv, sum3.core_sems, 0, sum3.sibling)
    grads = e.grads
    down_copies = []

    def down_piece():
        k = len(down_copies)
        rows = slice(k * TOK // DOWN_PIECES, (k + 1) * TOK // DOWN_PIECES)
        down_copies.append(send(e.down.at[rows], e.down_back.at[rows], e.down_sems, k, tp_peer))

    w2, dmix = e.need("w2"), e.need("dmix")

    @pl.loop(0, INNER // 256)
    def _(j):
        at = pl.ds(pl.multiple_of(QW + j * 256, 256), 256)
        to = pl.ds(pl.multiple_of(j * 256, 256), 256)
        e.dgated[:, to] = nn(dmix[...], w2[:, :, :, :, at].reshape(WID, 256))

    e.need("z", "y", "pre", "cum", "seg_ext")
    mixer_back_in_body(
        e.dgated, e.z, e.y, e.pre, e.cum, e.seg_ext, e.dgated, grads.at[:, C_Z : C_Z + INNER], e.dfirst
    )
    state_copy = send(e.dfirst, e.dlast, e.ctx_sems, 0, ctx_peer)
    e.need("down", "mixed")
    down_piece()
    e.datt[...] = nn(dmix[...], w2[:, :, :, :, 0:QW].reshape(WID, QW)).astype(bf16)
    for j in range(4):
        early.piece(j, tn(dmix[...], e.mixed[:, j * 256 : (j + 1) * 256]))
    down_piece()
    e.need("own3", "normed")
    core3.wait_recv()

    def add_half(first):
        for j in range(half3 // 512):
            at = slice(j * 512, (j + 1) * 512)
            cols = slice(first + j * 512, first + (j + 1) * 512)
            total = e.own3[:, :, :, at].astype(f32) + sum3.crecv[:, :, :, cols].astype(f32)
            sum3.crecv[:, :, :, cols] = total.astype(bf16)

    add_half(0)
    e.fetch_from("own3", e.h_w3_grad.at[:, :, core, :, half3:])
    sum3.a.start()
    for j in range(3):
        at = C_Z + j * 256
        early.piece(4 + j, tn(e.normed[...], grads[:, at : at + 256]))
    e.need("own3")
    add_half(half3)
    sum3.b.start()
    e.need("q", "k2", "v2", "k2p", "v2p", "seg_row", "lse", "cos", "sin")
    attend_back_body(
        e.q, e.k2, e.v2, e.k2p, e.v2p, e.seg_ext.at[HALO : HALO + TOK], e.seg_row, e.lse, e.datt,
        e.cos, e.sin, grads.at[:, C_Q : C_Q + QW], e.dkv, e.dkv_p, e.dk_s, e.dv_s, e.dkp_s, e.dvp_s,
        between=down_piece,
    )
    kv_copy = send(e.dkv_p, e.dkv_back, e.ctx_sems, 1, ctx_peer)
    early.piece(7, tn(e.normed[...], grads[:, 0:QW]))
    for j in range(8):
        early.add(j)
    early.start()
    sum3.forward()
    down_piece()
    state_copy.wait_recv()
    e.sc_state[...] = jnp.where(ctx > 0, 0.0, e.dlast[...].astype(f32))
    e.need("hp", "dt", "states", "step")
    e.skip[...] = spread(jnp.broadcast_to(e.hp[2:3, :], (8, 128)))

    def after_first_span():
        down_piece()
        early.forward()

    def after_second_span():
        down_piece()
        sum3.turn()

    def after_third_span():
        down_piece()
        early.turn()

    heads = mixer_back_body(
        e.dgated, e.pre, e.dt, e.cum, e.seg_ext, e.seg_row, e.states, None, e.skip.at[0:1],
        e.hp.at[1:2], e.step, e.hp.at[0:1], e.ext, grads.at[:, C_DT : C_DT + 128], None, e.sc_state,
        between={2: after_first_span, 1: after_second_span, 0: after_third_span},
    )
    rim_copy = send(e.ext.at[0:8], e.rim, e.ctx_sems, 2, ctx_peer)
    for copy in early.copies.values():
        copy.wait_send()
    w1_copy = pltpu.make_async_copy(e.h_w1, early.gbuf, e.own_sems.at[0])
    w1_copy.start()
    kv_copy.wait_recv()
    low = low_half((TOK, 128))
    both = e.dkv[...] + jnp.where(ctx > 0, 0.0, e.dkv_back[...].astype(f32))
    grads[:, C_KV : C_KV + 128] = jnp.where(low, turned(both, e.cos[...], -e.sin[...]), both).astype(bf16)
    e.need("taps", "cin")
    rim_copy.wait_recv()
    e.ext[TOK : TOK + 8, :] = jnp.where(ctx > 0, 0.0, e.rim[...])
    dtaps = conv_back(e.ext, e.taps, e.seg_ext, e.cin, grads)
    small.start(jnp.concatenate([dtaps, heads], axis=1))
    w1_copy.wait()

    def rows_at(c):
        return slice(c * TOK // 4, (c + 1) * TOK // 4)

    dn_copies = []
    for c in range(4):
        rows = rows_at(c)

        @pl.loop(0, 4)
        def _(j):
            to = pl.ds(pl.multiple_of(j * 256, 256), 256)
            e.dn[rows, to] = nt(grads[rows, :], early.gbuf[j].reshape(256, W1C)).astype(bf16)

        dn_copies.append(send(e.dn.at[rows], e.dn_back.at[rows], e.dn_sems, c, tp_peer))
    for j in range(4):
        at = C_U + j * 256
        tail.piece(j, tn(e.normed[...], grads[:, at : at + 256]))
    tok = e.need("tok")
    gains = e.need("gains")
    e.need("dgain2")
    gain = gains[HEADS - 8 : HEADS - 7, :]
    dgain1 = jnp.zeros((1, WID), f32)
    for c in range(4):
        rows = rows_at(c)
        unit = unit_rows(tok[rows, :].astype(f32))[0]
        dgain1 = dgain1 + jnp.sum(e.dn[rows, :].astype(f32) * unit, axis=0, keepdims=True)
    sub = lax.broadcasted_iota(jnp.int32, (128, WID), 0)
    gain_rows = jnp.where(
        sub == HEADS, dgain1, jnp.where(sub == HEADS + 1, e.dgain2[0:1, :] * 0.5, 0.0)
    )
    block = tn(e.normed[...], grads[:, 256:512])
    tail.piece(4, jnp.concatenate([block[:, 0:128], block[:, 128:256] + gain_rows.T], axis=1))
    small.along_z()
    for j in range(5):
        tail.add(j)
    tail.start()
    sum3.finish()
    early.finish()
    fin_copy = send(e.fin_early, e.fin_early_back, e.fin_sems, 0, ctx_peer)
    tail.forward()
    small.along_y()
    late = e.need("late")
    for copy in down_copies:
        copy.wait()
    for c in range(4):
        rows = rows_at(c)
        down = e.down[rows, :].astype(f32) + e.down_back[rows, :].astype(f32)
        e.down[rows, :] = (late[rows, :] + down).astype(bf16)
    block_copy = pltpu.make_async_copy(e.down, e.h_block_out, e.own_sems.at[2])
    block_copy.start()
    e.fetch_from("late", e.h_grad_mid)
    tail.turn()
    small.along_ctx()
    tail.finish()
    late_copy = send(e.fin_late, e.fin_late_back, e.fin_sems, 1, ctx_peer)
    e.need("late")
    for c in range(4):
        rows = rows_at(c)
        dn_copies[c].wait_recv()
        dh = (e.dn[rows, :].astype(f32) + e.dn_back[rows, :].astype(f32)) * gain
        unit, r = unit_rows(tok[rows, :].astype(f32))
        late[rows, :] = late[rows, :] + r * (dh - unit * jnp.mean(unit * dh, axis=1, keepdims=True))
    out_copy = pltpu.make_async_copy(late, e.h_tok_grad, e.own_sems.at[1])
    out_copy.start()
    sums = small.along_tp()
    fin_copy.wait_recv()
    e.parts_early[...] = e.fin_early[...].astype(f32) + e.fin_early_back[...].astype(f32)
    e.store("parts_early")
    late_copy.wait_recv()
    total = e.fin_late[...].astype(f32) + e.fin_late_back[...].astype(f32)
    shared = slice(INNER, LATE)
    e.share[...] = total[:, shared].astype(bf16)
    share_copy = send(e.share, e.share_back, e.fin_sems, 2, tp_peer)
    e.parts_late[:, 0:INNER] = total[:, 0:INNER]
    e.sums[...] = sums
    e.sums[0:4, INNER:CONV] = small.over_tp()
    share_copy.wait_recv()
    both = e.share[...].astype(f32) + e.share_back[...].astype(f32)
    col = lax.broadcasted_iota(jnp.int32, both.shape, 1)
    single = (col >= 256) & (col < 384 + HEADS)
    e.parts_late[:, shared] = jnp.where(single, total[:, shared], both)
    e.store("parts_late", "sums")

    out_copy.wait()
    block_copy.wait()
    core3.wait_send()
    for ring in (sum3, tail):
        ring.close()
    for ring in (early.a, early.b, early.a2, early.b2):
        ring.close()
    small.close()
    for copy in [state_copy, kv_copy, rim_copy, fin_copy, late_copy, share_copy] + dn_copies:
        copy.wait_send()
    e.settle()


BACKWARD_OUTS = [
    ("parts_early", (32, W3C + EARLY), f32),
    ("parts_late", (32, LATE), f32),
    ("sums", (8, SMALL), f32),
]


def backward(ins):
    same = [
        "dmix", "z", "y", "pre", "cum", "seg_ext", "mixed", "down", "q", "k2", "v2", "k2p", "v2p",
        "seg_row", "lse", "hp", "dt", "states", "step", "normed", "taps", "cin", "tok", "gains", "dgain2",
    ]
    early = [
        (n, (4, 4, 2, 32, W1C), d) if n == "se_gbuf" else (n, s, d)
        for n, s, d in [x for x in reduce_space("se_", EARLY) if len(x) == 3]
    ] + [x for x in reduce_space("se_", EARLY) if len(x) == 2]
    outs = run(
        backward_body,
        [(n, a, True) for n, a in ins.items()],
        [(n, s, d, True) for n, s, d in BACKWARD_OUTS] + [("tok_grad", (TOK, WID), f32, True), ("block_out", (TOK, WID), bf16, True)],
        BACKWARD_OUTS
        + [(n, ins[n].shape, ins[n].dtype) for n in same]
        + [
            ("w2", (4, 4, 2, 32, W2C), bf16),
            ("own3", (4, 4, 32, W3C // 2), bf16),
            ("cos", (TOK, 128), f32),
            ("sin", (TOK, 128), f32),
            ("late", (TOK, WID), f32),
            ("down_back", (TOK, WID), bf16),
            ("dgated", (TOK, INNER), f32),
            ("datt", (TOK, QW), bf16),
            ("grads", (TOK, W1C), bf16),
            ("dkv", (TOK, 128), f32),
            ("dkv_p", (TOK, 128), bf16),
            ("dkv_back", (TOK, 128), bf16),
            ("dk_s", (TOK, 128), f32),
            ("dv_s", (TOK, 128), f32),
            ("dkp_s", (TOK, 128), f32),
            ("dvp_s", (TOK, 128), f32),
            ("dfirst", (STATE, INNER), bf16),
            ("dlast", (STATE, INNER), bf16),
            ("skip", (8, INNER), f32),
            ("sc_state", (STATE, INNER), f32),
            ("ext", (TOK + 8, CONV), f32),
            ("rim", (8, CONV), f32),
            ("dn", (TOK, WID), bf16),
            ("dn_back", (TOK, WID), bf16),
            ("fin_early", (32, W3C + EARLY), bf16),
            ("fin_early_back", (32, W3C + EARLY), bf16),
            ("fin_late", (32, LATE), bf16),
            ("fin_late_back", (32, LATE), bf16),
            ("share", (32, LATE - INNER), bf16),
            ("share_back", (32, LATE - INNER), bf16),
            ("sm_core", (2, 8, SMALL), f32),
            ("sm_z", (4, 8, SMALL), f32),
            ("sm_y", (4, 8, SMALL), f32),
            ("sm_ctx", (2, 8, SMALL), f32),
            ("sm_tp", (2, 4, CONV - INNER), f32),
            ("small_sems", dma_sems(2, 9)),
            ("ctx_sems", dma_sems(2, 3)),
            ("down_sems", dma_sems(2, DOWN_PIECES)),
            ("dn_sems", dma_sems(2, 4)),
            ("fin_sems", dma_sems(2, 3)),
            ("own_sems", dma_sems(3)),
        ]
        + reduce_space("s3_", W3C, own_buffer=False)
        + early
        + reduce_space("sl_", LATE),
        0,
    )
    return dict(zip([n for n, _, _ in BACKWARD_OUTS] + ["tok_grad", "block_out"], outs))


def outputs_body(
    early, late, sums,
    gain1, gain2, query, keyval, attn, inner, state, step, conv_i, conv_s, decay, bias, skip,
    inner_o, gate_up, down,
):
    flipped = late[:, LATE - 128 :].T
    gain1[...] = flipped[HEADS : HEADS + 1, :]
    gain2[...] = flipped[HEADS + 1 : HEADS + 2, :]
    step[...] = flipped[0:HEADS, :]
    at2 = W3C
    query[...] = early[:, at2 + W2C + INNER :]
    for i in range(2):
        at = CONV + 64 * i
        keyval[:, i, :] = late[:, at : at + 64]
        gate_up[:, i, :] = early[:, FFH * i : FFH * (i + 1)]
    inner[:, 0, :] = early[:, at2 + W2C : at2 + W2C + INNER]
    inner[:, 1, :] = late[:, 0:INNER]
    state[...] = late[:, INNER:CONV]
    attn[...] = early[:, at2 : at2 + QW]
    inner_o[...] = early[:, at2 + QW : at2 + W2C]
    down[...] = early[:, 2 * FFH : 3 * FFH]
    conv_i[...] = sums[0:4, 0:INNER]
    conv_s[...] = sums[0:4, INNER:CONV]
    for n, ref in enumerate((decay, bias, skip)):
        ref[...] = sums[n : n + 1, CONV : CONV + HEADS]


outputs = kernel_call(
    outputs_body,
    [
        ((1, 32), f32),
        ((1, 32), f32),
        ((32, QW), f32),
        ((32, 2, 64), f32),
        ((32, QW), f32),
        ((32, 2, INNER), f32),
        ((32, 256), f32),
        ((HEADS, 32), f32),
        ((4, INNER), f32),
        ((4, CONV - INNER), f32),
        ((1, HEADS), f32),
        ((1, HEADS), f32),
        ((1, HEADS), f32),
        ((32, INNER), f32),
        ((32, 2, FFH), f32),
        ((32, FFH), f32),
    ],
    mem=61,
)


def rope_tables():
    indices = np.arange(HEAD_WIDTH // 2, dtype=np.float32)
    frequency = np.exp(indices * np.float32(-2.0 * math.log(ROPE_BASE) / HEAD_WIDTH))
    angles = np.arange(2 * TOK, dtype=np.float32)[:, None] * frequency[None, :].astype(np.float32)
    angles = angles.astype(np.float64)
    return tuple(np.tile(t(angles), (1, 4)).astype(np.float32) for t in (np.cos, np.sin))


def shards(
    tokens, segments, cotangent, gain_mixer, gain_ffn, query_proj, key_value_weight, attn_out,
    inner_proj, state_proj, step_proj, conv_inner, conv_state, decay_log, step_bias, skip_gain,
    inner_out, gate_up, down_proj,
):
    rows = query_proj.shape[0]
    tok = tokens.reshape(TOK, WID)
    cot = cotangent.reshape(TOK, WID)
    shard1, shard2 = pack(
        query_proj, key_value_weight, attn_out.T, inner_proj, state_proj, step_proj.T,
        gain_mixer.reshape(1, rows), gain_ffn.reshape(1, rows), inner_out.T, gate_up, down_proj.T,
    )
    cos, sin = (jnp.asarray(t) for t in rope_tables())
    kept = forward(
        dict(
            shard1=shard1, shard2=shard2, tok=tok, cos=cos, sin=sin, seg=segments,
            taps_i=conv_inner, taps_s=conv_state, step_bias=step_bias.reshape(1, HEADS),
            decay_log=decay_log.reshape(1, HEADS), skip_gain=skip_gain.reshape(1, HEADS),
        )
    )
    kept |= dict(tok=tok, cos=cos, sin=sin)
    between = middle({n: kept[n] for n in ("w23", "mixed", "gains", "tok")} | dict(cot=cot))
    done = backward(kept | between)
    out = outputs(done["parts_early"], done["parts_late"], done["sums"])
    forms = [(rows,)] * 2 + [None] * 2 + ["T"] + [None] * 2 + ["T"] + [None] * 2
    forms += [(HEADS,)] * 3 + ["T", None, "T"]
    out = [a if f is None else a.T if f == "T" else a.reshape(f) for a, f in zip(out, forms)]
    return (done["block_out"][None], done["tok_grad"][None], *out)


def solution(mesh):
    return jax.shard_map(
        shards,
        mesh=mesh,
        in_specs=(
            P("fsdp", "ctx", None), P("fsdp", None), P("fsdp", "ctx", None), P("fsdp"), P("fsdp"),
            P("fsdp", "tp"), P("fsdp", None, "tp"), P("tp", "fsdp"), P("fsdp", None, "tp"),
            P("fsdp", None), P("fsdp", "tp"), P(None, "tp"), P(), P("tp"), P("tp"), P("tp"),
            P("tp", "fsdp"), P("fsdp", None, "tp"), P("tp", "fsdp"),
        ),
        out_specs=(
            P("fsdp", "ctx", None), P("fsdp", "ctx", None), P("fsdp"), P("fsdp"), P("fsdp", "tp"),
            P("fsdp", None, "tp"), P("tp", "fsdp"), P("fsdp", None, "tp"), P("fsdp", None),
            P("fsdp", "tp"), P(None, "tp"), P(), P("tp"), P("tp"), P("tp"), P("tp", "fsdp"),
            P("fsdp", None, "tp"), P("tp", "fsdp"),
        ),
        check_vma=False,
    )
```

```python
import functools
import math

import jax
import jax.numpy as jnp
import numpy as np
from jax import lax
from jax.experimental import pallas as pl
from jax.experimental.pallas import tpu as pltpu

from jax.sharding import PartitionSpec as P

f32 = jnp.float32
bf16 = jnp.bfloat16
EPS = 1e-05
NEG = -1e30
ROPE_BASE = 100000000000.0
HEAD_WIDTH = 64
HIGH = lax.Precision.HIGHEST

TOK = 512
WID = 1024
SPAN = 128
SPANS = TOK // SPAN
QW = 256
HEADS = 12
INNER = 768
STATE = 128
CONV = INNER + 2 * STATE
HALO = 16
W1C = 2304
W2C = 1024
W3C = 3072
FFH = 1024
C_Q, C_KV, C_DT, C_Z, C_U = 0, 256, 384, 512, 1280


def vmem(n):
    return [pl.BlockSpec(memory_space=pltpu.VMEM)] * n


def kernel_call(body, outs, scratch=(), mem=24, cost=None):
    def call(*args):
        return pl.pallas_call(
            body,
            out_shape=[jax.ShapeDtypeStruct(s, d) for s, d in outs],
            in_specs=vmem(len(args)),
            out_specs=vmem(len(outs)),
            scratch_shapes=list(scratch),
            compiler_params=pltpu.CompilerParams(vmem_limit_bytes=mem * 1024 * 1024),
            cost_estimate=cost,
        )(*args)

    return call


def nt(a, b):
    return lax.dot_general(a, b, (((1,), (1,)), ((), ())), preferred_element_type=f32)


def tn(a, b):
    return lax.dot_general(a, b, (((0,), (0,)), ((), ())), preferred_element_type=f32)


def nn(a, b):
    return jnp.dot(a, b, preferred_element_type=f32)


def split_halves(v):
    hi = v.astype(bf16)
    return hi, (v - hi.astype(f32)).astype(bf16)


def head_matrix(rows, columns):
    row = lax.broadcasted_iota(jnp.int32, (rows, columns), 0)
    col = lax.broadcasted_iota(jnp.int32, (rows, columns), 1)
    return row, col


def spread(v):
    row, col = head_matrix(128, INNER)
    e = jnp.where(row == col // 64, 1.0, 0.0).astype(bf16)
    hi, lo = split_halves(v)
    return nn(hi, e) + nn(lo, e)


def gathered_heads(v):
    row, col = head_matrix(INNER, 128)
    e = jnp.where(row // 64 == col, 1.0, 0.0).astype(bf16)
    hi, lo = split_halves(v)
    return nn(hi, e) + nn(lo, e)


def low_half(shape):
    return lax.broadcasted_iota(jnp.int32, shape, len(shape) - 1) % 128 < 64


def sigmoid(v):
    return 1.0 / (1.0 + jnp.exp(-v))


def turned(v, cos, sin):
    lane = lax.broadcasted_iota(jnp.int32, v.shape, 1) % 64
    w = v.shape[1]
    swapped = jnp.where(lane < 32, pltpu.roll(v, w - 32, 1), pltpu.roll(v, 32, 1))
    return v * cos + jnp.where(lane < 32, -swapped, swapped) * sin


def unit_rows(v):
    r = lax.rsqrt(jnp.mean(v * v, axis=1, keepdims=True) + EPS)
    return v * r, r


def own_bias(rows, start, seg_col, seg_row):
    end = start + rows
    query = lax.broadcasted_iota(jnp.int32, (rows, end), 0) + start
    key = lax.broadcasted_iota(jnp.int32, (rows, end), 1)
    keep = (key <= query) & (seg_col[start:end, 0:1] == seg_row[0:1, TOK : TOK + end])
    return keep


QB = 256


def attend_body(q, k2, v2, k2p, v2p, seg_col, seg_row, out, lse):
    low = low_half((QB, 128))
    for b in range(TOK // QB):
        start, end = b * QB, (b + 1) * QB
        keep = own_bias(QB, start, seg_col, seg_row)
        keep_p = seg_col[start:end, 0:1] == seg_row[0:1, 0:TOK]
        logs = []
        for pair in range(2):
            cols = slice(128 * pair, 128 * pair + 128)
            qp = q[start:end, cols]
            halves = []
            for side in range(2):
                mine = low if side == 0 else ~low
                qh = jnp.where(mine, qp.astype(f32) * 0.125, 0.0).astype(bf16)
                s1 = jnp.where(keep, nt(qh, k2[0:end, :]), NEG)
                s0 = jnp.where(keep_p, nt(qh, k2p[...]), NEG)
                m = jnp.maximum(
                    jnp.max(s1, axis=1, keepdims=True), jnp.max(s0, axis=1, keepdims=True)
                )
                p1, p0 = jnp.exp(s1 - m), jnp.exp(s0 - m)
                total = jnp.sum(p1, axis=1, keepdims=True) + jnp.sum(p0, axis=1, keepdims=True)
                o = nn(p1.astype(bf16), v2[0:end, :]) + nn(p0.astype(bf16), v2p[...])
                halves.append(o / total)
                logs.append(m + jnp.log(total))
            out[start:end, cols] = jnp.where(low, halves[0], halves[1]).astype(bf16)
        lane = lax.broadcasted_iota(jnp.int32, (QB, 128), 1)
        kept = jnp.zeros((QB, 128), f32)
        for h in range(4):
            kept = jnp.where(lane == h, logs[h], kept)
        lse[start:end, :] = kept


def attend_back_body(
    q, k2, v2, k2p, v2p, seg_col, seg_row, lse, dout, cos, sin, dq, dkv, dkv_p, dk_s, dv_s, dkp_s, dvp_s,
    between=None,
):
    low = low_half((QB, 128))
    for ref in (dk_s, dv_s, dkp_s, dvp_s):
        ref[...] = jnp.zeros_like(ref)
    for b in range(TOK // QB):
        start, end = b * QB, (b + 1) * QB
        keep = own_bias(QB, start, seg_col, seg_row)
        keep_p = seg_col[start:end, 0:1] == seg_row[0:1, 0:TOK]
        for pair in range(2):
            cols = slice(128 * pair, 128 * pair + 128)
            qp = q[start:end, cols]
            dop = dout[start:end, cols]
            halves = []
            for side in range(2):
                mine = low if side == 0 else ~low
                qh = jnp.where(mine, qp.astype(f32) * 0.125, 0.0).astype(bf16)
                doh = jnp.where(mine, dop.astype(f32), 0.0).astype(bf16)
                h = 2 * pair + side
                log_total = lse[start:end, h : h + 1]
                p1 = jnp.exp(jnp.where(keep, nt(qh, k2[0:end, :]), NEG) - log_total)
                p0 = jnp.exp(jnp.where(keep_p, nt(qh, k2p[...]), NEG) - log_total)
                dp1 = nt(doh, v2[0:end, :])
                dp0 = nt(doh, v2p[...])
                delta = jnp.sum(p1 * dp1, axis=1, keepdims=True) + jnp.sum(
                    p0 * dp0, axis=1, keepdims=True
                )
                ds1 = (p1 * (dp1 - delta)).astype(bf16)
                ds0 = (p0 * (dp0 - delta)).astype(bf16)
                dv_s[0:end, :] += tn(p1.astype(bf16), doh)
                dvp_s[...] += tn(p0.astype(bf16), doh)
                dk_s[0:end, :] += tn(ds1, qh)
                dkp_s[...] += tn(ds0, qh)
                halves.append(nn(ds1, k2[0:end, :]) + nn(ds0, k2p[...]))
            if between and pair == 0 and b in between:
                between[b]()
            dqp = jnp.where(low, halves[0], halves[1]) * 0.125
            dq[start:end, cols] = turned(dqp, cos[start:end, :], -sin[start:end, :]).astype(bf16)
    low = low_half((TOK, 128))

    def joined(dk, dv):
        dk, dv = dk[...], dv[...]
        return jnp.where(low, dk + pltpu.roll(dk, 64, 1), dv + pltpu.roll(dv, 64, 1))

    dkv[...] = joined(dk_s, dv_s)
    dkv_p[...] = joined(dkp_s, dvp_s).astype(bf16)


def tap_mask(seg_ext, k):
    now = seg_ext[HALO : HALO + TOK, 0:1]
    at = HALO - 3 + k
    return jnp.where(seg_ext[at : at + TOK, 0:1] == now, 1.0, 0.0)


def lower_ones():
    row, col = head_matrix(SPAN, SPAN)
    return jnp.where(row >= col, 1.0, 0.0)


def rows_of(c):
    return slice(c * SPAN, (c + 1) * SPAN)


def mixer_in_body(cin, taps, step, bias, rate, seg_ext, pre, dt, cum, last):
    run = jnp.zeros((TOK, CONV), f32)
    for k in range(4):
        at = HALO - 3 + k
        run = run + cin[at : at + TOK, :] * taps[k : k + 1, :] * tap_mask(seg_ext, k)
    pre[...] = run
    lane = lax.broadcasted_iota(jnp.int32, (TOK, 128), 1)
    steps = step[...] + bias[...]
    soft = jnp.maximum(steps, 0.0) + jnp.log(1.0 + jnp.exp(-jnp.abs(steps)))
    dt[...] = jnp.where(lane < HEADS, soft, 0.0)
    tri = lower_ones()
    state = jnp.zeros((STATE, INNER), f32)
    for c in range(SPANS):
        rows = rows_of(c)
        own_dt = dt[rows, :]
        total = jnp.dot(tri, own_dt * rate[...], precision=HIGH, preferred_element_type=f32)
        cum[rows, :] = total
        out = pre[rows, 0 : INNER + STATE]
        out = out * sigmoid(out)
        seg = seg_ext[HALO + c * SPAN : HALO + (c + 1) * SPAN, 0:1]
        seg_last = seg[SPAN - 1 : SPAN, :]
        end = total[SPAN - 1 : SPAN, :]
        tail = jnp.where(seg == seg_last, jnp.exp(jnp.minimum(end - total, 0.0)), 0.0) * own_dt
        fresh = tn(out[:, INNER:].astype(bf16), (out[:, 0:INNER] * spread(tail)).astype(bf16))
        if c == 0:
            state = fresh
        else:
            seg_prev = seg_ext[HALO + c * SPAN - 1 : HALO + c * SPAN, 0:1]
            keep = jnp.where(seg_last == seg_prev, jnp.exp(end), 0.0)
            state = state * spread(jnp.broadcast_to(keep, (8, 128)))[0:1, :] + fresh
    last[...] = state.astype(bf16)


def span_parts(c, cum, seg_ext):
    total = cum[rows_of(c), :]
    seg = seg_ext[HALO + c * SPAN : HALO + (c + 1) * SPAN, 0:1]
    seg_last = seg[SPAN - 1 : SPAN, :]
    seg_prev = seg_ext[HALO + c * SPAN - 1 : HALO + c * SPAN, 0:1]
    end = total[SPAN - 1 : SPAN, :]
    entering = jnp.where(seg == seg_prev, jnp.exp(total), 0.0)
    tail = jnp.where(seg == seg_last, jnp.exp(jnp.minimum(end - total, 0.0)), 0.0)
    return total, entering, tail


def span_bias(c, seg_ext, seg_row):
    row, col = head_matrix(SPAN, SPAN)
    seg = seg_ext[HALO + c * SPAN : HALO + (c + 1) * SPAN, 0:1]
    other = seg_row[0:1, TOK + c * SPAN : TOK + (c + 1) * SPAN]
    return jnp.where((row >= col) & (seg == other), 0.0, NEG)


def mixer_out_body(
    pre, dt, cum, seg_ext, seg_row, first, z, skip, y, gated, states, sc_state
):
    if first is not None:
        sc_state[...] = first[...].astype(f32)
    low2 = low_half((SPAN, 128))
    for c in range(SPANS):
        rows = rows_of(c)
        total, entering, tail = span_parts(c, cum, seg_ext)
        out = pre[rows, :]
        out = out * sigmoid(out)
        x = out[:, 0:INNER]
        b = out[:, INNER : INNER + STATE].astype(bf16)
        cm = out[:, INNER + STATE :].astype(bf16)
        own_dt = dt[rows, :]
        xs = x * spread(own_dt)
        state = sc_state[...]
        state_b = state.astype(bf16)
        states[c] = state_b
        wide_in = spread(entering)
        run = nn(cm, state_b) * wide_in + x * skip[...]
        inter = nt(cm, b)
        bias = span_bias(c, seg_ext, seg_row)
        total_t = total.T
        gate = z[rows, :]
        gate = gate * sigmoid(gate)
        for pair in range(HEADS // 2):
            cols = slice(128 * pair, 128 * pair + 128)
            parts = []
            for side in range(2):
                h = 2 * pair + side
                decay = jnp.exp(total[:, h : h + 1] - total_t[h : h + 1, :] + bias)
                parts.append((decay * inter).astype(bf16))
            xp = xs[:, cols]
            stack = jnp.concatenate(
                [jnp.where(low2, xp, 0.0).astype(bf16), jnp.where(low2, 0.0, xp).astype(bf16)], axis=0
            )
            yp = run[:, cols] + nn(jnp.concatenate(parts, axis=1), stack)
            y[rows, cols] = yp
            gated[rows, cols] = (yp * gate[:, cols]).astype(bf16)
        if c < SPANS - 1:
            sc_state[...] = state * wide_in[SPAN - 1 : SPAN, :] + tn(
                b, (xs * spread(tail)).astype(bf16)
            )


def mixer_back_in_body(dgated, z, y, pre, cum, seg_ext, dy, dz, first):
    state = jnp.zeros((STATE, INNER), f32)
    for c in reversed(range(SPANS)):
        rows = rows_of(c)
        total, entering, tail = span_parts(c, cum, seg_ext)
        gate = z[rows, :]
        sig = sigmoid(gate)
        grad = dgated[rows, :]
        own = grad * (gate * sig)
        dy[rows, :] = own
        dz[rows, :] = (grad * y[rows, :] * (sig * (1.0 + gate * (1.0 - sig)))).astype(bf16)
        cm = pre[rows, INNER + STATE :]
        cm = (cm * sigmoid(cm)).astype(bf16)
        wide_in = spread(entering)
        fresh = tn(cm, (own * wide_in).astype(bf16))
        state = fresh if c == SPANS - 1 else state * wide_in[SPAN - 1 : SPAN, :] + fresh
    first[...] = state.astype(bf16)


def mixer_back_body(
    dy, pre, dt, cum, seg_ext, seg_row, states, last, skip, rate, step, bias,
    dpre, dstep, heads, sc_state, between=None,
):
    if last is not None:
        sc_state[...] = last[...].astype(f32)
    low2 = low_half((SPAN, 128))
    lane = lax.broadcasted_iota(jnp.int32, (SPAN, 128), 1)
    tri = lower_ones()
    sum_decay = jnp.zeros((1, 128), f32)
    sum_bias = jnp.zeros((1, 128), f32)
    sum_skip = jnp.zeros((1, 128), f32)
    for c in reversed(range(SPANS)):
        if between and c in between:
            between[c]()
        rows = rows_of(c)
        total, entering, tail = span_parts(c, cum, seg_ext)
        lin = pre[rows, :]
        sig = sigmoid(lin)
        out = lin * sig
        slope = sig * (1.0 + lin * (1.0 - sig))
        x = out[:, 0:INNER]
        b = out[:, INNER : INNER + STATE].astype(bf16)
        cm = out[:, INNER + STATE :].astype(bf16)
        own_dt = dt[rows, :]
        wide_dt = spread(own_dt)
        xs = x * wide_dt
        grad = dy[rows, :]
        wide_in = spread(entering)
        wide_tail = spread(tail)
        dstate = sc_state[...]
        dstate_b = dstate.astype(bf16)
        state_b = states[c]
        gin = grad * wide_in
        gin_b = gin.astype(bf16)
        y_state = nn(cm, state_b)
        xt = xs * wide_tail
        xt_b = xt.astype(bf16)
        from_state = nn(b, dstate_b)
        dcm = nt(gin_b, state_b)
        db = nt(xt_b, dstate_b)
        dcum = gathered_heads(gin * y_state)
        moved = gathered_heads(xt * from_state)
        kept = jnp.sum(dstate * state_b.astype(f32), axis=0, keepdims=True)
        kept = kept * wide_in[SPAN - 1 : SPAN, :]
        kept = gathered_heads(jnp.broadcast_to(kept, (8, INNER)))[0:1, :]
        at_end = jnp.sum(moved, axis=0, keepdims=True) + kept
        sub = lax.broadcasted_iota(jnp.int32, (SPAN, 128), 0)
        dcum = dcum - moved + jnp.where(sub == SPAN - 1, at_end, 0.0)
        sc_state[...] = dstate * wide_in[SPAN - 1 : SPAN, :] + tn(cm, gin_b)
        inter = nt(cm, b)
        bias_m = span_bias(c, seg_ext, seg_row)
        total_t = total.T
        dinter = jnp.zeros((SPAN, SPAN), f32)
        col_sums = jnp.zeros((128, SPAN), f32)
        sub_t = lax.broadcasted_iota(jnp.int32, (128, SPAN), 0)
        ddt = jnp.zeros((SPAN, 128), f32)
        dskip = jnp.zeros((SPAN, 128), f32)
        for pair in range(HEADS // 2):
            cols = slice(128 * pair, 128 * pair + 128)
            gp, xp = grad[:, cols], xs[:, cols]
            gp_b, xp_b = gp.astype(bf16), xp.astype(bf16)
            stack = jnp.concatenate(
                [jnp.where(low2, gp, 0.0).astype(bf16), jnp.where(low2, 0.0, gp).astype(bf16)], axis=0
            )
            dm = nt(stack, xp_b)
            parts = []
            for side in range(2):
                h = 2 * pair + side
                decay = jnp.exp(total[:, h : h + 1] - total_t[h : h + 1, :] + bias_m)
                dmh = dm[side * SPAN : (side + 1) * SPAN, :] * decay
                dinter = dinter + dmh
                weight = decay * inter
                parts.append(weight.astype(bf16))
                q = dmh * inter
                dcum = dcum + jnp.where(lane == h, jnp.sum(q, axis=1, keepdims=True), 0.0)
                col_sums = col_sums + jnp.where(sub_t == h, jnp.sum(q, axis=0, keepdims=True), 0.0)
            both = tn(jnp.concatenate(parts, axis=1), gp_b)
            dxs = jnp.where(low2, both[0:SPAN, :], both[SPAN:, :]) + from_state[:, cols] * wide_tail[:, cols]
            xo = x[:, cols]
            dx = dxs * wide_dt[:, cols] + gp * skip[:, cols]
            dpre[rows, cols] = dx * slope[:, cols]
            pick_row, pick_col = head_matrix(128, 128)
            pick = jnp.where(pick_col == 2 * pair + pick_row // 64, 1.0, 0.0).astype(bf16)
            hi, lo = split_halves(dxs * xo)
            ddt = ddt + nn(hi, pick) + nn(lo, pick)
            hi, lo = split_halves(gp * xo)
            dskip = dskip + nn(hi, pick) + nn(lo, pick)
        dinter_b = dinter.astype(bf16)
        dcm = dcm + nn(dinter_b, b)
        db = db + tn(dinter_b, cm)
        dpre[rows, INNER : INNER + STATE] = db * slope[:, INNER : INNER + STATE]
        dpre[rows, INNER + STATE :] = dcm * slope[:, INNER + STATE :]
        dcum = dcum - col_sums.T
        dlog = lax.dot_general(
            tri, dcum, (((0,), (0,)), ((), ())), precision=HIGH, preferred_element_type=f32
        )
        ddt = ddt + dlog * rate[...]
        dsp = jnp.where(lane < HEADS, ddt * sigmoid(step[rows, :] + bias[...]), 0.0)
        dstep[rows, :] = dsp.astype(bf16)
        sum_decay = sum_decay + jnp.sum(dlog * own_dt, axis=0, keepdims=True)
        sum_bias = sum_bias + jnp.sum(dsp, axis=0, keepdims=True)
        sum_skip = sum_skip + jnp.sum(dskip, axis=0, keepdims=True)
    sub8 = lax.broadcasted_iota(jnp.int32, (8, 128), 0)
    sums = jnp.where(
        sub8 == 0,
        sum_decay * rate[...],
        jnp.where(sub8 == 1, sum_bias, jnp.where(sub8 == 2, sum_skip, 0.0)),
    )
    if heads is not None:
        heads[...] = sums
    return sums


MESH = pl.DeviceIdType.MESH
SMALL = CONV + 128
BC0 = C_U + INNER


def place():
    f = lax.axis_index("fsdp")
    core = lax.rem(f, 2)
    chip = lax.div(f, 2)
    return lax.div(chip, 4), lax.rem(chip, 4), core


def at_yz(y, z, core):
    return {"fsdp": (lax.rem(y, 4) * 4 + lax.rem(z, 4)) * 2 + core}


def torus_peers():
    y, z, core = place()
    return (
        [at_yz(y, z, 1 - core), {"ctx": 1 - lax.axis_index("ctx")}]
        + [at_yz(y, z + n, core) for n in (1, 2, 3)]
        + [at_yz(y + n, z, core) for n in (1, 2, 3)]
    )


def greet(peers):
    barrier = pltpu.get_barrier_semaphore()
    for peer in peers:
        pl.semaphore_signal(barrier, inc=1, device_id=peer, device_id_type=MESH)
    pl.semaphore_wait(barrier, len(peers))


def send(src, dst, sems, k, peer):
    copy = pltpu.make_async_remote_copy(
        src_ref=src,
        dst_ref=dst,
        send_sem=sems.at[0, k],
        recv_sem=sems.at[1, k],
        device_id=peer,
        device_id_type=MESH,
    )
    copy.start()
    return copy


class Refs:
    def __init__(self, names, refs):
        self.__dict__.update(zip(names, refs))
        self.pending, self.stored, self.used = {}, [], 0

    def fetch(self, *names):
        for name in names:
            self.fetch_from(name, getattr(self, "h_" + name))

    def fetch_from(self, name, src):
        copy = pltpu.make_async_copy(src, getattr(self, name), self.io_sems.at[self.used])
        self.used += 1
        copy.start()
        self.pending[name] = copy

    def need(self, *names):
        for name in names:
            if name in self.pending:
                self.pending.pop(name).wait()
        return getattr(self, names[0])

    def store(self, *names):
        for name in names:
            copy = pltpu.make_async_copy(
                getattr(self, name), getattr(self, "h_" + name), self.io_sems.at[self.used]
            )
            self.used += 1
            copy.start()
            self.stored.append(copy)

    def store_part(self, name, part):
        copy = pltpu.make_async_copy(
            part(getattr(self, name)), part(getattr(self, "h_" + name)), self.io_sems.at[self.used]
        )
        self.used += 1
        copy.start()
        self.stored.append(copy)

    def settle(self):
        for copy in self.stored:
            copy.wait()


def run(body, ins, outs, scratch, collective_id):
    any_spec, vmem_spec = pl.BlockSpec(memory_space=pl.ANY), pl.BlockSpec(memory_space=pltpu.VMEM)
    spaces = [(s[0], s[1] if len(s) == 2 else pltpu.VMEM(s[1], s[2])) for s in scratch]
    spaces.append(("io_sems", pltpu.SemaphoreType.DMA((len(ins) + len(outs) + 4,))))
    names = (
        [("h_" if hbm else "") + n for n, _, hbm in ins]
        + [("h_" if hbm else "") + n for n, _, _, hbm in outs]
        + [n for n, _ in spaces]
    )

    def kernel(*refs):
        body(Refs(names, refs))

    return pl.pallas_call(
        kernel,
        out_shape=[jax.ShapeDtypeStruct(s, d) for _, s, d, _ in outs],
        in_specs=[any_spec if hbm else vmem_spec for _, _, hbm in ins],
        out_specs=[any_spec if hbm else vmem_spec for _, _, _, hbm in outs],
        scratch_shapes=[s for _, s in spaces],
        compiler_params=pltpu.CompilerParams(
            vmem_limit_bytes=63 * 1024 * 1024, collective_id=collective_id, has_side_effects=True
        ),
        cost_estimate=pl.CostEstimate(flops=10**11, bytes_accessed=10**8, transcendentals=0),
    )(*[a for _, a, _ in ins])


def dma_sems(*shape):
    return pltpu.SemaphoreType.DMA(shape)


class DirectGather:
    def __init__(self, block, me, peers, sems):
        self.block, self.me, self.sems, self.peers = block, me, sems, peers

    def start(self):
        own = self.block(self.me)
        self.copies = [send(own, own, self.sems, n, p) for n, p in enumerate(self.peers)]

    def finish(self):
        for copy in self.copies:
            copy.wait_recv()

    def close(self):
        for copy in self.copies:
            copy.wait_send()


class RingGather:
    def __init__(self, block, me, peers, sems):
        self.block, self.me, self.sems = block, me, sems
        self.right, self.left = peers[0], peers[2]

    def ahead(self, n):
        return lax.rem(self.me + n, 4)

    def start(self):
        own = self.block(self.me, None)
        self.near = (
            send(own, own, self.sems, 0, self.right),
            send(own, own, self.sems, 1, self.left),
        )

    def forward(self):
        self.far = []
        for side, (peer, n) in enumerate(((self.right, 3), (self.left, 1))):
            self.near[side].wait_recv()
            part = self.block(self.ahead(n), side)
            self.far.append(send(part, part, self.sems, 2 + side, peer))

    def finish(self):
        for copy in self.far:
            copy.wait_recv()

    def close(self):
        for copy in list(self.near) + self.far:
            copy.wait_send()


class Gather:
    def __init__(self, whole, sems, cross_sems):
        y, z, core = place()
        self.whole, self.y, self.z, self.core = whole, y, z, core
        width = whole.shape[-1]
        half = width // 256 * 128
        ca, cb = slice(0, half), slice(half, width)
        self.ca, self.cb = ca, cb
        peers = torus_peers()
        self.sibling, zs, ys = peers[0], peers[2:5], peers[5:8]
        self.sems, self.across = cross_sems, []

        def two(h):
            return slice(0, 4) if h is None else slice(2 * h, 2 * h + 2)

        self.a1 = DirectGather(lambda d: whole.at[y, d, core, :, ca], z, zs, sems.at[0])
        self.b1 = DirectGather(lambda d: whole.at[d, z, core, :, cb], y, ys, sems.at[1])
        self.a2 = RingGather(lambda d, h: whole.at[d, two(h), core, :, ca], y, ys, sems.at[2])
        self.b2 = RingGather(lambda d, h: whole.at[two(h), d, core, :, cb], z, zs, sems.at[3])

    def cross(self, view):
        self.across.append(send(view, view, self.sems, len(self.across), self.sibling))

    def start(self):
        self.a1.start()
        self.b1.start()

    def turn(self):
        self.a1.finish()
        self.a2.start()
        self.b1.finish()
        self.b2.start()
        self.cross(self.whole.at[self.y, :, self.core, :, self.ca])
        self.cross(self.whole.at[:, self.z, self.core, :, self.cb])

    def forward(self):
        a2, b2 = self.a2, self.b2
        a2.forward()
        b2.forward()
        for n in (1, 3):
            self.cross(a2.block(a2.ahead(n), None))
            self.cross(b2.block(b2.ahead(n), None))

    def finish(self):
        a2, b2 = self.a2, self.b2
        a2.finish()
        self.cross(a2.block(a2.ahead(2), None))
        b2.finish()
        self.cross(b2.block(b2.ahead(2), None))

    def rows(self, ref, n):
        return ref.at[lax.rem(self.y + n, 4), :, :, :, self.ca]

    def planes(self, ref, n):
        return ref.at[:, lax.rem(self.z + n, 4), :, :, self.cb]

    def arrived(self):
        for copy in self.across:
            copy.wait_recv()

    def close(self):
        for ring in (self.a1, self.b1, self.a2, self.b2):
            ring.close()
        for copy in self.across:
            copy.wait_send()


class RingSum:
    def __init__(self, chunk, me, peers, sems, far, near, joined):
        self.chunk, self.me, self.sems = chunk, me, sems
        self.right, self.left = peers[0], peers[2]
        self.far, self.near, self.joined = far, near, joined

    def ahead(self, n):
        return lax.rem(self.me + n, 4)

    def start(self):
        c, s = self.chunk, self.sems
        self.far_copies = (
            send(c(self.ahead(2), 0), self.far.at[0], s, 0, self.right),
            send(c(self.ahead(2), 1), self.far.at[1], s, 1, self.left),
        )
        self.direct = (
            send(c(self.ahead(1), 1), self.near.at[0, 1], s, 2, self.right),
            send(c(self.ahead(3), 0), self.near.at[1, 0], s, 3, self.left),
        )

    def forward(self):
        c, s = self.chunk, self.sems
        passed = []
        for side, (peer, n) in enumerate(((self.right, 1), (self.left, 3))):
            self.far_copies[side].wait_recv()
            own = c(self.ahead(n), side)[...]
            self.joined[side] = (own.astype(f32) + self.far[side].astype(f32)).astype(bf16)
            passed.append(send(self.joined.at[side], self.near.at[side, side], s, 4 + side, peer))
        self.passed = tuple(passed)

    def finish(self):
        for copy in self.direct + self.passed:
            copy.wait_recv()

    def total(self, half):
        own = self.chunk(self.me, half)[...].astype(f32)
        return own + self.near[0, half].astype(f32) + self.near[1, half].astype(f32)

    def close(self):
        for copy in self.far_copies + self.direct + self.passed:
            copy.wait_send()


class DirectSum:
    def __init__(self, chunk, me, peers, sems, arrived):
        self.chunk, self.me, self.peers, self.sems, self.arrived = chunk, me, peers, sems, arrived

    def start(self):
        self.copies = [
            send(self.chunk(lax.rem(self.me + n + 1, 4)), self.arrived.at[n], self.sems, n, p)
            for n, p in enumerate(self.peers)
        ]

    def total(self):
        for copy in self.copies:
            copy.wait_recv()
        a = self.arrived
        own = self.chunk(self.me)[...].astype(f32)
        return (own + a[0].astype(f32)) + (a[1].astype(f32) + a[2].astype(f32))

    def close(self):
        for copy in self.copies:
            copy.wait_send()


class Reduce:
    def __init__(self, e, name, fin):
        y, z, core = place()
        g = lambda part: getattr(e, name + part)
        self.gbuf, crecv, self.core, self.fin = getattr(e, name + "gbuf", None), g("crecv"), core, fin
        self.crecv, self.core_sems = crecv, g("core_sems")
        peers = torus_peers()
        self.sibling, zs, ys = peers[0], peers[2:5], peers[5:8]
        width = crecv.shape[-1]
        half = width // 256 * 128
        ca, cb = self.ca, self.cb = slice(0, half), slice(half, width)
        one_a, one_b = self.one_a, self.one_b = g("one_a"), g("one_b")
        s = g("ring_sems")
        self.a = RingSum(
            lambda d, h: crecv.at[2 * h : 2 * h + 2, d, :, ca], z, zs, s.at[0],
            g("far_a"), g("near_a"), g("join_a"),
        )
        self.b = RingSum(
            lambda d, h: crecv.at[d, 2 * h : 2 * h + 2, :, cb], y, ys, s.at[1],
            g("far_b"), g("near_b"), g("join_b"),
        )
        self.a2 = DirectSum(lambda d: one_a.at[d], y, ys, s.at[2], g("late_a"))
        self.b2 = DirectSum(lambda d: one_b.at[d], z, zs, s.at[3], g("late_b"))
        self.copies = {}

    def piece(self, j, block):
        cols = slice(j * 256, (j + 1) * 256)
        self.gbuf[:, :, :, :, cols] = block.astype(bf16).reshape(4, 4, 2, 32, 256)
        self.copies[j] = send(
            self.gbuf.at[:, :, 1 - self.core, :, cols],
            self.crecv.at[:, :, :, cols],
            self.core_sems,
            j,
            self.sibling,
        )

    def add(self, j):
        cols = slice(j * 256, (j + 1) * 256)
        self.copies[j].wait_recv()
        own = self.gbuf[:, :, self.core, :, cols].astype(f32)
        self.crecv[:, :, :, cols] = (own + self.crecv[:, :, :, cols].astype(f32)).astype(bf16)

    def start(self):
        self.a.start()
        self.b.start()

    def forward(self):
        self.a.forward()
        self.b.forward()

    def turn(self):
        for ring, one, second in ((self.a, self.one_a, self.a2), (self.b, self.one_b, self.b2)):
            ring.finish()
            for h in range(2):
                one[2 * h : 2 * h + 2] = ring.total(h).astype(bf16)
            second.start()

    def finish(self):
        self.fin[:, self.ca] = self.a2.total().astype(bf16)
        self.fin[:, self.cb] = self.b2.total().astype(bf16)

    def close(self):
        for ring in (self.a, self.b, self.a2, self.b2):
            ring.close()
        for copy in self.copies.values():
            copy.wait_send()


def reduce_space(name, width, own_buffer=True):
    half = width // 256 * 128
    space = [(name + "crecv", (4, 4, 32, width), bf16)]
    if own_buffer:
        space.append((name + "gbuf", (4, 4, 2, 32, width), bf16))
    for side, wide in (("a", half), ("b", width - half)):
        space += [
            (name + "far_" + side, (2, 2, 32, wide), bf16),
            (name + "near_" + side, (2, 2, 2, 32, wide), bf16),
            (name + "join_" + side, (2, 2, 32, wide), bf16),
            (name + "one_" + side, (4, 32, wide), bf16),
            (name + "late_" + side, (3, 32, wide), bf16),
        ]
    return space + [
        (name + "core_sems", dma_sems(2, width // 256)),
        (name + "ring_sems", dma_sems(4, 2, 6)),
    ]


class SmallSum:
    def __init__(self, e):
        self.sems = e.small_sems
        self.bufs = e.sm_core, e.sm_z, e.sm_y, e.sm_ctx, e.sm_tp
        self.y, self.z, self.core = place()
        self.all = []

    def spread_to(self, buf, at, first_sem, peers):
        self.last = [
            send(buf.at[at], buf.at[at], self.sems, first_sem + n, peer)
            for n, peer in enumerate(peers)
        ]
        self.all += self.last

    def wait(self):
        for copy in self.last:
            copy.wait_recv()

    def start(self, block):
        buf = self.bufs[0]
        buf[self.core] = block
        self.spread_to(buf, self.core, 0, torus_peers()[0:1])

    def along_z(self):
        self.wait()
        buf = self.bufs[1]
        buf[self.z] = self.bufs[0][0] + self.bufs[0][1]
        self.spread_to(buf, self.z, 1, torus_peers()[2:5])

    def along_y(self):
        self.wait()
        buf, old = self.bufs[2], self.bufs[1]
        buf[self.y] = (old[0] + old[1]) + (old[2] + old[3])
        self.spread_to(buf, self.y, 4, torus_peers()[5:8])

    def along_ctx(self):
        self.wait()
        ctx = lax.axis_index("ctx")
        buf, old = self.bufs[3], self.bufs[2]
        buf[ctx] = (old[0] + old[1]) + (old[2] + old[3])
        self.spread_to(buf, ctx, 7, torus_peers()[1:2])

    def along_tp(self):
        self.wait()
        tp = lax.axis_index("tp")
        self.bufs[4][tp] = self.bufs[3][0] + self.bufs[3][1]
        self.spread_to(self.bufs[4], tp, 8, [{"tp": 1 - tp}])

    def result(self):
        self.wait()
        own = self.bufs[4][lax.axis_index("tp")]
        both = self.bufs[4][0] + self.bufs[4][1]
        row = lax.broadcasted_iota(jnp.int32, (8, SMALL), 0)
        col = lax.broadcasted_iota(jnp.int32, (8, SMALL), 1)
        shared = ((row >= 4) & (col < CONV)) | ((col >= INNER) & (col < CONV))
        return jnp.where(shared, both, own)

    def close(self):
        for copy in self.all:
            copy.wait_send()


def column_of(row):
    r, c = head_matrix(32, 32)
    return jnp.sum(jnp.where(r == c, jnp.broadcast_to(row.astype(f32), (32, 32)), 0.0), axis=1, keepdims=True)


def pack_body(
    query, keyval, attn, inner, state, step, gain1, gain2, inner_o, gate_up, down, first, second
):
    first[:, C_Q : C_Q + QW] = query[...]
    lane = lax.broadcasted_iota(jnp.int32, (32, 128), 1)
    tail_cols = jnp.where(lane == HEADS, column_of(gain1[...]), 0.0)
    tail_cols = jnp.where(lane == HEADS + 1, column_of(gain2[...]), tail_cols)
    first[:, C_DT : C_DT + 128] = tail_cols.astype(bf16)
    first[:, C_DT : C_DT + HEADS] = step[...].astype(f32).T.astype(bf16)
    for i in range(2):
        first[:, C_KV + 64 * i : C_KV + 64 * i + 64] = keyval[:, i, :]
        first[:, C_Z + INNER * i : C_Z + INNER * (i + 1)] = inner[:, i, :]
        second[:, W2C + FFH * i : W2C + FFH * (i + 1)] = gate_up[:, i, :]
    first[:, BC0 : BC0 + 256] = state[...]
    second[:, 0:QW] = attn[...]
    second[:, QW:W2C] = inner_o[...]
    second[:, W2C + 2 * FFH :] = down[...]


pack = kernel_call(pack_body, [((32, W1C), bf16), ((32, W2C + W3C), bf16)], mem=61)


def place_segments(e):
    seg, seg_ext, seg_row, wide = e.seg, e.seg_ext, e.seg_row, e.wide
    late = lax.axis_index("ctx")
    row = seg[...].astype(f32)
    wide[...] = jnp.broadcast_to(row, (128, 2 * TOK)).T
    own = pl.ds(pl.multiple_of(late * TOK, TOK), TOK)
    before = pl.ds(pl.multiple_of(late * (TOK - HALO), HALO), HALO)
    after = pl.ds(pl.multiple_of((1 - late) * TOK, TOK), 8)
    seg_ext[0:HALO, :] = jnp.where(late > 0, wide[before, :], -1.0)
    seg_ext[HALO : HALO + TOK, :] = wide[own, :]
    seg_ext[HALO + TOK :, :] = jnp.where(late > 0, -2.0, wide[after, :])
    seg_row[:, 0:TOK] = jnp.broadcast_to(jnp.where(late > 0, row[:, 0:TOK], -1.0), (8, TOK))
    seg_row[:, TOK:] = jnp.broadcast_to(seg[0:1, own].astype(f32), (8, TOK))


def forward_body(e):
    py, pz, core = place()
    late = lax.axis_index("ctx")
    ctx_peer = {"ctx": 1 - late}
    e.fetch("tok", "cos", "sin")
    load1 = pltpu.make_async_copy(e.h_shard1, e.w1.at[py, pz, core], e.own_sems.at[0])
    load2 = pltpu.make_async_copy(e.h_shard2, e.w23.at[py, pz, core], e.own_sems.at[1])
    load1.start()
    load2.start()
    diagonal = {"ctx": 1 - late, "tp": 1 - lax.axis_index("tp")}
    greet(torus_peers() + [diagonal])
    one = Gather(e.w1, e.sems1, e.cross1)
    two = Gather(e.w23, e.sems2, e.cross2)
    load1.wait()
    one.start()
    load2.wait()
    mine3 = e.w23.at[py, pz, core, :, W2C:]
    shard_copy = send(mine3, e.shard_x, e.ctx_sems, 2, diagonal)
    tok = e.need("tok")
    tok_copy = send(tok.at[TOK - HALO : TOK], e.prior, e.ctx_sems, 0, ctx_peer)
    e.unit[...] = unit_rows(tok[...].astype(f32))[0]
    e.unit_t[...] = e.unit[...].T
    one.turn()
    two.start()
    place_segments(e)
    taps, hp, skip = e.taps, e.hp, e.skip
    taps[...] = jnp.zeros_like(taps)
    taps[0:4, 0:INNER] = e.taps_i[...].astype(f32)
    taps[0:4, INNER:] = e.taps_s[...].astype(f32)
    hp[...] = jnp.zeros_like(hp)
    hp[0:1, 0:HEADS] = e.step_bias[...]
    hp[1:2, 0:HEADS] = -jnp.exp(e.decay_log[...])
    hp[2:3, 0:HEADS] = e.skip_gain[...]
    skip[...] = spread(jnp.broadcast_to(hp[2:3, :], (8, 128)))
    e.store("seg_ext", "seg_row", "taps", "hp")
    one.forward()
    two.turn()
    tok_copy.wait_recv()
    one.finish()
    one.arrived()
    e.store("w1")
    w1, normed, norm_p = e.w1, e.normed, e.norm_p

    def columns(at, size):
        return w1[:, :, :, :, at].reshape(WID, size)

    flipped = columns(slice(C_DT, C_DT + 128), 128).astype(f32).T
    e.gains[...] = flipped[8:16, :]
    g = flipped[HEADS : HEADS + 1, :]
    normed[...] = (e.unit[...] * g).astype(bf16)
    norm_p[...] = (unit_rows(e.prior[...].astype(f32))[0] * g).astype(bf16)
    e.normed_t[...] = (e.unit_t[...] * columns(slice(C_DT, C_DT + 128), 128)[:, HEADS : HEADS + 1].astype(f32)).astype(bf16)
    e.store("normed_t", "gains")
    own = pl.ds(pl.multiple_of(late * TOK, TOK), TOK)
    lin = nn(normed[...], columns(slice(0, 256), 256))
    e.need("cos", "sin")
    c, s = e.cos[own, :], e.sin[own, :]
    for i in range(2):
        cols = slice(128 * i, 128 * i + 128)
        e.q[:, cols] = turned(lin[:, cols], c, s).astype(bf16)
    low = low_half((TOK, 128))

    def pair(both, kk, vv):
        other = pltpu.roll(both, 64, 1)
        kk[...] = jnp.where(low, both, other).astype(bf16)
        vv[...] = jnp.where(low, other, both).astype(bf16)

    lin = nn(normed[...], columns(slice(256, 512), 256))
    both = jnp.where(low, turned(lin[:, 0:128], c, s), lin[:, 0:128])
    e.kv[...] = both.astype(bf16)
    kv_copy = send(e.kv, e.kv_prior, e.ctx_sems, 3, ctx_peer)
    pair(both, e.k2, e.v2)
    e.step[...] = lin[:, 128:256]
    e.store("q", "k2", "v2", "step")

    @pl.loop(0, 4)
    def _(j):
        at = pl.ds(pl.multiple_of(C_U + j * 256, 256), 256)
        to = pl.ds(pl.multiple_of(j * 256, 256), 256)
        block = columns(at, 256)
        e.cin[0:HALO, to] = nn(norm_p[...], block)
        e.cin[HALO : HALO + TOK, to] = nn(normed[...], block)

    e.store("cin")
    mixer_in_body(
        e.cin, taps, e.step, hp.at[0:1], hp.at[1:2], e.seg_ext, e.pre, e.dt, e.cum, e.last
    )
    state_copy = send(e.last, e.first, e.ctx_sems, 1, ctx_peer)
    e.store("pre", "dt", "cum")

    @pl.loop(0, 3)
    def _(j):
        at = pl.ds(pl.multiple_of(C_Z + j * 256, 256), 256)
        to = pl.ds(pl.multiple_of(j * 256, 256), 256)
        e.z[:, to] = nn(normed[...], columns(at, 256))

    e.store("z")
    kv_copy.wait_recv()
    pair(e.kv_prior[...].astype(f32), e.k2p, e.v2p)
    e.store("k2p", "v2p")
    attend_body(
        e.q, e.k2, e.v2, e.k2p, e.v2p, e.seg_ext.at[HALO : HALO + TOK], e.seg_row,
        e.mixed.at[:, 0:QW], e.lse,
    )
    e.store("lse")
    two.forward()
    shard_copy.wait_recv()
    e.store("shard_x")
    state_copy.wait_recv()
    e.sc_state[...] = jnp.where(late > 0, e.first[...].astype(f32), 0.0)
    mixer_out_body(
        e.pre, e.dt, e.cum, e.seg_ext, e.seg_row, None, e.z, skip.at[0:1], e.y,
        e.mixed.at[:, QW:], e.states, e.sc_state,
    )
    e.store("mixed", "y", "states")
    for copy in two.across[0:6]:
        copy.wait_recv()
    for n in (0, 1, 3):
        e.store_part("w23", lambda ref: two.rows(ref, n))
        e.store_part("w23", lambda ref: two.planes(ref, n))
    two.finish()
    for copy in two.across[6:]:
        copy.wait_recv()
    e.store_part("w23", lambda ref: two.rows(ref, 2))
    e.store_part("w23", lambda ref: two.planes(ref, 2))
    one.close()
    two.close()
    tok_copy.wait_send()
    shard_copy.wait_send()
    kv_copy.wait_send()
    state_copy.wait_send()
    e.settle()


FORWARD_OUTS = [
    ("w1", (4, 4, 2, 32, W1C), bf16),
    ("w23", (4, 4, 2, 32, W2C + W3C), bf16),
    ("normed_t", (WID, TOK), bf16),
    ("q", (TOK, QW), bf16),
    ("k2", (TOK, 128), bf16),
    ("v2", (TOK, 128), bf16),
    ("k2p", (TOK, 128), bf16),
    ("v2p", (TOK, 128), bf16),
    ("z", (TOK, INNER), f32),
    ("cin", (HALO + TOK, CONV), f32),
    ("step", (TOK, 128), f32),
    ("gains", (8, WID), f32),
    ("pre", (TOK, CONV), f32),
    ("dt", (TOK, 128), f32),
    ("cum", (TOK, 128), f32),
    ("states", (SPANS, STATE, INNER), bf16),
    ("y", (TOK, INNER), f32),
    ("mixed", (TOK, QW + INNER), bf16),
    ("lse", (TOK, 128), f32),
    ("seg_ext", (HALO + TOK + 8, 128), f32),
    ("seg_row", (8, 2 * TOK), f32),
    ("taps", (8, CONV), f32),
    ("hp", (8, 128), f32),
    ("shard_x", (32, W3C), bf16),
]


def forward(ins):
    hbm = ("shard1", "shard2", "tok", "cos", "sin")
    outs = run(
        forward_body,
        [(n, a, n in hbm) for n, a in ins.items()],
        [(n, s, d, True) for n, s, d in FORWARD_OUTS],
        FORWARD_OUTS
        + [
            ("tok", (TOK, WID), bf16),
            ("cos", (2 * TOK, 128), f32),
            ("sin", (2 * TOK, 128), f32),
            ("prior", (HALO, WID), bf16),
            ("norm_p", (HALO, WID), bf16),
            ("normed", (TOK, WID), bf16),
            ("unit", (TOK, WID), f32),
            ("unit_t", (WID, TOK), f32),
            ("kv", (TOK, 128), bf16),
            ("kv_prior", (TOK, 128), bf16),
            ("wide", (2 * TOK, 128), f32),
            ("last", (STATE, INNER), bf16),
            ("first", (STATE, INNER), bf16),
            ("skip", (8, INNER), f32),
            ("sc_state", (STATE, INNER), f32),
            ("own_sems", dma_sems(2)),
            ("sems1", dma_sems(4, 2, 4)),
            ("cross1", dma_sems(2, 8)),
            ("sems2", dma_sems(4, 2, 4)),
            ("cross2", dma_sems(2, 8)),
            ("ctx_sems", dma_sems(2, 4)),
        ],
        1,
    )
    return dict(zip([n for n, _, _ in FORWARD_OUTS], outs))


SENT = 128
CHUNK = 256
CHUNKS = TOK // CHUNK


def middle_body(e):
    py, pz, core = place()
    tp_peer = {"tp": 1 - lax.axis_index("tp")}
    load_x = pltpu.make_async_copy(e.h_shard_x, e.w3x.at[py, pz, core], e.own_sems.at[0])
    load_x.start()
    e.fetch_from("w2", e.h_w23.at[:, :, :, :, 0:W2C])
    e.fetch("mixed")
    greet(torus_peers() + [tp_peer])
    other = Gather(e.w3x, e.gather_sems, e.cross_sems)
    load_x.wait()
    other.start()
    part, part_back = e.part, e.part_back
    normed2, dact, mid, dn, down = e.normed2, e.dact, e.mid, e.dn, e.down

    w2, mixed = e.need("w2"), e.need("mixed")
    e.fetch("cot", "gains", "tok")
    e.fetch_from("w3", e.h_w23.at[:, :, :, :, W2C:])
    copies = []
    for c in range(TOK // SENT):
        rows = slice(c * SENT, (c + 1) * SENT)
        part[rows, :] = nt(mixed[rows, :], w2[...].reshape(WID, W2C)).astype(bf16)
        copies.append(send(part.at[rows], part_back.at[rows], e.sems, c, tp_peer))
    tok, cot, gains = e.need("tok"), e.need("cot"), e.need("gains")
    e.cot_t[...] = cot[...].astype(f32).T.astype(bf16)
    gain = gains[HEADS + 1 - 8 : HEADS + 2 - 8, :]
    other.turn()
    e.need("w3")

    def cols(w, at, size):
        return w[:, :, :, :, at].reshape(WID, size)

    def rows_at(c):
        return slice(c * CHUNK, (c + 1) * CHUNK)

    def hidden_back(w):
        @pl.loop(0, FFH // 256)
        def _(j):
            at = pl.ds(pl.multiple_of(2 * FFH + j * 256, 256), 256)
            to = pl.ds(pl.multiple_of(j * 256, 256), 256)
            dact[:, to] = nn(cot[...], cols(w, at, 256))

    def swiglu(w, act, dgu, rows):
        @pl.loop(0, FFH // 256)
        def _(j):
            at = pl.ds(pl.multiple_of(j * 256, 256), 256)
            at_up = pl.ds(pl.multiple_of(FFH + j * 256, 256), 256)
            gate = nn(normed2[rows, :], cols(w, at, 256))
            up = nn(normed2[rows, :], cols(w, at_up, 256))
            sig = sigmoid(gate)
            silu = gate * sig
            da = dact[rows, at]
            act[rows, at] = (silu * up).astype(bf16)
            dgu[rows, at] = (da * up * (sig + silu * (1.0 - sig))).astype(bf16)
            dgu[rows, at_up] = (da * silu).astype(bf16)

    def out_products(w, act, dgu, rows, first):
        @pl.loop(0, 4)
        def _(j):
            to = pl.ds(pl.multiple_of(j * 256, 256), 256)
            a = nt(dgu[rows, :], w[j, :, :, :, 0 : 2 * FFH].reshape(256, 2 * FFH))
            b = nt(act[rows, :], w[j, :, :, :, 2 * FFH :].reshape(256, FFH))
            dn[rows, to] = a if first else dn[rows, to] + a
            down[rows, to] = b if first else down[rows, to] + b

    hidden_back(e.w3)
    for c in range(CHUNKS):
        rows = rows_at(c)
        for part_copy in copies[c * CHUNK // SENT : (c + 1) * CHUNK // SENT]:
            part_copy.wait_recv()
        m = tok[rows, :].astype(f32) + (part[rows, :].astype(f32) + part_back[rows, :].astype(f32))
        mid[rows, :] = m
        normed2[rows, :] = (unit_rows(m)[0] * gain).astype(bf16)
        swiglu(e.w3, e.act, e.dgu, rows)
        out_products(e.w3, e.act, e.dgu, rows, True)
        if c == 0:
            other.forward()
    other.finish()
    e.normed2_t[...] = normed2[...].astype(f32).T.astype(bf16)

    @pl.loop(0, FFH // 256)
    def _(j):
        at = pl.ds(pl.multiple_of(j * 256, 256), 256)
        to = pl.ds(pl.multiple_of(2 * FFH + j * 256, 256), 256)
        e.w3_grad[:, :, :, :, to] = nn(e.cot_t[...], e.act[:, at]).astype(bf16).reshape(4, 4, 2, 32, 256)

    @pl.loop(0, 2 * FFH // 256)
    def _(j):
        at = pl.ds(pl.multiple_of(j * 256, 256), 256)
        block = nn(e.normed2_t[...], e.dgu[:, at]).astype(bf16)
        e.w3_grad[:, :, :, :, at] = block.reshape(4, 4, 2, 32, 256)

    e.store("w3_grad")
    other.arrived()
    hidden_back(e.w3x)
    taken = jnp.zeros((1, WID), f32)
    for c in range(CHUNKS):
        rows = rows_at(c)
        swiglu(e.w3x, e.act_x, e.dgu_x, rows)
        out_products(e.w3x, e.act_x, e.dgu_x, rows, False)
        e.block_out[rows, :] = (mid[rows, :] + down[rows, :]).astype(bf16)
        dh = dn[rows, :]
        unit, r = unit_rows(mid[rows, :])
        taken = taken + jnp.sum(dh * unit, axis=0, keepdims=True)
        scaled = dh * gain
        g = cot[rows, :].astype(f32) + r * (
            scaled - unit * jnp.mean(unit * scaled, axis=1, keepdims=True)
        )
        e.grad_mid[rows, :] = g
        e.dmix[rows, :] = g.astype(bf16)
    e.dgain2[...] = jnp.broadcast_to(taken, (8, WID))
    e.store("dmix", "grad_mid", "dgain2", "block_out")
    other.close()
    for copy in copies:
        copy.wait_send()
    e.settle()


MIDDLE_OUTS = [
    ("block_out", (TOK, WID), bf16),
    ("grad_mid", (TOK, WID), f32),
    ("dmix", (TOK, WID), bf16),
    ("w3_grad", (4, 4, 2, 32, W3C), bf16),
    ("dgain2", (8, WID), f32),
]


def middle(ins):
    outs = run(
        middle_body,
        [(n, a, True) for n, a in ins.items()],
        [(n, s, d, True) for n, s, d in MIDDLE_OUTS],
        MIDDLE_OUTS
        + [
            ("w2", (4, 4, 2, 32, W2C), bf16),
            ("w3", (4, 4, 2, 32, W3C), bf16),
            ("w3x", (4, 4, 2, 32, W3C), bf16),
            ("mixed", (TOK, WID), bf16),
            ("gains", (8, WID), f32),
            ("tok", (TOK, WID), bf16),
            ("cot", (TOK, WID), bf16),
            ("part", (TOK, WID), bf16),
            ("part_back", (TOK, WID), bf16),
            ("mid", (TOK, WID), f32),
            ("dn", (TOK, WID), f32),
            ("down", (TOK, WID), f32),
            ("normed2", (TOK, WID), bf16),
            ("normed2_t", (WID, TOK), bf16),
            ("cot_t", (WID, TOK), bf16),
            ("act", (TOK, FFH), bf16),
            ("dgu", (TOK, 2 * FFH), bf16),
            ("act_x", (TOK, FFH), bf16),
            ("dgu_x", (TOK, 2 * FFH), bf16),
            ("dact", (TOK, FFH), f32),
            ("sems", dma_sems(2, TOK // SENT)),
            ("own_sems", dma_sems(1)),
            ("gather_sems", dma_sems(4, 2, 4)),
            ("cross_sems", dma_sems(2, 8)),
        ],
        2,
    )
    return dict(zip([n for n, _, _ in MIDDLE_OUTS], outs))


EARLY = W2C + INNER + QW
LATE = CONV + 256


def conv_back(ext, taps, seg_ext, cin, grads):
    run = jnp.zeros((TOK, CONV), f32)
    now = seg_ext[HALO : HALO + TOK, 0:1]
    sub = lax.broadcasted_iota(jnp.int32, (8, CONV), 0)
    taken = jnp.zeros((8, CONV), f32)
    for k in range(4):
        ahead = 3 - k
        same = jnp.where(seg_ext[HALO + ahead : HALO + ahead + TOK, 0:1] == now, 1.0, 0.0)
        run = run + ext[ahead : ahead + TOK, :] * taps[k : k + 1, :] * same
        at = HALO - 3 + k
        part = ext[0:TOK, :] * cin[at : at + TOK, :] * tap_mask(seg_ext, k)
        taken = taken + jnp.where(sub == k, jnp.sum(part, axis=0, keepdims=True), 0.0)
    grads[:, C_U:] = run.astype(bf16)
    return taken


def backward_body(e):
    py, pz, core = place()
    ctx, tp = lax.axis_index("ctx"), lax.axis_index("tp")
    ctx_peer, tp_peer = {"ctx": 1 - ctx}, {"tp": 1 - tp}
    own_rows = pl.ds(pl.multiple_of(ctx * TOK, TOK), TOK)
    half3 = W3C // 2
    e.fetch_from("w2", e.h_w23.at[:, :, :, :, 0:W2C])
    e.fetch("dmix")
    greet(torus_peers() + [tp_peer])
    sum3 = Reduce(e, "s3_", e.fin_three)
    early = Reduce(e, "se_", e.fin_early)
    tail = Reduce(e, "sl_", e.fin_late)
    small = SmallSum(e)
    core3 = send(e.h_w3_grad.at[:, :, 1 - core], sum3.crecv, sum3.core_sems, 0, sum3.sibling)
    grads = e.grads

    w2, dmix = e.need("w2"), e.need("dmix")
    e.fetch("z", "y", "pre", "cum", "seg_ext")
    e.fetch("q", "k2", "v2", "k2p", "v2p", "seg_row", "lse")
    e.fetch_from("cos", e.h_cos.at[own_rows])
    e.fetch_from("sin", e.h_sin.at[own_rows])
    e.fetch_from("own3", e.h_w3_grad.at[:, :, core, :, 0:half3])

    @pl.loop(0, INNER // 256)
    def _(j):
        at = pl.ds(pl.multiple_of(QW + j * 256, 256), 256)
        to = pl.ds(pl.multiple_of(j * 256, 256), 256)
        e.dgated[:, to] = nn(dmix[...], w2[:, :, :, :, at].reshape(WID, 256))

    e.need("z", "y", "pre", "cum", "seg_ext")
    mixer_back_in_body(
        e.dgated, e.z, e.y, e.pre, e.cum, e.seg_ext, e.dgated, grads.at[:, C_Z : C_Z + INNER], e.dfirst
    )
    state_copy = send(e.dfirst, e.dlast, e.ctx_sems, 0, ctx_peer)
    e.fetch("hp", "dt", "states", "step", "taps", "cin", "mixed", "normed_t", "w1", "tok", "gains", "dgain2")
    e.need("q", "k2", "v2", "k2p", "v2p", "seg_row", "lse", "cos", "sin")

    def add_half(first):
        for j in range(half3 // 512):
            at = slice(j * 512, (j + 1) * 512)
            cols = slice(first + j * 512, first + (j + 1) * 512)
            total = e.own3[:, :, :, at].astype(f32) + sum3.crecv[:, :, :, cols].astype(f32)
            sum3.crecv[:, :, :, cols] = total.astype(bf16)

    e.need("own3")
    core3.wait_recv()
    add_half(0)
    e.fetch_from("own3", e.h_w3_grad.at[:, :, core, :, half3:])
    sum3.a.start()
    e.datt[...] = nn(dmix[...], w2[:, :, :, :, 0:QW].reshape(WID, QW)).astype(bf16)
    e.need("own3")
    add_half(half3)
    sum3.b.start()
    attend_back_body(
        e.q, e.k2, e.v2, e.k2p, e.v2p, e.seg_ext.at[HALO : HALO + TOK], e.seg_row, e.lse, e.datt,
        e.cos, e.sin, grads.at[:, C_Q : C_Q + QW], e.dkv, e.dkv_p, e.dk_s, e.dv_s, e.dkp_s, e.dvp_s,
        between={1: sum3.forward},
    )
    kv_copy = send(e.dkv_p, e.dkv_back, e.ctx_sems, 1, ctx_peer)
    state_copy.wait_recv()
    e.sc_state[...] = jnp.where(ctx > 0, 0.0, e.dlast[...].astype(f32))
    e.need("hp", "dt", "states", "step")
    e.skip[...] = spread(jnp.broadcast_to(e.hp[2:3, :], (8, 128)))
    heads = mixer_back_body(
        e.dgated, e.pre, e.dt, e.cum, e.seg_ext, e.seg_row, e.states, None, e.skip.at[0:1],
        e.hp.at[1:2], e.step, e.hp.at[0:1], e.ext, grads.at[:, C_DT : C_DT + 128], None, e.sc_state,
    )
    rim_copy = send(e.ext.at[0:8], e.rim, e.ctx_sems, 2, ctx_peer)
    e.dmix_t[...] = dmix[...].astype(f32).T.astype(bf16)
    normed_t = e.need("normed_t")
    e.need("mixed")
    for j in range(4):
        early.piece(j, nn(e.dmix_t[...], e.mixed[:, j * 256 : (j + 1) * 256]))
    kv_copy.wait_recv()
    low = low_half((TOK, 128))
    both = e.dkv[...] + jnp.where(ctx > 0, 0.0, e.dkv_back[...].astype(f32))
    grads[:, C_KV : C_KV + 128] = jnp.where(low, turned(both, e.cos[...], -e.sin[...]), both).astype(bf16)
    e.need("taps", "cin")
    rim_copy.wait_recv()
    e.ext[TOK : TOK + 8, :] = jnp.where(ctx > 0, 0.0, e.rim[...])
    dtaps = conv_back(e.ext, e.taps, e.seg_ext, e.cin, grads)
    rim_copy.wait_send()
    late = e.ext.at[0:TOK]
    late_load = pltpu.make_async_copy(e.h_grad_mid, late, e.own_sems.at[0])
    late_load.start()

    def rows_at(c):
        return slice(c * TOK // 4, (c + 1) * TOK // 4)

    w1 = e.need("w1")
    dn_copies = []

    def dn_part(c):
        rows = rows_at(c)

        @pl.loop(0, 4)
        def _(j):
            to = pl.ds(pl.multiple_of(j * 256, 256), 256)
            e.dn[rows, to] = nt(grads[rows, :], w1[j].reshape(256, W1C)).astype(bf16)

        dn_copies.append(send(e.dn.at[rows], e.dn_back.at[rows], e.dn_sems, c, tp_peer))

    dn_part(0)
    for j in range(3):
        at = C_Z + j * 256
        early.piece(4 + j, nn(normed_t[...], grads[:, at : at + 256]))
    early.piece(7, nn(normed_t[...], grads[:, 0:QW]))
    for j in range(8):
        early.add(j)
    early.start()
    sum3.turn()
    dn_part(1)
    for j in range(4):
        at = C_U + j * 256
        tail.piece(j, nn(normed_t[...], grads[:, at : at + 256]))
    tail.piece(4, nn(normed_t[...], grads[:, 256:512]))
    dn_part(2)
    for j in range(5):
        tail.add(j)
    tail.start()
    early.forward()
    dn_part(3)
    sum3.finish()
    three_copy = send(e.fin_three, e.fin_three_back, e.fin_sems, 3, ctx_peer)
    tok = e.need("tok")
    gains = e.need("gains")
    e.need("dgain2")
    gain = gains[HEADS - 8 : HEADS - 7, :]
    dgain1 = jnp.zeros((1, WID), f32)
    for c in range(4):
        rows = rows_at(c)
        unit = unit_rows(tok[rows, :].astype(f32))[0]
        dgain1 = dgain1 + jnp.sum(e.dn[rows, :].astype(f32) * unit, axis=0, keepdims=True)
    sub = lax.broadcasted_iota(jnp.int32, (8, WID), 0)
    gain_rows = jnp.where(sub == 4, dgain1, jnp.where(sub == 5, e.dgain2[0:1, :] * 0.5, dtaps))
    small.start(jnp.concatenate([gain_rows, heads], axis=1))
    tail.forward()
    early.turn()
    small.along_z()
    tail.turn()
    early.finish()
    fin_copy = send(e.fin_early, e.fin_early_back, e.fin_sems, 0, ctx_peer)
    small.along_y()
    tail.finish()
    late_copy = send(e.fin_late, e.fin_late_back, e.fin_sems, 1, ctx_peer)
    small.along_ctx()
    late_load.wait()
    for c in range(4):
        rows = rows_at(c)
        dn_copies[c].wait_recv()
        dh = (e.dn[rows, :].astype(f32) + e.dn_back[rows, :].astype(f32)) * gain
        unit, r = unit_rows(tok[rows, :].astype(f32))
        late[rows, :] = late[rows, :] + r * (dh - unit * jnp.mean(unit * dh, axis=1, keepdims=True))
    out_copy = pltpu.make_async_copy(late, e.h_tok_grad, e.own_sems.at[1])
    out_copy.start()
    small.along_tp()
    late_copy.wait_recv()
    total = e.fin_late[...].astype(f32) + e.fin_late_back[...].astype(f32)
    e.share[...] = total[:, INNER:CONV].astype(bf16)
    share_copy = send(e.share, e.share_back, e.fin_sems, 2, tp_peer)
    e.parts_late[...] = total
    three_copy.wait_recv()
    e.parts_early[:, 0:W3C] = e.fin_three[...].astype(f32) + e.fin_three_back[...].astype(f32)
    fin_copy.wait_recv()
    e.parts_early[:, W3C:] = e.fin_early[...].astype(f32) + e.fin_early_back[...].astype(f32)
    e.store("parts_early")
    e.sums[...] = small.result()
    share_copy.wait_recv()
    e.parts_late[:, INNER:CONV] = e.share[...].astype(f32) + e.share_back[...].astype(f32)
    e.store("parts_late", "sums")

    out_copy.wait()
    core3.wait_send()
    for ring in (sum3, early, tail):
        ring.close()
    small.close()
    for copy in [state_copy, kv_copy, three_copy, fin_copy, late_copy, share_copy] + dn_copies:
        copy.wait_send()
    e.settle()


BACKWARD_OUTS = [
    ("parts_early", (32, W3C + EARLY), f32),
    ("parts_late", (32, LATE), f32),
    ("sums", (8, SMALL), f32),
]


def backward(ins):
    same = [
        "dmix", "z", "y", "pre", "cum", "seg_ext", "mixed", "q", "k2", "v2", "k2p", "v2p",
        "seg_row", "lse", "hp", "dt", "states", "step", "normed_t", "taps", "cin", "tok", "gains", "dgain2",
    ]
    outs = run(
        backward_body,
        [(n, a, True) for n, a in ins.items()],
        [(n, s, d, True) for n, s, d in BACKWARD_OUTS] + [("tok_grad", (TOK, WID), f32, True)],
        BACKWARD_OUTS
        + [(n, ins[n].shape, ins[n].dtype) for n in same]
        + [
            ("w2", (4, 4, 2, 32, W2C), bf16),
            ("own3", (4, 4, 32, W3C // 2), bf16),
            ("cos", (TOK, 128), f32),
            ("sin", (TOK, 128), f32),
            ("w1", (4, 4, 2, 32, W1C), bf16),
            ("dgated", (TOK, INNER), f32),
            ("datt", (TOK, QW), bf16),
            ("dmix_t", (WID, TOK), bf16),
            ("grads", (TOK, W1C), bf16),
            ("dkv", (TOK, 128), f32),
            ("dkv_p", (TOK, 128), bf16),
            ("dkv_back", (TOK, 128), bf16),
            ("dk_s", (TOK, 128), f32),
            ("dv_s", (TOK, 128), f32),
            ("dkp_s", (TOK, 128), f32),
            ("dvp_s", (TOK, 128), f32),
            ("dfirst", (STATE, INNER), bf16),
            ("dlast", (STATE, INNER), bf16),
            ("skip", (8, INNER), f32),
            ("sc_state", (STATE, INNER), f32),
            ("ext", (TOK + 8, CONV), f32),
            ("rim", (8, CONV), f32),
            ("dn", (TOK, WID), bf16),
            ("dn_back", (TOK, WID), bf16),
            ("fin_three", (32, W3C), bf16),
            ("fin_three_back", (32, W3C), bf16),
            ("fin_early", (32, EARLY), bf16),
            ("fin_early_back", (32, EARLY), bf16),
            ("fin_late", (32, LATE), bf16),
            ("fin_late_back", (32, LATE), bf16),
            ("share", (32, CONV - INNER), bf16),
            ("share_back", (32, CONV - INNER), bf16),
            ("sm_core", (2, 8, SMALL), f32),
            ("sm_z", (4, 8, SMALL), f32),
            ("sm_y", (4, 8, SMALL), f32),
            ("sm_ctx", (2, 8, SMALL), f32),
            ("sm_tp", (2, 8, SMALL), f32),
            ("small_sems", dma_sems(2, 9)),
            ("ctx_sems", dma_sems(2, 3)),
            ("dn_sems", dma_sems(2, 4)),
            ("fin_sems", dma_sems(2, 4)),
            ("own_sems", dma_sems(3)),
        ]
        + reduce_space("s3_", W3C, own_buffer=False)
        + reduce_space("se_", EARLY)
        + reduce_space("sl_", LATE),
        0,
    )
    return dict(zip([n for n, _, _ in BACKWARD_OUTS] + ["tok_grad"], outs))


def outputs_body(
    early, late, sums, block_in, tok_in,
    gain1, gain2, query, keyval, attn, inner, state, step, conv_i, conv_s, decay, bias, skip,
    inner_o, gate_up, down, block_out, tok_out, tok_held, block_held, sems,
):
    passes = ((tok_in, tok_held, tok_out), (block_in, block_held, block_out))
    loads = [pltpu.make_async_copy(a, b, sems.at[0, n]) for n, (a, b, _) in enumerate(passes)]
    copies = [pltpu.make_async_copy(b, c, sems.at[1, n]) for n, (_, b, c) in enumerate(passes)]
    for load in loads:
        load.start()
    for load, copy in zip(loads, copies):
        load.wait()
        copy.start()
    gains = pltpu.roll(sums[:, 0:WID], lax.rem(WID - 32 * lax.axis_index("fsdp"), WID), 1)
    gain1[...] = gains[4:5, 0:32]
    gain2[...] = gains[5:6, 0:32]
    step[...] = late[:, LATE - 128 :].T[0:HEADS, :]
    at2 = W3C
    query[...] = early[:, at2 + W2C + INNER :]
    for i in range(2):
        at = CONV + 64 * i
        keyval[:, i, :] = late[:, at : at + 64]
        gate_up[:, i, :] = early[:, FFH * i : FFH * (i + 1)]
    inner[:, 0, :] = early[:, at2 + W2C : at2 + W2C + INNER]
    inner[:, 1, :] = late[:, 0:INNER]
    state[...] = late[:, INNER:CONV]
    attn[...] = early[:, at2 : at2 + QW]
    inner_o[...] = early[:, at2 + QW : at2 + W2C]
    down[...] = early[:, 2 * FFH : 3 * FFH]
    conv_i[...] = sums[0:4, 0:INNER]
    conv_s[...] = sums[0:4, INNER:CONV]
    for n, ref in enumerate((decay, bias, skip)):
        ref[...] = sums[n : n + 1, CONV : CONV + HEADS]
    for copy in copies:
        copy.wait()


OUTPUTS = [
    ((1, 32), f32),
    ((1, 32), f32),
    ((32, QW), f32),
    ((32, 2, 64), f32),
    ((32, QW), f32),
    ((32, 2, INNER), f32),
    ((32, 256), f32),
    ((HEADS, 32), f32),
    ((4, INNER), f32),
    ((4, CONV - INNER), f32),
    ((1, HEADS), f32),
    ((1, HEADS), f32),
    ((1, HEADS), f32),
    ((32, INNER), f32),
    ((32, 2, FFH), f32),
    ((32, FFH), f32),
    ((TOK, WID), bf16),
    ((TOK, WID), f32),
]


def outputs(*args):
    any_spec = pl.BlockSpec(memory_space=pl.ANY)
    return pl.pallas_call(
        outputs_body,
        out_shape=[jax.ShapeDtypeStruct(s, d) for s, d in OUTPUTS],
        in_specs=vmem(3) + [any_spec] * 2,
        out_specs=vmem(16) + [any_spec] * 2,
        scratch_shapes=[pltpu.VMEM((TOK, WID), f32), pltpu.VMEM((TOK, WID), bf16), dma_sems(2, 2)],
        compiler_params=pltpu.CompilerParams(vmem_limit_bytes=61 * 1024 * 1024),
    )(*args)


def rope_tables():
    indices = np.arange(HEAD_WIDTH // 2, dtype=np.float32)
    frequency = np.exp(indices * np.float32(-2.0 * math.log(ROPE_BASE) / HEAD_WIDTH))
    angles = np.arange(2 * TOK, dtype=np.float32)[:, None] * frequency[None, :].astype(np.float32)
    angles = angles.astype(np.float64)
    return tuple(np.tile(t(angles), (1, 4)).astype(np.float32) for t in (np.cos, np.sin))


def shards(
    tokens, segments, cotangent, gain_mixer, gain_ffn, query_proj, key_value_weight, attn_out,
    inner_proj, state_proj, step_proj, conv_inner, conv_state, decay_log, step_bias, skip_gain,
    inner_out, gate_up, down_proj,
):
    rows = query_proj.shape[0]
    tok = tokens.reshape(TOK, WID)
    cot = cotangent.reshape(TOK, WID)
    shard1, shard2 = pack(
        query_proj, key_value_weight, attn_out.T, inner_proj, state_proj, step_proj.T,
        gain_mixer.reshape(1, rows), gain_ffn.reshape(1, rows), inner_out.T, gate_up, down_proj.T,
    )
    cos, sin = (jnp.asarray(t) for t in rope_tables())
    kept = forward(
        dict(
            shard1=shard1, shard2=shard2, tok=tok, cos=cos, sin=sin, seg=segments,
            taps_i=conv_inner, taps_s=conv_state, step_bias=step_bias.reshape(1, HEADS),
            decay_log=decay_log.reshape(1, HEADS), skip_gain=skip_gain.reshape(1, HEADS),
        )
    )
    kept |= dict(tok=tok, cos=cos, sin=sin)
    between = middle({n: kept[n] for n in ("w23", "shard_x", "mixed", "gains", "tok")} | dict(cot=cot))
    block_out = between.pop("block_out")
    del kept["shard_x"]
    done = backward(kept | between)
    *out, block_out, tok_grad = outputs(
        done["parts_early"], done["parts_late"], done["sums"], block_out, done["tok_grad"]
    )
    forms = [(rows,)] * 2 + [None] * 2 + ["T"] + [None] * 2 + ["T"] + [None] * 2
    forms += [(HEADS,)] * 3 + ["T", None, "T"]
    out = [a if f is None else a.T if f == "T" else a.reshape(f) for a, f in zip(out, forms)]
    return (block_out[None], tok_grad[None], *out)


def solution(mesh):
    return jax.shard_map(
        shards,
        mesh=mesh,
        in_specs=(
            P("fsdp", "ctx", None), P("fsdp", None), P("fsdp", "ctx", None), P("fsdp"), P("fsdp"),
            P("fsdp", "tp"), P("fsdp", None, "tp"), P("tp", "fsdp"), P("fsdp", None, "tp"),
            P("fsdp", None), P("fsdp", "tp"), P(None, "tp"), P(), P("tp"), P("tp"), P("tp"),
            P("tp", "fsdp"), P("fsdp", None, "tp"), P("tp", "fsdp"),
        ),
        out_specs=(
            P("fsdp", "ctx", None), P("fsdp", "ctx", None), P("fsdp"), P("fsdp"), P("fsdp", "tp"),
            P("fsdp", None, "tp"), P("tp", "fsdp"), P("fsdp", None, "tp"), P("fsdp", None),
            P("fsdp", "tp"), P(None, "tp"), P(), P("tp"), P("tp"), P("tp"), P("tp", "fsdp"),
            P("fsdp", None, "tp"), P("tp", "fsdp"),
        ),
        check_vma=False,
    )
```

```python
import functools
import math

import jax
import jax.numpy as jnp
import numpy as np
from jax import lax
from jax.experimental import pallas as pl
from jax.experimental.pallas import tpu as pltpu

from jax.sharding import PartitionSpec as P

f32 = jnp.float32
bf16 = jnp.bfloat16
EPS = 1e-05
NEG = -1e30
ROPE_BASE = 100000000000.0
HEAD_WIDTH = 64
HIGH = lax.Precision.HIGHEST

TOK = 512
WID = 1024
SPAN = 128
SPANS = TOK // SPAN
QW = 256
HEADS = 12
INNER = 768
STATE = 128
CONV = INNER + 2 * STATE
HALO = 16
W1C = 2304
W2C = 1024
W3C = 3072
FFH = 1024
C_Q, C_KV, C_DT, C_Z, C_U = 0, 256, 384, 512, 1280


def vmem(n):
    return [pl.BlockSpec(memory_space=pltpu.VMEM)] * n


def kernel_call(body, outs, scratch=(), mem=24, cost=None):
    def call(*args):
        return pl.pallas_call(
            body,
            out_shape=[jax.ShapeDtypeStruct(s, d) for s, d in outs],
            in_specs=vmem(len(args)),
            out_specs=vmem(len(outs)),
            scratch_shapes=list(scratch),
            compiler_params=pltpu.CompilerParams(vmem_limit_bytes=mem * 1024 * 1024),
            cost_estimate=cost,
        )(*args)

    return call


def nt(a, b):
    return lax.dot_general(a, b, (((1,), (1,)), ((), ())), preferred_element_type=f32)


def tn(a, b):
    return lax.dot_general(a, b, (((0,), (0,)), ((), ())), preferred_element_type=f32)


def nn(a, b):
    return jnp.dot(a, b, preferred_element_type=f32)


def split_halves(v):
    hi = v.astype(bf16)
    return hi, (v - hi.astype(f32)).astype(bf16)


def head_matrix(rows, columns):
    row = lax.broadcasted_iota(jnp.int32, (rows, columns), 0)
    col = lax.broadcasted_iota(jnp.int32, (rows, columns), 1)
    return row, col


def spread(v):
    row, col = head_matrix(128, INNER)
    e = jnp.where(row == col // 64, 1.0, 0.0).astype(bf16)
    hi, lo = split_halves(v)
    return nn(hi, e) + nn(lo, e)


def gathered_heads(v):
    row, col = head_matrix(INNER, 128)
    e = jnp.where(row // 64 == col, 1.0, 0.0).astype(bf16)
    hi, lo = split_halves(v)
    return nn(hi, e) + nn(lo, e)


def low_half(shape):
    return lax.broadcasted_iota(jnp.int32, shape, len(shape) - 1) % 128 < 64


def sigmoid(v):
    return 1.0 / (1.0 + jnp.exp(-v))


def turned(v, cos, sin):
    lane = lax.broadcasted_iota(jnp.int32, v.shape, 1) % 64
    w = v.shape[1]
    swapped = jnp.where(lane < 32, pltpu.roll(v, w - 32, 1), pltpu.roll(v, 32, 1))
    return v * cos + jnp.where(lane < 32, -swapped, swapped) * sin


def unit_rows(v):
    r = lax.rsqrt(jnp.mean(v * v, axis=1, keepdims=True) + EPS)
    return v * r, r


def own_bias(rows, start, seg_col, seg_row):
    end = start + rows
    query = lax.broadcasted_iota(jnp.int32, (rows, end), 0) + start
    key = lax.broadcasted_iota(jnp.int32, (rows, end), 1)
    keep = (key <= query) & (seg_col[start:end, 0:1] == seg_row[0:1, TOK : TOK + end])
    return keep


QB = 256


def attend_body(q, k2, v2, k2p, v2p, seg_col, seg_row, out, lse):
    low = low_half((QB, 128))
    for b in range(TOK // QB):
        start, end = b * QB, (b + 1) * QB
        keep = own_bias(QB, start, seg_col, seg_row)
        keep_p = seg_col[start:end, 0:1] == seg_row[0:1, 0:TOK]
        logs = []
        for pair in range(2):
            cols = slice(128 * pair, 128 * pair + 128)
            qp = q[start:end, cols]
            halves = []
            for side in range(2):
                mine = low if side == 0 else ~low
                qh = jnp.where(mine, qp.astype(f32) * 0.125, 0.0).astype(bf16)
                s1 = jnp.where(keep, nt(qh, k2[0:end, :]), NEG)
                s0 = jnp.where(keep_p, nt(qh, k2p[...]), NEG)
                m = jnp.maximum(
                    jnp.max(s1, axis=1, keepdims=True), jnp.max(s0, axis=1, keepdims=True)
                )
                p1, p0 = jnp.exp(s1 - m), jnp.exp(s0 - m)
                total = jnp.sum(p1, axis=1, keepdims=True) + jnp.sum(p0, axis=1, keepdims=True)
                o = nn(p1.astype(bf16), v2[0:end, :]) + nn(p0.astype(bf16), v2p[...])
                halves.append(o / total)
                logs.append(m + jnp.log(total))
            out[start:end, cols] = jnp.where(low, halves[0], halves[1]).astype(bf16)
        lane = lax.broadcasted_iota(jnp.int32, (QB, 128), 1)
        kept = jnp.zeros((QB, 128), f32)
        for h in range(4):
            kept = jnp.where(lane == h, logs[h], kept)
        lse[start:end, :] = kept


def attend_back_body(
    q, k2, v2, k2p, v2p, seg_col, seg_row, lse, dout, cos, sin, dq, dkv, dkv_p, dk_s, dv_s, dkp_s, dvp_s,
    between=None,
):
    low = low_half((QB, 128))
    for ref in (dk_s, dv_s, dkp_s, dvp_s):
        ref[...] = jnp.zeros_like(ref)
    for b in range(TOK // QB):
        start, end = b * QB, (b + 1) * QB
        keep = own_bias(QB, start, seg_col, seg_row)
        keep_p = seg_col[start:end, 0:1] == seg_row[0:1, 0:TOK]
        for pair in range(2):
            cols = slice(128 * pair, 128 * pair + 128)
            qp = q[start:end, cols]
            dop = dout[start:end, cols]
            halves = []
            for side in range(2):
                mine = low if side == 0 else ~low
                qh = jnp.where(mine, qp.astype(f32) * 0.125, 0.0).astype(bf16)
                doh = jnp.where(mine, dop.astype(f32), 0.0).astype(bf16)
                h = 2 * pair + side
                log_total = lse[start:end, h : h + 1]
                p1 = jnp.exp(jnp.where(keep, nt(qh, k2[0:end, :]), NEG) - log_total)
                p0 = jnp.exp(jnp.where(keep_p, nt(qh, k2p[...]), NEG) - log_total)
                dp1 = nt(doh, v2[0:end, :])
                dp0 = nt(doh, v2p[...])
                delta = jnp.sum(p1 * dp1, axis=1, keepdims=True) + jnp.sum(
                    p0 * dp0, axis=1, keepdims=True
                )
                ds1 = (p1 * (dp1 - delta)).astype(bf16)
                ds0 = (p0 * (dp0 - delta)).astype(bf16)
                dv_s[0:end, :] += tn(p1.astype(bf16), doh)
                dvp_s[...] += tn(p0.astype(bf16), doh)
                dk_s[0:end, :] += tn(ds1, qh)
                dkp_s[...] += tn(ds0, qh)
                halves.append(nn(ds1, k2[0:end, :]) + nn(ds0, k2p[...]))
            if between and pair == 0 and b in between:
                between[b]()
            dqp = jnp.where(low, halves[0], halves[1]) * 0.125
            dq[start:end, cols] = turned(dqp, cos[start:end, :], -sin[start:end, :]).astype(bf16)
    low = low_half((TOK, 128))

    def joined(dk, dv):
        dk, dv = dk[...], dv[...]
        return jnp.where(low, dk + pltpu.roll(dk, 64, 1), dv + pltpu.roll(dv, 64, 1))

    dkv[...] = joined(dk_s, dv_s)
    dkv_p[...] = joined(dkp_s, dvp_s).astype(bf16)


def tap_mask(seg_ext, k):
    now = seg_ext[HALO : HALO + TOK, 0:1]
    at = HALO - 3 + k
    return jnp.where(seg_ext[at : at + TOK, 0:1] == now, 1.0, 0.0)


def lower_ones():
    row, col = head_matrix(SPAN, SPAN)
    return jnp.where(row >= col, 1.0, 0.0)


def rows_of(c):
    return slice(c * SPAN, (c + 1) * SPAN)


def mixer_in_body(cin, taps, step, bias, rate, seg_ext, pre, dt, cum, last):
    run = jnp.zeros((TOK, CONV), f32)
    for k in range(4):
        at = HALO - 3 + k
        run = run + cin[at : at + TOK, :] * taps[k : k + 1, :] * tap_mask(seg_ext, k)
    pre[...] = run
    lane = lax.broadcasted_iota(jnp.int32, (TOK, 128), 1)
    steps = step[...] + bias[...]
    u = jnp.exp(-jnp.abs(steps))
    log_part = jnp.where(
        u < 0.02, u * (1.0 - u * (0.5 - u * (1.0 / 3.0 - 0.25 * u))), jnp.log(1.0 + u)
    )
    soft = jnp.maximum(steps, 0.0) + log_part
    dt[...] = jnp.where(lane < HEADS, soft, 0.0)
    tri = lower_ones()
    state = jnp.zeros((STATE, INNER), f32)
    for c in range(SPANS):
        rows = rows_of(c)
        own_dt = dt[rows, :]
        total = jnp.dot(tri, own_dt * rate[...], precision=HIGH, preferred_element_type=f32)
        cum[rows, :] = total
        out = pre[rows, 0 : INNER + STATE]
        out = out * sigmoid(out)
        seg = seg_ext[HALO + c * SPAN : HALO + (c + 1) * SPAN, 0:1]
        seg_last = seg[SPAN - 1 : SPAN, :]
        end = total[SPAN - 1 : SPAN, :]
        tail = jnp.where(seg == seg_last, jnp.exp(jnp.minimum(end - total, 0.0)), 0.0) * own_dt
        fresh = tn(out[:, INNER:].astype(bf16), (out[:, 0:INNER] * spread(tail)).astype(bf16))
        if c == 0:
            state = fresh
        else:
            seg_prev = seg_ext[HALO + c * SPAN - 1 : HALO + c * SPAN, 0:1]
            keep = jnp.where(seg_last == seg_prev, jnp.exp(end), 0.0)
            state = state * spread(jnp.broadcast_to(keep, (8, 128)))[0:1, :] + fresh
    last[...] = state.astype(bf16)


def span_parts(c, cum, seg_ext):
    total = cum[rows_of(c), :]
    seg = seg_ext[HALO + c * SPAN : HALO + (c + 1) * SPAN, 0:1]
    seg_last = seg[SPAN - 1 : SPAN, :]
    seg_prev = seg_ext[HALO + c * SPAN - 1 : HALO + c * SPAN, 0:1]
    end = total[SPAN - 1 : SPAN, :]
    entering = jnp.where(seg == seg_prev, jnp.exp(total), 0.0)
    tail = jnp.where(seg == seg_last, jnp.exp(jnp.minimum(end - total, 0.0)), 0.0)
    return total, entering, tail


def span_bias(c, seg_ext, seg_row):
    row, col = head_matrix(SPAN, SPAN)
    seg = seg_ext[HALO + c * SPAN : HALO + (c + 1) * SPAN, 0:1]
    other = seg_row[0:1, TOK + c * SPAN : TOK + (c + 1) * SPAN]
    return jnp.where((row >= col) & (seg == other), 0.0, NEG)


def mixer_out_body(
    pre, dt, cum, seg_ext, seg_row, first, z, skip, y, gated, states, sc_state
):
    if first is not None:
        sc_state[...] = first[...].astype(f32)
    low2 = low_half((SPAN, 128))
    for c in range(SPANS):
        rows = rows_of(c)
        total, entering, tail = span_parts(c, cum, seg_ext)
        out = pre[rows, :]
        out = out * sigmoid(out)
        x = out[:, 0:INNER]
        b = out[:, INNER : INNER + STATE].astype(bf16)
        cm = out[:, INNER + STATE :].astype(bf16)
        own_dt = dt[rows, :]
        xs = x * spread(own_dt)
        state = sc_state[...]
        state_b = state.astype(bf16)
        states[c] = state_b
        wide_in = spread(entering)
        run = nn(cm, state_b) * wide_in + x * skip[...]
        inter = nt(cm, b)
        bias = span_bias(c, seg_ext, seg_row)
        total_t = total.T
        gate = z[rows, :]
        gate = gate * sigmoid(gate)
        for pair in range(HEADS // 2):
            cols = slice(128 * pair, 128 * pair + 128)
            parts = []
            for side in range(2):
                h = 2 * pair + side
                decay = jnp.exp(total[:, h : h + 1] - total_t[h : h + 1, :] + bias)
                parts.append((decay * inter).astype(bf16))
            xp = xs[:, cols]
            stack = jnp.concatenate(
                [jnp.where(low2, xp, 0.0).astype(bf16), jnp.where(low2, 0.0, xp).astype(bf16)], axis=0
            )
            yp = run[:, cols] + nn(jnp.concatenate(parts, axis=1), stack)
            y[rows, cols] = yp
            gated[rows, cols] = (yp * gate[:, cols]).astype(bf16)
        if c < SPANS - 1:
            sc_state[...] = state * wide_in[SPAN - 1 : SPAN, :] + tn(
                b, (xs * spread(tail)).astype(bf16)
            )


def mixer_back_in_body(dgated, z, y, pre, cum, seg_ext, dy, dz, first):
    state = jnp.zeros((STATE, INNER), f32)
    for c in reversed(range(SPANS)):
        rows = rows_of(c)
        total, entering, tail = span_parts(c, cum, seg_ext)
        gate = z[rows, :]
        sig = sigmoid(gate)
        grad = dgated[rows, :]
        own = grad * (gate * sig)
        dy[rows, :] = own
        dz[rows, :] = (grad * y[rows, :] * (sig * (1.0 + gate * (1.0 - sig)))).astype(bf16)
        cm = pre[rows, INNER + STATE :]
        cm = (cm * sigmoid(cm)).astype(bf16)
        wide_in = spread(entering)
        fresh = tn(cm, (own * wide_in).astype(bf16))
        state = fresh if c == SPANS - 1 else state * wide_in[SPAN - 1 : SPAN, :] + fresh
    first[...] = state.astype(bf16)


def mixer_back_body(
    dy, pre, dt, cum, seg_ext, seg_row, states, last, skip, rate, step, bias,
    dpre, dstep, heads, sc_state, between=None,
):
    if last is not None:
        sc_state[...] = last[...].astype(f32)
    low2 = low_half((SPAN, 128))
    lane = lax.broadcasted_iota(jnp.int32, (SPAN, 128), 1)
    tri = lower_ones()
    sum_decay = jnp.zeros((1, 128), f32)
    sum_bias = jnp.zeros((1, 128), f32)
    sum_skip = jnp.zeros((1, 128), f32)
    for c in reversed(range(SPANS)):
        if between and c in between:
            between[c]()
        rows = rows_of(c)
        total, entering, tail = span_parts(c, cum, seg_ext)
        lin = pre[rows, :]
        sig = sigmoid(lin)
        out = lin * sig
        slope = sig * (1.0 + lin * (1.0 - sig))
        x = out[:, 0:INNER]
        b = out[:, INNER : INNER + STATE].astype(bf16)
        cm = out[:, INNER + STATE :].astype(bf16)
        own_dt = dt[rows, :]
        wide_dt = spread(own_dt)
        xs = x * wide_dt
        grad = dy[rows, :]
        wide_in = spread(entering)
        wide_tail = spread(tail)
        dstate = sc_state[...]
        dstate_b = dstate.astype(bf16)
        state_b = states[c]
        gin = grad * wide_in
        gin_b = gin.astype(bf16)
        y_state = nn(cm, state_b)
        xt = xs * wide_tail
        xt_b = xt.astype(bf16)
        from_state = nn(b, dstate_b)
        dcm = nt(gin_b, state_b)
        db = nt(xt_b, dstate_b)
        dcum = gathered_heads(gin * y_state)
        moved = gathered_heads(xt * from_state)
        kept = jnp.sum(dstate * state_b.astype(f32), axis=0, keepdims=True)
        kept = kept * wide_in[SPAN - 1 : SPAN, :]
        kept = gathered_heads(jnp.broadcast_to(kept, (8, INNER)))[0:1, :]
        at_end = jnp.sum(moved, axis=0, keepdims=True) + kept
        sub = lax.broadcasted_iota(jnp.int32, (SPAN, 128), 0)
        dcum = dcum - moved + jnp.where(sub == SPAN - 1, at_end, 0.0)
        sc_state[...] = dstate * wide_in[SPAN - 1 : SPAN, :] + tn(cm, gin_b)
        inter = nt(cm, b)
        bias_m = span_bias(c, seg_ext, seg_row)
        total_t = total.T
        dinter = jnp.zeros((SPAN, SPAN), f32)
        col_sums = jnp.zeros((128, SPAN), f32)
        sub_t = lax.broadcasted_iota(jnp.int32, (128, SPAN), 0)
        ddt = jnp.zeros((SPAN, 128), f32)
        dskip = jnp.zeros((SPAN, 128), f32)
        for pair in range(HEADS // 2):
            cols = slice(128 * pair, 128 * pair + 128)
            gp, xp = grad[:, cols], xs[:, cols]
            gp_b, xp_b = gp.astype(bf16), xp.astype(bf16)
            stack = jnp.concatenate(
                [jnp.where(low2, gp, 0.0).astype(bf16), jnp.where(low2, 0.0, gp).astype(bf16)], axis=0
            )
            dm = nt(stack, xp_b)
            parts = []
            for side in range(2):
                h = 2 * pair + side
                decay = jnp.exp(total[:, h : h + 1] - total_t[h : h + 1, :] + bias_m)
                dmh = dm[side * SPAN : (side + 1) * SPAN, :] * decay
                dinter = dinter + dmh
                weight = decay * inter
                parts.append(weight.astype(bf16))
                q = dmh * inter
                dcum = dcum + jnp.where(lane == h, jnp.sum(q, axis=1, keepdims=True), 0.0)
                col_sums = col_sums + jnp.where(sub_t == h, jnp.sum(q, axis=0, keepdims=True), 0.0)
            both = tn(jnp.concatenate(parts, axis=1), gp_b)
            dxs = jnp.where(low2, both[0:SPAN, :], both[SPAN:, :]) + from_state[:, cols] * wide_tail[:, cols]
            xo = x[:, cols]
            dx = dxs * wide_dt[:, cols] + gp * skip[:, cols]
            dpre[rows, cols] = dx * slope[:, cols]
            pick_row, pick_col = head_matrix(128, 128)
            pick = jnp.where(pick_col == 2 * pair + pick_row // 64, 1.0, 0.0).astype(bf16)
            hi, lo = split_halves(dxs * xo)
            ddt = ddt + nn(hi, pick) + nn(lo, pick)
            hi, lo = split_halves(gp * xo)
            dskip = dskip + nn(hi, pick) + nn(lo, pick)
        dinter_b = dinter.astype(bf16)
        dcm = dcm + nn(dinter_b, b)
        db = db + tn(dinter_b, cm)
        dpre[rows, INNER : INNER + STATE] = db * slope[:, INNER : INNER + STATE]
        dpre[rows, INNER + STATE :] = dcm * slope[:, INNER + STATE :]
        dcum = dcum - col_sums.T
        dlog = lax.dot_general(
            tri, dcum, (((0,), (0,)), ((), ())), precision=HIGH, preferred_element_type=f32
        )
        ddt = ddt + dlog * rate[...]
        dsp = jnp.where(lane < HEADS, ddt * sigmoid(step[rows, :] + bias[...]), 0.0)
        dstep[rows, :] = dsp.astype(bf16)
        sum_decay = sum_decay + jnp.sum(dlog * own_dt, axis=0, keepdims=True)
        sum_bias = sum_bias + jnp.sum(dsp, axis=0, keepdims=True)
        sum_skip = sum_skip + jnp.sum(dskip, axis=0, keepdims=True)
    sub8 = lax.broadcasted_iota(jnp.int32, (8, 128), 0)
    sums = jnp.where(
        sub8 == 0,
        sum_decay * rate[...],
        jnp.where(sub8 == 1, sum_bias, jnp.where(sub8 == 2, sum_skip, 0.0)),
    )
    if heads is not None:
        heads[...] = sums
    return sums


MESH = pl.DeviceIdType.MESH
SMALL = CONV + 128
BC0 = C_U + INNER


def place():
    f = lax.axis_index("fsdp")
    core = lax.rem(f, 2)
    chip = lax.div(f, 2)
    return lax.div(chip, 4), lax.rem(chip, 4), core


def at_yz(y, z, core):
    return {"fsdp": (lax.rem(y, 4) * 4 + lax.rem(z, 4)) * 2 + core}


def torus_peers():
    y, z, core = place()
    return (
        [at_yz(y, z, 1 - core), {"ctx": 1 - lax.axis_index("ctx")}]
        + [at_yz(y, z + n, core) for n in (1, 2, 3)]
        + [at_yz(y + n, z, core) for n in (1, 2, 3)]
    )


def greet(peers):
    barrier = pltpu.get_barrier_semaphore()
    for peer in peers:
        pl.semaphore_signal(barrier, inc=1, device_id=peer, device_id_type=MESH)
    pl.semaphore_wait(barrier, len(peers))


def send(src, dst, sems, k, peer):
    copy = pltpu.make_async_remote_copy(
        src_ref=src,
        dst_ref=dst,
        send_sem=sems.at[0, k],
        recv_sem=sems.at[1, k],
        device_id=peer,
        device_id_type=MESH,
    )
    copy.start()
    return copy


class Refs:
    def __init__(self, names, refs):
        self.__dict__.update(zip(names, refs))
        self.pending, self.stored, self.used = {}, [], 0

    def fetch(self, *names):
        for name in names:
            self.fetch_from(name, getattr(self, "h_" + name))

    def fetch_from(self, name, src):
        copy = pltpu.make_async_copy(src, getattr(self, name), self.io_sems.at[self.used])
        self.used += 1
        copy.start()
        self.pending[name] = copy

    def need(self, *names):
        for name in names:
            if name in self.pending:
                self.pending.pop(name).wait()
        return getattr(self, names[0])

    def store(self, *names):
        for name in names:
            copy = pltpu.make_async_copy(
                getattr(self, name), getattr(self, "h_" + name), self.io_sems.at[self.used]
            )
            self.used += 1
            copy.start()
            self.stored.append(copy)

    def store_part(self, name, part):
        copy = pltpu.make_async_copy(
            part(getattr(self, name)), part(getattr(self, "h_" + name)), self.io_sems.at[self.used]
        )
        self.used += 1
        copy.start()
        self.stored.append(copy)

    def settle(self):
        for copy in self.stored:
            copy.wait()


def run(body, ins, outs, scratch, collective_id):
    any_spec, vmem_spec = pl.BlockSpec(memory_space=pl.ANY), pl.BlockSpec(memory_space=pltpu.VMEM)
    spaces = [(s[0], s[1] if len(s) == 2 else pltpu.VMEM(s[1], s[2])) for s in scratch]
    spaces.append(("io_sems", pltpu.SemaphoreType.DMA((len(ins) + len(outs) + 4,))))
    names = (
        [("h_" if hbm else "") + n for n, _, hbm in ins]
        + [("h_" if hbm else "") + n for n, _, _, hbm in outs]
        + [n for n, _ in spaces]
    )

    def kernel(*refs):
        body(Refs(names, refs))

    return pl.pallas_call(
        kernel,
        out_shape=[jax.ShapeDtypeStruct(s, d) for _, s, d, _ in outs],
        in_specs=[any_spec if hbm else vmem_spec for _, _, hbm in ins],
        out_specs=[any_spec if hbm else vmem_spec for _, _, _, hbm in outs],
        scratch_shapes=[s for _, s in spaces],
        compiler_params=pltpu.CompilerParams(
            vmem_limit_bytes=63 * 1024 * 1024, collective_id=collective_id, has_side_effects=True
        ),
        cost_estimate=pl.CostEstimate(flops=10**11, bytes_accessed=10**8, transcendentals=0),
    )(*[a for _, a, _ in ins])


def dma_sems(*shape):
    return pltpu.SemaphoreType.DMA(shape)


class DirectGather:
    def __init__(self, block, me, peers, sems):
        self.block, self.me, self.sems, self.peers = block, me, sems, peers

    def start(self):
        own = self.block(self.me)
        self.copies = [send(own, own, self.sems, n, p) for n, p in enumerate(self.peers)]

    def finish(self):
        for copy in self.copies:
            copy.wait_recv()

    def close(self):
        for copy in self.copies:
            copy.wait_send()


class RingGather:
    def __init__(self, block, me, peers, sems):
        self.block, self.me, self.sems = block, me, sems
        self.right, self.left = peers[0], peers[2]

    def ahead(self, n):
        return lax.rem(self.me + n, 4)

    def start(self):
        own = self.block(self.me, None)
        self.near = (
            send(own, own, self.sems, 0, self.right),
            send(own, own, self.sems, 1, self.left),
        )

    def forward(self):
        self.far = []
        for side, (peer, n) in enumerate(((self.right, 3), (self.left, 1))):
            self.near[side].wait_recv()
            part = self.block(self.ahead(n), side)
            self.far.append(send(part, part, self.sems, 2 + side, peer))

    def finish(self):
        for copy in self.far:
            copy.wait_recv()

    def close(self):
        for copy in list(self.near) + self.far:
            copy.wait_send()


class Gather:
    def __init__(self, whole, sems, cross_sems):
        y, z, core = place()
        self.whole, self.y, self.z, self.core = whole, y, z, core
        width = whole.shape[-1]
        half = width // 256 * 128
        ca, cb = slice(0, half), slice(half, width)
        self.ca, self.cb = ca, cb
        peers = torus_peers()
        self.sibling, zs, ys = peers[0], peers[2:5], peers[5:8]
        self.sems, self.across = cross_sems, []

        def two(h):
            return slice(0, 4) if h is None else slice(2 * h, 2 * h + 2)

        self.a1 = DirectGather(lambda d: whole.at[y, d, core, :, ca], z, zs, sems.at[0])
        self.b1 = DirectGather(lambda d: whole.at[d, z, core, :, cb], y, ys, sems.at[1])
        self.a2 = RingGather(lambda d, h: whole.at[d, two(h), core, :, ca], y, ys, sems.at[2])
        self.b2 = RingGather(lambda d, h: whole.at[two(h), d, core, :, cb], z, zs, sems.at[3])

    def cross(self, view):
        self.across.append(send(view, view, self.sems, len(self.across), self.sibling))

    def start(self):
        self.a1.start()
        self.b1.start()

    def turn(self):
        self.a1.finish()
        self.a2.start()
        self.b1.finish()
        self.b2.start()
        self.cross(self.whole.at[self.y, :, self.core, :, self.ca])
        self.cross(self.whole.at[:, self.z, self.core, :, self.cb])

    def forward(self):
        a2, b2 = self.a2, self.b2
        a2.forward()
        b2.forward()
        for n in (1, 3):
            self.cross(a2.block(a2.ahead(n), None))
            self.cross(b2.block(b2.ahead(n), None))

    def near(self):
        for ring in (self.a2, self.b2):
            for copy in ring.near:
                copy.wait_recv()
            ring.far = []
            for n in (1, 3):
                self.cross(ring.block(ring.ahead(n), None))

    def far(self):
        self.a1.copies = self.b1.copies = []
        for ring in (self.a2, self.b2):
            ring.near, ring.far = [], []
            for side, (peer, n) in enumerate(((ring.right, 3), (ring.left, 1))):
                part = ring.block(ring.ahead(n), side)
                ring.far.append(send(part, part, ring.sems, 2 + side, peer))

    def finish(self):
        a2, b2 = self.a2, self.b2
        a2.finish()
        self.cross(a2.block(a2.ahead(2), None))
        b2.finish()
        self.cross(b2.block(b2.ahead(2), None))

    def rows(self, ref, n):
        return ref.at[lax.rem(self.y + n, 4), :, :, :, self.ca]

    def planes(self, ref, n):
        return ref.at[:, lax.rem(self.z + n, 4), :, :, self.cb]

    def arrived(self):
        for copy in self.across:
            copy.wait_recv()

    def close(self):
        for ring in (self.a1, self.b1, self.a2, self.b2):
            ring.close()
        for copy in self.across:
            copy.wait_send()


class RingSum:
    def __init__(self, chunk, me, peers, sems, far, near, joined):
        self.chunk, self.me, self.sems = chunk, me, sems
        self.right, self.left = peers[0], peers[2]
        self.far, self.near, self.joined = far, near, joined

    def ahead(self, n):
        return lax.rem(self.me + n, 4)

    def start(self):
        c, s = self.chunk, self.sems
        self.far_copies = (
            send(c(self.ahead(2), 0), self.far.at[0], s, 0, self.right),
            send(c(self.ahead(2), 1), self.far.at[1], s, 1, self.left),
        )
        self.direct = (
            send(c(self.ahead(1), 1), self.near.at[0, 1], s, 2, self.right),
            send(c(self.ahead(3), 0), self.near.at[1, 0], s, 3, self.left),
        )

    def forward(self):
        c, s = self.chunk, self.sems
        passed = []
        for side, (peer, n) in enumerate(((self.right, 1), (self.left, 3))):
            self.far_copies[side].wait_recv()
            own = c(self.ahead(n), side)[...]
            self.joined[side] = (own.astype(f32) + self.far[side].astype(f32)).astype(bf16)
            passed.append(send(self.joined.at[side], self.near.at[side, side], s, 4 + side, peer))
        self.passed = tuple(passed)

    def finish(self):
        for copy in self.direct + self.passed:
            copy.wait_recv()

    def total(self, half):
        own = self.chunk(self.me, half)[...].astype(f32)
        return own + self.near[0, half].astype(f32) + self.near[1, half].astype(f32)

    def close(self):
        for copy in self.far_copies + self.direct + self.passed:
            copy.wait_send()


class DirectSum:
    def __init__(self, chunk, me, peers, sems, arrived):
        self.chunk, self.me, self.peers, self.sems, self.arrived = chunk, me, peers, sems, arrived

    def start(self):
        self.copies = [
            send(self.chunk(lax.rem(self.me + n + 1, 4)), self.arrived.at[n], self.sems, n, p)
            for n, p in enumerate(self.peers)
        ]

    def total(self):
        for copy in self.copies:
            copy.wait_recv()
        a = self.arrived
        own = self.chunk(self.me)[...].astype(f32)
        return (own + a[0].astype(f32)) + (a[1].astype(f32) + a[2].astype(f32))

    def close(self):
        for copy in self.copies:
            copy.wait_send()


class Reduce:
    def __init__(self, e, name, fin):
        y, z, core = place()
        g = lambda part: getattr(e, name + part)
        self.gbuf, crecv, self.core, self.fin = getattr(e, name + "gbuf", None), g("crecv"), core, fin
        self.crecv, self.core_sems = crecv, g("core_sems")
        peers = torus_peers()
        self.sibling, zs, ys = peers[0], peers[2:5], peers[5:8]
        width = crecv.shape[-1]
        half = width // 256 * 128
        ca, cb = self.ca, self.cb = slice(0, half), slice(half, width)
        one_a, one_b = self.one_a, self.one_b = g("one_a"), g("one_b")
        s = g("ring_sems")
        self.a = RingSum(
            lambda d, h: crecv.at[2 * h : 2 * h + 2, d, :, ca], z, zs, s.at[0],
            g("far_a"), g("near_a"), g("join_a"),
        )
        self.b = RingSum(
            lambda d, h: crecv.at[d, 2 * h : 2 * h + 2, :, cb], y, ys, s.at[1],
            g("far_b"), g("near_b"), g("join_b"),
        )
        self.a2 = DirectSum(lambda d: one_a.at[d], y, ys, s.at[2], g("late_a"))
        self.b2 = DirectSum(lambda d: one_b.at[d], z, zs, s.at[3], g("late_b"))
        self.copies = {}

    def piece(self, j, block):
        cols = slice(j * 256, (j + 1) * 256)
        self.gbuf[:, :, :, :, cols] = block.astype(bf16).reshape(4, 4, 2, 32, 256)
        self.copies[j] = send(
            self.gbuf.at[:, :, 1 - self.core, :, cols],
            self.crecv.at[:, :, :, cols],
            self.core_sems,
            j,
            self.sibling,
        )

    def add(self, j):
        cols = slice(j * 256, (j + 1) * 256)
        self.copies[j].wait_recv()
        own = self.gbuf[:, :, self.core, :, cols].astype(f32)
        self.crecv[:, :, :, cols] = (own + self.crecv[:, :, :, cols].astype(f32)).astype(bf16)

    def start(self):
        self.a.start()
        self.b.start()

    def forward(self):
        self.a.forward()
        self.b.forward()

    def turn(self):
        for ring, one, second in ((self.a, self.one_a, self.a2), (self.b, self.one_b, self.b2)):
            ring.finish()
            for h in range(2):
                one[2 * h : 2 * h + 2] = ring.total(h).astype(bf16)
            second.start()

    def finish(self):
        self.fin[:, self.ca] = self.a2.total().astype(bf16)
        self.fin[:, self.cb] = self.b2.total().astype(bf16)

    def close(self):
        for ring in (self.a, self.b, self.a2, self.b2):
            ring.close()
        for copy in self.copies.values():
            copy.wait_send()


def reduce_space(name, width, own_buffer=True):
    half = width // 256 * 128
    space = [(name + "crecv", (4, 4, 32, width), bf16)]
    if own_buffer:
        space.append((name + "gbuf", (4, 4, 2, 32, width), bf16))
    for side, wide in (("a", half), ("b", width - half)):
        space += [
            (name + "far_" + side, (2, 2, 32, wide), bf16),
            (name + "near_" + side, (2, 2, 2, 32, wide), bf16),
            (name + "join_" + side, (2, 2, 32, wide), bf16),
            (name + "one_" + side, (4, 32, wide), bf16),
            (name + "late_" + side, (3, 32, wide), bf16),
        ]
    return space + [
        (name + "core_sems", dma_sems(2, width // 256)),
        (name + "ring_sems", dma_sems(4, 2, 6)),
    ]


class SmallSum:
    def __init__(self, e):
        self.sems = e.small_sems
        self.bufs = e.sm_core, e.sm_z, e.sm_y, e.sm_ctx, e.sm_tp
        self.y, self.z, self.core = place()
        self.all = []

    def spread_to(self, buf, at, first_sem, peers):
        self.last = [
            send(buf.at[at], buf.at[at], self.sems, first_sem + n, peer)
            for n, peer in enumerate(peers)
        ]
        self.all += self.last

    def wait(self):
        for copy in self.last:
            copy.wait_recv()

    def start(self, block):
        buf = self.bufs[0]
        buf[self.core] = block
        self.spread_to(buf, self.core, 0, torus_peers()[0:1])

    def along_z(self):
        self.wait()
        buf = self.bufs[1]
        buf[self.z] = self.bufs[0][0] + self.bufs[0][1]
        self.spread_to(buf, self.z, 1, torus_peers()[2:5])

    def along_y(self):
        self.wait()
        buf, old = self.bufs[2], self.bufs[1]
        buf[self.y] = (old[0] + old[1]) + (old[2] + old[3])
        self.spread_to(buf, self.y, 4, torus_peers()[5:8])

    def along_ctx(self):
        self.wait()
        ctx = lax.axis_index("ctx")
        buf, old = self.bufs[3], self.bufs[2]
        buf[ctx] = (old[0] + old[1]) + (old[2] + old[3])
        self.spread_to(buf, ctx, 7, torus_peers()[1:2])

    def along_tp(self):
        self.wait()
        tp = lax.axis_index("tp")
        self.bufs[4][tp] = self.bufs[3][0] + self.bufs[3][1]
        self.spread_to(self.bufs[4], tp, 8, [{"tp": 1 - tp}])

    def result(self):
        self.wait()
        own = self.bufs[4][lax.axis_index("tp")]
        both = self.bufs[4][0] + self.bufs[4][1]
        row = lax.broadcasted_iota(jnp.int32, (8, SMALL), 0)
        col = lax.broadcasted_iota(jnp.int32, (8, SMALL), 1)
        shared = ((row >= 4) & (col < CONV)) | ((col >= INNER) & (col < CONV))
        return jnp.where(shared, both, own)

    def close(self):
        for copy in self.all:
            copy.wait_send()


def column_of(row):
    r, c = head_matrix(32, 32)
    return jnp.sum(jnp.where(r == c, jnp.broadcast_to(row.astype(f32), (32, 32)), 0.0), axis=1, keepdims=True)


def pack_body(
    query, keyval, attn, inner, state, step, gain1, gain2, inner_o, gate_up, down, first, second
):
    first[:, C_Q : C_Q + QW] = query[...]
    lane = lax.broadcasted_iota(jnp.int32, (32, 128), 1)
    tail_cols = jnp.where(lane == HEADS, column_of(gain1[...]), 0.0)
    tail_cols = jnp.where(lane == HEADS + 1, column_of(gain2[...]), tail_cols)
    first[:, C_DT : C_DT + 128] = tail_cols.astype(bf16)
    first[:, C_DT : C_DT + HEADS] = step[...].astype(f32).T.astype(bf16)
    for i in range(2):
        first[:, C_KV + 64 * i : C_KV + 64 * i + 64] = keyval[:, i, :]
        first[:, C_Z + INNER * i : C_Z + INNER * (i + 1)] = inner[:, i, :]
        second[:, W2C + FFH * i : W2C + FFH * (i + 1)] = gate_up[:, i, :]
    first[:, BC0 : BC0 + 256] = state[...]
    second[:, 0:QW] = attn[...]
    second[:, QW:W2C] = inner_o[...]
    second[:, W2C + 2 * FFH :] = down[...]


def place_segments(e):
    seg, seg_ext, seg_row, wide = e.seg, e.seg_ext, e.seg_row, e.wide
    late = lax.axis_index("ctx")
    row = seg[...].astype(f32)
    wide[...] = jnp.broadcast_to(row, (128, 2 * TOK)).T
    own = pl.ds(pl.multiple_of(late * TOK, TOK), TOK)
    before = pl.ds(pl.multiple_of(late * (TOK - HALO), HALO), HALO)
    after = pl.ds(pl.multiple_of((1 - late) * TOK, TOK), 8)
    seg_ext[0:HALO, :] = jnp.where(late > 0, wide[before, :], -1.0)
    seg_ext[HALO : HALO + TOK, :] = wide[own, :]
    seg_ext[HALO + TOK :, :] = jnp.where(late > 0, -2.0, wide[after, :])
    seg_row[:, 0:TOK] = jnp.broadcast_to(jnp.where(late > 0, row[:, 0:TOK], -1.0), (8, TOK))
    seg_row[:, TOK:] = jnp.broadcast_to(seg[0:1, own].astype(f32), (8, TOK))


def forward_body(e):
    py, pz, core = place()
    late = lax.axis_index("ctx")
    ctx_peer = {"ctx": 1 - late}
    e.fetch("tok", "cos", "sin")
    pack_body(
        e.query, e.keyval, e.attn, e.inner, e.state, e.step_w, e.gain1, e.gain2, e.inner_o, e.gate_up,
        e.down_w, e.shard1, e.shard2,
    )
    e.w1[py, pz, core] = e.shard1[...]
    e.w2[py, pz, core] = e.shard2[:, 0:W2C]
    e.w3[py, pz, core] = e.shard2[:, W2C:]
    diagonal = {"ctx": 1 - late, "tp": 1 - lax.axis_index("tp")}
    greet(torus_peers() + [diagonal])
    one = Gather(e.w1, e.sems1, e.cross1)
    two = Gather(e.w2, e.sems2, e.cross2)
    three = Gather(e.w3, e.sems3, e.cross3)
    one.start()
    mine3 = e.w3.at[py, pz, core]
    shard_copy = send(mine3, e.shard_x, e.ctx_sems, 2, diagonal)
    tok = e.need("tok")
    tok_copy = send(tok.at[TOK - HALO : TOK], e.prior, e.ctx_sems, 0, ctx_peer)
    e.unit[...] = unit_rows(tok[...].astype(f32))[0]
    e.unit_t[...] = e.unit[...].T
    one.turn()
    two.start()
    place_segments(e)
    taps, hp, skip = e.taps, e.hp, e.skip
    taps[...] = jnp.zeros_like(taps)
    taps[0:4, 0:INNER] = e.taps_i[...].astype(f32)
    taps[0:4, INNER:] = e.taps_s[...].astype(f32)
    hp[...] = jnp.zeros_like(hp)
    hp[0:1, 0:HEADS] = e.step_bias[...]
    hp[1:2, 0:HEADS] = -jnp.exp(e.decay_log[...])
    hp[2:3, 0:HEADS] = e.skip_gain[...]
    skip[...] = spread(jnp.broadcast_to(hp[2:3, :], (8, 128)))
    e.store("seg_ext", "seg_row", "taps", "hp")
    one.forward()
    two.turn()
    three.start()
    tok_copy.wait_recv()
    one.finish()
    one.arrived()
    e.store("w1")
    w1, normed, norm_p = e.w1, e.normed, e.norm_p

    def columns(at, size):
        return w1[:, :, :, :, at].reshape(WID, size)

    flipped = columns(slice(C_DT, C_DT + 128), 128).astype(f32).T
    e.gains[...] = flipped[8:16, :]
    g = flipped[HEADS : HEADS + 1, :]
    normed[...] = (e.unit[...] * g).astype(bf16)
    norm_p[...] = (unit_rows(e.prior[...].astype(f32))[0] * g).astype(bf16)
    e.normed_t[...] = (e.unit_t[...] * columns(slice(C_DT, C_DT + 128), 128)[:, HEADS : HEADS + 1].astype(f32)).astype(bf16)
    e.store("normed_t", "gains")
    own = pl.ds(pl.multiple_of(late * TOK, TOK), TOK)
    lin = nn(normed[...], columns(slice(0, 256), 256))
    e.need("cos", "sin")
    c, s = e.cos[own, :], e.sin[own, :]
    for i in range(2):
        cols = slice(128 * i, 128 * i + 128)
        e.q[:, cols] = turned(lin[:, cols], c, s).astype(bf16)
    low = low_half((TOK, 128))

    def pair(both, kk, vv):
        other = pltpu.roll(both, 64, 1)
        kk[...] = jnp.where(low, both, other).astype(bf16)
        vv[...] = jnp.where(low, other, both).astype(bf16)

    lin = nn(normed[...], columns(slice(256, 512), 256))
    both = jnp.where(low, turned(lin[:, 0:128], c, s), lin[:, 0:128])
    e.kv[...] = both.astype(bf16)
    kv_copy = send(e.kv, e.kv_prior, e.ctx_sems, 3, ctx_peer)
    pair(both, e.k2, e.v2)
    e.step[...] = lin[:, 128:256]
    e.store("q", "k2", "v2", "step")
    two.forward()

    @pl.loop(0, 4)
    def _(j):
        at = pl.ds(pl.multiple_of(C_U + j * 256, 256), 256)
        to = pl.ds(pl.multiple_of(j * 256, 256), 256)
        block = columns(at, 256)
        e.cin[0:HALO, to] = nn(norm_p[...], block)
        e.cin[HALO : HALO + TOK, to] = nn(normed[...], block)

    e.store("cin")
    three.turn()
    mixer_in_body(
        e.cin, taps, e.step, hp.at[0:1], hp.at[1:2], e.seg_ext, e.pre, e.dt, e.cum, e.last
    )
    state_copy = send(e.last, e.first, e.ctx_sems, 1, ctx_peer)
    e.store("pre", "dt", "cum")

    @pl.loop(0, 3)
    def _(j):
        at = pl.ds(pl.multiple_of(C_Z + j * 256, 256), 256)
        to = pl.ds(pl.multiple_of(j * 256, 256), 256)
        e.z[:, to] = nn(normed[...], columns(at, 256))

    e.store("z")
    kv_copy.wait_recv()
    pair(e.kv_prior[...].astype(f32), e.k2p, e.v2p)
    e.store("k2p", "v2p")
    attend_body(
        e.q, e.k2, e.v2, e.k2p, e.v2p, e.seg_ext.at[HALO : HALO + TOK], e.seg_row,
        e.mixed.at[:, 0:QW], e.lse,
    )
    e.store("lse")
    two.finish()
    three.near()
    shard_copy.wait_recv()
    e.store("shard_x")
    state_copy.wait_recv()
    e.sc_state[...] = jnp.where(late > 0, e.first[...].astype(f32), 0.0)
    mixer_out_body(
        e.pre, e.dt, e.cum, e.seg_ext, e.seg_row, None, e.z, skip.at[0:1], e.y,
        e.mixed.at[:, QW:], e.states, e.sc_state,
    )
    e.store("mixed", "y", "states")
    two.arrived()
    e.store("w2")
    three.arrived()
    for n in (0, 1, 3):
        e.store_part("w3", lambda ref: three.rows(ref, n))
        e.store_part("w3", lambda ref: three.planes(ref, n))
    three.close()
    one.close()
    two.close()
    tok_copy.wait_send()
    shard_copy.wait_send()
    kv_copy.wait_send()
    state_copy.wait_send()
    e.settle()


FORWARD_OUTS = [
    ("w1", (4, 4, 2, 32, W1C), bf16),
    ("w2", (4, 4, 2, 32, W2C), bf16),
    ("w3", (4, 4, 2, 32, W3C), bf16),
    ("normed_t", (WID, TOK), bf16),
    ("q", (TOK, QW), bf16),
    ("k2", (TOK, 128), bf16),
    ("v2", (TOK, 128), bf16),
    ("k2p", (TOK, 128), bf16),
    ("v2p", (TOK, 128), bf16),
    ("z", (TOK, INNER), f32),
    ("cin", (HALO + TOK, CONV), f32),
    ("step", (TOK, 128), f32),
    ("gains", (8, WID), f32),
    ("pre", (TOK, CONV), f32),
    ("dt", (TOK, 128), f32),
    ("cum", (TOK, 128), f32),
    ("states", (SPANS, STATE, INNER), bf16),
    ("y", (TOK, INNER), f32),
    ("mixed", (TOK, QW + INNER), bf16),
    ("lse", (TOK, 128), f32),
    ("seg_ext", (HALO + TOK + 8, 128), f32),
    ("seg_row", (8, 2 * TOK), f32),
    ("taps", (8, CONV), f32),
    ("hp", (8, 128), f32),
    ("shard_x", (32, W3C), bf16),
]


def forward(ins):
    hbm = ("tok", "cos", "sin")
    outs = run(
        forward_body,
        [(n, a, n in hbm) for n, a in ins.items()],
        [(n, s, d, True) for n, s, d in FORWARD_OUTS],
        FORWARD_OUTS
        + [
            ("tok", (TOK, WID), bf16),
            ("cos", (2 * TOK, 128), f32),
            ("sin", (2 * TOK, 128), f32),
            ("prior", (HALO, WID), bf16),
            ("norm_p", (HALO, WID), bf16),
            ("normed", (TOK, WID), bf16),
            ("unit", (TOK, WID), f32),
            ("unit_t", (WID, TOK), f32),
            ("kv", (TOK, 128), bf16),
            ("kv_prior", (TOK, 128), bf16),
            ("wide", (2 * TOK, 128), f32),
            ("last", (STATE, INNER), bf16),
            ("first", (STATE, INNER), bf16),
            ("skip", (8, INNER), f32),
            ("sc_state", (STATE, INNER), f32),
            ("shard1", (32, W1C), bf16),
            ("shard2", (32, W2C + W3C), bf16),
            ("sems1", dma_sems(4, 2, 4)),
            ("cross1", dma_sems(2, 8)),
            ("sems2", dma_sems(4, 2, 4)),
            ("cross2", dma_sems(2, 8)),
            ("sems3", dma_sems(4, 2, 4)),
            ("cross3", dma_sems(2, 8)),
            ("ctx_sems", dma_sems(2, 4)),
        ],
        1,
    )
    return dict(zip([n for n, _, _ in FORWARD_OUTS], outs))


SENT = 128
CHUNK = 256
CHUNKS = TOK // CHUNK


def middle_body(e):
    py, pz, core = place()
    tp_peer = {"tp": 1 - lax.axis_index("tp")}
    load_x = pltpu.make_async_copy(e.h_shard_x, e.w3x.at[py, pz, core], e.own_sems.at[0])
    load_x.start()
    e.fetch("w2", "mixed")
    mine = Gather(e.w3, e.mine_sems, e.mine_cross)
    parts = [part(ref, n) for n in (1, 3, 0) for part in (mine.rows, mine.planes) for ref in (e.h_w3, e.w3)]
    loads = [
        pltpu.make_async_copy(a, b, e.own_sems.at[1 + n])
        for n, (a, b) in enumerate(zip(parts[0::2], parts[1::2]))
    ]
    for load in loads:
        load.start()
    greet(torus_peers() + [tp_peer])
    other = Gather(e.w3x, e.gather_sems, e.cross_sems)
    load_x.wait()
    other.start()
    for load in loads[0:4]:
        load.wait()
    mine.far()
    part, part_back = e.part, e.part_back
    normed2, dact, mid, dn, down = e.normed2, e.dact, e.mid, e.dn, e.down

    w2, mixed = e.need("w2"), e.need("mixed")
    e.fetch("cot", "gains", "tok")
    copies = []
    for c in range(TOK // SENT):
        rows = slice(c * SENT, (c + 1) * SENT)
        part[rows, :] = nt(mixed[rows, :], w2[...].reshape(WID, W2C)).astype(bf16)
        copies.append(send(part.at[rows], part_back.at[rows], e.sems, c, tp_peer))
    tok, cot, gains = e.need("tok"), e.need("cot"), e.need("gains")
    e.cot_t[...] = cot[...].astype(f32).T.astype(bf16)
    gain = gains[HEADS + 1 - 8 : HEADS + 2 - 8, :]
    other.turn()
    mine.finish()
    for load in loads[4:]:
        load.wait()
    mine.arrived()

    def cols(w, at, size):
        return w[:, :, :, :, at].reshape(WID, size)

    def rows_at(c):
        return slice(c * CHUNK, (c + 1) * CHUNK)

    def hidden_back(w):
        @pl.loop(0, FFH // 256)
        def _(j):
            at = pl.ds(pl.multiple_of(2 * FFH + j * 256, 256), 256)
            to = pl.ds(pl.multiple_of(j * 256, 256), 256)
            dact[:, to] = nn(cot[...], cols(w, at, 256))

    def swiglu(w, act, dgu, rows):
        @pl.loop(0, FFH // 256)
        def _(j):
            at = pl.ds(pl.multiple_of(j * 256, 256), 256)
            at_up = pl.ds(pl.multiple_of(FFH + j * 256, 256), 256)
            gate = nn(normed2[rows, :], cols(w, at, 256))
            up = nn(normed2[rows, :], cols(w, at_up, 256))
            sig = sigmoid(gate)
            silu = gate * sig
            da = dact[rows, at]
            act[rows, at] = (silu * up).astype(bf16)
            dgu[rows, at] = (da * up * (sig + silu * (1.0 - sig))).astype(bf16)
            dgu[rows, at_up] = (da * silu).astype(bf16)

    def out_products(w, act, dgu, rows, first):
        @pl.loop(0, 4)
        def _(j):
            to = pl.ds(pl.multiple_of(j * 256, 256), 256)
            a = nt(dgu[rows, :], w[j, :, :, :, 0 : 2 * FFH].reshape(256, 2 * FFH))
            b = nt(act[rows, :], w[j, :, :, :, 2 * FFH :].reshape(256, FFH))
            dn[rows, to] = a if first else dn[rows, to] + a
            down[rows, to] = b if first else down[rows, to] + b

    hidden_back(e.w3)
    for c in range(CHUNKS):
        rows = rows_at(c)
        for part_copy in copies[c * CHUNK // SENT : (c + 1) * CHUNK // SENT]:
            part_copy.wait_recv()
        m = tok[rows, :].astype(f32) + (part[rows, :].astype(f32) + part_back[rows, :].astype(f32))
        mid[rows, :] = m
        normed2[rows, :] = (unit_rows(m)[0] * gain).astype(bf16)
        swiglu(e.w3, e.act, e.dgu, rows)
        out_products(e.w3, e.act, e.dgu, rows, True)
        if c == 0:
            other.forward()
    other.finish()
    e.normed2_t[...] = normed2[...].astype(f32).T.astype(bf16)

    @pl.loop(0, FFH // 256)
    def _(j):
        at = pl.ds(pl.multiple_of(j * 256, 256), 256)
        to = pl.ds(pl.multiple_of(2 * FFH + j * 256, 256), 256)
        e.w3_grad[:, :, :, :, to] = nn(e.cot_t[...], e.act[:, at]).astype(bf16).reshape(4, 4, 2, 32, 256)

    @pl.loop(0, 2 * FFH // 256)
    def _(j):
        at = pl.ds(pl.multiple_of(j * 256, 256), 256)
        block = nn(e.normed2_t[...], e.dgu[:, at]).astype(bf16)
        e.w3_grad[:, :, :, :, at] = block.reshape(4, 4, 2, 32, 256)

    e.store("w3_grad")
    other.arrived()
    hidden_back(e.w3x)
    taken = jnp.zeros((1, WID), f32)
    swiglu(e.w3x, e.act_x, e.dgu_x, slice(0, TOK))
    out_products(e.w3x, e.act_x, e.dgu_x, slice(0, TOK), False)
    for c in range(CHUNKS):
        rows = rows_at(c)
        e.block_out[rows, :] = (mid[rows, :] + down[rows, :]).astype(bf16)
        dh = dn[rows, :]
        unit, r = unit_rows(mid[rows, :])
        taken = taken + jnp.sum(dh * unit, axis=0, keepdims=True)
        scaled = dh * gain
        g = cot[rows, :].astype(f32) + r * (
            scaled - unit * jnp.mean(unit * scaled, axis=1, keepdims=True)
        )
        e.grad_mid[rows, :] = g
        e.dmix[rows, :] = g.astype(bf16)
    e.dgain2[...] = jnp.broadcast_to(taken, (8, WID))
    e.store("dmix", "grad_mid", "dgain2", "block_out")
    mine.close()
    other.close()
    for copy in copies:
        copy.wait_send()
    e.settle()


MIDDLE_OUTS = [
    ("block_out", (TOK, WID), bf16),
    ("grad_mid", (TOK, WID), f32),
    ("dmix", (TOK, WID), bf16),
    ("w3_grad", (4, 4, 2, 32, W3C), bf16),
    ("dgain2", (8, WID), f32),
]


def middle(ins):
    outs = run(
        middle_body,
        [(n, a, True) for n, a in ins.items()],
        [(n, s, d, True) for n, s, d in MIDDLE_OUTS],
        MIDDLE_OUTS
        + [
            ("w2", (4, 4, 2, 32, W2C), bf16),
            ("w3", (4, 4, 2, 32, W3C), bf16),
            ("w3x", (4, 4, 2, 32, W3C), bf16),
            ("mixed", (TOK, WID), bf16),
            ("gains", (8, WID), f32),
            ("tok", (TOK, WID), bf16),
            ("cot", (TOK, WID), bf16),
            ("part", (TOK, WID), bf16),
            ("part_back", (TOK, WID), bf16),
            ("mid", (TOK, WID), f32),
            ("dn", (TOK, WID), f32),
            ("down", (TOK, WID), f32),
            ("normed2", (TOK, WID), bf16),
            ("normed2_t", (WID, TOK), bf16),
            ("cot_t", (WID, TOK), bf16),
            ("act", (TOK, FFH), bf16),
            ("dgu", (TOK, 2 * FFH), bf16),
            ("act_x", (TOK, FFH), bf16),
            ("dgu_x", (TOK, 2 * FFH), bf16),
            ("dact", (TOK, FFH), f32),
            ("sems", dma_sems(2, TOK // SENT)),
            ("own_sems", dma_sems(7)),
            ("mine_sems", dma_sems(4, 2, 4)),
            ("mine_cross", dma_sems(2, 8)),
            ("gather_sems", dma_sems(4, 2, 4)),
            ("cross_sems", dma_sems(2, 8)),
        ],
        2,
    )
    return dict(zip([n for n, _, _ in MIDDLE_OUTS], outs))


EARLY = W2C + INNER + QW
LATE = CONV + 256


def conv_back(ext, taps, seg_ext, cin, grads):
    run = jnp.zeros((TOK, CONV), f32)
    now = seg_ext[HALO : HALO + TOK, 0:1]
    sub = lax.broadcasted_iota(jnp.int32, (8, CONV), 0)
    taken = jnp.zeros((8, CONV), f32)
    for k in range(4):
        ahead = 3 - k
        same = jnp.where(seg_ext[HALO + ahead : HALO + ahead + TOK, 0:1] == now, 1.0, 0.0)
        run = run + ext[ahead : ahead + TOK, :] * taps[k : k + 1, :] * same
        at = HALO - 3 + k
        part = ext[0:TOK, :] * cin[at : at + TOK, :] * tap_mask(seg_ext, k)
        taken = taken + jnp.where(sub == k, jnp.sum(part, axis=0, keepdims=True), 0.0)
    grads[:, C_U:] = run.astype(bf16)
    return taken


def backward_body(e):
    py, pz, core = place()
    ctx, tp = lax.axis_index("ctx"), lax.axis_index("tp")
    ctx_peer, tp_peer = {"ctx": 1 - ctx}, {"tp": 1 - tp}
    own_rows = pl.ds(pl.multiple_of(ctx * TOK, TOK), TOK)
    half3 = W3C // 2
    e.fetch("w2")
    e.fetch("dmix")
    greet(torus_peers() + [tp_peer])
    sum3 = Reduce(e, "s3_", e.fin_three)
    early = Reduce(e, "se_", e.fin_early)
    tail = Reduce(e, "sl_", e.fin_late)
    small = SmallSum(e)
    core3 = send(e.h_w3_grad.at[:, :, 1 - core], sum3.crecv, sum3.core_sems, 0, sum3.sibling)
    grads = e.grads

    w2, dmix = e.need("w2"), e.need("dmix")
    e.fetch("z", "y", "pre", "cum", "seg_ext")
    e.fetch("q", "k2", "v2", "k2p", "v2p", "seg_row", "lse")
    e.fetch_from("cos", e.h_cos.at[own_rows])
    e.fetch_from("sin", e.h_sin.at[own_rows])
    e.fetch_from("own3", e.h_w3_grad.at[:, :, core, :, 0:half3])

    @pl.loop(0, INNER // 256)
    def _(j):
        at = pl.ds(pl.multiple_of(QW + j * 256, 256), 256)
        to = pl.ds(pl.multiple_of(j * 256, 256), 256)
        e.dgated[:, to] = nn(dmix[...], w2[:, :, :, :, at].reshape(WID, 256))

    e.need("z", "y", "pre", "cum", "seg_ext")
    mixer_back_in_body(
        e.dgated, e.z, e.y, e.pre, e.cum, e.seg_ext, e.dgated, grads.at[:, C_Z : C_Z + INNER], e.dfirst
    )
    state_copy = send(e.dfirst, e.dlast, e.ctx_sems, 0, ctx_peer)
    e.fetch("hp", "dt", "states", "step", "taps", "cin", "mixed", "normed_t", "w1", "tok", "gains", "dgain2")
    e.need("q", "k2", "v2", "k2p", "v2p", "seg_row", "lse", "cos", "sin")

    def add_half(first):
        for j in range(half3 // 512):
            at = slice(j * 512, (j + 1) * 512)
            cols = slice(first + j * 512, first + (j + 1) * 512)
            total = e.own3[:, :, :, at].astype(f32) + sum3.crecv[:, :, :, cols].astype(f32)
            sum3.crecv[:, :, :, cols] = total.astype(bf16)

    e.need("own3")
    core3.wait_recv()
    add_half(0)
    e.fetch_from("own3", e.h_w3_grad.at[:, :, core, :, half3:])
    sum3.a.start()
    e.datt[...] = nn(dmix[...], w2[:, :, :, :, 0:QW].reshape(WID, QW)).astype(bf16)
    e.need("own3")
    add_half(half3)
    sum3.b.start()
    attend_back_body(
        e.q, e.k2, e.v2, e.k2p, e.v2p, e.seg_ext.at[HALO : HALO + TOK], e.seg_row, e.lse, e.datt,
        e.cos, e.sin, grads.at[:, C_Q : C_Q + QW], e.dkv, e.dkv_p, e.dk_s, e.dv_s, e.dkp_s, e.dvp_s,
        between={1: sum3.forward},
    )
    kv_copy = send(e.dkv_p, e.dkv_back, e.ctx_sems, 1, ctx_peer)
    state_copy.wait_recv()
    e.sc_state[...] = jnp.where(ctx > 0, 0.0, e.dlast[...].astype(f32))
    e.need("hp", "dt", "states", "step")
    e.skip[...] = spread(jnp.broadcast_to(e.hp[2:3, :], (8, 128)))
    heads = mixer_back_body(
        e.dgated, e.pre, e.dt, e.cum, e.seg_ext, e.seg_row, e.states, None, e.skip.at[0:1],
        e.hp.at[1:2], e.step, e.hp.at[0:1], e.ext, grads.at[:, C_DT : C_DT + 128], None, e.sc_state,
    )
    rim_copy = send(e.ext.at[0:8], e.rim, e.ctx_sems, 2, ctx_peer)
    e.dmix_t[...] = dmix[...].astype(f32).T.astype(bf16)
    normed_t = e.need("normed_t")
    e.need("mixed")
    for j in range(2):
        early.piece(j, nn(e.dmix_t[...], e.mixed[:, j * 256 : (j + 1) * 256]))
    kv_copy.wait_recv()
    low = low_half((TOK, 128))
    both = e.dkv[...] + jnp.where(ctx > 0, 0.0, e.dkv_back[...].astype(f32))
    grads[:, C_KV : C_KV + 128] = jnp.where(low, turned(both, e.cos[...], -e.sin[...]), both).astype(bf16)
    e.need("taps", "cin")
    rim_copy.wait_recv()
    e.ext[TOK : TOK + 8, :] = jnp.where(ctx > 0, 0.0, e.rim[...])
    dtaps = conv_back(e.ext, e.taps, e.seg_ext, e.cin, grads)
    rim_copy.wait_send()
    late = e.ext.at[0:TOK]
    late_load = pltpu.make_async_copy(e.h_grad_mid, late, e.own_sems.at[0])
    late_load.start()

    def rows_at(c):
        return slice(c * TOK // 4, (c + 1) * TOK // 4)

    w1 = e.need("w1")
    dn_copies = []

    def dn_part(c):
        rows = rows_at(c)

        @pl.loop(0, 4)
        def _(j):
            to = pl.ds(pl.multiple_of(j * 256, 256), 256)
            e.dn[rows, to] = nt(grads[rows, :], w1[j].reshape(256, W1C)).astype(bf16)

        dn_copies.append(send(e.dn.at[rows], e.dn_back.at[rows], e.dn_sems, c, tp_peer))

    dn_part(0)
    for j in (2, 3):
        early.piece(j, nn(e.dmix_t[...], e.mixed[:, j * 256 : (j + 1) * 256]))
    for j in range(3):
        at = C_Z + j * 256
        early.piece(4 + j, nn(normed_t[...], grads[:, at : at + 256]))
    early.piece(7, nn(normed_t[...], grads[:, 0:QW]))
    for j in range(8):
        early.add(j)
    early.start()
    sum3.turn()
    dn_part(1)
    for j in range(4):
        at = C_U + j * 256
        tail.piece(j, nn(normed_t[...], grads[:, at : at + 256]))
    tail.piece(4, nn(normed_t[...], grads[:, 256:512]))
    dn_part(2)
    for j in range(5):
        tail.add(j)
    tail.start()
    early.forward()
    dn_part(3)
    sum3.finish()
    three_copy = send(e.fin_three, e.fin_three_back, e.fin_sems, 3, ctx_peer)
    tok = e.need("tok")
    gains = e.need("gains")
    e.need("dgain2")
    gain = gains[HEADS - 8 : HEADS - 7, :]
    dgain1 = jnp.zeros((1, WID), f32)
    for c in range(4):
        rows = rows_at(c)
        unit = unit_rows(tok[rows, :].astype(f32))[0]
        dgain1 = dgain1 + jnp.sum(e.dn[rows, :].astype(f32) * unit, axis=0, keepdims=True)
    sub = lax.broadcasted_iota(jnp.int32, (8, WID), 0)
    gain_rows = jnp.where(sub == 4, dgain1, jnp.where(sub == 5, e.dgain2[0:1, :] * 0.5, dtaps))
    small.start(jnp.concatenate([gain_rows, heads], axis=1))
    tail.forward()
    early.turn()
    small.along_z()
    tail.turn()
    early.finish()
    fin_copy = send(e.fin_early, e.fin_early_back, e.fin_sems, 0, ctx_peer)
    small.along_y()
    tail.finish()
    late_copy = send(e.fin_late, e.fin_late_back, e.fin_sems, 1, ctx_peer)
    small.along_ctx()
    late_load.wait()
    for c in range(4):
        rows = rows_at(c)
        dn_copies[c].wait_recv()
        dh = (e.dn[rows, :].astype(f32) + e.dn_back[rows, :].astype(f32)) * gain
        unit, r = unit_rows(tok[rows, :].astype(f32))
        late[rows, :] = late[rows, :] + r * (dh - unit * jnp.mean(unit * dh, axis=1, keepdims=True))
    out_copy = pltpu.make_async_copy(late, e.h_tok_grad, e.own_sems.at[1])
    out_copy.start()
    small.along_tp()
    late_copy.wait_recv()
    total = e.fin_late[...].astype(f32) + e.fin_late_back[...].astype(f32)
    e.share[...] = total[:, INNER:CONV].astype(bf16)
    share_copy = send(e.share, e.share_back, e.fin_sems, 2, tp_peer)
    e.parts_late[...] = total
    three_copy.wait_recv()
    e.parts_early[:, 0:W3C] = e.fin_three[...].astype(f32) + e.fin_three_back[...].astype(f32)
    fin_copy.wait_recv()
    e.parts_early[:, W3C:] = e.fin_early[...].astype(f32) + e.fin_early_back[...].astype(f32)
    e.store("parts_early")
    e.sums[...] = small.result()
    share_copy.wait_recv()
    e.parts_late[:, INNER:CONV] = e.share[...].astype(f32) + e.share_back[...].astype(f32)
    e.store("parts_late", "sums")

    out_copy.wait()
    core3.wait_send()
    for ring in (sum3, early, tail):
        ring.close()
    small.close()
    for copy in [state_copy, kv_copy, three_copy, fin_copy, late_copy, share_copy] + dn_copies:
        copy.wait_send()
    e.settle()


BACKWARD_OUTS = [
    ("parts_early", (32, W3C + EARLY), f32),
    ("parts_late", (32, LATE), f32),
    ("sums", (8, SMALL), f32),
]


def backward(ins):
    same = [
        "dmix", "z", "y", "pre", "cum", "seg_ext", "mixed", "q", "k2", "v2", "k2p", "v2p",
        "seg_row", "lse", "hp", "dt", "states", "step", "normed_t", "taps", "cin", "tok", "gains", "dgain2",
    ]
    outs = run(
        backward_body,
        [(n, a, True) for n, a in ins.items()],
        [(n, s, d, True) for n, s, d in BACKWARD_OUTS] + [("tok_grad", (TOK, WID), f32, True)],
        BACKWARD_OUTS
        + [(n, ins[n].shape, ins[n].dtype) for n in same]
        + [
            ("w2", (4, 4, 2, 32, W2C), bf16),
            ("own3", (4, 4, 32, W3C // 2), bf16),
            ("cos", (TOK, 128), f32),
            ("sin", (TOK, 128), f32),
            ("w1", (4, 4, 2, 32, W1C), bf16),
            ("dgated", (TOK, INNER), f32),
            ("datt", (TOK, QW), bf16),
            ("dmix_t", (WID, TOK), bf16),
            ("grads", (TOK, W1C), bf16),
            ("dkv", (TOK, 128), f32),
            ("dkv_p", (TOK, 128), bf16),
            ("dkv_back", (TOK, 128), bf16),
            ("dk_s", (TOK, 128), f32),
            ("dv_s", (TOK, 128), f32),
            ("dkp_s", (TOK, 128), f32),
            ("dvp_s", (TOK, 128), f32),
            ("dfirst", (STATE, INNER), bf16),
            ("dlast", (STATE, INNER), bf16),
            ("skip", (8, INNER), f32),
            ("sc_state", (STATE, INNER), f32),
            ("ext", (TOK + 8, CONV), f32),
            ("rim", (8, CONV), f32),
            ("dn", (TOK, WID), bf16),
            ("dn_back", (TOK, WID), bf16),
            ("fin_three", (32, W3C), bf16),
            ("fin_three_back", (32, W3C), bf16),
            ("fin_early", (32, EARLY), bf16),
            ("fin_early_back", (32, EARLY), bf16),
            ("fin_late", (32, LATE), bf16),
            ("fin_late_back", (32, LATE), bf16),
            ("share", (32, CONV - INNER), bf16),
            ("share_back", (32, CONV - INNER), bf16),
            ("sm_core", (2, 8, SMALL), f32),
            ("sm_z", (4, 8, SMALL), f32),
            ("sm_y", (4, 8, SMALL), f32),
            ("sm_ctx", (2, 8, SMALL), f32),
            ("sm_tp", (2, 8, SMALL), f32),
            ("small_sems", dma_sems(2, 9)),
            ("ctx_sems", dma_sems(2, 3)),
            ("dn_sems", dma_sems(2, 4)),
            ("fin_sems", dma_sems(2, 4)),
            ("own_sems", dma_sems(3)),
        ]
        + reduce_space("s3_", W3C, own_buffer=False)
        + reduce_space("se_", EARLY)
        + reduce_space("sl_", LATE),
        0,
    )
    return dict(zip([n for n, _, _ in BACKWARD_OUTS] + ["tok_grad"], outs))


def outputs_body(
    early, late, sums, block_in, tok_in,
    gain1, gain2, query, keyval, attn, inner, state, step, conv_i, conv_s, decay, bias, skip,
    inner_o, gate_up, down, block_out, tok_out, tok_held, block_held, sems,
):
    passes = ((tok_in, tok_held, tok_out), (block_in, block_held, block_out))
    loads = [pltpu.make_async_copy(a, b, sems.at[0, n]) for n, (a, b, _) in enumerate(passes)]
    copies = [pltpu.make_async_copy(b, c, sems.at[1, n]) for n, (_, b, c) in enumerate(passes)]
    for load in loads:
        load.start()
    for load, copy in zip(loads, copies):
        load.wait()
        copy.start()
    gains = pltpu.roll(sums[:, 0:WID], lax.rem(WID - 32 * lax.axis_index("fsdp"), WID), 1)
    gain1[...] = gains[4:5, 0:32]
    gain2[...] = gains[5:6, 0:32]
    step[...] = late[:, LATE - 128 :].T[0:HEADS, :]
    at2 = W3C
    query[...] = early[:, at2 + W2C + INNER :]
    for i in range(2):
        at = CONV + 64 * i
        keyval[:, i, :] = late[:, at : at + 64]
        gate_up[:, i, :] = early[:, FFH * i : FFH * (i + 1)]
    inner[:, 0, :] = early[:, at2 + W2C : at2 + W2C + INNER]
    inner[:, 1, :] = late[:, 0:INNER]
    state[...] = late[:, INNER:CONV]
    attn[...] = early[:, at2 : at2 + QW]
    inner_o[...] = early[:, at2 + QW : at2 + W2C]
    down[...] = early[:, 2 * FFH : 3 * FFH]
    conv_i[...] = sums[0:4, 0:INNER]
    conv_s[...] = sums[0:4, INNER:CONV]
    for n, ref in enumerate((decay, bias, skip)):
        ref[...] = sums[n : n + 1, CONV : CONV + HEADS]
    for copy in copies:
        copy.wait()


OUTPUTS = [
    ((1, 32), f32),
    ((1, 32), f32),
    ((32, QW), f32),
    ((32, 2, 64), f32),
    ((32, QW), f32),
    ((32, 2, INNER), f32),
    ((32, 256), f32),
    ((HEADS, 32), f32),
    ((4, INNER), f32),
    ((4, CONV - INNER), f32),
    ((1, HEADS), f32),
    ((1, HEADS), f32),
    ((1, HEADS), f32),
    ((32, INNER), f32),
    ((32, 2, FFH), f32),
    ((32, FFH), f32),
    ((TOK, WID), bf16),
    ((TOK, WID), f32),
]


def outputs(*args):
    any_spec = pl.BlockSpec(memory_space=pl.ANY)
    return pl.pallas_call(
        outputs_body,
        out_shape=[jax.ShapeDtypeStruct(s, d) for s, d in OUTPUTS],
        in_specs=vmem(3) + [any_spec] * 2,
        out_specs=vmem(16) + [any_spec] * 2,
        scratch_shapes=[pltpu.VMEM((TOK, WID), f32), pltpu.VMEM((TOK, WID), bf16), dma_sems(2, 2)],
        compiler_params=pltpu.CompilerParams(vmem_limit_bytes=61 * 1024 * 1024),
    )(*args)


def rope_tables():
    indices = np.arange(HEAD_WIDTH // 2, dtype=np.float32)
    frequency = np.exp(indices * np.float32(-2.0 * math.log(ROPE_BASE) / HEAD_WIDTH))
    angles = np.arange(2 * TOK, dtype=np.float32)[:, None] * frequency[None, :].astype(np.float32)
    angles = angles.astype(np.float64)
    return tuple(np.tile(t(angles), (1, 4)).astype(np.float32) for t in (np.cos, np.sin))


def shards(
    tokens, segments, cotangent, gain_mixer, gain_ffn, query_proj, key_value_weight, attn_out,
    inner_proj, state_proj, step_proj, conv_inner, conv_state, decay_log, step_bias, skip_gain,
    inner_out, gate_up, down_proj,
):
    rows = query_proj.shape[0]
    tok = tokens.reshape(TOK, WID)
    cot = cotangent.reshape(TOK, WID)
    cos, sin = (jnp.asarray(t) for t in rope_tables())
    kept = forward(
        dict(
            query=query_proj, keyval=key_value_weight, attn=attn_out.T, inner=inner_proj, state=state_proj,
            step_w=step_proj.T, gain1=gain_mixer.reshape(1, rows), gain2=gain_ffn.reshape(1, rows),
            inner_o=inner_out.T, gate_up=gate_up, down_w=down_proj.T, tok=tok, cos=cos, sin=sin, seg=segments,
            taps_i=conv_inner, taps_s=conv_state, step_bias=step_bias.reshape(1, HEADS),
            decay_log=decay_log.reshape(1, HEADS), skip_gain=skip_gain.reshape(1, HEADS),
        )
    )
    kept |= dict(tok=tok, cos=cos, sin=sin)
    between = middle({n: kept[n] for n in ("w2", "w3", "shard_x", "mixed", "gains", "tok")} | dict(cot=cot))
    block_out = between.pop("block_out")
    del kept["shard_x"], kept["w3"]
    done = backward(kept | between)
    *out, block_out, tok_grad = outputs(
        done["parts_early"], done["parts_late"], done["sums"], block_out, done["tok_grad"]
    )
    forms = [(rows,)] * 2 + [None] * 2 + ["T"] + [None] * 2 + ["T"] + [None] * 2
    forms += [(HEADS,)] * 3 + ["T", None, "T"]
    out = [a if f is None else a.T if f == "T" else a.reshape(f) for a, f in zip(out, forms)]
    return (block_out[None], tok_grad[None], *out)


def solution(mesh):
    return jax.shard_map(
        shards,
        mesh=mesh,
        in_specs=(
            P("fsdp", "ctx", None), P("fsdp", None), P("fsdp", "ctx", None), P("fsdp"), P("fsdp"),
            P("fsdp", "tp"), P("fsdp", None, "tp"), P("tp", "fsdp"), P("fsdp", None, "tp"),
            P("fsdp", None), P("fsdp", "tp"), P(None, "tp"), P(), P("tp"), P("tp"), P("tp"),
            P("tp", "fsdp"), P("fsdp", None, "tp"), P("tp", "fsdp"),
        ),
        out_specs=(
            P("fsdp", "ctx", None), P("fsdp", "ctx", None), P("fsdp"), P("fsdp"), P("fsdp", "tp"),
            P("fsdp", None, "tp"), P("tp", "fsdp"), P("fsdp", None, "tp"), P("fsdp", None),
            P("fsdp", "tp"), P(None, "tp"), P(), P("tp"), P("tp"), P("tp"), P("tp", "fsdp"),
            P("fsdp", None, "tp"), P("tp", "fsdp"),
        ),
        check_vma=False,
    )
```

```python
import functools
import math

import jax
import jax.numpy as jnp
import numpy as np
from jax import lax
from jax.experimental import pallas as pl
from jax.experimental.pallas import tpu as pltpu

from jax.sharding import PartitionSpec as P


class Names:
    def __getattr__(self, name):
        return name


N = Names()
f32 = jnp.float32
bf16 = jnp.bfloat16
EPS = 1e-05
NEG = -1e30
ROPE_BASE = 100000000000.0
HEAD_WIDTH = 64
HIGH = lax.Precision.HIGHEST

TOK = 512
WID = 1024
SPAN = 128
SPANS = TOK // SPAN
QW = 256
HEADS = 12
INNER = 768
STATE = 128
CONV = INNER + 2 * STATE
HALO = 16
W1C = 2304
W2C = 1024
W3C = 3072
FFH = 1024
C_Q, C_KV, C_DT, C_Z, C_U = 0, 256, 384, 512, 1280


def vmem(n):
    return [pl.BlockSpec(memory_space=pltpu.VMEM)] * n


def kernel_call(body, outs, scratch=(), mem=24, cost=None):
    def call(*args):
        return pl.pallas_call(
            body,
            out_shape=[jax.ShapeDtypeStruct(s, d) for s, d in outs],
            in_specs=vmem(len(args)),
            out_specs=vmem(len(outs)),
            scratch_shapes=list(scratch),
            compiler_params=pltpu.CompilerParams(vmem_limit_bytes=mem * 1024 * 1024),
            cost_estimate=cost,
        )(*args)

    return call


def nt(a, b):
    return lax.dot_general(a, b, (((1,), (1,)), ((), ())), preferred_element_type=f32)


def tn(a, b):
    return lax.dot_general(a, b, (((0,), (0,)), ((), ())), preferred_element_type=f32)


def nn(a, b):
    return jnp.dot(a, b, preferred_element_type=f32)


def split_halves(v):
    hi = v.astype(bf16)
    return hi, (v - hi.astype(f32)).astype(bf16)


def head_matrix(rows, columns):
    row = lax.broadcasted_iota(jnp.int32, (rows, columns), 0)
    col = lax.broadcasted_iota(jnp.int32, (rows, columns), 1)
    return row, col


def spread(v):
    row, col = head_matrix(128, INNER)
    e = jnp.where(row == col // 64, 1.0, 0.0).astype(bf16)
    hi, lo = split_halves(v)
    return nn(hi, e) + nn(lo, e)


def gathered_heads(v):
    row, col = head_matrix(INNER, 128)
    e = jnp.where(row // 64 == col, 1.0, 0.0).astype(bf16)
    hi, lo = split_halves(v)
    return nn(hi, e) + nn(lo, e)


def low_half(shape):
    return lax.broadcasted_iota(jnp.int32, shape, len(shape) - 1) % 128 < 64


def sigmoid(v):
    return 1.0 / (1.0 + jnp.exp(-v))


def turned(v, cos, sin):
    lane = lax.broadcasted_iota(jnp.int32, v.shape, 1) % 64
    w = v.shape[1]
    swapped = jnp.where(lane < 32, pltpu.roll(v, w - 32, 1), pltpu.roll(v, 32, 1))
    return v * cos + jnp.where(lane < 32, -swapped, swapped) * sin


def unit_rows(v):
    r = lax.rsqrt(jnp.mean(v * v, axis=1, keepdims=True) + EPS)
    return v * r, r


def own_bias(rows, start, seg_col, seg_row):
    end = start + rows
    query = lax.broadcasted_iota(jnp.int32, (rows, end), 0) + start
    key = lax.broadcasted_iota(jnp.int32, (rows, end), 1)
    keep = (key <= query) & (seg_col[start:end, 0:1] == seg_row[0:1, TOK : TOK + end])
    return keep


QB = 256


def attend_body(q, k2, v2, k2p, v2p, seg_col, seg_row, out, lse):
    low = low_half((QB, 128))
    for b in range(TOK // QB):
        start, end = b * QB, (b + 1) * QB
        keep = own_bias(QB, start, seg_col, seg_row)
        keep_p = seg_col[start:end, 0:1] == seg_row[0:1, 0:TOK]
        logs = []
        for pair in range(2):
            cols = slice(128 * pair, 128 * pair + 128)
            qp = q[start:end, cols]
            halves = []
            for side in range(2):
                mine = low if side == 0 else ~low
                qh = jnp.where(mine, qp.astype(f32) * 0.125, 0.0).astype(bf16)
                s1 = jnp.where(keep, nt(qh, k2[0:end, :]), NEG)
                s0 = jnp.where(keep_p, nt(qh, k2p[...]), NEG)
                m = jnp.maximum(
                    jnp.max(s1, axis=1, keepdims=True), jnp.max(s0, axis=1, keepdims=True)
                )
                p1, p0 = jnp.exp(s1 - m), jnp.exp(s0 - m)
                total = jnp.sum(p1, axis=1, keepdims=True) + jnp.sum(p0, axis=1, keepdims=True)
                o = nn(p1.astype(bf16), v2[0:end, :]) + nn(p0.astype(bf16), v2p[...])
                halves.append(o / total)
                logs.append(m + jnp.log(total))
            out[start:end, cols] = jnp.where(low, halves[0], halves[1]).astype(bf16)
        lane = lax.broadcasted_iota(jnp.int32, (QB, 128), 1)
        kept = jnp.zeros((QB, 128), f32)
        for h in range(4):
            kept = jnp.where(lane == h, logs[h], kept)
        lse[start:end, :] = kept


def attend_back_body(
    q, k2, v2, k2p, v2p, seg_col, seg_row, lse, dout, cos, sin, dq, dkv, dkv_p, dk_s, dv_s, dkp_s, dvp_s,
    between=None,
):
    low = low_half((QB, 128))
    for ref in (dk_s, dv_s, dkp_s, dvp_s):
        ref[...] = jnp.zeros_like(ref)
    for b in range(TOK // QB):
        start, end = b * QB, (b + 1) * QB
        keep = own_bias(QB, start, seg_col, seg_row)
        keep_p = seg_col[start:end, 0:1] == seg_row[0:1, 0:TOK]
        for pair in range(2):
            cols = slice(128 * pair, 128 * pair + 128)
            qp = q[start:end, cols]
            dop = dout[start:end, cols]
            halves = []
            for side in range(2):
                mine = low if side == 0 else ~low
                qh = jnp.where(mine, qp.astype(f32) * 0.125, 0.0).astype(bf16)
                doh = jnp.where(mine, dop.astype(f32), 0.0).astype(bf16)
                h = 2 * pair + side
                log_total = lse[start:end, h : h + 1]
                p1 = jnp.exp(jnp.where(keep, nt(qh, k2[0:end, :]), NEG) - log_total)
                p0 = jnp.exp(jnp.where(keep_p, nt(qh, k2p[...]), NEG) - log_total)
                dp1 = nt(doh, v2[0:end, :])
                dp0 = nt(doh, v2p[...])
                delta = jnp.sum(p1 * dp1, axis=1, keepdims=True) + jnp.sum(
                    p0 * dp0, axis=1, keepdims=True
                )
                ds1 = (p1 * (dp1 - delta)).astype(bf16)
                ds0 = (p0 * (dp0 - delta)).astype(bf16)
                dv_s[0:end, :] += tn(p1.astype(bf16), doh)
                dvp_s[...] += tn(p0.astype(bf16), doh)
                dk_s[0:end, :] += tn(ds1, qh)
                dkp_s[...] += tn(ds0, qh)
                halves.append(nn(ds1, k2[0:end, :]) + nn(ds0, k2p[...]))
            if between and pair == 0 and b in between:
                between[b]()
            dqp = jnp.where(low, halves[0], halves[1]) * 0.125
            dq[start:end, cols] = turned(dqp, cos[start:end, :], -sin[start:end, :]).astype(bf16)
    low = low_half((TOK, 128))

    def joined(dk, dv):
        dk, dv = dk[...], dv[...]
        return jnp.where(low, dk + pltpu.roll(dk, 64, 1), dv + pltpu.roll(dv, 64, 1))

    dkv[...] = joined(dk_s, dv_s)
    dkv_p[...] = joined(dkp_s, dvp_s).astype(bf16)


def tap_mask(seg_ext, k):
    now = seg_ext[HALO : HALO + TOK, 0:1]
    at = HALO - 3 + k
    return jnp.where(seg_ext[at : at + TOK, 0:1] == now, 1.0, 0.0)


def lower_ones():
    row, col = head_matrix(SPAN, SPAN)
    return jnp.where(row >= col, 1.0, 0.0)


def rows_of(c):
    return slice(c * SPAN, (c + 1) * SPAN)


def mixer_in_body(cin, taps, step, bias, rate, seg_ext, pre, dt, cum, last):
    run = jnp.zeros((TOK, CONV), f32)
    for k in range(4):
        at = HALO - 3 + k
        run = run + cin[at : at + TOK, :] * taps[k : k + 1, :] * tap_mask(seg_ext, k)
    pre[...] = run
    lane = lax.broadcasted_iota(jnp.int32, (TOK, 128), 1)
    steps = step[...] + bias[...]
    u = jnp.exp(-jnp.abs(steps))
    log_part = jnp.where(
        u < 0.02, u * (1.0 - u * (0.5 - u * (1.0 / 3.0 - 0.25 * u))), jnp.log(1.0 + u)
    )
    soft = jnp.maximum(steps, 0.0) + log_part
    dt[...] = jnp.where(lane < HEADS, soft, 0.0)
    tri = lower_ones()
    state = jnp.zeros((STATE, INNER), f32)
    for c in range(SPANS):
        rows = rows_of(c)
        own_dt = dt[rows, :]
        total = jnp.dot(tri, own_dt * rate[...], precision=HIGH, preferred_element_type=f32)
        cum[rows, :] = total
        out = pre[rows, 0 : INNER + STATE]
        out = out * sigmoid(out)
        seg = seg_ext[HALO + c * SPAN : HALO + (c + 1) * SPAN, 0:1]
        seg_last = seg[SPAN - 1 : SPAN, :]
        end = total[SPAN - 1 : SPAN, :]
        tail = jnp.where(seg == seg_last, jnp.exp(jnp.minimum(end - total, 0.0)), 0.0) * own_dt
        fresh = tn(out[:, INNER:].astype(bf16), (out[:, 0:INNER] * spread(tail)).astype(bf16))
        if c == 0:
            state = fresh
        else:
            seg_prev = seg_ext[HALO + c * SPAN - 1 : HALO + c * SPAN, 0:1]
            keep = jnp.where(seg_last == seg_prev, jnp.exp(end), 0.0)
            state = state * spread(jnp.broadcast_to(keep, (8, 128)))[0:1, :] + fresh
    last[...] = state.astype(bf16)


def span_parts(c, cum, seg_ext):
    total = cum[rows_of(c), :]
    seg = seg_ext[HALO + c * SPAN : HALO + (c + 1) * SPAN, 0:1]
    seg_last = seg[SPAN - 1 : SPAN, :]
    seg_prev = seg_ext[HALO + c * SPAN - 1 : HALO + c * SPAN, 0:1]
    end = total[SPAN - 1 : SPAN, :]
    entering = jnp.where(seg == seg_prev, jnp.exp(total), 0.0)
    tail = jnp.where(seg == seg_last, jnp.exp(jnp.minimum(end - total, 0.0)), 0.0)
    return total, entering, tail


def span_bias(c, seg_ext, seg_row):
    row, col = head_matrix(SPAN, SPAN)
    seg = seg_ext[HALO + c * SPAN : HALO + (c + 1) * SPAN, 0:1]
    other = seg_row[0:1, TOK + c * SPAN : TOK + (c + 1) * SPAN]
    return jnp.where((row >= col) & (seg == other), 0.0, NEG)


def mixer_out_body(
    pre, dt, cum, seg_ext, seg_row, first, z, skip, y, gated, states, sc_state
):
    if first is not None:
        sc_state[...] = first[...].astype(f32)
    low2 = low_half((SPAN, 128))
    for c in range(SPANS):
        rows = rows_of(c)
        total, entering, tail = span_parts(c, cum, seg_ext)
        out = pre[rows, :]
        out = out * sigmoid(out)
        x = out[:, 0:INNER]
        b = out[:, INNER : INNER + STATE].astype(bf16)
        cm = out[:, INNER + STATE :].astype(bf16)
        own_dt = dt[rows, :]
        xs = x * spread(own_dt)
        state = sc_state[...]
        state_b = state.astype(bf16)
        states[c] = state_b
        wide_in = spread(entering)
        run = nn(cm, state_b) * wide_in + x * skip[...]
        inter = nt(cm, b)
        bias = span_bias(c, seg_ext, seg_row)
        total_t = total.T
        gate = z[rows, :]
        gate = gate * sigmoid(gate)
        for pair in range(HEADS // 2):
            cols = slice(128 * pair, 128 * pair + 128)
            parts = []
            for side in range(2):
                h = 2 * pair + side
                decay = jnp.exp(total[:, h : h + 1] - total_t[h : h + 1, :] + bias)
                parts.append((decay * inter).astype(bf16))
            xp = xs[:, cols]
            stack = jnp.concatenate(
                [jnp.where(low2, xp, 0.0).astype(bf16), jnp.where(low2, 0.0, xp).astype(bf16)], axis=0
            )
            yp = run[:, cols] + nn(jnp.concatenate(parts, axis=1), stack)
            y[rows, cols] = yp
            gated[rows, cols] = (yp * gate[:, cols]).astype(bf16)
        if c < SPANS - 1:
            sc_state[...] = state * wide_in[SPAN - 1 : SPAN, :] + tn(
                b, (xs * spread(tail)).astype(bf16)
            )


def mixer_back_in_body(dgated, z, y, pre, cum, seg_ext, dy, dz, first):
    state = jnp.zeros((STATE, INNER), f32)
    for c in reversed(range(SPANS)):
        rows = rows_of(c)
        total, entering, tail = span_parts(c, cum, seg_ext)
        gate = z[rows, :]
        sig = sigmoid(gate)
        grad = dgated[rows, :]
        own = grad * (gate * sig)
        dy[rows, :] = own
        dz[rows, :] = (grad * y[rows, :] * (sig * (1.0 + gate * (1.0 - sig)))).astype(bf16)
        cm = pre[rows, INNER + STATE :]
        cm = (cm * sigmoid(cm)).astype(bf16)
        wide_in = spread(entering)
        fresh = tn(cm, (own * wide_in).astype(bf16))
        state = fresh if c == SPANS - 1 else state * wide_in[SPAN - 1 : SPAN, :] + fresh
    first[...] = state.astype(bf16)


def mixer_back_body(
    dy, pre, dt, cum, seg_ext, seg_row, states, last, skip, rate, step, bias,
    dpre, dstep, heads, sc_state, between=None,
):
    if last is not None:
        sc_state[...] = last[...].astype(f32)
    low2 = low_half((SPAN, 128))
    lane = lax.broadcasted_iota(jnp.int32, (SPAN, 128), 1)
    tri = lower_ones()
    sum_decay = jnp.zeros((1, 128), f32)
    sum_bias = jnp.zeros((1, 128), f32)
    sum_skip = jnp.zeros((1, 128), f32)
    for c in reversed(range(SPANS)):
        if between and c in between:
            between[c]()
        rows = rows_of(c)
        total, entering, tail = span_parts(c, cum, seg_ext)
        lin = pre[rows, :]
        sig = sigmoid(lin)
        out = lin * sig
        slope = sig * (1.0 + lin * (1.0 - sig))
        x = out[:, 0:INNER]
        b = out[:, INNER : INNER + STATE].astype(bf16)
        cm = out[:, INNER + STATE :].astype(bf16)
        own_dt = dt[rows, :]
        wide_dt = spread(own_dt)
        xs = x * wide_dt
        grad = dy[rows, :]
        wide_in = spread(entering)
        wide_tail = spread(tail)
        dstate = sc_state[...]
        dstate_b = dstate.astype(bf16)
        state_b = states[c]
        gin = grad * wide_in
        gin_b = gin.astype(bf16)
        y_state = nn(cm, state_b)
        xt = xs * wide_tail
        xt_b = xt.astype(bf16)
        from_state = nn(b, dstate_b)
        dcm = nt(gin_b, state_b)
        db = nt(xt_b, dstate_b)
        dcum = gathered_heads(gin * y_state)
        moved = gathered_heads(xt * from_state)
        kept = jnp.sum(dstate * state_b.astype(f32), axis=0, keepdims=True)
        kept = kept * wide_in[SPAN - 1 : SPAN, :]
        kept = gathered_heads(jnp.broadcast_to(kept, (8, INNER)))[0:1, :]
        at_end = jnp.sum(moved, axis=0, keepdims=True) + kept
        sub = lax.broadcasted_iota(jnp.int32, (SPAN, 128), 0)
        dcum = dcum - moved + jnp.where(sub == SPAN - 1, at_end, 0.0)
        sc_state[...] = dstate * wide_in[SPAN - 1 : SPAN, :] + tn(cm, gin_b)
        inter = nt(cm, b)
        bias_m = span_bias(c, seg_ext, seg_row)
        total_t = total.T
        dinter = jnp.zeros((SPAN, SPAN), f32)
        col_sums = jnp.zeros((128, SPAN), f32)
        sub_t = lax.broadcasted_iota(jnp.int32, (128, SPAN), 0)
        ddt = jnp.zeros((SPAN, 128), f32)
        dskip = jnp.zeros((SPAN, 128), f32)
        for pair in range(HEADS // 2):
            cols = slice(128 * pair, 128 * pair + 128)
            gp, xp = grad[:, cols], xs[:, cols]
            gp_b, xp_b = gp.astype(bf16), xp.astype(bf16)
            stack = jnp.concatenate(
                [jnp.where(low2, gp, 0.0).astype(bf16), jnp.where(low2, 0.0, gp).astype(bf16)], axis=0
            )
            dm = nt(stack, xp_b)
            parts = []
            for side in range(2):
                h = 2 * pair + side
                decay = jnp.exp(total[:, h : h + 1] - total_t[h : h + 1, :] + bias_m)
                dmh = dm[side * SPAN : (side + 1) * SPAN, :] * decay
                dinter = dinter + dmh
                weight = decay * inter
                parts.append(weight.astype(bf16))
                q = dmh * inter
                dcum = dcum + jnp.where(lane == h, jnp.sum(q, axis=1, keepdims=True), 0.0)
                col_sums = col_sums + jnp.where(sub_t == h, jnp.sum(q, axis=0, keepdims=True), 0.0)
            both = tn(jnp.concatenate(parts, axis=1), gp_b)
            dxs = jnp.where(low2, both[0:SPAN, :], both[SPAN:, :]) + from_state[:, cols] * wide_tail[:, cols]
            xo = x[:, cols]
            dx = dxs * wide_dt[:, cols] + gp * skip[:, cols]
            dpre[rows, cols] = dx * slope[:, cols]
            pick_row, pick_col = head_matrix(128, 128)
            pick = jnp.where(pick_col == 2 * pair + pick_row // 64, 1.0, 0.0).astype(bf16)
            hi, lo = split_halves(dxs * xo)
            ddt = ddt + nn(hi, pick) + nn(lo, pick)
            hi, lo = split_halves(gp * xo)
            dskip = dskip + nn(hi, pick) + nn(lo, pick)
        dinter_b = dinter.astype(bf16)
        dcm = dcm + nn(dinter_b, b)
        db = db + tn(dinter_b, cm)
        dpre[rows, INNER : INNER + STATE] = db * slope[:, INNER : INNER + STATE]
        dpre[rows, INNER + STATE :] = dcm * slope[:, INNER + STATE :]
        dcum = dcum - col_sums.T
        dlog = lax.dot_general(
            tri, dcum, (((0,), (0,)), ((), ())), precision=HIGH, preferred_element_type=f32
        )
        ddt = ddt + dlog * rate[...]
        dsp = jnp.where(lane < HEADS, ddt * sigmoid(step[rows, :] + bias[...]), 0.0)
        dstep[rows, :] = dsp.astype(bf16)
        sum_decay = sum_decay + jnp.sum(dlog * own_dt, axis=0, keepdims=True)
        sum_bias = sum_bias + jnp.sum(dsp, axis=0, keepdims=True)
        sum_skip = sum_skip + jnp.sum(dskip, axis=0, keepdims=True)
    sub8 = lax.broadcasted_iota(jnp.int32, (8, 128), 0)
    sums = jnp.where(
        sub8 == 0,
        sum_decay * rate[...],
        jnp.where(sub8 == 1, sum_bias, jnp.where(sub8 == 2, sum_skip, 0.0)),
    )
    if heads is not None:
        heads[...] = sums
    return sums


MESH = pl.DeviceIdType.MESH
SMALL = CONV + 128
BC0 = C_U + INNER


def place():
    f = lax.axis_index("fsdp")
    core = lax.rem(f, 2)
    chip = lax.div(f, 2)
    return lax.div(chip, 4), lax.rem(chip, 4), core


def at_yz(y, z, core):
    return {"fsdp": (lax.rem(y, 4) * 4 + lax.rem(z, 4)) * 2 + core}


def torus_peers():
    y, z, core = place()
    return (
        [at_yz(y, z, 1 - core), {"ctx": 1 - lax.axis_index("ctx")}]
        + [at_yz(y, z + n, core) for n in (1, 2, 3)]
        + [at_yz(y + n, z, core) for n in (1, 2, 3)]
    )


def greet(peers):
    barrier = pltpu.get_barrier_semaphore()
    for peer in peers:
        pl.semaphore_signal(barrier, inc=1, device_id=peer, device_id_type=MESH)
    pl.semaphore_wait(barrier, len(peers))


def send(src, dst, sems, k, peer):
    copy = pltpu.make_async_remote_copy(
        src_ref=src,
        dst_ref=dst,
        send_sem=sems.at[0, k],
        recv_sem=sems.at[1, k],
        device_id=peer,
        device_id_type=MESH,
    )
    copy.start()
    return copy


class Refs:
    def __init__(self, names, refs):
        self.__dict__.update(zip(names, refs))
        self.pending, self.stored, self.used = {}, [], 0

    def fetch(self, *names):
        for name in names:
            self.fetch_from(name, getattr(self, "h_" + name))

    def fetch_from(self, name, src):
        copy = pltpu.make_async_copy(src, getattr(self, name), self.io_sems.at[self.used])
        self.used += 1
        copy.start()
        self.pending[name] = copy

    def need(self, *names):
        for name in names:
            if name in self.pending:
                self.pending.pop(name).wait()
        return getattr(self, names[0])

    def store(self, *names):
        for name in names:
            copy = pltpu.make_async_copy(
                getattr(self, name), getattr(self, "h_" + name), self.io_sems.at[self.used]
            )
            self.used += 1
            copy.start()
            self.stored.append(copy)

    def store_part(self, name, part):
        copy = pltpu.make_async_copy(
            part(getattr(self, name)), part(getattr(self, "h_" + name)), self.io_sems.at[self.used]
        )
        self.used += 1
        copy.start()
        self.stored.append(copy)

    def settle(self):
        for copy in self.stored:
            copy.wait()


def run(body, ins, outs, scratch, collective_id):
    any_spec, vmem_spec = pl.BlockSpec(memory_space=pl.ANY), pl.BlockSpec(memory_space=pltpu.VMEM)
    spaces = [(s[0], s[1] if len(s) == 2 else pltpu.VMEM(s[1], s[2])) for s in scratch]
    spaces.append((N.io_sems, pltpu.SemaphoreType.DMA((len(ins) + len(outs) + 4,))))
    names = (
        [("h_" if hbm else "") + n for n, _, hbm in ins]
        + [("h_" if hbm else "") + n for n, _, _, hbm in outs]
        + [n for n, _ in spaces]
    )

    def kernel(*refs):
        body(Refs(names, refs))

    return pl.pallas_call(
        kernel,
        out_shape=[jax.ShapeDtypeStruct(s, d) for _, s, d, _ in outs],
        in_specs=[any_spec if hbm else vmem_spec for _, _, hbm in ins],
        out_specs=[any_spec if hbm else vmem_spec for _, _, _, hbm in outs],
        scratch_shapes=[s for _, s in spaces],
        compiler_params=pltpu.CompilerParams(
            vmem_limit_bytes=63 * 1024 * 1024, collective_id=collective_id, has_side_effects=True
        ),
        cost_estimate=pl.CostEstimate(flops=10**11, bytes_accessed=10**8, transcendentals=0),
    )(*[a for _, a, _ in ins])


def dma_sems(*shape):
    return pltpu.SemaphoreType.DMA(shape)


class DirectGather:
    def __init__(self, block, me, peers, sems):
        self.block, self.me, self.sems, self.peers = block, me, sems, peers

    def start(self):
        own = self.block(self.me)
        self.copies = [send(own, own, self.sems, n, p) for n, p in enumerate(self.peers)]

    def finish(self):
        for copy in self.copies:
            copy.wait_recv()

    def close(self):
        for copy in self.copies:
            copy.wait_send()


class RingGather:
    def __init__(self, block, me, peers, sems):
        self.block, self.me, self.sems = block, me, sems
        self.right, self.left = peers[0], peers[2]

    def ahead(self, n):
        return lax.rem(self.me + n, 4)

    def start(self):
        own = self.block(self.me, None)
        self.near = (
            send(own, own, self.sems, 0, self.right),
            send(own, own, self.sems, 1, self.left),
        )

    def forward(self):
        self.far = []
        for side, (peer, n) in enumerate(((self.right, 3), (self.left, 1))):
            self.near[side].wait_recv()
            part = self.block(self.ahead(n), side)
            self.far.append(send(part, part, self.sems, 2 + side, peer))

    def finish(self):
        for copy in self.far:
            copy.wait_recv()

    def close(self):
        for copy in list(self.near) + self.far:
            copy.wait_send()


class Gather:
    def __init__(self, whole, sems, cross_sems):
        y, z, core = place()
        self.whole, self.y, self.z, self.core = whole, y, z, core
        width = whole.shape[-1]
        half = width // 256 * 128
        ca, cb = slice(0, half), slice(half, width)
        self.ca, self.cb = ca, cb
        peers = torus_peers()
        self.sibling, zs, ys = peers[0], peers[2:5], peers[5:8]
        self.sems, self.across = cross_sems, []

        def two(h):
            return slice(0, 4) if h is None else slice(2 * h, 2 * h + 2)

        self.a1 = DirectGather(lambda d: whole.at[y, d, core, :, ca], z, zs, sems.at[0])
        self.b1 = DirectGather(lambda d: whole.at[d, z, core, :, cb], y, ys, sems.at[1])
        self.a2 = RingGather(lambda d, h: whole.at[d, two(h), core, :, ca], y, ys, sems.at[2])
        self.b2 = RingGather(lambda d, h: whole.at[two(h), d, core, :, cb], z, zs, sems.at[3])

    def cross(self, view):
        self.across.append(send(view, view, self.sems, len(self.across), self.sibling))

    def start(self):
        self.a1.start()
        self.b1.start()

    def turn(self):
        self.a1.finish()
        self.a2.start()
        self.b1.finish()
        self.b2.start()
        self.cross(self.whole.at[self.y, :, self.core, :, self.ca])
        self.cross(self.whole.at[:, self.z, self.core, :, self.cb])

    def forward(self):
        a2, b2 = self.a2, self.b2
        a2.forward()
        b2.forward()
        for n in (1, 3):
            self.cross(a2.block(a2.ahead(n), None))
            self.cross(b2.block(b2.ahead(n), None))

    def near(self):
        for ring in (self.a2, self.b2):
            for copy in ring.near:
                copy.wait_recv()
            ring.far = []
            for n in (1, 3):
                self.cross(ring.block(ring.ahead(n), None))

    def far(self):
        self.a1.copies = self.b1.copies = []
        for ring in (self.a2, self.b2):
            ring.near, ring.far = [], []
            for side, (peer, n) in enumerate(((ring.right, 3), (ring.left, 1))):
                part = ring.block(ring.ahead(n), side)
                ring.far.append(send(part, part, ring.sems, 2 + side, peer))

    def finish(self):
        a2, b2 = self.a2, self.b2
        a2.finish()
        self.cross(a2.block(a2.ahead(2), None))
        b2.finish()
        self.cross(b2.block(b2.ahead(2), None))

    def rows(self, ref, n):
        return ref.at[lax.rem(self.y + n, 4), :, :, :, self.ca]

    def planes(self, ref, n):
        return ref.at[:, lax.rem(self.z + n, 4), :, :, self.cb]

    def arrived(self):
        for copy in self.across:
            copy.wait_recv()

    def close(self):
        for ring in (self.a1, self.b1, self.a2, self.b2):
            ring.close()
        for copy in self.across:
            copy.wait_send()


class RingSum:
    def __init__(self, chunk, me, peers, sems, far, near, joined):
        self.chunk, self.me, self.sems = chunk, me, sems
        self.right, self.left = peers[0], peers[2]
        self.far, self.near, self.joined = far, near, joined

    def ahead(self, n):
        return lax.rem(self.me + n, 4)

    def start(self):
        c, s = self.chunk, self.sems
        self.far_copies = (
            send(c(self.ahead(2), 0), self.far.at[0], s, 0, self.right),
            send(c(self.ahead(2), 1), self.far.at[1], s, 1, self.left),
        )
        self.direct = (
            send(c(self.ahead(1), 1), self.near.at[0, 1], s, 2, self.right),
            send(c(self.ahead(3), 0), self.near.at[1, 0], s, 3, self.left),
        )

    def forward(self):
        c, s = self.chunk, self.sems
        passed = []
        for side, (peer, n) in enumerate(((self.right, 1), (self.left, 3))):
            self.far_copies[side].wait_recv()
            own = c(self.ahead(n), side)[...]
            self.joined[side] = (own.astype(f32) + self.far[side].astype(f32)).astype(bf16)
            passed.append(send(self.joined.at[side], self.near.at[side, side], s, 4 + side, peer))
        self.passed = tuple(passed)

    def finish(self):
        for copy in self.direct + self.passed:
            copy.wait_recv()

    def total(self, half):
        own = self.chunk(self.me, half)[...].astype(f32)
        return own + self.near[0, half].astype(f32) + self.near[1, half].astype(f32)

    def close(self):
        for copy in self.far_copies + self.direct + self.passed:
            copy.wait_send()


class DirectSum:
    def __init__(self, chunk, me, peers, sems, arrived):
        self.chunk, self.me, self.peers, self.sems, self.arrived = chunk, me, peers, sems, arrived

    def start(self):
        self.copies = [
            send(self.chunk(lax.rem(self.me + n + 1, 4)), self.arrived.at[n], self.sems, n, p)
            for n, p in enumerate(self.peers)
        ]

    def total(self):
        for copy in self.copies:
            copy.wait_recv()
        a = self.arrived
        own = self.chunk(self.me)[...].astype(f32)
        return (own + a[0].astype(f32)) + (a[1].astype(f32) + a[2].astype(f32))

    def close(self):
        for copy in self.copies:
            copy.wait_send()


class Reduce:
    def __init__(self, e, name, fin):
        y, z, core = place()
        g = lambda part: getattr(e, name + part)
        self.gbuf, crecv, self.core, self.fin = getattr(e, name + N.gbuf, None), g(N.crecv), core, fin
        self.crecv, self.core_sems = crecv, g(N.core_sems)
        peers = torus_peers()
        self.sibling, zs, ys = peers[0], peers[2:5], peers[5:8]
        width = crecv.shape[-1]
        half = width // 256 * 128
        ca, cb = self.ca, self.cb = slice(0, half), slice(half, width)
        one_a, one_b = self.one_a, self.one_b = g(N.one_a), g(N.one_b)
        s = g(N.ring_sems)
        self.a = RingSum(
            lambda d, h: crecv.at[2 * h : 2 * h + 2, d, :, ca], z, zs, s.at[0],
            g(N.far_a), g(N.near_a), g(N.join_a),
        )
        self.b = RingSum(
            lambda d, h: crecv.at[d, 2 * h : 2 * h + 2, :, cb], y, ys, s.at[1],
            g(N.far_b), g(N.near_b), g(N.join_b),
        )
        self.a2 = DirectSum(lambda d: one_a.at[d], y, ys, s.at[2], g(N.late_a))
        self.b2 = DirectSum(lambda d: one_b.at[d], z, zs, s.at[3], g(N.late_b))
        self.copies = {}

    def piece(self, j, block):
        cols = slice(j * 256, (j + 1) * 256)
        self.gbuf[:, :, :, :, cols] = block.astype(bf16).reshape(4, 4, 2, 32, 256)
        self.copies[j] = send(
            self.gbuf.at[:, :, 1 - self.core, :, cols],
            self.crecv.at[:, :, :, cols],
            self.core_sems,
            j,
            self.sibling,
        )

    def add(self, j):
        cols = slice(j * 256, (j + 1) * 256)
        self.copies[j].wait_recv()
        own = self.gbuf[:, :, self.core, :, cols].astype(f32)
        self.crecv[:, :, :, cols] = (own + self.crecv[:, :, :, cols].astype(f32)).astype(bf16)

    def start(self):
        self.a.start()
        self.b.start()

    def forward(self):
        self.a.forward()
        self.b.forward()

    def turn(self):
        for ring, one, second in ((self.a, self.one_a, self.a2), (self.b, self.one_b, self.b2)):
            ring.finish()
            for h in range(2):
                one[2 * h : 2 * h + 2] = ring.total(h).astype(bf16)
            second.start()

    def finish(self):
        self.fin[:, self.ca] = self.a2.total().astype(bf16)
        self.fin[:, self.cb] = self.b2.total().astype(bf16)

    def close(self):
        for ring in (self.a, self.b, self.a2, self.b2):
            ring.close()
        for copy in self.copies.values():
            copy.wait_send()


def reduce_space(name, width, own_buffer=True):
    half = width // 256 * 128
    space = [(name + N.crecv, (4, 4, 32, width), bf16)]
    if own_buffer:
        space.append((name + N.gbuf, (4, 4, 2, 32, width), bf16))
    for side, wide in ((N.a, half), (N.b, width - half)):
        space += [
            (name + N.far_ + side, (2, 2, 32, wide), bf16),
            (name + N.near_ + side, (2, 2, 2, 32, wide), bf16),
            (name + N.join_ + side, (2, 2, 32, wide), bf16),
            (name + N.one_ + side, (4, 32, wide), bf16),
            (name + N.late_ + side, (3, 32, wide), bf16),
        ]
    return space + [
        (name + N.core_sems, dma_sems(2, width // 256)),
        (name + N.ring_sems, dma_sems(4, 2, 6)),
    ]


class SmallSum:
    def __init__(self, e):
        self.sems = e.small_sems
        self.bufs = e.sm_core, e.sm_z, e.sm_y, e.sm_ctx, e.sm_tp
        self.y, self.z, self.core = place()
        self.all = []

    def spread_to(self, buf, at, first_sem, peers):
        self.last = [
            send(buf.at[at], buf.at[at], self.sems, first_sem + n, peer)
            for n, peer in enumerate(peers)
        ]
        self.all += self.last

    def wait(self):
        for copy in self.last:
            copy.wait_recv()

    def start(self, block):
        buf = self.bufs[0]
        buf[self.core] = block
        self.spread_to(buf, self.core, 0, torus_peers()[0:1])

    def along_z(self):
        self.wait()
        buf = self.bufs[1]
        buf[self.z] = self.bufs[0][0] + self.bufs[0][1]
        self.spread_to(buf, self.z, 1, torus_peers()[2:5])

    def along_y(self):
        self.wait()
        buf, old = self.bufs[2], self.bufs[1]
        buf[self.y] = (old[0] + old[1]) + (old[2] + old[3])
        self.spread_to(buf, self.y, 4, torus_peers()[5:8])

    def along_ctx(self):
        self.wait()
        ctx = lax.axis_index("ctx")
        buf, old = self.bufs[3], self.bufs[2]
        buf[ctx] = (old[0] + old[1]) + (old[2] + old[3])
        self.spread_to(buf, ctx, 7, torus_peers()[1:2])

    def along_tp(self):
        self.wait()
        tp = lax.axis_index("tp")
        self.bufs[4][tp] = self.bufs[3][0] + self.bufs[3][1]
        self.spread_to(self.bufs[4], tp, 8, [{"tp": 1 - tp}])

    def result(self):
        self.wait()
        own = self.bufs[4][lax.axis_index("tp")]
        both = self.bufs[4][0] + self.bufs[4][1]
        row = lax.broadcasted_iota(jnp.int32, (8, SMALL), 0)
        col = lax.broadcasted_iota(jnp.int32, (8, SMALL), 1)
        shared = ((row >= 4) & (col < CONV)) | ((col >= INNER) & (col < CONV))
        return jnp.where(shared, both, own)

    def close(self):
        for copy in self.all:
            copy.wait_send()


def column_of(row):
    r, c = head_matrix(32, 32)
    return jnp.sum(jnp.where(r == c, jnp.broadcast_to(row.astype(f32), (32, 32)), 0.0), axis=1, keepdims=True)


def pack_body(
    query, keyval, attn, inner, state, step, gain1, gain2, inner_o, gate_up, down, first, second
):
    first[:, C_Q : C_Q + QW] = query[...]
    lane = lax.broadcasted_iota(jnp.int32, (32, 128), 1)
    tail_cols = jnp.where(lane == HEADS, column_of(gain1[...]), 0.0)
    tail_cols = jnp.where(lane == HEADS + 1, column_of(gain2[...]), tail_cols)
    first[:, C_DT : C_DT + 128] = tail_cols.astype(bf16)
    first[:, C_DT : C_DT + HEADS] = step[...].astype(f32).T.astype(bf16)
    for i in range(2):
        first[:, C_KV + 64 * i : C_KV + 64 * i + 64] = keyval[:, i, :]
        first[:, C_Z + INNER * i : C_Z + INNER * (i + 1)] = inner[:, i, :]
        second[:, W2C + FFH * i : W2C + FFH * (i + 1)] = gate_up[:, i, :]
    first[:, BC0 : BC0 + 256] = state[...]
    second[:, 0:QW] = attn[...]
    second[:, QW:W2C] = inner_o[...]
    second[:, W2C + 2 * FFH :] = down[...]


def place_segments(e):
    seg, seg_ext, seg_row, wide = e.seg, e.seg_ext, e.seg_row, e.wide
    late = lax.axis_index("ctx")
    row = seg[...].astype(f32)
    wide[...] = jnp.broadcast_to(row, (128, 2 * TOK)).T
    own = pl.ds(pl.multiple_of(late * TOK, TOK), TOK)
    before = pl.ds(pl.multiple_of(late * (TOK - HALO), HALO), HALO)
    after = pl.ds(pl.multiple_of((1 - late) * TOK, TOK), 8)
    seg_ext[0:HALO, :] = jnp.where(late > 0, wide[before, :], -1.0)
    seg_ext[HALO : HALO + TOK, :] = wide[own, :]
    seg_ext[HALO + TOK :, :] = jnp.where(late > 0, -2.0, wide[after, :])
    seg_row[:, 0:TOK] = jnp.broadcast_to(jnp.where(late > 0, row[:, 0:TOK], -1.0), (8, TOK))
    seg_row[:, TOK:] = jnp.broadcast_to(seg[0:1, own].astype(f32), (8, TOK))


def forward_body(e):
    py, pz, core = place()
    late = lax.axis_index("ctx")
    ctx_peer = {"ctx": 1 - late}
    e.fetch(N.tok, N.cos, N.sin)
    pack_body(
        e.query, e.keyval, e.attn, e.inner, e.state, e.step_w, e.gain1, e.gain2, e.inner_o, e.gate_up,
        e.down_w, e.shard1, e.shard2,
    )
    e.w1[py, pz, core] = e.shard1[...]
    e.w2[py, pz, core] = e.shard2[:, 0:W2C]
    e.w3[py, pz, core] = e.shard2[:, W2C:]
    diagonal = {"ctx": 1 - late, "tp": 1 - lax.axis_index("tp")}
    greet(torus_peers() + [diagonal])
    one = Gather(e.w1, e.sems1, e.cross1)
    two = Gather(e.w2, e.sems2, e.cross2)
    three = Gather(e.w3, e.sems3, e.cross3)
    one.start()
    mine3 = e.w3.at[py, pz, core]
    shard_copy = send(mine3, e.shard_x, e.ctx_sems, 2, diagonal)
    tok = e.need(N.tok)
    tok_copy = send(tok.at[TOK - HALO : TOK], e.prior, e.ctx_sems, 0, ctx_peer)
    e.unit[...] = unit_rows(tok[...].astype(f32))[0]
    e.unit_t[...] = e.unit[...].T
    one.turn()
    two.start()
    place_segments(e)
    taps, hp, skip = e.taps, e.hp, e.skip
    taps[...] = jnp.zeros_like(taps)
    taps[0:4, 0:INNER] = e.taps_i[...].astype(f32)
    taps[0:4, INNER:] = e.taps_s[...].astype(f32)
    hp[...] = jnp.zeros_like(hp)
    hp[0:1, 0:HEADS] = e.step_bias[...]
    hp[1:2, 0:HEADS] = -jnp.exp(e.decay_log[...])
    hp[2:3, 0:HEADS] = e.skip_gain[...]
    skip[...] = spread(jnp.broadcast_to(hp[2:3, :], (8, 128)))
    e.store(N.seg_ext, N.seg_row, N.taps, N.hp)
    one.forward()
    two.turn()
    three.start()
    tok_copy.wait_recv()
    one.finish()
    one.arrived()
    e.store(N.w1)
    w1, normed, norm_p = e.w1, e.normed, e.norm_p

    def columns(at, size):
        return w1[:, :, :, :, at].reshape(WID, size)

    flipped = columns(slice(C_DT, C_DT + 128), 128).astype(f32).T
    e.gains[...] = flipped[8:16, :]
    g = flipped[HEADS : HEADS + 1, :]
    normed[...] = (e.unit[...] * g).astype(bf16)
    norm_p[...] = (unit_rows(e.prior[...].astype(f32))[0] * g).astype(bf16)
    e.normed_t[...] = (e.unit_t[...] * columns(slice(C_DT, C_DT + 128), 128)[:, HEADS : HEADS + 1].astype(f32)).astype(bf16)
    e.store(N.normed_t, N.gains)
    own = pl.ds(pl.multiple_of(late * TOK, TOK), TOK)
    lin = nn(normed[...], columns(slice(0, 256), 256))
    e.need(N.cos, N.sin)
    c, s = e.cos[own, :], e.sin[own, :]
    for i in range(2):
        cols = slice(128 * i, 128 * i + 128)
        e.q[:, cols] = turned(lin[:, cols], c, s).astype(bf16)
    low = low_half((TOK, 128))

    def pair(both, kk, vv):
        other = pltpu.roll(both, 64, 1)
        kk[...] = jnp.where(low, both, other).astype(bf16)
        vv[...] = jnp.where(low, other, both).astype(bf16)

    lin = nn(normed[...], columns(slice(256, 512), 256))
    both = jnp.where(low, turned(lin[:, 0:128], c, s), lin[:, 0:128])
    e.kv[...] = both.astype(bf16)
    kv_copy = send(e.kv, e.kv_prior, e.ctx_sems, 3, ctx_peer)
    pair(both, e.k2, e.v2)
    e.step[...] = lin[:, 128:256]
    e.store(N.q, N.k2, N.v2, N.step)
    two.forward()

    @pl.loop(0, 4)
    def _(j):
        at = pl.ds(pl.multiple_of(C_U + j * 256, 256), 256)
        to = pl.ds(pl.multiple_of(j * 256, 256), 256)
        block = columns(at, 256)
        e.cin[0:HALO, to] = nn(norm_p[...], block)
        e.cin[HALO : HALO + TOK, to] = nn(normed[...], block)

    e.store(N.cin)
    three.turn()
    mixer_in_body(
        e.cin, taps, e.step, hp.at[0:1], hp.at[1:2], e.seg_ext, e.pre, e.dt, e.cum, e.last
    )
    state_copy = send(e.last, e.first, e.ctx_sems, 1, ctx_peer)
    e.store(N.pre, N.dt, N.cum)

    @pl.loop(0, 3)
    def _(j):
        at = pl.ds(pl.multiple_of(C_Z + j * 256, 256), 256)
        to = pl.ds(pl.multiple_of(j * 256, 256), 256)
        e.z[:, to] = nn(normed[...], columns(at, 256))

    e.store(N.z)
    kv_copy.wait_recv()
    pair(e.kv_prior[...].astype(f32), e.k2p, e.v2p)
    e.store(N.k2p, N.v2p)
    attend_body(
        e.q, e.k2, e.v2, e.k2p, e.v2p, e.seg_ext.at[HALO : HALO + TOK], e.seg_row,
        e.mixed.at[:, 0:QW], e.lse,
    )
    e.store(N.lse)
    two.finish()
    three.near()
    shard_copy.wait_recv()
    e.store(N.shard_x)
    state_copy.wait_recv()
    e.sc_state[...] = jnp.where(late > 0, e.first[...].astype(f32), 0.0)
    mixer_out_body(
        e.pre, e.dt, e.cum, e.seg_ext, e.seg_row, None, e.z, skip.at[0:1], e.y,
        e.mixed.at[:, QW:], e.states, e.sc_state,
    )
    e.store(N.mixed, N.y, N.states)
    two.arrived()
    e.store(N.w2)
    three.arrived()
    for n in (0, 1, 3):
        e.store_part(N.w3, lambda ref: three.rows(ref, n))
        e.store_part(N.w3, lambda ref: three.planes(ref, n))
    three.close()
    one.close()
    two.close()
    tok_copy.wait_send()
    shard_copy.wait_send()
    kv_copy.wait_send()
    state_copy.wait_send()
    e.settle()


FORWARD_OUTS = [
    (N.w1, (4, 4, 2, 32, W1C), bf16),
    (N.w2, (4, 4, 2, 32, W2C), bf16),
    (N.w3, (4, 4, 2, 32, W3C), bf16),
    (N.normed_t, (WID, TOK), bf16),
    (N.q, (TOK, QW), bf16),
    (N.k2, (TOK, 128), bf16),
    (N.v2, (TOK, 128), bf16),
    (N.k2p, (TOK, 128), bf16),
    (N.v2p, (TOK, 128), bf16),
    (N.z, (TOK, INNER), f32),
    (N.cin, (HALO + TOK, CONV), f32),
    (N.step, (TOK, 128), f32),
    (N.gains, (8, WID), f32),
    (N.pre, (TOK, CONV), f32),
    (N.dt, (TOK, 128), f32),
    (N.cum, (TOK, 128), f32),
    (N.states, (SPANS, STATE, INNER), bf16),
    (N.y, (TOK, INNER), f32),
    (N.mixed, (TOK, QW + INNER), bf16),
    (N.lse, (TOK, 128), f32),
    (N.seg_ext, (HALO + TOK + 8, 128), f32),
    (N.seg_row, (8, 2 * TOK), f32),
    (N.taps, (8, CONV), f32),
    (N.hp, (8, 128), f32),
    (N.shard_x, (32, W3C), bf16),
]


def forward(ins):
    hbm = (N.tok, N.cos, N.sin)
    outs = run(
        forward_body,
        [(n, a, n in hbm) for n, a in ins.items()],
        [(n, s, d, True) for n, s, d in FORWARD_OUTS],
        FORWARD_OUTS
        + [
            (N.tok, (TOK, WID), bf16),
            (N.cos, (2 * TOK, 128), f32),
            (N.sin, (2 * TOK, 128), f32),
            (N.prior, (HALO, WID), bf16),
            (N.norm_p, (HALO, WID), bf16),
            (N.normed, (TOK, WID), bf16),
            (N.unit, (TOK, WID), f32),
            (N.unit_t, (WID, TOK), f32),
            (N.kv, (TOK, 128), bf16),
            (N.kv_prior, (TOK, 128), bf16),
            (N.wide, (2 * TOK, 128), f32),
            (N.last, (STATE, INNER), bf16),
            (N.first, (STATE, INNER), bf16),
            (N.skip, (8, INNER), f32),
            (N.sc_state, (STATE, INNER), f32),
            (N.shard1, (32, W1C), bf16),
            (N.shard2, (32, W2C + W3C), bf16),
            (N.sems1, dma_sems(4, 2, 4)),
            (N.cross1, dma_sems(2, 8)),
            (N.sems2, dma_sems(4, 2, 4)),
            (N.cross2, dma_sems(2, 8)),
            (N.sems3, dma_sems(4, 2, 4)),
            (N.cross3, dma_sems(2, 8)),
            (N.ctx_sems, dma_sems(2, 4)),
        ],
        1,
    )
    return dict(zip([n for n, _, _ in FORWARD_OUTS], outs))


SENT = 128
CHUNK = 256
CHUNKS = TOK // CHUNK


def middle_body(e):
    py, pz, core = place()
    tp_peer = {"tp": 1 - lax.axis_index("tp")}
    load_x = pltpu.make_async_copy(e.h_shard_x, e.w3x.at[py, pz, core], e.own_sems.at[0])
    load_x.start()
    e.fetch(N.w2, N.mixed)
    mine = Gather(e.w3, e.mine_sems, e.mine_cross)
    parts = [part(ref, n) for n in (1, 3, 0) for part in (mine.rows, mine.planes) for ref in (e.h_w3, e.w3)]
    loads = [
        pltpu.make_async_copy(a, b, e.own_sems.at[1 + n])
        for n, (a, b) in enumerate(zip(parts[0::2], parts[1::2]))
    ]
    for load in loads:
        load.start()
    greet(torus_peers() + [tp_peer])
    other = Gather(e.w3x, e.gather_sems, e.cross_sems)
    load_x.wait()
    other.start()
    for load in loads[0:4]:
        load.wait()
    mine.far()
    part, part_back = e.part, e.part_back
    normed2, dact, mid, dn, down = e.normed2, e.dact, e.mid, e.dn, e.down

    w2, mixed = e.need(N.w2), e.need(N.mixed)
    e.fetch(N.cot, N.gains, N.tok)
    copies = []
    for c in range(TOK // SENT):
        rows = slice(c * SENT, (c + 1) * SENT)
        part[rows, :] = nt(mixed[rows, :], w2[...].reshape(WID, W2C)).astype(bf16)
        copies.append(send(part.at[rows], part_back.at[rows], e.sems, c, tp_peer))
    tok, cot, gains = e.need(N.tok), e.need(N.cot), e.need(N.gains)
    e.cot_t[...] = cot[...].astype(f32).T.astype(bf16)
    gain = gains[HEADS + 1 - 8 : HEADS + 2 - 8, :]
    other.turn()
    mine.finish()
    for load in loads[4:]:
        load.wait()
    mine.arrived()

    def cols(w, at, size):
        return w[:, :, :, :, at].reshape(WID, size)

    def rows_at(c):
        return slice(c * CHUNK, (c + 1) * CHUNK)

    def hidden_back(w):
        @pl.loop(0, FFH // 256)
        def _(j):
            at = pl.ds(pl.multiple_of(2 * FFH + j * 256, 256), 256)
            to = pl.ds(pl.multiple_of(j * 256, 256), 256)
            dact[:, to] = nn(cot[...], cols(w, at, 256))

    def swiglu(w, act, dgu, rows):
        @pl.loop(0, FFH // 256)
        def _(j):
            at = pl.ds(pl.multiple_of(j * 256, 256), 256)
            at_up = pl.ds(pl.multiple_of(FFH + j * 256, 256), 256)
            gate = nn(normed2[rows, :], cols(w, at, 256))
            up = nn(normed2[rows, :], cols(w, at_up, 256))
            sig = sigmoid(gate)
            silu = gate * sig
            da = dact[rows, at]
            act[rows, at] = (silu * up).astype(bf16)
            dgu[rows, at] = (da * up * (sig + silu * (1.0 - sig))).astype(bf16)
            dgu[rows, at_up] = (da * silu).astype(bf16)

    def out_products(w, act, dgu, rows, first):
        @pl.loop(0, 4)
        def _(j):
            to = pl.ds(pl.multiple_of(j * 256, 256), 256)
            a = nt(dgu[rows, :], w[j, :, :, :, 0 : 2 * FFH].reshape(256, 2 * FFH))
            b = nt(act[rows, :], w[j, :, :, :, 2 * FFH :].reshape(256, FFH))
            dn[rows, to] = a if first else dn[rows, to] + a
            down[rows, to] = b if first else down[rows, to] + b

    hidden_back(e.w3)
    for c in range(CHUNKS):
        rows = rows_at(c)
        for part_copy in copies[c * CHUNK // SENT : (c + 1) * CHUNK // SENT]:
            part_copy.wait_recv()
        m = tok[rows, :].astype(f32) + (part[rows, :].astype(f32) + part_back[rows, :].astype(f32))
        mid[rows, :] = m
        normed2[rows, :] = (unit_rows(m)[0] * gain).astype(bf16)
        swiglu(e.w3, e.act, e.dgu, rows)
        out_products(e.w3, e.act, e.dgu, rows, True)
        if c == 0:
            other.forward()
    other.finish()
    e.normed2_t[...] = normed2[...].astype(f32).T.astype(bf16)

    @pl.loop(0, FFH // 256)
    def _(j):
        at = pl.ds(pl.multiple_of(j * 256, 256), 256)
        to = pl.ds(pl.multiple_of(2 * FFH + j * 256, 256), 256)
        e.w3_grad[:, :, :, :, to] = nn(e.cot_t[...], e.act[:, at]).astype(bf16).reshape(4, 4, 2, 32, 256)

    @pl.loop(0, 2 * FFH // 256)
    def _(j):
        at = pl.ds(pl.multiple_of(j * 256, 256), 256)
        block = nn(e.normed2_t[...], e.dgu[:, at]).astype(bf16)
        e.w3_grad[:, :, :, :, at] = block.reshape(4, 4, 2, 32, 256)

    e.store(N.w3_grad)
    other.arrived()
    hidden_back(e.w3x)
    taken = jnp.zeros((1, WID), f32)
    swiglu(e.w3x, e.act_x, e.dgu_x, slice(0, TOK))
    out_products(e.w3x, e.act_x, e.dgu_x, slice(0, TOK), False)
    for c in range(CHUNKS):
        rows = rows_at(c)
        e.block_out[rows, :] = (mid[rows, :] + down[rows, :]).astype(bf16)
        dh = dn[rows, :]
        unit, r = unit_rows(mid[rows, :])
        taken = taken + jnp.sum(dh * unit, axis=0, keepdims=True)
        scaled = dh * gain
        g = cot[rows, :].astype(f32) + r * (
            scaled - unit * jnp.mean(unit * scaled, axis=1, keepdims=True)
        )
        e.grad_mid[rows, :] = g
        e.dmix[rows, :] = g.astype(bf16)
    e.dgain2[...] = jnp.broadcast_to(taken, (8, WID))
    e.store(N.dmix, N.grad_mid, N.dgain2, N.block_out)
    mine.close()
    other.close()
    for copy in copies:
        copy.wait_send()
    e.settle()


MIDDLE_OUTS = [
    (N.block_out, (TOK, WID), bf16),
    (N.grad_mid, (TOK, WID), f32),
    (N.dmix, (TOK, WID), bf16),
    (N.w3_grad, (4, 4, 2, 32, W3C), bf16),
    (N.dgain2, (8, WID), f32),
]


def middle(ins):
    outs = run(
        middle_body,
        [(n, a, True) for n, a in ins.items()],
        [(n, s, d, True) for n, s, d in MIDDLE_OUTS],
        MIDDLE_OUTS
        + [
            (N.w2, (4, 4, 2, 32, W2C), bf16),
            (N.w3, (4, 4, 2, 32, W3C), bf16),
            (N.w3x, (4, 4, 2, 32, W3C), bf16),
            (N.mixed, (TOK, WID), bf16),
            (N.gains, (8, WID), f32),
            (N.tok, (TOK, WID), bf16),
            (N.cot, (TOK, WID), bf16),
            (N.part, (TOK, WID), bf16),
            (N.part_back, (TOK, WID), bf16),
            (N.mid, (TOK, WID), f32),
            (N.dn, (TOK, WID), f32),
            (N.down, (TOK, WID), f32),
            (N.normed2, (TOK, WID), bf16),
            (N.normed2_t, (WID, TOK), bf16),
            (N.cot_t, (WID, TOK), bf16),
            (N.act, (TOK, FFH), bf16),
            (N.dgu, (TOK, 2 * FFH), bf16),
            (N.act_x, (TOK, FFH), bf16),
            (N.dgu_x, (TOK, 2 * FFH), bf16),
            (N.dact, (TOK, FFH), f32),
            (N.sems, dma_sems(2, TOK // SENT)),
            (N.own_sems, dma_sems(7)),
            (N.mine_sems, dma_sems(4, 2, 4)),
            (N.mine_cross, dma_sems(2, 8)),
            (N.gather_sems, dma_sems(4, 2, 4)),
            (N.cross_sems, dma_sems(2, 8)),
        ],
        2,
    )
    return dict(zip([n for n, _, _ in MIDDLE_OUTS], outs))


EARLY = W2C + INNER + QW
LATE = CONV + 256


def conv_back(ext, taps, seg_ext, cin, grads):
    run = jnp.zeros((TOK, CONV), f32)
    now = seg_ext[HALO : HALO + TOK, 0:1]
    sub = lax.broadcasted_iota(jnp.int32, (8, CONV), 0)
    taken = jnp.zeros((8, CONV), f32)
    for k in range(4):
        ahead = 3 - k
        same = jnp.where(seg_ext[HALO + ahead : HALO + ahead + TOK, 0:1] == now, 1.0, 0.0)
        run = run + ext[ahead : ahead + TOK, :] * taps[k : k + 1, :] * same
        at = HALO - 3 + k
        part = ext[0:TOK, :] * cin[at : at + TOK, :] * tap_mask(seg_ext, k)
        taken = taken + jnp.where(sub == k, jnp.sum(part, axis=0, keepdims=True), 0.0)
    grads[:, C_U:] = run.astype(bf16)
    return taken


def backward_body(e):
    py, pz, core = place()
    ctx, tp = lax.axis_index("ctx"), lax.axis_index("tp")
    ctx_peer, tp_peer = {"ctx": 1 - ctx}, {"tp": 1 - tp}
    own_rows = pl.ds(pl.multiple_of(ctx * TOK, TOK), TOK)
    half3 = W3C // 2
    e.fetch(N.w2)
    e.fetch(N.dmix)
    greet(torus_peers() + [tp_peer])
    sum3 = Reduce(e, N.s3_, e.fin_three)
    early = Reduce(e, N.se_, e.fin_early)
    tail = Reduce(e, N.sl_, e.fin_late)
    small = SmallSum(e)
    core3 = send(e.h_w3_grad.at[:, :, 1 - core], sum3.crecv, sum3.core_sems, 0, sum3.sibling)
    grads = e.grads

    w2, dmix = e.need(N.w2), e.need(N.dmix)
    e.fetch(N.z, N.y, N.pre, N.cum, N.seg_ext)
    e.fetch(N.q, N.k2, N.v2, N.k2p, N.v2p, N.seg_row, N.lse)
    e.fetch_from(N.cos, e.h_cos.at[own_rows])
    e.fetch_from(N.sin, e.h_sin.at[own_rows])
    e.fetch_from(N.own3, e.h_w3_grad.at[:, :, core, :, 0:half3])

    @pl.loop(0, INNER // 256)
    def _(j):
        at = pl.ds(pl.multiple_of(QW + j * 256, 256), 256)
        to = pl.ds(pl.multiple_of(j * 256, 256), 256)
        e.dgated[:, to] = nn(dmix[...], w2[:, :, :, :, at].reshape(WID, 256))

    e.need(N.z, N.y, N.pre, N.cum, N.seg_ext)
    mixer_back_in_body(
        e.dgated, e.z, e.y, e.pre, e.cum, e.seg_ext, e.dgated, grads.at[:, C_Z : C_Z + INNER], e.dfirst
    )
    state_copy = send(e.dfirst, e.dlast, e.ctx_sems, 0, ctx_peer)
    e.fetch(N.hp, N.dt, N.states, N.step, N.taps, N.cin, N.mixed, N.normed_t, N.w1, N.tok, N.gains, N.dgain2)
    e.need(N.q, N.k2, N.v2, N.k2p, N.v2p, N.seg_row, N.lse, N.cos, N.sin)

    def add_half(first):
        for j in range(half3 // 512):
            at = slice(j * 512, (j + 1) * 512)
            cols = slice(first + j * 512, first + (j + 1) * 512)
            total = e.own3[:, :, :, at].astype(f32) + sum3.crecv[:, :, :, cols].astype(f32)
            sum3.crecv[:, :, :, cols] = total.astype(bf16)

    e.need(N.own3)
    core3.wait_recv()
    add_half(0)
    e.fetch_from(N.own3, e.h_w3_grad.at[:, :, core, :, half3:])
    sum3.a.start()
    e.datt[...] = nn(dmix[...], w2[:, :, :, :, 0:QW].reshape(WID, QW)).astype(bf16)
    e.need(N.own3)
    add_half(half3)
    sum3.b.start()
    attend_back_body(
        e.q, e.k2, e.v2, e.k2p, e.v2p, e.seg_ext.at[HALO : HALO + TOK], e.seg_row, e.lse, e.datt,
        e.cos, e.sin, grads.at[:, C_Q : C_Q + QW], e.dkv, e.dkv_p, e.dk_s, e.dv_s, e.dkp_s, e.dvp_s,
        between={1: sum3.forward},
    )
    kv_copy = send(e.dkv_p, e.dkv_back, e.ctx_sems, 1, ctx_peer)
    state_copy.wait_recv()
    e.sc_state[...] = jnp.where(ctx > 0, 0.0, e.dlast[...].astype(f32))
    e.need(N.hp, N.dt, N.states, N.step)
    e.skip[...] = spread(jnp.broadcast_to(e.hp[2:3, :], (8, 128)))
    heads = mixer_back_body(
        e.dgated, e.pre, e.dt, e.cum, e.seg_ext, e.seg_row, e.states, None, e.skip.at[0:1],
        e.hp.at[1:2], e.step, e.hp.at[0:1], e.ext, grads.at[:, C_DT : C_DT + 128], None, e.sc_state,
    )
    rim_copy = send(e.ext.at[0:8], e.rim, e.ctx_sems, 2, ctx_peer)
    e.dmix_t[...] = dmix[...].astype(f32).T.astype(bf16)
    normed_t = e.need(N.normed_t)
    e.need(N.mixed)
    for j in range(2):
        early.piece(j, nn(e.dmix_t[...], e.mixed[:, j * 256 : (j + 1) * 256]))
    kv_copy.wait_recv()
    low = low_half((TOK, 128))
    both = e.dkv[...] + jnp.where(ctx > 0, 0.0, e.dkv_back[...].astype(f32))
    grads[:, C_KV : C_KV + 128] = jnp.where(low, turned(both, e.cos[...], -e.sin[...]), both).astype(bf16)
    e.need(N.taps, N.cin)
    rim_copy.wait_recv()
    e.ext[TOK : TOK + 8, :] = jnp.where(ctx > 0, 0.0, e.rim[...])
    dtaps = conv_back(e.ext, e.taps, e.seg_ext, e.cin, grads)
    rim_copy.wait_send()
    late = e.ext.at[0:TOK]
    late_load = pltpu.make_async_copy(e.h_grad_mid, late, e.own_sems.at[0])
    late_load.start()

    def rows_at(c):
        return slice(c * TOK // 4, (c + 1) * TOK // 4)

    w1 = e.need(N.w1)
    dn_copies = []

    def dn_part(c):
        rows = rows_at(c)

        @pl.loop(0, 4)
        def _(j):
            to = pl.ds(pl.multiple_of(j * 256, 256), 256)
            e.dn[rows, to] = nt(grads[rows, :], w1[j].reshape(256, W1C)).astype(bf16)

        dn_copies.append(send(e.dn.at[rows], e.dn_back.at[rows], e.dn_sems, c, tp_peer))

    dn_part(0)
    for j in (2, 3):
        early.piece(j, nn(e.dmix_t[...], e.mixed[:, j * 256 : (j + 1) * 256]))
    for j in range(3):
        at = C_Z + j * 256
        early.piece(4 + j, nn(normed_t[...], grads[:, at : at + 256]))
    early.piece(7, nn(normed_t[...], grads[:, 0:QW]))
    for j in range(8):
        early.add(j)
    early.start()
    sum3.turn()
    dn_part(1)
    for j in range(4):
        at = C_U + j * 256
        tail.piece(j, nn(normed_t[...], grads[:, at : at + 256]))
    tail.piece(4, nn(normed_t[...], grads[:, 256:512]))
    dn_part(2)
    for j in range(5):
        tail.add(j)
    tail.start()
    early.forward()
    dn_part(3)
    sum3.finish()
    three_copy = send(e.fin_three, e.fin_three_back, e.fin_sems, 3, ctx_peer)
    tok = e.need(N.tok)
    gains = e.need(N.gains)
    e.need(N.dgain2)
    gain = gains[HEADS - 8 : HEADS - 7, :]
    dgain1 = jnp.zeros((1, WID), f32)
    for c in range(4):
        rows = rows_at(c)
        unit = unit_rows(tok[rows, :].astype(f32))[0]
        dgain1 = dgain1 + jnp.sum(e.dn[rows, :].astype(f32) * unit, axis=0, keepdims=True)
    sub = lax.broadcasted_iota(jnp.int32, (8, WID), 0)
    gain_rows = jnp.where(sub == 4, dgain1, jnp.where(sub == 5, e.dgain2[0:1, :] * 0.5, dtaps))
    small.start(jnp.concatenate([gain_rows, heads], axis=1))
    tail.forward()
    early.turn()
    small.along_z()
    tail.turn()
    early.finish()
    fin_copy = send(e.fin_early, e.fin_early_back, e.fin_sems, 0, ctx_peer)
    small.along_y()
    tail.finish()
    late_copy = send(e.fin_late, e.fin_late_back, e.fin_sems, 1, ctx_peer)
    small.along_ctx()
    late_load.wait()
    for c in range(4):
        rows = rows_at(c)
        dn_copies[c].wait_recv()
        dh = (e.dn[rows, :].astype(f32) + e.dn_back[rows, :].astype(f32)) * gain
        unit, r = unit_rows(tok[rows, :].astype(f32))
        late[rows, :] = late[rows, :] + r * (dh - unit * jnp.mean(unit * dh, axis=1, keepdims=True))
    out_copy = pltpu.make_async_copy(late, e.h_tok_grad, e.own_sems.at[1])
    out_copy.start()
    small.along_tp()
    late_copy.wait_recv()
    total = e.fin_late[...].astype(f32) + e.fin_late_back[...].astype(f32)
    e.share[...] = total[:, INNER:CONV].astype(bf16)
    share_copy = send(e.share, e.share_back, e.fin_sems, 2, tp_peer)
    e.parts_late[...] = total
    three_copy.wait_recv()
    e.parts_early[:, 0:W3C] = e.fin_three[...].astype(f32) + e.fin_three_back[...].astype(f32)
    fin_copy.wait_recv()
    e.parts_early[:, W3C:] = e.fin_early[...].astype(f32) + e.fin_early_back[...].astype(f32)
    e.store(N.parts_early)
    e.sums[...] = small.result()
    share_copy.wait_recv()
    e.parts_late[:, INNER:CONV] = e.share[...].astype(f32) + e.share_back[...].astype(f32)
    e.store(N.parts_late, N.sums)

    out_copy.wait()
    core3.wait_send()
    for ring in (sum3, early, tail):
        ring.close()
    small.close()
    for copy in [state_copy, kv_copy, three_copy, fin_copy, late_copy, share_copy] + dn_copies:
        copy.wait_send()
    e.settle()


BACKWARD_OUTS = [
    (N.parts_early, (32, W3C + EARLY), f32),
    (N.parts_late, (32, LATE), f32),
    (N.sums, (8, SMALL), f32),
]


def backward(ins):
    same = [
        N.dmix, N.z, N.y, N.pre, N.cum, N.seg_ext, N.mixed, N.q, N.k2, N.v2, N.k2p, N.v2p,
        N.seg_row, N.lse, N.hp, N.dt, N.states, N.step, N.normed_t, N.taps, N.cin, N.tok, N.gains, N.dgain2,
    ]
    outs = run(
        backward_body,
        [(n, a, True) for n, a in ins.items()],
        [(n, s, d, True) for n, s, d in BACKWARD_OUTS] + [(N.tok_grad, (TOK, WID), f32, True)],
        BACKWARD_OUTS
        + [(n, ins[n].shape, ins[n].dtype) for n in same]
        + [
            (N.w2, (4, 4, 2, 32, W2C), bf16),
            (N.own3, (4, 4, 32, W3C // 2), bf16),
            (N.cos, (TOK, 128), f32),
            (N.sin, (TOK, 128), f32),
            (N.w1, (4, 4, 2, 32, W1C), bf16),
            (N.dgated, (TOK, INNER), f32),
            (N.datt, (TOK, QW), bf16),
            (N.dmix_t, (WID, TOK), bf16),
            (N.grads, (TOK, W1C), bf16),
            (N.dkv, (TOK, 128), f32),
            (N.dkv_p, (TOK, 128), bf16),
            (N.dkv_back, (TOK, 128), bf16),
            (N.dk_s, (TOK, 128), f32),
            (N.dv_s, (TOK, 128), f32),
            (N.dkp_s, (TOK, 128), f32),
            (N.dvp_s, (TOK, 128), f32),
            (N.dfirst, (STATE, INNER), bf16),
            (N.dlast, (STATE, INNER), bf16),
            (N.skip, (8, INNER), f32),
            (N.sc_state, (STATE, INNER), f32),
            (N.ext, (TOK + 8, CONV), f32),
            (N.rim, (8, CONV), f32),
            (N.dn, (TOK, WID), bf16),
            (N.dn_back, (TOK, WID), bf16),
            (N.fin_three, (32, W3C), bf16),
            (N.fin_three_back, (32, W3C), bf16),
            (N.fin_early, (32, EARLY), bf16),
            (N.fin_early_back, (32, EARLY), bf16),
            (N.fin_late, (32, LATE), bf16),
            (N.fin_late_back, (32, LATE), bf16),
            (N.share, (32, CONV - INNER), bf16),
            (N.share_back, (32, CONV - INNER), bf16),
            (N.sm_core, (2, 8, SMALL), f32),
            (N.sm_z, (4, 8, SMALL), f32),
            (N.sm_y, (4, 8, SMALL), f32),
            (N.sm_ctx, (2, 8, SMALL), f32),
            (N.sm_tp, (2, 8, SMALL), f32),
            (N.small_sems, dma_sems(2, 9)),
            (N.ctx_sems, dma_sems(2, 3)),
            (N.dn_sems, dma_sems(2, 4)),
            (N.fin_sems, dma_sems(2, 4)),
            (N.own_sems, dma_sems(3)),
        ]
        + reduce_space(N.s3_, W3C, own_buffer=False)
        + reduce_space(N.se_, EARLY)
        + reduce_space(N.sl_, LATE),
        0,
    )
    return dict(zip([n for n, _, _ in BACKWARD_OUTS] + [N.tok_grad], outs))


def outputs_body(
    early, late, sums, block_in, tok_in,
    gain1, gain2, query, keyval, attn, inner, state, step, conv_i, conv_s, decay, bias, skip,
    inner_o, gate_up, down, block_out, tok_out, tok_held, block_held, sems,
):
    passes = ((tok_in, tok_held, tok_out), (block_in, block_held, block_out))
    loads = [pltpu.make_async_copy(a, b, sems.at[0, n]) for n, (a, b, _) in enumerate(passes)]
    copies = [pltpu.make_async_copy(b, c, sems.at[1, n]) for n, (_, b, c) in enumerate(passes)]
    for load in loads:
        load.start()
    for load, copy in zip(loads, copies):
        load.wait()
        copy.start()
    gains = pltpu.roll(sums[:, 0:WID], lax.rem(WID - 32 * lax.axis_index("fsdp"), WID), 1)
    gain1[...] = gains[4:5, 0:32]
    gain2[...] = gains[5:6, 0:32]
    step[...] = late[:, LATE - 128 :].T[0:HEADS, :]
    at2 = W3C
    query[...] = early[:, at2 + W2C + INNER :]
    for i in range(2):
        at = CONV + 64 * i
        keyval[:, i, :] = late[:, at : at + 64]
        gate_up[:, i, :] = early[:, FFH * i : FFH * (i + 1)]
    inner[:, 0, :] = early[:, at2 + W2C : at2 + W2C + INNER]
    inner[:, 1, :] = late[:, 0:INNER]
    state[...] = late[:, INNER:CONV]
    attn[...] = early[:, at2 : at2 + QW]
    inner_o[...] = early[:, at2 + QW : at2 + W2C]
    down[...] = early[:, 2 * FFH : 3 * FFH]
    conv_i[...] = sums[0:4, 0:INNER]
    conv_s[...] = sums[0:4, INNER:CONV]
    for n, ref in enumerate((decay, bias, skip)):
        ref[...] = sums[n : n + 1, CONV : CONV + HEADS]
    for copy in copies:
        copy.wait()


OUTPUTS = [
    ((1, 32), f32),
    ((1, 32), f32),
    ((32, QW), f32),
    ((32, 2, 64), f32),
    ((32, QW), f32),
    ((32, 2, INNER), f32),
    ((32, 256), f32),
    ((HEADS, 32), f32),
    ((4, INNER), f32),
    ((4, CONV - INNER), f32),
    ((1, HEADS), f32),
    ((1, HEADS), f32),
    ((1, HEADS), f32),
    ((32, INNER), f32),
    ((32, 2, FFH), f32),
    ((32, FFH), f32),
    ((TOK, WID), bf16),
    ((TOK, WID), f32),
]


def outputs(*args):
    any_spec = pl.BlockSpec(memory_space=pl.ANY)
    return pl.pallas_call(
        outputs_body,
        out_shape=[jax.ShapeDtypeStruct(s, d) for s, d in OUTPUTS],
        in_specs=vmem(3) + [any_spec] * 2,
        out_specs=vmem(16) + [any_spec] * 2,
        scratch_shapes=[pltpu.VMEM((TOK, WID), f32), pltpu.VMEM((TOK, WID), bf16), dma_sems(2, 2)],
        compiler_params=pltpu.CompilerParams(vmem_limit_bytes=61 * 1024 * 1024),
    )(*args)


def rope_tables():
    indices = np.arange(HEAD_WIDTH // 2, dtype=np.float32)
    frequency = np.exp(indices * np.float32(-2.0 * math.log(ROPE_BASE) / HEAD_WIDTH))
    angles = np.arange(2 * TOK, dtype=np.float32)[:, None] * frequency[None, :].astype(np.float32)
    angles = angles.astype(np.float64)
    return tuple(np.tile(t(angles), (1, 4)).astype(np.float32) for t in (np.cos, np.sin))


def shards(
    tokens, segments, cotangent, gain_mixer, gain_ffn, query_proj, key_value_weight, attn_out,
    inner_proj, state_proj, step_proj, conv_inner, conv_state, decay_log, step_bias, skip_gain,
    inner_out, gate_up, down_proj,
):
    rows = query_proj.shape[0]
    tok = tokens.reshape(TOK, WID)
    cot = cotangent.reshape(TOK, WID)
    cos, sin = (jnp.asarray(t) for t in rope_tables())
    kept = forward(
        dict(
            query=query_proj, keyval=key_value_weight, attn=attn_out.T, inner=inner_proj, state=state_proj,
            step_w=step_proj.T, gain1=gain_mixer.reshape(1, rows), gain2=gain_ffn.reshape(1, rows),
            inner_o=inner_out.T, gate_up=gate_up, down_w=down_proj.T, tok=tok, cos=cos, sin=sin, seg=segments,
            taps_i=conv_inner, taps_s=conv_state, step_bias=step_bias.reshape(1, HEADS),
            decay_log=decay_log.reshape(1, HEADS), skip_gain=skip_gain.reshape(1, HEADS),
        )
    )
    kept |= dict(tok=tok, cos=cos, sin=sin)
    between = middle({n: kept[n] for n in (N.w2, N.w3, N.shard_x, N.mixed, N.gains, N.tok)} | dict(cot=cot))
    block_out = between.pop(N.block_out)
    del kept[N.shard_x], kept[N.w3]
    done = backward(kept | between)
    *out, block_out, tok_grad = outputs(
        done[N.parts_early], done[N.parts_late], done[N.sums], block_out, done[N.tok_grad]
    )
    forms = [(rows,)] * 2 + [None] * 2 + ["T"] + [None] * 2 + ["T"] + [None] * 2
    forms += [(HEADS,)] * 3 + ["T", None, "T"]
    out = [a if f is None else a.T if f == "T" else a.reshape(f) for a, f in zip(out, forms)]
    return (block_out[None], tok_grad[None], *out)


def solution(mesh):
    return jax.shard_map(
        shards,
        mesh=mesh,
        in_specs=(
            P("fsdp", "ctx", None), P("fsdp", None), P("fsdp", "ctx", None), P("fsdp"), P("fsdp"),
            P("fsdp", "tp"), P("fsdp", None, "tp"), P("tp", "fsdp"), P("fsdp", None, "tp"),
            P("fsdp", None), P("fsdp", "tp"), P(None, "tp"), P(), P("tp"), P("tp"), P("tp"),
            P("tp", "fsdp"), P("fsdp", None, "tp"), P("tp", "fsdp"),
        ),
        out_specs=(
            P("fsdp", "ctx", None), P("fsdp", "ctx", None), P("fsdp"), P("fsdp"), P("fsdp", "tp"),
            P("fsdp", None, "tp"), P("tp", "fsdp"), P("fsdp", None, "tp"), P("fsdp", None),
            P("fsdp", "tp"), P(None, "tp"), P(), P("tp"), P("tp"), P("tp"), P("tp", "fsdp"),
            P("fsdp", None, "tp"), P("tp", "fsdp"),
        ),
        check_vma=False,
    )
```
